32 devices in a mesh: seq: 8 (over z, x), tensor: 4 (over y, core).
Axes of the slice: x: 2, y: 2, z: 4, core: 2. Of those that a mesh axis runs over, the one named last changes fastest.
Arguments:
- tokens: bfloat16 [4096, 4096], P('seq', 'tensor'), may hold values from -6 to 6
- w_query: bfloat16 [4096, 2048], P(None, 'tensor'), may hold values from -0.09375 to 0.09375
- w_key: bfloat16 [4096, 2048], P(None, 'tensor'), may hold values from -0.09375 to 0.09375
- w_value: bfloat16 [4096, 4096], P(None, 'tensor'), may hold values from -0.09375 to 0.09375
- w_outgate: bfloat16 [4096, 4096], P(None, 'tensor'), may hold values from -0.09375 to 0.09375
- w_gates: bfloat16 [2, 4096, 8], P(None, None, 'tensor'), may hold values from -0.09375 to 0.09375
- gate_bias: float32 [2, 8], P(None, 'tensor'), may hold values from -2 to 78, as said below
- w_out: bfloat16 [4096, 4096], P('tensor'), may hold values from -0.09375 to 0.09375
- carry_matrix: float32 [8, 256, 512], P('tensor'), may hold values from -6 to 6
- carry_norm: float32 [8, 256], P('tensor'), may hold values from -6 to 6
- carry_max: float32 [8], P('tensor'), may hold values from 0 to 78
- doc_lengths: int32 [4], replicated, may hold values from 1 to 2048, 4096 in all
Outputs:
- layer_out: bfloat16 [4096, 4096], P('seq', 'tensor')
The draws below stay inside these ranges and needn't reach their ends.
Inputs may be any that keep to these rules, and one draw needn't show every extreme that they name: `doc_lengths`: the 4 lengths sum to 4096; the longest is exactly 2048. `gate_bias`: row 0 holds the input gates' biases, row 1 the forget gates' biases.
All inputs are finite; a program needn't handle non-finite values.
Results may differ from the reference program's by a relative error of at most 0.014.
Values may be sent and summed in bfloat16 or wider, within the bound.
No kernel may reach another device: no remote copies, remote signals or barrier semaphores. Data moves between devices by JAX's collectives and lax.ppermute only.
A program may use at most 128 MiB of HBM per device.

```python
import math
import jax
import jax.numpy as jnp
import numpy as np
from jax import lax

D = 4096
H = 8
QK = 256
V = 512
TOK_DEV = 512
NDOCS = 4
TOKENS = 4096
HEADS_DEV = 2
N_TENSOR = 4


def draw_gate_bias(key, part):
    slow_share = 0.5
    key = jax.random.fold_in(key, 1)
    streams = jax.random.split(key, 4)
    input_bias = jax.random.uniform(streams[0], (H,), minval=-2.0, maxval=2.0)
    slow_rate = jnp.exp(jax.random.uniform(streams[1], (H,), minval=jnp.log(0.05 / TOKENS), maxval=jnp.log(0.5 / TOKENS)))
    fast_rate = jnp.exp(jax.random.uniform(streams[2], (H,), minval=jnp.log(1.0 / 50.0), maxval=jnp.log(1.0 / 30.0)))
    chosen = jax.random.uniform(streams[3], (H,)) < slow_share
    rate = jnp.where(chosen, slow_rate, fast_rate)
    forget_bias = jnp.log1p(-rate) - jnp.log(rate)
    return jnp.stack([input_bias, forget_bias]).astype(jnp.float32)


def draw_carry_max(key, part):
    key = jax.random.fold_in(key, 2)
    return jax.random.uniform(key, (H,), minval=0.0, maxval=3.0).astype(jnp.float32)


def block_scale(stream_key, extent, shards, least, largest):
    gain = 1.0
    for dim, blocks in shards:
        draws = jax.random.uniform(jax.random.fold_in(jax.random.fold_in(stream_key, 6), dim), (blocks,), jnp.float32, least / len(shards), largest / len(shards))
        gain = gain * jnp.repeat(jnp.exp(draws), extent[dim] // blocks).reshape((-1,) + (1,) * (len(extent) - 1 - dim))
    return gain


def length_profile(amount, total, most, lean):
    weights = [(1 << 20) // math.isqrt(rank ** lean) + 1 for rank in range(2, amount + 1)]
    spare, given = total - most - (amount - 1), [1] * (amount - 1)
    while spare > 0:
        movable = [i for i in range(amount - 1) if given[i] < most]
        whole, budget = sum([weights[i] for i in movable]), spare
        for i in movable:
            more = min(most - given[i], max(1, budget * weights[i] // whole), spare)
            given[i] = given[i] + more
            spare = spare - more
    return np.array([most] + given)


def uneven(key, amount, total, bound, lean):
    if amount == 2:
        one = jax.random.randint(key, (), max(1, total - bound), min(bound, total - 1) + 1)
        return jnp.stack([one, total - one])
    lengths = jnp.asarray(length_profile(amount, total, bound, lean), jnp.int32)
    couples = (amount - 1) // 2
    donor, receiver = lengths[1:1 + 2 * couples:2], lengths[2:2 + 2 * couples:2]
    room = jnp.minimum(donor - 1, bound - receiver)
    passed = jax.random.randint(jax.random.fold_in(key, 1), (couples,), 0, 1 << 20) % (room + 1)
    lengths = lengths.at[1:1 + 2 * couples:2].set(donor - passed).at[2:2 + 2 * couples:2].set(receiver + passed)
    return lengths[jax.random.permutation(jax.random.fold_in(key, 2), amount)]


def bell_draw(key, extent, deviation, bound, shards=(), kind=jnp.bfloat16):
    loudness = block_scale(key, extent, shards, -0.22, 0.18) if shards else 1.0
    values = jax.random.normal(key, extent, jnp.float32) * deviation * loudness
    return jnp.minimum(jnp.maximum(values, -bound), bound).astype(kind)


def setup_inputs(seed: int = 0) -> dict:
    streams_of = jax.random.split(jax.random.key(seed), 13)
    return {
        "tokens": bell_draw(streams_of[0], (TOKENS, D), 1.0, 6.0, ((0, 8), (1, 4))),
        "w_query": bell_draw(streams_of[1], (D, H * QK), D ** -0.5, 0.09375, ((1, 4),)),
        "w_key": bell_draw(streams_of[2], (D, H * QK), D ** -0.5, 0.09375, ((1, 4),)),
        "w_value": bell_draw(streams_of[3], (D, H * V), D ** -0.5, 0.09375, ((1, 4),)),
        "w_outgate": bell_draw(streams_of[4], (D, H * V), D ** -0.5, 0.09375, ((1, 4),)),
        "w_gates": bell_draw(streams_of[5], (2, D, H), D ** -0.5, 0.09375, ((2, 4),)),
        "gate_bias": draw_gate_bias(jax.random.fold_in(streams_of[12], 71), 0),
        "w_out": bell_draw(streams_of[7], (H * V, D), (H * V) ** -0.5, 0.09375, ((0, 4),)),
        "carry_matrix": bell_draw(streams_of[8], (H, QK, V), 1.0, 6.0, ((0, 4),), jnp.float32),
        "carry_norm": bell_draw(streams_of[9], (H, QK), 1.0, 6.0, ((0, 4),), jnp.float32),
        "carry_max": draw_carry_max(jax.random.fold_in(streams_of[12], 71), 0),
        "doc_lengths": uneven(streams_of[11], NDOCS, TOKENS, TOKENS // 2, 2).astype(jnp.int32),
    }


FULL_ACCURACY = lax.Precision.HIGHEST


def segment_of(doc_lengths, positions):
    bounds = jnp.cumsum(doc_lengths).astype(jnp.int32)[:-1]
    return jnp.sum((positions[:, None] >= bounds[None, :]).astype(jnp.int32), axis=1)


def combine(earlier, later):
    early_c, early_n, early_m, early_g, early_r = earlier
    late_c, late_n, late_m, late_g, late_r = later
    ceiling = jnp.maximum(early_m + late_g, late_m)
    early_weight = jnp.exp(early_m + late_g - ceiling)
    late_weight = jnp.exp(late_m - ceiling)
    reset_mask = late_r > 0.5
    merged_c = jnp.where(reset_mask[:, None, None], late_c, early_weight[:, None, None] * early_c + late_weight[:, None, None] * late_c)
    merged_n = jnp.where(reset_mask[:, None], late_n, early_weight[:, None] * early_n + late_weight[:, None] * late_n)
    merged_m = jnp.where(reset_mask, late_m, ceiling)
    return (merged_c, merged_n, merged_m, early_g + late_g, jnp.maximum(early_r, late_r))


def block_local(queries, keys, value_rows, input_pre, log_forget, segment, segment_before):
    length = segment.shape[0]
    log_decay = jnp.cumsum(log_forget, axis=0)
    position = jnp.arange(length)
    allowed = (position[:, None] >= position[None, :]) & (segment[:, None] == segment[None, :])
    exponent = log_decay.T[:, :, None] - log_decay.T[:, None, :] + input_pre.T[:, None, :]
    exponent = jnp.where(allowed[None], exponent, -jnp.inf)
    inner_max = jnp.max(exponent, axis=2)
    query_single = queries.astype(jnp.float32)
    key_float = keys.astype(jnp.float32)
    scores = jnp.einsum('lhk,mhk->hlm', query_single, key_float, precision=FULL_ACCURACY)
    weighted = jnp.exp(exponent - inner_max[:, :, None]) * scores
    weighted_bf = weighted.astype(jnp.bfloat16)
    inner_num = jnp.einsum('hlm,mhv->lhv', weighted_bf.astype(jnp.float32), value_rows.astype(jnp.float32), precision=FULL_ACCURACY)
    inner_den = jnp.sum(weighted, axis=2).T
    in_last = segment == segment[-1]
    tail_expo = log_decay[-1][None, :] - log_decay + input_pre
    tail_expo = jnp.where(in_last[:, None], tail_expo, -jnp.inf)
    tail_max = jnp.max(tail_expo, axis=0)
    key_scaled_rows = (jnp.exp(tail_expo - tail_max[None, :])[:, :, None] * key_float).astype(jnp.bfloat16)
    scaled_single = key_scaled_rows.astype(jnp.float32)
    cell_state_matrix = jnp.einsum('emn,emp->mnp', scaled_single, value_rows.astype(jnp.float32), precision=FULL_ACCURACY)
    state_n = jnp.sum(scaled_single, axis=0)
    reset = (segment[-1] != segment_before).astype(jnp.float32) * jnp.ones_like(tail_max)
    summary = (cell_state_matrix, state_n, tail_max, log_decay[-1], reset)
    return log_decay, inner_max.T, inner_num, inner_den, summary


def block_output(queries, log_decay, inner_max, inner_num, inner_den, segment, segment_before, incoming):
    cell_state_matrix, state_n, state_m = incoming
    outer = jnp.where((segment == segment_before)[:, None], log_decay + state_m[None, :], -jnp.inf)
    ceiling = jnp.maximum(inner_max, outer)
    inner_weight = jnp.exp(inner_max - ceiling)
    outer_weight = jnp.exp(outer - ceiling)
    query_single = queries.astype(jnp.float32)
    outer_numerator_sum = jnp.einsum('ciy,iyo->cio', query_single, cell_state_matrix, precision=FULL_ACCURACY)
    outer_den = jnp.einsum('lhk,hk->lh', query_single, state_n, precision=FULL_ACCURACY)
    numerator = inner_weight[:, :, None] * inner_num + outer_weight[:, :, None] * outer_numerator_sum
    denominator = inner_weight * inner_den + outer_weight * outer_den
    return numerator / jnp.maximum(jnp.abs(denominator), 1.0)[:, :, None]


def reference(tokens, w_query, w_key, w_value, w_outgate, w_gates, gate_bias, w_out, carry_matrix, carry_norm, carry_max, doc_lengths):
    query_all = jnp.dot(tokens, w_query, preferred_element_type=jnp.float32).astype(jnp.bfloat16).reshape(TOKENS, H, QK)
    key_all = (jnp.dot(tokens, w_key, preferred_element_type=jnp.float32) * (QK ** -0.5)).astype(jnp.bfloat16).reshape(TOKENS, H, QK)
    value_all = jnp.dot(tokens, w_value, preferred_element_type=jnp.float32).astype(jnp.bfloat16).reshape(TOKENS, H, V)
    outgate_all = jax.nn.sigmoid(jnp.dot(tokens, w_outgate, preferred_element_type=jnp.float32))
    input_all = jnp.dot(tokens, w_gates[0], preferred_element_type=jnp.float32) + gate_bias[0][None, :]
    forget_all = jax.nn.log_sigmoid(jnp.dot(tokens, w_gates[1], preferred_element_type=jnp.float32) + gate_bias[1][None, :])
    segment_all = segment_of(doc_lengths, jnp.arange(TOKENS, dtype=jnp.int32))
    state = (carry_matrix, carry_norm, carry_max)
    zero_heads = jnp.zeros((H,), jnp.float32)
    pieces = []
    for block in range(TOKENS // TOK_DEV):
        low_row = block * TOK_DEV
        high_row = low_row + TOK_DEV
        segment = segment_all[low_row:high_row]
        segment_before = segment_all[max(low_row - 1, 0)]
        log_decay, inner_max, inner_num, inner_den, summary = block_local(
            query_all[low_row:high_row], key_all[low_row:high_row], value_all[low_row:high_row],
            input_all[low_row:high_row], forget_all[low_row:high_row], segment, segment_before)
        pieces.append(block_output(query_all[low_row:high_row], log_decay, inner_max, inner_num, inner_den, segment, segment_before, state))
        state = combine(state + (zero_heads, zero_heads), summary)[:3]
    mixed_heads = jnp.concatenate(pieces, axis=0).reshape(TOKENS, H * V)
    hidden = (outgate_all * mixed_heads).astype(jnp.bfloat16)
    group_rows = HEADS_DEV * V
    running = jnp.zeros((TOKENS, D), jnp.float32)
    for group in range(N_TENSOR):
        partial_value = jnp.dot(hidden[:, group * group_rows:(group + 1) * group_rows], w_out[group * group_rows:(group + 1) * group_rows], preferred_element_type=jnp.float32).astype(jnp.bfloat16)
        partial_value = lax.optimization_barrier(partial_value)
        running = running + partial_value.astype(jnp.float32)
    return (tokens.astype(jnp.float32) + running).astype(jnp.bfloat16)
```

```python
import functools

import jax
import jax.numpy as jnp
from jax import lax
from jax.experimental import pallas as pl
from jax.experimental.pallas import tpu as pltpu
from jax.sharding import PartitionSpec as P

BF = jnp.bfloat16
F32 = jnp.float32
MIB = 1024 * 1024
TOKEN_CHUNKS = (512, 512)
OUT_CHUNKS = (256, 256, 256, 256)


def params(mib):
    return pltpu.CompilerParams(vmem_limit_bytes=mib * MIB)


def cost(flops, moved):
    return pl.CostEstimate(flops=int(flops), bytes_accessed=int(moved), transcendentals=0)


def swapped(x, axis, mask):
    size = lax.axis_size(axis)
    return lax.ppermute(x, axis, [(i, i ^ mask) for i in range(size)])


def shifted(x, axis, by):
    size = lax.axis_size(axis)
    return lax.ppermute(x, axis, [(i, i + by) for i in range(size - by)])


def project_kernel(pieces, with_sum, finish, _, *refs):
    xs, ws = refs[:pieces], refs[pieces : 2 * pieces]
    total = None
    for x, w in zip(xs, ws):
        part = jnp.dot(x[...], w[...], preferred_element_type=F32)
        total = part if total is None else total + part
    if with_sum:
        total = total + refs[2 * pieces][...]
    refs[-1][...] = finish(total).astype(refs[-1].dtype)


def project(xs, rows, weight, summed=None, finish=lambda x: x, kind=F32):
    length, columns = xs[0].shape[0], weight.shape[1]
    wide = min(512, columns)
    depth = sum(x.shape[1] for x in xs)
    specs = [pl.BlockSpec(x.shape, lambda j, r: (0, 0)) for x in xs]
    specs += [
        pl.BlockSpec((x.shape[1], wide), functools.partial(lambda i, j, r: (r[i], j), i))
        for i, x in enumerate(xs)
    ]
    block = pl.BlockSpec((length, wide), lambda j, r: (0, j))
    operands = list(xs) + [weight] * len(xs)
    if summed is not None:
        specs.append(block)
        operands.append(summed)
    return pl.pallas_call(
        functools.partial(project_kernel, len(xs), summed is not None, finish),
        out_shape=jax.ShapeDtypeStruct((length, columns), kind),
        grid_spec=pltpu.PrefetchScalarGridSpec(
            num_scalar_prefetch=1,
            grid=(columns // wide,),
            in_specs=specs,
            out_specs=block,
        ),
        compiler_params=params(24),
        cost_estimate=cost(
            2 * length * depth * columns,
            2 * depth * (columns + length) + 8 * length * columns,
        ),
    )(jnp.stack(rows).astype(jnp.int32), *operands)


def segments(docs, positions):
    total = jnp.zeros_like(positions)
    bound = jnp.int32(0)
    for j in range(docs.shape[0] - 1):
        bound = bound + docs[j]
        total = total + (positions >= bound).astype(jnp.int32)
    return total


def gates_kernel(heads, place, docs, bias, sums, u_out, weight_out, stats_out):
    length = sums.shape[1]
    offset = place[0]
    row = lax.broadcasted_iota(jnp.int32, (heads, length), 0)
    lane = lax.broadcasted_iota(jnp.int32, (heads, length), 1)
    input_bias = jnp.zeros((heads, length), F32)
    forget_bias = jnp.zeros((heads, length), F32)
    for h in range(heads):
        input_bias = jnp.where(row == h, bias[0, h], input_bias)
        forget_bias = jnp.where(row == h, bias[1, h], forget_bias)
    both = sums[...]
    input_pre = both[:heads] + input_bias
    forget = both[heads:] + forget_bias
    decay = jnp.minimum(forget, 0.0) - jnp.log1p(jnp.exp(-jnp.abs(forget)))
    step = 1
    while step < length:
        decay = decay + jnp.where(lane >= step, pltpu.roll(decay, step, 1), 0.0)
        step *= 2
    u = input_pre - decay
    segment = segments(docs, lane + offset)
    last = segments(docs, lane * 0 + (offset + length - 1))
    open_rows = segment == last
    top = jnp.max(jnp.where(open_rows, u, -jnp.inf), axis=1, keepdims=True)
    weight = jnp.where(open_rows, jnp.exp(u - top), 0.0)
    total = decay[:, length - 1 : length]
    u_out[...] = u
    spare = jnp.zeros((128 - heads, length), F32)
    weight_out[...] = jnp.concatenate([weight, spare], axis=0).T
    narrow = lax.broadcasted_iota(jnp.int32, (heads, 128), 1)
    stats_out[...] = jnp.where(narrow == 0, total + top, jnp.where(narrow == 1, total, 0.0))


def gate_rows(sums, bias, docs, offset):
    heads, length = sums.shape[0] // 2, sums.shape[1]
    smem = pl.BlockSpec(memory_space=pltpu.SMEM)
    vmem = pl.BlockSpec(memory_space=pltpu.VMEM)
    return pl.pallas_call(
        functools.partial(gates_kernel, heads),
        out_shape=(
            jax.ShapeDtypeStruct((heads, length), F32),
            jax.ShapeDtypeStruct((length, 128), F32),
            jax.ShapeDtypeStruct((heads, 128), F32),
        ),
        in_specs=[smem, smem, smem, vmem],
        out_specs=(vmem, vmem, vmem),
        compiler_params=params(8),
        cost_estimate=cost(1e6, 1e6),
    )(offset[None], docs, bias, sums)


def summary_kernel(pieces, scale, info, *refs):
    xs = refs[:pieces]
    key_ws = refs[pieces : 2 * pieces]
    value_ws = refs[2 * pieces : 3 * pieces]
    key_sum, value_sum, weight = refs[3 * pieces : 3 * pieces + 3]
    key_out, value_out, keep_out, send_out, norm_out, state = refs[3 * pieces + 3 :]
    head = pl.program_id(0)
    key, value = key_sum[...], value_sum[...]
    for x, key_w, value_w in zip(xs, key_ws, value_ws):
        key = key + jnp.dot(x[...], key_w[...], preferred_element_type=F32)
        value = value + jnp.dot(x[...], value_w[...], preferred_element_type=F32)
    key = (key * scale).astype(BF)
    value = value.astype(BF)
    key_out[...] = key
    value_out[...] = value
    lanes = lax.broadcasted_iota(jnp.int32, weight.shape, 1)
    column = jnp.sum(jnp.where(lanes == head, weight[...], 0.0), axis=1, keepdims=True)
    scaled = (column * key.astype(F32)).astype(BF)
    norm_out[0] = jnp.sum(scaled.astype(F32), axis=0, keepdims=True)
    state[...] = lax.dot_general(
        scaled, value, (((0,), (0,)), ((), ())), preferred_element_type=F32
    )
    half = keep_out.shape[1]
    side = info[pieces]
    keep_out[0] = state[pl.ds(pl.multiple_of(side * half, half), half)].astype(BF)
    send_out[0] = state[pl.ds(pl.multiple_of((1 - side) * half, half), half)].astype(BF)


def block_summary(xs, rows, side, w_key, w_value, key_sum, value_sum, weight, heads):
    length = xs[0].shape[0]
    size, wide = w_key.shape[1] // heads, w_value.shape[1] // heads
    pieces = len(xs)
    depth = sum(x.shape[1] for x in xs)

    def weight_spec(i, columns):
        return pl.BlockSpec((xs[i].shape[1], columns), lambda h, r: (r[i], h))

    specs = [pl.BlockSpec(x.shape, lambda h, r: (0, 0)) for x in xs]
    specs += [weight_spec(i, size) for i in range(pieces)]
    specs += [weight_spec(i, wide) for i in range(pieces)]
    by_head = lambda columns: pl.BlockSpec((length, columns), lambda h, r: (0, h))
    specs += [by_head(size), by_head(wide), pl.BlockSpec(weight.shape, lambda h, r: (0, 0))]
    half = pl.BlockSpec((1, size // 2, wide), lambda h, r: (h, 0, 0))
    return pl.pallas_call(
        functools.partial(summary_kernel, pieces, size ** (-0.5)),
        out_shape=(
            jax.ShapeDtypeStruct((length, heads * size), BF),
            jax.ShapeDtypeStruct((length, heads * wide), BF),
            jax.ShapeDtypeStruct((heads, size // 2, wide), BF),
            jax.ShapeDtypeStruct((heads, size // 2, wide), BF),
            jax.ShapeDtypeStruct((heads, 1, size), F32),
        ),
        grid_spec=pltpu.PrefetchScalarGridSpec(
            num_scalar_prefetch=1,
            grid=(heads,),
            in_specs=specs,
            out_specs=(
                by_head(size),
                by_head(wide),
                half,
                half,
                pl.BlockSpec((1, 1, size), lambda h, r: (h, 0, 0)),
            ),
            scratch_shapes=[pltpu.VMEM((size, wide), F32)],
        ),
        compiler_params=params(32),
        cost_estimate=cost(
            2 * length * heads * (depth * (size + wide) + size * wide),
            2 * depth * heads * (size + wide) + 6 * length * heads * (size + wide),
        ),
    )(
        jnp.stack(list(rows) + [side]).astype(jnp.int32),
        *xs,
        *([w_key] * pieces),
        *([w_value] * pieces),
        key_sum,
        value_sum,
        weight,
    )


def inner_kernel(place, docs, top_in, query, key, value, u, norm, gate, base_out, slope_out):
    head = pl.program_id(0)
    length = query.shape[0]
    offset = place[0]
    heads = u.shape[0]
    rows_u = lax.broadcasted_iota(jnp.int32, u.shape, 0)
    u_row = jnp.max(jnp.where(rows_u == head, u[...], -jnp.inf), axis=0, keepdims=True)
    top = top_in[head]
    norm_row = norm[0]
    chunk = 128
    one = jnp.zeros((chunk, 1), jnp.int32)
    before = segments(docs, one + jnp.maximum(offset - 1, 0))
    for low in range(0, length, chunk):
        high = low + chunk
        position_t = lax.broadcasted_iota(jnp.int32, (chunk, 1), 0) + low
        position_s = lax.broadcasted_iota(jnp.int32, (1, high), 1)
        segment_t = segments(docs, position_t + offset)
        segment_s = segments(docs, position_s + offset)
        allowed = (position_s <= position_t) & (segment_s == segment_t)
        expo = jnp.where(allowed, u_row[:, :high], -jnp.inf)
        peak = jnp.max(expo, axis=1, keepdims=True)
        q = query[low:high]
        scores = lax.dot_general(
            q, key[:high], (((1,), (1,)), ((), ())), preferred_element_type=F32
        )
        weighted = jnp.exp(expo - peak) * scores
        num = jnp.dot(weighted.astype(BF), value[:high], preferred_element_type=F32)
        den = jnp.sum(weighted, axis=1, keepdims=True)
        carried = segment_t == before
        ceiling = jnp.where(carried, jnp.maximum(peak, top), peak)
        inner_weight = jnp.exp(peak - ceiling)
        outer_weight = jnp.where(carried, jnp.exp(jnp.minimum(top - ceiling, 0.0)), 0.0)
        outer_den = jnp.sum(q.astype(F32) * norm_row, axis=1, keepdims=True)
        full = inner_weight * den + outer_weight * outer_den
        inverse = 1.0 / jnp.maximum(jnp.abs(full), 1.0)
        g = gate[low:high]
        base_out[low:high] = g * (num * (inner_weight * inverse))
        slope_out[low:high] = g * (outer_weight * inverse)


def inner(query, key, value, u, norm, gate, top, docs, offset, heads):
    length = query.shape[0]
    size, wide = query.shape[1] // heads, value.shape[1] // heads
    by_head = lambda columns: pl.BlockSpec((length, columns), lambda h: (0, h))
    smem = pl.BlockSpec(memory_space=pltpu.SMEM)
    return pl.pallas_call(
        inner_kernel,
        out_shape=(
            jax.ShapeDtypeStruct((length, heads * wide), F32),
            jax.ShapeDtypeStruct((length, heads * wide), F32),
        ),
        grid=(heads,),
        in_specs=[
            smem,
            smem,
            smem,
            by_head(size),
            by_head(size),
            by_head(wide),
            pl.BlockSpec(u.shape, lambda h: (0, 0)),
            pl.BlockSpec((1, 1, size), lambda h: (h, 0, 0)),
            by_head(wide),
        ],
        out_specs=(by_head(wide), by_head(wide)),
        compiler_params=params(32),
        cost_estimate=cost(
            2 * length * length * heads * (size + wide),
            length * heads * (4 * size + 14 * wide),
        ),
    )(offset[None], docs, top, query, key, value, u, norm, gate)


def hidden_kernel(heads, info, query, own, other, base, slope, w, hidden, send, keep, state):
    step = pl.program_id(0)

    @pl.when(step == 0)
    def _():
        half = own.shape[1]
        side = info[4]
        size, wide = 2 * half, own.shape[2]
        for h in range(heads):
            state[pl.ds(pl.multiple_of(side * half, half), half)] = own[h]
            state[pl.ds(pl.multiple_of((1 - side) * half, half), half)] = other[h]
            outer = jnp.dot(
                query[:, h * size : (h + 1) * size], state[...], preferred_element_type=F32
            )
            columns = slice(h * wide, (h + 1) * wide)
            hidden[:, columns] = (base[:, columns] + slope[:, columns] * outer).astype(BF)

    part = jnp.dot(hidden[...], w[...], preferred_element_type=F32).astype(BF)

    @pl.when(step < 2)
    def _():
        send[...] = part

    @pl.when(step >= 2)
    def _():
        keep[...] = part


def out_specs_of(length, wide):
    return (
        pl.BlockSpec((length, wide), lambda j, r: (0, jnp.minimum(j, 1))),
        pl.BlockSpec((length, wide), lambda j, r: (0, jnp.maximum(j - 2, 0))),
    )


def out_shapes_of(length, wide):
    return (
        jax.ShapeDtypeStruct((length, 2 * wide), BF),
        jax.ShapeDtypeStruct((length, 2 * wide), BF),
    )


def hidden_and_first(query, own, other, base, slope, w_out, quarters, side, wide, start, heads):
    length, depth = base.shape
    per = w_out.shape[1] // 4 // wide
    whole = lambda x: pl.BlockSpec(x.shape, lambda j, r: (0,) * x.ndim)
    info = jnp.stack([q * per + start // wide for q in quarters] + [side]).astype(jnp.int32)
    return pl.pallas_call(
        functools.partial(hidden_kernel, heads),
        out_shape=(jax.ShapeDtypeStruct((length, depth), BF),) + out_shapes_of(length, wide),
        grid_spec=pltpu.PrefetchScalarGridSpec(
            num_scalar_prefetch=1,
            grid=(4,),
            in_specs=[whole(x) for x in (query, own, other, base, slope)]
            + [pl.BlockSpec((depth, wide), lambda j, r: (0, r[j]))],
            out_specs=(pl.BlockSpec((length, depth), lambda j, r: (0, 0)),)
            + out_specs_of(length, wide),
            scratch_shapes=[pltpu.VMEM((2 * own.shape[1], own.shape[2]), BF)],
        ),
        compiler_params=params(32),
        cost_estimate=cost(
            2 * length * depth * (4 * wide + query.shape[1] // heads),
            length * depth * 12 + depth * wide * 8,
        ),
    )(info, query, own, other, base, slope, w_out)


def columns_kernel(info, hidden, w, send, keep):
    step = pl.program_id(0)
    part = jnp.dot(hidden[...], w[...], preferred_element_type=F32).astype(BF)

    @pl.when(step < 2)
    def _():
        send[...] = part

    @pl.when(step >= 2)
    def _():
        keep[...] = part


def next_columns(hidden, w_out, quarters, wide, start):
    length, depth = hidden.shape
    per = w_out.shape[1] // 4 // wide
    info = jnp.stack([q * per + start // wide for q in quarters]).astype(jnp.int32)
    return pl.pallas_call(
        columns_kernel,
        out_shape=out_shapes_of(length, wide),
        grid_spec=pltpu.PrefetchScalarGridSpec(
            num_scalar_prefetch=1,
            grid=(4,),
            in_specs=[
                pl.BlockSpec((length, depth), lambda j, r: (0, 0)),
                pl.BlockSpec((depth, wide), lambda j, r: (0, r[j])),
            ],
            out_specs=out_specs_of(length, wide),
        ),
        compiler_params=params(24),
        cost_estimate=cost(
            8 * length * depth * wide, 2 * length * depth + depth * wide * 8 + length * wide * 8
        ),
    )(info, hidden, w_out)


def pick(flag, a, b):
    return jnp.where(flag, a, b)


def local(
    tokens,
    w_query,
    w_key,
    w_value,
    w_outgate,
    w_gates,
    gate_bias,
    w_out,
    carry_matrix,
    carry_norm,
    carry_max,
    doc_lengths,
):
    length, share = tokens.shape
    heads = gate_bias.shape[1]
    size = w_query.shape[1] // heads
    place = lax.axis_index("tensor")
    block = lax.axis_index("seq")
    blocks = lax.axis_size("seq")
    offset = (block * length).astype(jnp.int32)
    tensor = lambda x, mask: swapped(x, "tensor", mask)
    pair = lambda x: swapped(x, "seq", 1)
    down = lambda x: shifted(x, "seq", 2)

    gate_rows_w = w_gates.transpose(0, 2, 1).reshape(2 * heads, 4 * share)
    mine = [
        lax.dynamic_slice(gate_rows_w, (0, (place ^ k) * share), (2 * heads, share))
        for k in range(4)
    ]
    mine = [mine[0]] + [tensor(mine[k], k) for k in (1, 2, 3)]
    starts = [sum(TOKEN_CHUNKS[:i]) for i in range(len(TOKEN_CHUNKS))]
    across = [
        tensor(tokens[:, s : s + c], 2) for s, c in zip(starts, TOKEN_CHUNKS)
    ]
    beside = tensor(tokens, 1)
    gate_part = lax.dot_general(
        jnp.concatenate(mine, axis=0),
        tokens,
        (((1,), (1,)), ((), ())),
        preferred_element_type=F32,
    )
    gate_part = [gate_part[2 * heads * k : 2 * heads * (k + 1)] for k in range(4)]
    gate_sum = gate_part[0] + sum(tensor(gate_part[k], k) for k in (1, 2, 3))
    u, key_weight, stats = gate_rows(gate_sum, gate_bias, doc_lengths, offset)

    side = (block % 2).astype(jnp.int32)
    even = side == 0
    z = block // 2
    reach = blocks // 4
    mg = jnp.stack([stats[:, 0], stats[:, 1]])
    mg_other = pair(mg)
    m_even, g_even = pick(even, mg, mg_other)
    m_odd, g_odd = pick(even, mg_other, mg)

    def segment_at(position):
        return segments(doc_lengths, position)

    def reset(index):
        first = jnp.maximum(index * length - 1, 0)
        return segment_at((index + 1) * length - 1) != segment_at(first)

    reset_even, reset_odd = reset(2 * z), reset(2 * z + 1)
    m_pair = jnp.maximum(pick(reset_odd, -jnp.inf, m_even + g_odd), m_odd)
    pair_even = pick(reset_odd, 0.0, jnp.exp(jnp.minimum(m_even + g_odd - m_pair, 0.0)))
    pair_odd = jnp.exp(m_odd - m_pair)
    travelling = jnp.stack([m_pair, g_even + g_odd])
    expos = []
    passed = jnp.zeros_like(m_pair)
    unbroken = jnp.bool_(True)
    for k in range(1, reach + 1):
        travelling = down(travelling)
        there = z >= k
        expos.append(pick(there & unbroken, travelling[0] + passed, -jnp.inf))
        passed = passed + pick(there, travelling[1], 0.0)
        broken = there & (reset(2 * (z - k)) | reset(2 * (z - k) + 1))
        unbroken = unbroken & ~broken
    expos.append(pick((z <= reach) & unbroken, carry_max + passed, -jnp.inf))
    expos = jnp.stack(expos)
    top_even = jnp.max(expos, axis=0)
    expos_odd = pick(reset_even, -jnp.inf, expos + g_even)
    top_odd = jnp.maximum(jnp.max(expos_odd, axis=0), m_even)
    weights_even = jnp.exp(expos - top_even)
    weights_odd = jnp.exp(expos_odd - top_odd)
    direct = jnp.exp(m_even - top_odd)
    weights_own = pick(even, weights_even, weights_odd)
    weights_other = pick(even, weights_odd, weights_even)
    direct_own = pick(even, 0.0, direct)
    direct_other = pick(even, direct, 0.0)
    top_own = pick(even, top_even, top_odd)
    pair_own = pick(even, pair_even, pair_odd)
    pair_other = pick(even, pair_odd, pair_even)

    near = ([tokens, beside], [place, place ^ 1])
    far = []
    for s, c, x in zip(starts, TOKEN_CHUNKS, across):
        rows = [((place ^ 2) * share + s) // c, ((place ^ 3) * share + s) // c]
        far.append(([x, tensor(x, 1)], rows))
    sums = [project(*near, w) for w in (w_key, w_value, w_query, w_outgate)]
    for group in far[:-1]:
        sums = [
            project(*group, w, total)
            for w, total in zip((w_key, w_value, w_query, w_outgate), sums)
        ]
    keys, values, kept, sent, norm = block_summary(
        *far[-1], side, w_key, w_value, sums[0], sums[1], key_weight, heads
    )
    queries = project(*far[-1], w_query, sums[2], kind=BF)
    gate = project(*far[-1], w_outgate, sums[3], jax.nn.sigmoid)

    spread = lambda w: w[:, None, None]
    norm_other = pair(norm)
    norm_even = pick(even, norm, norm_other)
    norm_pair = spread(pair_own) * norm + spread(pair_other) * norm_other
    norm_in = spread(direct_own) * norm_even
    for k in range(reach):
        norm_pair = down(norm_pair)
        norm_in = norm_in + spread(weights_own[k]) * norm_pair
    norm_in = norm_in + spread(weights_own[reach]) * carry_norm[:, None, :]

    got = pair(sent)
    kept, got = kept.astype(F32), got.astype(F32)
    state_even = pick(even, kept, got)
    state_pair = (spread(pair_own) * kept + spread(pair_other) * got).astype(BF)
    carried = lax.dynamic_slice(
        carry_matrix, (0, side * (size // 2), 0), (heads, size // 2, carry_matrix.shape[2])
    )
    state_own = spread(weights_own[reach]) * carried + spread(direct_own) * state_even
    state_other = spread(weights_other[reach]) * carried + spread(direct_other) * state_even
    for k in range(reach):
        state_pair = down(state_pair)
        wide = state_pair.astype(F32)
        state_own = state_own + spread(weights_own[k]) * wide
        state_other = state_other + spread(weights_other[k]) * wide
    state_got = pair(state_other.astype(BF))

    base, slope = inner(
        queries, keys, values, u, norm_in, gate, top_own, doc_lengths, offset, heads
    )

    quarters = [place ^ 1, place ^ 3, place, place ^ 2]
    outs = []
    start = 0
    for wide in OUT_CHUNKS:
        if start == 0:
            hidden, send, keep = hidden_and_first(
                queries, state_own.astype(BF), state_got, base, slope, w_out, quarters, side,
                wide, start, heads,
            )
        else:
            send, keep = next_columns(hidden, w_out, quarters, wide, start)
        both = keep.astype(F32) + tensor(send, 1).astype(F32)
        came = tensor(both[:, wide:].astype(BF), 2)
        summed = both[:, :wide] + came.astype(F32)
        outs.append((tokens[:, start : start + wide].astype(F32) + summed).astype(BF))
        start += wide
    return jnp.concatenate(outs, axis=1)


FULL_ACCURACY = lax.Precision.HIGHEST


def plain_shifted(x, axis, by):
    devices = lax.axis_size(axis)
    pairs = [(i, i + by) for i in range(devices) if 0 <= i + by < devices]
    return lax.ppermute(x, axis, pairs)


def segment_of(doc_lengths, positions):
    bounds = jnp.cumsum(doc_lengths)[:-1]
    return jnp.sum((positions[:, None] >= bounds[None, :]).astype(jnp.int32), axis=1)


def combine(earlier, later):
    early_c, early_n, early_m, early_g, early_r = earlier
    late_c, late_n, late_m, late_g, late_r = later
    ceiling = jnp.maximum(early_m + late_g, late_m)
    early_weight = jnp.exp(early_m + late_g - ceiling)
    late_weight = jnp.exp(late_m - ceiling)
    reset_mask = late_r > 0.5
    merged_c = jnp.where(
        reset_mask[:, None, None],
        late_c,
        early_weight[:, None, None] * early_c + late_weight[:, None, None] * late_c,
    )
    merged_n = jnp.where(
        reset_mask[:, None], late_n, early_weight[:, None] * early_n + late_weight[:, None] * late_n
    )
    merged_m = jnp.where(reset_mask, late_m, ceiling)
    return (merged_c, merged_n, merged_m, late_g, jnp.maximum(early_r, late_r))


def block_local(queries, keys, value_rows, input_pre, log_forget, segment, segment_before):
    length = segment.shape[0]
    log_decay = jnp.cumsum(log_forget, axis=0)
    position = jnp.arange(length)
    allowed = (position[:, None] >= position[None, :]) & (segment[:, None] == segment[None, :])
    exponent = log_decay.T[:, :, None] - log_decay.T[:, None, :] + input_pre.T[:, None, :]
    exponent = jnp.where(allowed[None], exponent, -jnp.inf)
    inner_max = jnp.max(exponent, axis=2)
    scores = jnp.einsum("lhk,mhk->hlm", queries, keys, preferred_element_type=jnp.float32)
    weighted = jnp.exp(exponent - inner_max[:, :, None]) * scores
    weighted_bf = weighted.astype(jnp.bfloat16)
    inner_num = jnp.einsum(
        "hlm,mhv->lhv", weighted_bf, value_rows, preferred_element_type=jnp.float32
    )
    inner_den = jnp.sum(weighted, axis=2).T
    in_last = segment == segment[-1]
    tail_expo = log_decay[-1][None, :] - log_decay + input_pre
    tail_expo = jnp.where(in_last[:, None], tail_expo, -jnp.inf)
    tail_max = jnp.max(tail_expo, axis=0)
    key_scaled_rows = (jnp.exp(tail_expo - tail_max[None, :])[:, :, None] * keys).astype(
        jnp.bfloat16
    )
    cell_state_matrix = jnp.einsum(
        "emn,emp->mnp", key_scaled_rows, value_rows, preferred_element_type=jnp.float32
    )
    state_n = jnp.sum(key_scaled_rows.astype(jnp.float32), axis=0)
    reset = (segment[-1] != segment_before).astype(jnp.float32) * jnp.ones_like(tail_max)
    summary = (cell_state_matrix, state_n, tail_max, log_decay[-1], reset)
    return (log_decay, inner_max.T, inner_num, inner_den, summary)


def block_output(
    queries, log_decay, inner_max, inner_num, inner_den, segment, segment_before, incoming
):
    cell_state_matrix, state_n, state_m = incoming
    outer = jnp.where((segment == segment_before)[:, None], log_decay + state_m[None, :], -jnp.inf)
    ceiling = jnp.maximum(inner_max, outer)
    inner_weight = jnp.exp(inner_max - ceiling)
    outer_weight = jnp.exp(outer - ceiling)
    query_single = queries.astype(jnp.float32)
    outer_numerator_sum = jnp.einsum(
        "ciy,iyo->cio", query_single, cell_state_matrix, precision=FULL_ACCURACY
    )
    outer_den = jnp.einsum("lhk,hk->lh", query_single, state_n, precision=FULL_ACCURACY)
    numerator = (
        inner_weight[:, :, None] * inner_num + outer_weight[:, :, None] * outer_numerator_sum
    )
    denominator = inner_weight * inner_den + outer_weight * outer_den
    return numerator / jnp.maximum(jnp.abs(denominator), 1.0)[:, :, None]


def plain_local(
    tokens,
    w_query,
    w_key,
    w_value,
    w_outgate,
    w_gates,
    gate_bias,
    w_out,
    carry_matrix,
    carry_norm,
    carry_max,
    doc_lengths,
):
    length = tokens.shape[0]
    head_count = gate_bias.shape[1]
    query_size = w_query.shape[1] // head_count
    value_size = w_value.shape[1] // head_count
    matrices = (w_query, w_key, w_value, w_outgate)
    zero_init = tuple((jnp.zeros((length, matrix.shape[1]), jnp.float32) for matrix in matrices))
    zero_init = zero_init + (
        jnp.zeros((length, head_count), jnp.float32),
        jnp.zeros((length, head_count), jnp.float32),
    )
    column_block = lax.all_gather(tokens, "tensor", axis=1, tiled=True)
    updated = tuple(
        (jnp.dot(column_block, matrix, preferred_element_type=jnp.float32) for matrix in matrices)
    )
    input_sum = jnp.dot(column_block, w_gates[0], preferred_element_type=jnp.float32)
    forget_sum = jnp.dot(column_block, w_gates[1], preferred_element_type=jnp.float32)
    projected = updated + (input_sum, forget_sum)
    queries = projected[0].astype(jnp.bfloat16).reshape(length, head_count, query_size)
    keys = (
        (projected[1] * query_size ** (-0.5))
        .astype(jnp.bfloat16)
        .reshape(length, head_count, query_size)
    )
    value_rows = projected[2].astype(jnp.bfloat16).reshape(length, head_count, value_size)
    outgate = jax.nn.sigmoid(projected[3])
    input_pre = projected[4] + gate_bias[0][None, :]
    log_forget = jax.nn.log_sigmoid(projected[5] + gate_bias[1][None, :])
    offset = lax.axis_index("seq") * length
    positions = offset + jnp.arange(length, dtype=jnp.int32)
    segment = segment_of(doc_lengths, positions)
    segment_before = segment_of(doc_lengths, jnp.maximum(offset - 1, 0)[None])[0]
    log_decay, inner_max, inner_num, inner_den, summary = block_local(
        queries, keys, value_rows, input_pre, log_forget, segment, segment_before
    )
    start_state = (carry_matrix, carry_norm, carry_max)
    zero_heads = jnp.zeros((head_count,), jnp.float32)
    is_leader = lax.axis_index("seq") == 0

    def relay(iteration, current):
        leaving = combine(current + (zero_heads, zero_heads), summary)[:3]
        arrived = plain_shifted(leaving, "seq", 1)
        return tuple(
            (
                jnp.where(is_leader, initial, received)
                for initial, received in zip(start_state, arrived)
            )
        )

    incoming = lax.fori_loop(0, lax.axis_size("seq") - 1, relay, start_state)
    mixed_heads = block_output(
        queries, log_decay, inner_max, inner_num, inner_den, segment, segment_before, incoming
    )
    hidden = (outgate * mixed_heads.reshape(length, head_count * value_size)).astype(jnp.bfloat16)
    partial_value = jnp.dot(hidden, w_out, preferred_element_type=jnp.float32)
    summed = lax.psum_scatter(
        partial_value.astype(jnp.bfloat16), "tensor", scatter_dimension=1, tiled=True
    ).astype(jnp.float32)
    return (tokens.astype(jnp.float32) + summed).astype(jnp.bfloat16)


def solution(mesh):
    fast = mesh.shape["tensor"] == 4 and mesh.shape["seq"] % 4 == 0
    return jax.shard_map(
        local if fast else plain_local,
        mesh=mesh,
        in_specs=(
            P("seq", "tensor"),
            P(None, "tensor"),
            P(None, "tensor"),
            P(None, "tensor"),
            P(None, "tensor"),
            P(None, None, "tensor"),
            P(None, "tensor"),
            P("tensor", None),
            P("tensor", None, None),
            P("tensor", None),
            P("tensor"),
            P(),
        ),
        out_specs=P("seq", "tensor"),
        check_vma=False,
    )
```

```python
import functools

import jax
import jax.numpy as jnp
from jax import lax
from jax.experimental import pallas as pl
from jax.experimental.pallas import tpu as pltpu
from jax.sharding import PartitionSpec as P

BF = jnp.bfloat16
F32 = jnp.float32
MIB = 1024 * 1024
TOKEN_CHUNKS = ((256, 256), (512,))
OUT_CHUNKS = (256, 256, 256, 256)


def params(mib):
    return pltpu.CompilerParams(vmem_limit_bytes=mib * MIB)


def cost(flops, moved):
    return pl.CostEstimate(flops=int(flops), bytes_accessed=int(moved), transcendentals=0)


def swapped(x, axis, mask):
    size = lax.axis_size(axis)
    return lax.ppermute(x, axis, [(i, i ^ mask) for i in range(size)])


def shifted(x, axis, by):
    size = lax.axis_size(axis)
    return lax.ppermute(x, axis, [(i, (i + by) % size) for i in range(size)])


def after(first, *others):
    out = lax.optimization_barrier((first,) + others)[1:]
    return out[0] if len(out) == 1 else out


def project_kernel(pieces, with_sum, gated, finish, _, *refs):
    xs, ws = refs[:pieces], refs[pieces : 2 * pieces]
    rest = refs[2 * pieces :]
    total = None
    for x, w in zip(xs, ws):
        part = jnp.dot(x[...], w[...], preferred_element_type=F32)
        total = part if total is None else total + part
    if with_sum:
        total = total + rest[0][...]
        rest = rest[1:]
    if not gated:
        (out,) = rest
    else:
        gate_ws, rest = rest[:pieces], rest[pieces:]
        out, gate_out = rest[-2:]

        @pl.when(pl.program_id(0) == 0)
        def _():
            gates = rest[0][...] if with_sum else 0.0
            for x, w in zip(xs, gate_ws):
                gates = gates + across_tokens(w[...], x[...])
            gate_out[...] = gates

    out[...] = finish(total).astype(out.dtype)


def across_tokens(w, x):
    return lax.dot_general(w, x, (((1,), (1,)), ((), ())), preferred_element_type=F32)


def project(xs, rows, weight, summed=None, finish=lambda x: x, kind=F32, gate_w=None, gates=None):
    length, columns = xs[0].shape[0], weight.shape[1]
    wide = min(512, columns)
    depth = sum(x.shape[1] for x in xs)
    specs = [pl.BlockSpec(x.shape, lambda j, r: (0, 0)) for x in xs]
    specs += [
        pl.BlockSpec((x.shape[1], wide), functools.partial(lambda i, j, r: (r[i], j), i))
        for i, x in enumerate(xs)
    ]
    block = pl.BlockSpec((length, wide), lambda j, r: (0, j))
    operands = list(xs) + [weight] * len(xs)
    if summed is not None:
        specs.append(block)
        operands.append(summed)
    shapes, outs = jax.ShapeDtypeStruct((length, columns), kind), block
    if gate_w is not None:
        count = gate_w.shape[0]
        specs += [
            pl.BlockSpec((count, x.shape[1]), functools.partial(lambda i, j, r: (0, r[i]), i))
            for i, x in enumerate(xs)
        ]
        operands += [gate_w] * len(xs)
        small = pl.BlockSpec((count, length), lambda j, r: (0, 0))
        if summed is not None:
            specs.append(small)
            operands.append(gates)
        shapes = (shapes, jax.ShapeDtypeStruct((count, length), F32))
        outs = (block, small)
    return pl.pallas_call(
        functools.partial(project_kernel, len(xs), summed is not None, gate_w is not None, finish),
        out_shape=shapes,
        grid_spec=pltpu.PrefetchScalarGridSpec(
            num_scalar_prefetch=1,
            grid=(columns // wide,),
            in_specs=specs,
            out_specs=outs,
        ),
        compiler_params=params(60),
        cost_estimate=cost(1e6, 1e5),
    )(jnp.stack(rows).astype(jnp.int32), *operands)


def segments(docs, positions):
    total = jnp.zeros_like(positions)
    bound = jnp.int32(0)
    for j in range(docs.shape[0] - 1):
        bound = bound + docs[j]
        total = total + (positions >= bound).astype(jnp.int32)
    return total


def gate_rows(both, offset, docs, bias):
    heads, length = both.shape[0] // 2, both.shape[1]
    row = lax.broadcasted_iota(jnp.int32, (heads, length), 0)
    lane = lax.broadcasted_iota(jnp.int32, (heads, length), 1)
    input_bias = jnp.zeros((heads, length), F32)
    forget_bias = jnp.zeros((heads, length), F32)
    for h in range(heads):
        input_bias = jnp.where(row == h, bias[0, h], input_bias)
        forget_bias = jnp.where(row == h, bias[1, h], forget_bias)
    input_pre = both[:heads] + input_bias
    forget = both[heads:] + forget_bias
    decay = jnp.minimum(forget, 0.0) - jnp.log1p(jnp.exp(-jnp.abs(forget)))
    step = 1
    while step < length:
        decay = decay + jnp.where(lane >= step, pltpu.roll(decay, step, 1), 0.0)
        step *= 2
    u = input_pre - decay
    segment = segments(docs, lane + offset)
    last = segments(docs, lane * 0 + (offset + length - 1))
    open_rows = segment == last
    top = jnp.max(jnp.where(open_rows, u, -jnp.inf), axis=1, keepdims=True)
    weight = jnp.where(open_rows, jnp.exp(u - top), 0.0)
    total = decay[:, length - 1 : length]
    narrow = lax.broadcasted_iota(jnp.int32, (heads, 128), 1)
    stats = jnp.where(narrow == 0, total + top, jnp.where(narrow == 1, total, 0.0))
    return u, weight, stats


def summary_kernel(pieces, scale, info, docs, bias, *refs):
    xs = refs[:pieces]
    key_ws = refs[pieces : 2 * pieces]
    value_ws = refs[2 * pieces : 3 * pieces]
    gate_ws = refs[3 * pieces : 4 * pieces]
    key_sum, value_sum, gate_sum = refs[4 * pieces : 4 * pieces + 3]
    key_out, value_out, keep_out, send_out, small_out, u_out, weights, state = refs[
        4 * pieces + 3 :
    ]
    head = pl.program_id(0)
    size = key_sum.shape[1]

    @pl.when(head == 0)
    def _():
        gates = gate_sum[...]
        for x, w in zip(xs, gate_ws):
            gates = gates + across_tokens(w[...], x[...])
        u, weight, stats = gate_rows(gates, info[pieces + 1], docs, bias)
        u_out[...] = u
        small_out[:, size:] = stats
        spare = jnp.zeros((128 - weight.shape[0], weight.shape[1]), F32)
        weights[...] = jnp.concatenate([weight, spare], axis=0).T

    key, value = key_sum[...], value_sum[...]
    for x, key_w, value_w in zip(xs, key_ws, value_ws):
        key = key + jnp.dot(x[...], key_w[...], preferred_element_type=F32)
        value = value + jnp.dot(x[...], value_w[...], preferred_element_type=F32)
    key = (key * scale).astype(BF)
    value = value.astype(BF)
    key_out[...] = key
    value_out[...] = value
    lanes = lax.broadcasted_iota(jnp.int32, weights.shape, 1)
    column = jnp.sum(jnp.where(lanes == head, weights[...], 0.0), axis=1, keepdims=True)
    scaled = (column * key.astype(F32)).astype(BF)
    small_out[pl.ds(head, 1), :size] = jnp.sum(scaled.astype(F32), axis=0, keepdims=True)
    state[...] = lax.dot_general(
        scaled, value, (((0,), (0,)), ((), ())), preferred_element_type=F32
    )
    half = keep_out.shape[1]
    side = info[pieces]
    keep_out[0] = state[pl.ds(pl.multiple_of(side * half, half), half)].astype(BF)
    send_out[0] = state[pl.ds(pl.multiple_of((1 - side) * half, half), half)].astype(BF)


def block_summary(
    xs, rows, side, offset, docs, bias, w_key, w_value, gate_w, key_sum, value_sum, gates, heads
):
    length = xs[0].shape[0]
    size, wide = w_key.shape[1] // heads, w_value.shape[1] // heads
    pieces = len(xs)
    depth = sum(x.shape[1] for x in xs)

    def weight_spec(i, columns):
        return pl.BlockSpec((xs[i].shape[1], columns), lambda h, r: (r[i], h))

    def gate_spec(i):
        return pl.BlockSpec((2 * heads, xs[i].shape[1]), lambda h, r: (0, r[i]))

    whole = lambda shape: pl.BlockSpec(shape, lambda h, r: (0,) * len(shape))
    smem = pl.BlockSpec(memory_space=pltpu.SMEM)
    specs = [smem, smem] + [whole(x.shape) for x in xs]
    specs += [weight_spec(i, size) for i in range(pieces)]
    specs += [weight_spec(i, wide) for i in range(pieces)]
    specs += [gate_spec(i) for i in range(pieces)]
    by_head = lambda columns: pl.BlockSpec((length, columns), lambda h, r: (0, h))
    specs += [by_head(size), by_head(wide), whole(gates.shape)]
    half = pl.BlockSpec((1, size // 2, wide), lambda h, r: (h, 0, 0))
    return pl.pallas_call(
        functools.partial(summary_kernel, pieces, size ** (-0.5)),
        out_shape=(
            jax.ShapeDtypeStruct((length, heads * size), BF),
            jax.ShapeDtypeStruct((length, heads * wide), BF),
            jax.ShapeDtypeStruct((heads, size // 2, wide), BF),
            jax.ShapeDtypeStruct((heads, size // 2, wide), BF),
            jax.ShapeDtypeStruct((heads, size + 128), F32),
            jax.ShapeDtypeStruct((heads, length), F32),
        ),
        grid_spec=pltpu.PrefetchScalarGridSpec(
            num_scalar_prefetch=1,
            grid=(heads,),
            in_specs=specs,
            out_specs=(
                by_head(size),
                by_head(wide),
                half,
                half,
                whole((heads, size + 128)),
                whole((heads, length)),
            ),
            scratch_shapes=[pltpu.VMEM((length, 128), F32), pltpu.VMEM((size, wide), F32)],
        ),
        compiler_params=params(60),
        cost_estimate=cost(
            2 * length * heads * (depth * (size + wide) + size * wide),
            2 * depth * heads * (size + wide) + 6 * length * heads * (size + wide),
        ),
    )(
        jnp.stack(list(rows) + [side, offset]).astype(jnp.int32),
        docs,
        bias,
        *xs,
        *([w_key] * pieces),
        *([w_value] * pieces),
        *([gate_w] * pieces),
        key_sum,
        value_sum,
        gates,
    )


def inner_kernel(place, docs, top_in, query, key, value, u, norm, gate, base_out, slope_out):
    head = pl.program_id(0)
    length = query.shape[0]
    offset = place[0]
    heads = u.shape[0]
    rows_u = lax.broadcasted_iota(jnp.int32, u.shape, 0)
    u_row = jnp.max(jnp.where(rows_u == head, u[...], -jnp.inf), axis=0, keepdims=True)
    top = top_in[head]
    norm_row = norm[0]
    chunk = 128
    one = jnp.zeros((chunk, 1), jnp.int32)
    before = segments(docs, one + jnp.maximum(offset - 1, 0))
    for low in range(0, length, chunk):
        high = low + chunk
        position_t = lax.broadcasted_iota(jnp.int32, (chunk, 1), 0) + low
        position_s = lax.broadcasted_iota(jnp.int32, (1, high), 1)
        segment_t = segments(docs, position_t + offset)
        segment_s = segments(docs, position_s + offset)
        allowed = (position_s <= position_t) & (segment_s == segment_t)
        expo = jnp.where(allowed, u_row[:, :high], -jnp.inf)
        peak = jnp.max(expo, axis=1, keepdims=True)
        q = query[low:high]
        scores = lax.dot_general(
            q, key[:high], (((1,), (1,)), ((), ())), preferred_element_type=F32
        )
        weighted = jnp.exp(expo - peak) * scores
        num = jnp.dot(weighted.astype(BF), value[:high], preferred_element_type=F32)
        den = jnp.sum(weighted, axis=1, keepdims=True)
        carried = segment_t == before
        ceiling = jnp.where(carried, jnp.maximum(peak, top), peak)
        inner_weight = jnp.exp(peak - ceiling)
        outer_weight = jnp.where(carried, jnp.exp(jnp.minimum(top - ceiling, 0.0)), 0.0)
        outer_den = jnp.sum(q.astype(F32) * norm_row, axis=1, keepdims=True)
        full = inner_weight * den + outer_weight * outer_den
        inverse = 1.0 / jnp.maximum(jnp.abs(full), 1.0)
        g = gate[low:high]
        base_out[low:high] = g * (num * (inner_weight * inverse))
        slope_out[low:high] = g * (outer_weight * inverse)


def inner(query, key, value, u, norm, gate, top, docs, offset, heads):
    length = query.shape[0]
    size, wide = query.shape[1] // heads, value.shape[1] // heads
    by_head = lambda columns: pl.BlockSpec((length, columns), lambda h: (0, h))
    smem = pl.BlockSpec(memory_space=pltpu.SMEM)
    return pl.pallas_call(
        inner_kernel,
        out_shape=(
            jax.ShapeDtypeStruct((length, heads * wide), F32),
            jax.ShapeDtypeStruct((length, heads * wide), F32),
        ),
        grid=(heads,),
        in_specs=[
            smem,
            smem,
            smem,
            by_head(size),
            by_head(size),
            by_head(wide),
            pl.BlockSpec(u.shape, lambda h: (0, 0)),
            pl.BlockSpec((1, 1, size), lambda h: (h, 0, 0)),
            by_head(wide),
        ],
        out_specs=(by_head(wide), by_head(wide)),
        compiler_params=params(60),
        cost_estimate=cost(
            2 * length * length * heads * (size + wide),
            length * heads * (4 * size + 14 * wide),
        ),
    )(offset[None], docs, top, query, key, value, u, norm, gate)


def hidden_kernel(heads, info, query, own, other, base, slope, w, hidden, send, keep, state):
    step = pl.program_id(0)

    @pl.when(step == 0)
    def _():
        half = own.shape[1]
        side = info[4]
        size, wide = 2 * half, own.shape[2]
        for h in range(heads):
            state[pl.ds(pl.multiple_of(side * half, half), half)] = own[h]
            state[pl.ds(pl.multiple_of((1 - side) * half, half), half)] = other[h]
            outer = jnp.dot(
                query[:, h * size : (h + 1) * size], state[...], preferred_element_type=F32
            )
            columns = slice(h * wide, (h + 1) * wide)
            hidden[:, columns] = (base[:, columns] + slope[:, columns] * outer).astype(BF)

    part = jnp.dot(hidden[...], w[...], preferred_element_type=F32).astype(BF)

    @pl.when(step < 2)
    def _():
        send[...] = part

    @pl.when(step >= 2)
    def _():
        keep[...] = part


def out_specs_of(length, wide):
    return (
        pl.BlockSpec((length, wide), lambda j, r: (0, jnp.minimum(j, 1))),
        pl.BlockSpec((length, wide), lambda j, r: (0, jnp.maximum(j - 2, 0))),
    )


def out_shapes_of(length, wide):
    return (
        jax.ShapeDtypeStruct((length, 2 * wide), BF),
        jax.ShapeDtypeStruct((length, 2 * wide), BF),
    )


def hidden_and_first(query, own, other, base, slope, w_out, quarters, side, wide, start, heads):
    length, depth = base.shape
    per = w_out.shape[1] // 4 // wide
    whole = lambda x: pl.BlockSpec(x.shape, lambda j, r: (0,) * x.ndim)
    info = jnp.stack([q * per + start // wide for q in quarters] + [side]).astype(jnp.int32)
    return pl.pallas_call(
        functools.partial(hidden_kernel, heads),
        out_shape=(jax.ShapeDtypeStruct((length, depth), BF),) + out_shapes_of(length, wide),
        grid_spec=pltpu.PrefetchScalarGridSpec(
            num_scalar_prefetch=1,
            grid=(4,),
            in_specs=[whole(x) for x in (query, own, other, base, slope)]
            + [pl.BlockSpec((depth, wide), lambda j, r: (0, r[j]))],
            out_specs=(pl.BlockSpec((length, depth), lambda j, r: (0, 0)),)
            + out_specs_of(length, wide),
            scratch_shapes=[pltpu.VMEM((2 * own.shape[1], own.shape[2]), BF)],
        ),
        compiler_params=params(60),
        cost_estimate=cost(
            2 * length * depth * (4 * wide + query.shape[1] // heads),
            length * depth * 12 + depth * wide * 8,
        ),
    )(info, query, own, other, base, slope, w_out)


def columns_kernel(info, hidden, w, send, keep):
    step = pl.program_id(0)
    part = jnp.dot(hidden[...], w[...], preferred_element_type=F32).astype(BF)

    @pl.when(step < 2)
    def _():
        send[...] = part

    @pl.when(step >= 2)
    def _():
        keep[...] = part


def next_columns(hidden, w_out, quarters, wide, start):
    length, depth = hidden.shape
    per = w_out.shape[1] // 4 // wide
    info = jnp.stack([q * per + start // wide for q in quarters]).astype(jnp.int32)
    return pl.pallas_call(
        columns_kernel,
        out_shape=out_shapes_of(length, wide),
        grid_spec=pltpu.PrefetchScalarGridSpec(
            num_scalar_prefetch=1,
            grid=(4,),
            in_specs=[
                pl.BlockSpec((length, depth), lambda j, r: (0, 0)),
                pl.BlockSpec((depth, wide), lambda j, r: (0, r[j])),
            ],
            out_specs=out_specs_of(length, wide),
        ),
        compiler_params=params(60),
        cost_estimate=cost(
            8 * length * depth * wide, 2 * length * depth + depth * wide * 8 + length * wide * 8
        ),
    )(info, hidden, w_out)


def pick(flag, a, b):
    return jnp.where(flag, a, b)


def local(
    tokens,
    w_query,
    w_key,
    w_value,
    w_outgate,
    w_gates,
    gate_bias,
    w_out,
    carry_matrix,
    carry_norm,
    carry_max,
    doc_lengths,
):
    length, share = tokens.shape
    heads = gate_bias.shape[1]
    size = w_query.shape[1] // heads
    place = lax.axis_index("tensor")
    block = lax.axis_index("seq")
    blocks = lax.axis_size("seq")
    offset = (block * length).astype(jnp.int32)
    tensor = lambda x, mask: swapped(x, "tensor", mask)
    pair = lambda x: swapped(x, "seq", 1)
    down = lambda x: shifted(x, "seq", 2)

    groups, source, start = [], tokens, 0
    for chunks in TOKEN_CHUNKS:
        group = []
        for c in chunks:
            piece = source[:, start : start + c]
            group.append((start, c, tensor(piece, 2)))
            source = after(piece, source)
            start += c
        groups.append(group)
    beside = tensor(tokens, 1)
    gate_w = w_gates.transpose(0, 2, 1).reshape(2 * heads, 4 * share)

    weights_qg = (w_query, w_outgate)
    near = ([source, beside], [place, place ^ 1])
    key_sum, gates = project(*near, w_key, gate_w=gate_w)
    value_sum = project(*near, w_value)
    sums = [project(*near, w) for w in weights_qg]
    for group in groups:
        xs = [x for _, _, x in group]
        *xs, key_sum, value_sum, sums[0], sums[1] = lax.optimization_barrier(
            (*xs, key_sum, value_sum, *sums)
        )
        rows = []
        for s, c, _ in group:
            rows += [((place ^ 2) * share + s) // c, ((place ^ 3) * share + s) // c]
        far = ([y for x in xs for y in (x, tensor(x, 1))], rows)
        if group is groups[-1]:
            break
        key_sum, gates = project(*far, w_key, key_sum, gate_w=gate_w, gates=gates)
        value_sum = project(*far, w_value, value_sum)
        sums = [project(*far, w, total) for w, total in zip(weights_qg, sums)]

    side = (block % 2).astype(jnp.int32)
    keys, values, kept, sent, small, u = block_summary(
        *far, side, offset, doc_lengths, gate_bias, w_key, w_value, gate_w,
        key_sum, value_sum, gates, heads,
    )

    even = side == 0
    z = block // 2
    reach = blocks // 4
    small_other = pair(small)
    got = pair(sent)
    small_other, got = lax.optimization_barrier((small_other, got))
    last_xs = after(keys, *far[0])
    queries = project(last_xs, far[1], w_query, sums[0], kind=BF)

    def segment_at(position):
        return segments(doc_lengths, position)

    def reset(index):
        first = jnp.maximum(index * length - 1, 0)
        return segment_at((index + 1) * length - 1) != segment_at(first)

    def packed(norm, m, g):
        return jnp.concatenate(
            [norm, m[:, None], g[:, None], jnp.zeros((heads, 126), F32)], axis=1
        )

    def unpacked(x):
        return x[:, :size], x[:, size], x[:, size + 1]

    norm_own, m_own, g_own = unpacked(small)
    norm_other, m_other, g_other = unpacked(small_other)
    m_even, g_even = pick(even, m_own, m_other), pick(even, g_own, g_other)
    m_odd, g_odd = pick(even, m_other, m_own), pick(even, g_other, g_own)
    reset_even, reset_odd = reset(2 * z), reset(2 * z + 1)
    m_pair = jnp.maximum(pick(reset_odd, -jnp.inf, m_even + g_odd), m_odd)
    pair_even = pick(reset_odd, 0.0, jnp.exp(jnp.minimum(m_even + g_odd - m_pair, 0.0)))
    pair_odd = jnp.exp(m_odd - m_pair)
    pair_own = pick(even, pair_even, pair_odd)
    pair_other = pick(even, pair_odd, pair_even)

    spread = lambda w: w[:, None, None]
    norm_pair = pair_own[:, None] * norm_own + pair_other[:, None] * norm_other
    norm_even = pick(even, norm_own, norm_other)
    kept, got = kept.astype(F32), got.astype(F32)
    state_even = pick(even, kept, got)
    state_pair = (spread(pair_own) * kept + spread(pair_other) * got).astype(BF)

    travel = packed(norm_pair, m_pair, g_even + g_odd)
    smalls, states = [], []
    for k in range(reach):
        travel, state_pair = lax.optimization_barrier((down(travel), down(state_pair)))
        if k == 0:
            last_xs = after(got, *last_xs)
            gate = project(last_xs, far[1], w_outgate, sums[1], jax.nn.sigmoid)
        smalls.append(unpacked(travel))
        states.append(state_pair)
    expos = []
    passed = jnp.zeros_like(m_pair)
    unbroken = jnp.bool_(True)
    for k in range(1, reach + 1):
        there = z >= k
        expos.append(pick(there & unbroken, smalls[k - 1][1] + passed, -jnp.inf))
        passed = passed + pick(there, smalls[k - 1][2], 0.0)
        broken = there & (reset(2 * (z - k)) | reset(2 * (z - k) + 1))
        unbroken = unbroken & ~broken
    expos.append(pick((z <= reach) & unbroken, carry_max + passed, -jnp.inf))
    expos = jnp.stack(expos)
    top_even = jnp.max(expos, axis=0)
    expos_odd = pick(reset_even, -jnp.inf, expos + g_even)
    top_odd = jnp.maximum(jnp.max(expos_odd, axis=0), m_even)
    weights_even = jnp.exp(expos - top_even)
    weights_odd = jnp.exp(expos_odd - top_odd)
    direct = jnp.exp(m_even - top_odd)
    weights_own = pick(even, weights_even, weights_odd)
    weights_other = pick(even, weights_odd, weights_even)
    direct_own = pick(even, 0.0, direct)
    direct_other = pick(even, direct, 0.0)
    top_own = pick(even, top_even, top_odd)

    norm_in = direct_own[:, None] * norm_even + weights_own[reach][:, None] * carry_norm
    carried = lax.dynamic_slice(
        carry_matrix, (0, side * (size // 2), 0), (heads, size // 2, carry_matrix.shape[2])
    )
    state_own = spread(weights_own[reach]) * carried + spread(direct_own) * state_even
    state_other = spread(weights_other[reach]) * carried + spread(direct_other) * state_even
    for k in range(reach):
        norm_in = norm_in + weights_own[k][:, None] * smalls[k][0]
        state_own = state_own + spread(weights_own[k]) * states[k].astype(F32)
        state_other = state_other + spread(weights_other[k]) * states[k].astype(F32)
    state_got = pair(state_other.astype(BF))
    base, slope = inner(
        queries, keys, values, u, norm_in[:, None, :], gate, top_own, doc_lengths, offset, heads
    )

    quarters = [place ^ 1, place ^ 3, place, place ^ 2]
    out = tokens
    start = 0
    leaving = []
    for wide in OUT_CHUNKS:
        if start == 0:
            hidden, send, keep = hidden_and_first(
                queries, state_own.astype(BF), state_got, base, slope, w_out, quarters, side,
                wide, start, heads,
            )
        else:
            now = after(leaving[-2], hidden) if len(leaving) > 1 else hidden
            send, keep = next_columns(now, w_out, quarters, wide, start)
        both = keep.astype(F32) + tensor(send, 1).astype(F32)
        leaving.append(both[:, wide:].astype(BF))
        came = tensor(leaving[-1], 2)
        summed = both[:, :wide] + came.astype(F32)
        columns = slice(start, start + wide)
        out = out.at[:, columns].set((tokens[:, columns].astype(F32) + summed).astype(BF))
        start += wide
    return out


FULL_ACCURACY = lax.Precision.HIGHEST


def plain_shifted(x, axis, by):
    devices = lax.axis_size(axis)
    pairs = [(i, i + by) for i in range(devices) if 0 <= i + by < devices]
    return lax.ppermute(x, axis, pairs)


def segment_of(doc_lengths, positions):
    bounds = jnp.cumsum(doc_lengths)[:-1]
    return jnp.sum((positions[:, None] >= bounds[None, :]).astype(jnp.int32), axis=1)


def combine(earlier, later):
    early_c, early_n, early_m, early_g, early_r = earlier
    late_c, late_n, late_m, late_g, late_r = later
    ceiling = jnp.maximum(early_m + late_g, late_m)
    early_weight = jnp.exp(early_m + late_g - ceiling)
    late_weight = jnp.exp(late_m - ceiling)
    reset_mask = late_r > 0.5
    merged_c = jnp.where(
        reset_mask[:, None, None],
        late_c,
        early_weight[:, None, None] * early_c + late_weight[:, None, None] * late_c,
    )
    merged_n = jnp.where(
        reset_mask[:, None], late_n, early_weight[:, None] * early_n + late_weight[:, None] * late_n
    )
    merged_m = jnp.where(reset_mask, late_m, ceiling)
    return (merged_c, merged_n, merged_m, late_g, jnp.maximum(early_r, late_r))


def block_local(queries, keys, value_rows, input_pre, log_forget, segment, segment_before):
    length = segment.shape[0]
    log_decay = jnp.cumsum(log_forget, axis=0)
    position = jnp.arange(length)
    allowed = (position[:, None] >= position[None, :]) & (segment[:, None] == segment[None, :])
    exponent = log_decay.T[:, :, None] - log_decay.T[:, None, :] + input_pre.T[:, None, :]
    exponent = jnp.where(allowed[None], exponent, -jnp.inf)
    inner_max = jnp.max(exponent, axis=2)
    scores = jnp.einsum("lhk,mhk->hlm", queries, keys, preferred_element_type=jnp.float32)
    weighted = jnp.exp(exponent - inner_max[:, :, None]) * scores
    weighted_bf = weighted.astype(jnp.bfloat16)
    inner_num = jnp.einsum(
        "hlm,mhv->lhv", weighted_bf, value_rows, preferred_element_type=jnp.float32
    )
    inner_den = jnp.sum(weighted, axis=2).T
    in_last = segment == segment[-1]
    tail_expo = log_decay[-1][None, :] - log_decay + input_pre
    tail_expo = jnp.where(in_last[:, None], tail_expo, -jnp.inf)
    tail_max = jnp.max(tail_expo, axis=0)
    key_scaled_rows = (jnp.exp(tail_expo - tail_max[None, :])[:, :, None] * keys).astype(
        jnp.bfloat16
    )
    cell_state_matrix = jnp.einsum(
        "emn,emp->mnp", key_scaled_rows, value_rows, preferred_element_type=jnp.float32
    )
    state_n = jnp.sum(key_scaled_rows.astype(jnp.float32), axis=0)
    reset = (segment[-1] != segment_before).astype(jnp.float32) * jnp.ones_like(tail_max)
    summary = (cell_state_matrix, state_n, tail_max, log_decay[-1], reset)
    return (log_decay, inner_max.T, inner_num, inner_den, summary)


def block_output(
    queries, log_decay, inner_max, inner_num, inner_den, segment, segment_before, incoming
):
    cell_state_matrix, state_n, state_m = incoming
    outer = jnp.where((segment == segment_before)[:, None], log_decay + state_m[None, :], -jnp.inf)
    ceiling = jnp.maximum(inner_max, outer)
    inner_weight = jnp.exp(inner_max - ceiling)
    outer_weight = jnp.exp(outer - ceiling)
    query_single = queries.astype(jnp.float32)
    outer_numerator_sum = jnp.einsum(
        "ciy,iyo->cio", query_single, cell_state_matrix, precision=FULL_ACCURACY
    )
    outer_den = jnp.einsum("lhk,hk->lh", query_single, state_n, precision=FULL_ACCURACY)
    numerator = (
        inner_weight[:, :, None] * inner_num + outer_weight[:, :, None] * outer_numerator_sum
    )
    denominator = inner_weight * inner_den + outer_weight * outer_den
    return numerator / jnp.maximum(jnp.abs(denominator), 1.0)[:, :, None]


def plain_local(
    tokens,
    w_query,
    w_key,
    w_value,
    w_outgate,
    w_gates,
    gate_bias,
    w_out,
    carry_matrix,
    carry_norm,
    carry_max,
    doc_lengths,
):
    length = tokens.shape[0]
    head_count = gate_bias.shape[1]
    query_size = w_query.shape[1] // head_count
    value_size = w_value.shape[1] // head_count
    matrices = (w_query, w_key, w_value, w_outgate)
    zero_init = tuple((jnp.zeros((length, matrix.shape[1]), jnp.float32) for matrix in matrices))
    zero_init = zero_init + (
        jnp.zeros((length, head_count), jnp.float32),
        jnp.zeros((length, head_count), jnp.float32),
    )
    column_block = lax.all_gather(tokens, "tensor", axis=1, tiled=True)
    updated = tuple(
        (jnp.dot(column_block, matrix, preferred_element_type=jnp.float32) for matrix in matrices)
    )
    input_sum = jnp.dot(column_block, w_gates[0], preferred_element_type=jnp.float32)
    forget_sum = jnp.dot(column_block, w_gates[1], preferred_element_type=jnp.float32)
    projected = updated + (input_sum, forget_sum)
    queries = projected[0].astype(jnp.bfloat16).reshape(length, head_count, query_size)
    keys = (
        (projected[1] * query_size ** (-0.5))
        .astype(jnp.bfloat16)
        .reshape(length, head_count, query_size)
    )
    value_rows = projected[2].astype(jnp.bfloat16).reshape(length, head_count, value_size)
    outgate = jax.nn.sigmoid(projected[3])
    input_pre = projected[4] + gate_bias[0][None, :]
    log_forget = jax.nn.log_sigmoid(projected[5] + gate_bias[1][None, :])
    offset = lax.axis_index("seq") * length
    positions = offset + jnp.arange(length, dtype=jnp.int32)
    segment = segment_of(doc_lengths, positions)
    segment_before = segment_of(doc_lengths, jnp.maximum(offset - 1, 0)[None])[0]
    log_decay, inner_max, inner_num, inner_den, summary = block_local(
        queries, keys, value_rows, input_pre, log_forget, segment, segment_before
    )
    start_state = (carry_matrix, carry_norm, carry_max)
    zero_heads = jnp.zeros((head_count,), jnp.float32)
    is_leader = lax.axis_index("seq") == 0

    def relay(iteration, current):
        leaving = combine(current + (zero_heads, zero_heads), summary)[:3]
        arrived = plain_shifted(leaving, "seq", 1)
        return tuple(
            (
                jnp.where(is_leader, initial, received)
                for initial, received in zip(start_state, arrived)
            )
        )

    incoming = lax.fori_loop(0, lax.axis_size("seq") - 1, relay, start_state)
    mixed_heads = block_output(
        queries, log_decay, inner_max, inner_num, inner_den, segment, segment_before, incoming
    )
    hidden = (outgate * mixed_heads.reshape(length, head_count * value_size)).astype(jnp.bfloat16)
    partial_value = jnp.dot(hidden, w_out, preferred_element_type=jnp.float32)
    summed = lax.psum_scatter(
        partial_value.astype(jnp.bfloat16), "tensor", scatter_dimension=1, tiled=True
    ).astype(jnp.float32)
    return (tokens.astype(jnp.float32) + summed).astype(jnp.bfloat16)


def solution(mesh):
    fast = mesh.shape["tensor"] == 4 and mesh.shape["seq"] % 4 == 0
    return jax.shard_map(
        local if fast else plain_local,
        mesh=mesh,
        in_specs=(
            P("seq", "tensor"),
            P(None, "tensor"),
            P(None, "tensor"),
            P(None, "tensor"),
            P(None, "tensor"),
            P(None, None, "tensor"),
            P(None, "tensor"),
            P("tensor", None),
            P("tensor", None, None),
            P("tensor", None),
            P("tensor"),
            P(),
        ),
        out_specs=P("seq", "tensor"),
        check_vma=False,
    )
```

```python
import functools

import jax
import jax.numpy as jnp
from jax import lax
from jax.experimental import pallas as pl
from jax.experimental.pallas import tpu as pltpu
from jax.sharding import PartitionSpec as P

BF = jnp.bfloat16
F32 = jnp.float32
MIB = 1024 * 1024
TOKEN_CHUNKS = ((256, 256), (512,))
OUT_CHUNKS = (256, 256, 256, 256)


def params(mib):
    return pltpu.CompilerParams(vmem_limit_bytes=mib * MIB)


def cost(flops, moved):
    return pl.CostEstimate(flops=int(flops), bytes_accessed=int(moved), transcendentals=0)


def swapped(x, axis, mask):
    size = lax.axis_size(axis)
    return lax.ppermute(x, axis, [(i, i ^ mask) for i in range(size)])


def shifted(x, axis, by):
    size = lax.axis_size(axis)
    return lax.ppermute(x, axis, [(i, (i + by) % size) for i in range(size)])


def after(first, *others):
    out = lax.optimization_barrier((first,) + others)[1:]
    return out[0] if len(out) == 1 else out


SMEM_SPEC = pl.BlockSpec(memory_space=pltpu.SMEM)
VMEM_SPEC = pl.BlockSpec(memory_space=pltpu.VMEM)
HBM_SPEC = pl.BlockSpec(memory_space=pltpu.HBM)


def in_hbm(x):
    return pltpu.with_memory_space_constraint(x, pltpu.HBM)


def across_tokens(w, x):
    return lax.dot_general(w, x, (((1,), (1,)), ((), ())), preferred_element_type=F32)


def row_start(place, share, owner, first):
    return pl.multiple_of((place ^ owner) * share + first, 128)


def stage_kernel(xs_at, ahead_at, share, with_sum, info, *refs):
    refs = list(refs)
    take = lambda n: [refs.pop(0) for _ in range(n)]
    pieces = len(xs_at)
    xs, ws, (gate_w,) = take(pieces), take(4), take(1)
    sums = take(5) if with_sum else None
    outs = take(5)
    ahead = take(4) if ahead_at else []
    held = take(4)
    sems, ahead_sems = take(2) if ahead_at else (take(1)[0], None)
    place = info[0]

    def copies(at, targets, semaphores):
        result = []
        for i, (w, target) in enumerate(zip(ws, targets)):
            low, group = 0, []
            for p, (owner, first, count) in enumerate(at):
                group.append(
                    pltpu.make_async_copy(
                        w.at[pl.ds(row_start(place, share, owner, first), count)],
                        target.at[pl.ds(low, count)],
                        semaphores.at[i, p],
                    )
                )
                low += count
            result.append(group)
        return result

    now = copies(xs_at, held, sems)
    for group in now:
        for copy in group:
            copy.start()
    later = copies(ahead_at, ahead, ahead_sems) if ahead_at else []
    for group in later:
        for copy in group:
            copy.start()
    gates = sums[4][...] if with_sum else 0.0
    for (owner, first, count), x in zip(xs_at, xs):
        gates = gates + across_tokens(
            gate_w[:, pl.ds(row_start(place, share, owner, first), count)], x[...]
        )
    outs[4][...] = gates
    for i in range(4):
        for copy in now[i]:
            copy.wait()

        def body(j, _, i=i):
            columns = pl.ds(pl.multiple_of(j * 256, 256), 256)
            total = sums[i][:, columns] if with_sum else None
            low = 0
            for (_, _, count), x in zip(xs_at, xs):
                part = jnp.dot(
                    x[...], held[i][low : low + count, columns], preferred_element_type=F32
                )
                total = part if total is None else total + part
                low += count
            outs[i][:, columns] = total
            return 0

        lax.fori_loop(0, outs[i].shape[1] // 256, body, 0)
    for group in later:
        for copy in group:
            copy.wait()


def stage(info, xs, xs_at, weights, gate_w, share, sums=None, ahead_at=None):
    length = xs[0].shape[0]
    count = sum(c for _, _, c in xs_at)
    shapes = [pltpu.VMEM((length, w.shape[1]), F32) for w in weights]
    shapes.append(pltpu.VMEM((gate_w.shape[0], length), F32))
    scratch = [pltpu.VMEM((count, w.shape[1]), BF) for w in weights]
    scratch.append(pltpu.SemaphoreType.DMA((4, len(xs_at))))
    if ahead_at:
        rows = sum(c for _, _, c in ahead_at)
        shapes += [pltpu.VMEM((rows, w.shape[1]), BF) for w in weights]
        scratch.append(pltpu.SemaphoreType.DMA((4, len(ahead_at))))
    operands = [info, *xs, *[in_hbm(w) for w in weights], gate_w]
    specs = [SMEM_SPEC] + [VMEM_SPEC] * len(xs) + [HBM_SPEC] * 4 + [VMEM_SPEC]
    aliases = {}
    if sums is not None:
        aliases = {len(operands) + i: i for i in range(5)}
        operands += sums
        specs += [VMEM_SPEC] * 5
    return pl.pallas_call(
        functools.partial(stage_kernel, xs_at, ahead_at, share, sums is not None),
        out_shape=tuple(shapes),
        in_specs=specs,
        out_specs=(VMEM_SPEC,) * len(shapes),
        scratch_shapes=scratch,
        input_output_aliases=aliases,
        compiler_params=params(24),
        cost_estimate=cost(1e6, 1e5),
    )(*operands)


def last_kernel(xs_count, *refs):
    xs = refs[:xs_count]
    query_w, gate_w, query_sum, gate_sum, query_out, gate_out = refs[xs_count:]
    for w, total, out, finish in (
        (query_w, query_sum, query_out, lambda x: x),
        (gate_w, gate_sum, gate_out, jax.nn.sigmoid),
    ):

        def body(j, _, w=w, total=total, out=out, finish=finish):
            columns = pl.ds(pl.multiple_of(j * 256, 256), 256)
            low, value = 0, total[:, columns]
            for x in xs:
                count = x.shape[1]
                value = value + jnp.dot(
                    x[...], w[low : low + count, columns], preferred_element_type=F32
                )
                low += count
            out[:, columns] = finish(value).astype(out.dtype)
            return 0

        lax.fori_loop(0, out.shape[1] // 256, body, 0)


def last_stage(xs, query_w, gate_w, query_sum, gate_sum):
    return pl.pallas_call(
        functools.partial(last_kernel, len(xs)),
        out_shape=(
            pltpu.VMEM(query_sum.shape, BF),
            pltpu.VMEM(gate_sum.shape, F32),
        ),
        in_specs=[VMEM_SPEC] * (len(xs) + 4),
        out_specs=(VMEM_SPEC,) * 2,
        compiler_params=params(12),
        cost_estimate=cost(1e6, 1e5),
    )(*xs, query_w, gate_w, query_sum, gate_sum)


def segments(docs, positions):
    total = jnp.zeros_like(positions)
    bound = jnp.int32(0)
    for j in range(docs.shape[0] - 1):
        bound = bound + docs[j]
        total = total + (positions >= bound).astype(jnp.int32)
    return total


def gate_rows(both, offset, docs, bias):
    heads, length = both.shape[0] // 2, both.shape[1]
    row = lax.broadcasted_iota(jnp.int32, (heads, length), 0)
    lane = lax.broadcasted_iota(jnp.int32, (heads, length), 1)
    input_bias = jnp.zeros((heads, length), F32)
    forget_bias = jnp.zeros((heads, length), F32)
    for h in range(heads):
        input_bias = jnp.where(row == h, bias[0, h], input_bias)
        forget_bias = jnp.where(row == h, bias[1, h], forget_bias)
    input_pre = both[:heads] + input_bias
    forget = both[heads:] + forget_bias
    decay = jnp.minimum(forget, 0.0) - jnp.log1p(jnp.exp(-jnp.abs(forget)))
    step = 1
    while step < length:
        decay = decay + jnp.where(lane >= step, pltpu.roll(decay, step, 1), 0.0)
        step *= 2
    u = input_pre - decay
    segment = segments(docs, lane + offset)
    last = segments(docs, lane * 0 + (offset + length - 1))
    open_rows = segment == last
    top = jnp.max(jnp.where(open_rows, u, -jnp.inf), axis=1, keepdims=True)
    weight = jnp.where(open_rows, jnp.exp(u - top), 0.0)
    total = decay[:, length - 1 : length]
    narrow = lax.broadcasted_iota(jnp.int32, (heads, 128), 1)
    stats = jnp.where(narrow == 0, total + top, jnp.where(narrow == 1, total, 0.0))
    return u, weight, stats


def summary_kernel(xs_at, share, heads, info, docs, bias, *refs):
    xs = refs[: len(xs_at)]
    key_w, value_w, gate_w, key_sum, value_sum, gate_sum = refs[len(xs_at) : len(xs_at) + 6]
    key_out, value_out, keep_out, send_out, small_out, u_out, state = refs[len(xs_at) + 6 :]
    place, side, offset = info[0], info[1], info[2]
    size, wide = state.shape
    gates = gate_sum[...]
    for (owner, first, count), x in zip(xs_at, xs):
        gates = gates + across_tokens(
            gate_w[:, pl.ds(row_start(place, share, owner, first), count)], x[...]
        )
    u, weight, stats = gate_rows(gates, offset, docs, bias)
    u_out[...] = u
    small_out[:, size:] = stats
    spare = jnp.zeros((128 - weight.shape[0], weight.shape[1]), F32)
    columns = jnp.concatenate([weight, spare], axis=0).T
    half = size // 2
    for h in range(heads):
        key_at, value_at = slice(h * size, (h + 1) * size), slice(h * wide, (h + 1) * wide)
        key, value, low = key_sum[:, key_at], value_sum[:, value_at], 0
        for x in xs:
            count = x.shape[1]
            rows = slice(low, low + count)
            key = key + jnp.dot(x[...], key_w[rows, key_at], preferred_element_type=F32)
            value = value + jnp.dot(x[...], value_w[rows, value_at], preferred_element_type=F32)
            low += count
        key = (key * size ** (-0.5)).astype(BF)
        value = value.astype(BF)
        key_out[:, key_at] = key
        value_out[:, value_at] = value
        scaled = (columns[:, h : h + 1] * key.astype(F32)).astype(BF)
        small_out[h : h + 1, :size] = jnp.sum(scaled.astype(F32), axis=0, keepdims=True)
        state[...] = lax.dot_general(
            scaled, value, (((0,), (0,)), ((), ())), preferred_element_type=F32
        )
        keep_out[h] = state[pl.ds(pl.multiple_of(side * half, half), half)].astype(BF)
        send_out[h] = state[pl.ds(pl.multiple_of((1 - side) * half, half), half)].astype(BF)


def block_summary(
    info, docs, bias, xs, xs_at, key_w, value_w, gate_w, key_sum, value_sum, gates, share, heads
):
    length = xs[0].shape[0]
    size, wide = key_w.shape[1] // heads, value_w.shape[1] // heads
    return pl.pallas_call(
        functools.partial(summary_kernel, xs_at, share, heads),
        out_shape=(
            pltpu.VMEM((length, heads * size), BF),
            pltpu.VMEM((length, heads * wide), BF),
            pltpu.VMEM((heads, size // 2, wide), BF),
            pltpu.VMEM((heads, size // 2, wide), BF),
            pltpu.VMEM((heads, size + 128), F32),
            pltpu.VMEM((heads, length), F32),
        ),
        in_specs=[SMEM_SPEC] * 3 + [VMEM_SPEC] * (len(xs) + 6),
        out_specs=(VMEM_SPEC,) * 6,
        scratch_shapes=[pltpu.VMEM((size, wide), F32)],
        compiler_params=params(16),
        cost_estimate=cost(4e9, 4e6),
    )(info, docs, bias, *xs, key_w, value_w, gate_w, key_sum, value_sum, gates)


def inner_kernel(
    heads, info, docs, top_in, query, key, value, u, norm, gate, w_out,
    base_out, slope_out, w_here, sem,
):
    fetch = pltpu.make_async_copy(w_out, w_here, sem)
    fetch.start()
    length = query.shape[0]
    size, wide = query.shape[1] // heads, value.shape[1] // heads
    offset = info[2]
    chunk = 128
    one = jnp.zeros((chunk, 1), jnp.int32)
    before = segments(docs, one + jnp.maximum(offset - 1, 0))
    for head in range(heads):
        keys_at = slice(head * size, (head + 1) * size)
        values_at = slice(head * wide, (head + 1) * wide)
        u_row = u[head : head + 1, :]
        norm_row = norm[head : head + 1, :]
        top = top_in[head]
        for low in range(0, length, chunk):
            high = low + chunk
            position_t = lax.broadcasted_iota(jnp.int32, (chunk, 1), 0) + low
            position_s = lax.broadcasted_iota(jnp.int32, (1, high), 1)
            segment_t = segments(docs, position_t + offset)
            segment_s = segments(docs, position_s + offset)
            allowed = (position_s <= position_t) & (segment_s == segment_t)
            expo = jnp.where(allowed, u_row[:, :high], -jnp.inf)
            peak = jnp.max(expo, axis=1, keepdims=True)
            q = query[low:high, keys_at]
            scores = lax.dot_general(
                q, key[:high, keys_at], (((1,), (1,)), ((), ())), preferred_element_type=F32
            )
            weighted = jnp.exp(expo - peak) * scores
            num = jnp.dot(
                weighted.astype(BF), value[:high, values_at], preferred_element_type=F32
            )
            den = jnp.sum(weighted, axis=1, keepdims=True)
            carried = segment_t == before
            ceiling = jnp.where(carried, jnp.maximum(peak, top), peak)
            inner_weight = jnp.exp(peak - ceiling)
            outer_weight = jnp.where(carried, jnp.exp(jnp.minimum(top - ceiling, 0.0)), 0.0)
            outer_den = jnp.sum(q.astype(F32) * norm_row, axis=1, keepdims=True)
            full = inner_weight * den + outer_weight * outer_den
            inverse = 1.0 / jnp.maximum(jnp.abs(full), 1.0)
            g = gate[low:high, values_at]
            base_out[low:high, values_at] = g * (num * (inner_weight * inverse))
            slope_out[low:high, values_at] = g * (outer_weight * inverse)
    fetch.wait()


def inner(info, docs, top, query, key, value, u, norm, gate, w_out, heads):
    length, depth = value.shape
    return pl.pallas_call(
        functools.partial(inner_kernel, heads),
        out_shape=(
            pltpu.VMEM((length, depth), F32),
            pltpu.VMEM((length, depth), F32),
            pltpu.VMEM(w_out.shape, BF),
        ),
        in_specs=[SMEM_SPEC] * 3 + [VMEM_SPEC] * 6 + [HBM_SPEC],
        out_specs=(VMEM_SPEC,) * 3,
        scratch_shapes=[pltpu.SemaphoreType.DMA],
        compiler_params=params(12),
        cost_estimate=cost(1e6, 1e5),
    )(info, docs, top, query, key, value, u, norm, gate, in_hbm(w_out))


def some_columns(info, hidden, w, send, keep, start):
    place = info[0]
    wide = send.shape[1] // 2
    share = w.shape[1] // 4
    for step, owner in enumerate((1, 3, 0, 2)):
        columns = pl.ds(pl.multiple_of((place ^ owner) * share + start, 128), wide)
        part = jnp.dot(hidden[...], w[:, columns], preferred_element_type=F32).astype(BF)
        out = (send, keep)[step // 2]
        low = (step % 2) * wide
        out[:, low : low + wide] = part


def hidden_kernel(heads, info, query, own, other, base, slope, w, hidden, send, keep, state):
    half = own.shape[1]
    side = info[1]
    size, wide = 2 * half, own.shape[2]
    for h in range(heads):
        state[pl.ds(pl.multiple_of(side * half, half), half)] = own[h]
        state[pl.ds(pl.multiple_of((1 - side) * half, half), half)] = other[h]
        outer = jnp.dot(
            query[:, h * size : (h + 1) * size], state[...], preferred_element_type=F32
        )
        columns = slice(h * wide, (h + 1) * wide)
        hidden[:, columns] = (base[:, columns] + slope[:, columns] * outer).astype(BF)
    some_columns(info, hidden, w, send, keep, 0)


def hidden_and_first(info, query, own, other, base, slope, w_here, wide, heads):
    length, depth = base.shape
    return pl.pallas_call(
        functools.partial(hidden_kernel, heads),
        out_shape=(
            pltpu.VMEM((length, depth), BF),
            pltpu.VMEM((length, 2 * wide), BF),
            pltpu.VMEM((length, 2 * wide), BF),
        ),
        in_specs=[SMEM_SPEC] + [VMEM_SPEC] * 6,
        out_specs=(VMEM_SPEC,) * 3,
        scratch_shapes=[pltpu.VMEM((2 * own.shape[1], own.shape[2]), BF)],
        compiler_params=params(12),
        cost_estimate=cost(3e9, 8e6),
    )(info, query, own, other, base, slope, w_here)


def columns_kernel(start, info, hidden, w, send, keep):
    some_columns(info, hidden, w, send, keep, start)


def next_columns(info, hidden, w_here, wide, start):
    length = hidden.shape[0]
    return pl.pallas_call(
        functools.partial(columns_kernel, start),
        out_shape=(pltpu.VMEM((length, 2 * wide), BF),) * 2,
        in_specs=[SMEM_SPEC, VMEM_SPEC, VMEM_SPEC],
        out_specs=(VMEM_SPEC,) * 2,
        compiler_params=params(12),
        cost_estimate=cost(1e6, 1e5),
    )(info, hidden, w_here)


def pick(flag, a, b):
    return jnp.where(flag, a, b)


def local(
    tokens,
    w_query,
    w_key,
    w_value,
    w_outgate,
    w_gates,
    gate_bias,
    w_out,
    carry_matrix,
    carry_norm,
    carry_max,
    doc_lengths,
):
    length, share = tokens.shape
    heads = gate_bias.shape[1]
    size = w_query.shape[1] // heads
    place = lax.axis_index("tensor")
    block = lax.axis_index("seq")
    blocks = lax.axis_size("seq")
    offset = (block * length).astype(jnp.int32)
    tensor = lambda x, mask: swapped(x, "tensor", mask)
    pair = lambda x: swapped(x, "seq", 1)
    down = lambda x: shifted(x, "seq", 2)

    groups, source, start = [], tokens, 0
    for chunks in TOKEN_CHUNKS:
        group = []
        for c in chunks:
            piece = source[:, start : start + c]
            group.append((start, c, tensor(piece, 2)))
            source = after(piece, source)
            start += c
        groups.append(group)
    beside = tensor(tokens, 1)
    gate_w = w_gates.transpose(0, 2, 1).reshape(2 * heads, 4 * share)

    side = (block % 2).astype(jnp.int32)
    info = jnp.stack([place, side, offset]).astype(jnp.int32)
    weights = (w_key, w_value, w_query, w_outgate)
    at = [[(o, s, c) for s, c, _ in group for o in (2, 3)] for group in groups]
    near_at = [(0, 0, share), (1, 0, share)]
    sums = stage(info, [source, beside], near_at, weights, gate_w, share)
    for i, group in enumerate(groups):
        xs = lax.optimization_barrier((*[x for _, _, x in group], *sums))
        xs, sums = xs[: len(group)], xs[len(group) :]
        xs = [y for x in xs for y in (x, tensor(x, 1))]
        if i < len(groups) - 1:
            *sums, w_key_last, w_value_last, w_query_last, w_gate_last = stage(
                info, xs, at[i], weights, gate_w, share, sums, at[-1]
            )
    keys, values, kept, sent, small, u = block_summary(
        info, doc_lengths, gate_bias, xs, at[-1], w_key_last, w_value_last, gate_w,
        sums[0], sums[1], sums[4], share, heads,
    )

    even = side == 0
    z = block // 2
    reach = blocks // 4
    small_other = pair(small)
    got = pair(sent)
    small_other, got = lax.optimization_barrier((small_other, got))
    last_xs = after(keys, *xs)
    queries, gate = last_stage(last_xs, w_query_last, w_gate_last, sums[2], sums[3])

    def segment_at(position):
        return segments(doc_lengths, position)

    def reset(index):
        first = jnp.maximum(index * length - 1, 0)
        return segment_at((index + 1) * length - 1) != segment_at(first)

    def packed(norm, m, g):
        return jnp.concatenate(
            [norm, m[:, None], g[:, None], jnp.zeros((heads, 126), F32)], axis=1
        )

    def unpacked(x):
        return x[:, :size], x[:, size], x[:, size + 1]

    norm_own, m_own, g_own = unpacked(small)
    norm_other, m_other, g_other = unpacked(small_other)
    m_even, g_even = pick(even, m_own, m_other), pick(even, g_own, g_other)
    m_odd, g_odd = pick(even, m_other, m_own), pick(even, g_other, g_own)
    reset_even, reset_odd = reset(2 * z), reset(2 * z + 1)
    m_pair = jnp.maximum(pick(reset_odd, -jnp.inf, m_even + g_odd), m_odd)
    pair_even = pick(reset_odd, 0.0, jnp.exp(jnp.minimum(m_even + g_odd - m_pair, 0.0)))
    pair_odd = jnp.exp(m_odd - m_pair)
    pair_own = pick(even, pair_even, pair_odd)
    pair_other = pick(even, pair_odd, pair_even)

    spread = lambda w: w[:, None, None]
    norm_pair = pair_own[:, None] * norm_own + pair_other[:, None] * norm_other
    norm_even = pick(even, norm_own, norm_other)
    kept, got = kept.astype(F32), got.astype(F32)
    state_even = pick(even, kept, got)
    state_pair = (spread(pair_own) * kept + spread(pair_other) * got).astype(BF)

    travel = packed(norm_pair, m_pair, g_even + g_odd)
    smalls, states = [], []
    for k in range(reach):
        travel, state_pair = lax.optimization_barrier((down(travel), down(state_pair)))
        smalls.append(unpacked(travel))
        states.append(state_pair)
    expos = []
    passed = jnp.zeros_like(m_pair)
    unbroken = jnp.bool_(True)
    for k in range(1, reach + 1):
        there = z >= k
        expos.append(pick(there & unbroken, smalls[k - 1][1] + passed, -jnp.inf))
        passed = passed + pick(there, smalls[k - 1][2], 0.0)
        broken = there & (reset(2 * (z - k)) | reset(2 * (z - k) + 1))
        unbroken = unbroken & ~broken
    expos.append(pick((z <= reach) & unbroken, carry_max + passed, -jnp.inf))
    expos = jnp.stack(expos)
    top_even = jnp.max(expos, axis=0)
    expos_odd = pick(reset_even, -jnp.inf, expos + g_even)
    top_odd = jnp.maximum(jnp.max(expos_odd, axis=0), m_even)
    weights_even = jnp.exp(expos - top_even)
    weights_odd = jnp.exp(expos_odd - top_odd)
    direct = jnp.exp(m_even - top_odd)
    weights_own = pick(even, weights_even, weights_odd)
    weights_other = pick(even, weights_odd, weights_even)
    direct_own = pick(even, 0.0, direct)
    direct_other = pick(even, direct, 0.0)
    top_own = pick(even, top_even, top_odd)

    norm_in = direct_own[:, None] * norm_even + weights_own[reach][:, None] * carry_norm
    carried = lax.dynamic_slice(
        carry_matrix, (0, side * (size // 2), 0), (heads, size // 2, carry_matrix.shape[2])
    )
    state_own = spread(weights_own[reach]) * carried + spread(direct_own) * state_even
    state_other = spread(weights_other[reach]) * carried + spread(direct_other) * state_even
    for k in range(reach):
        norm_in = norm_in + weights_own[k][:, None] * smalls[k][0]
        state_own = state_own + spread(weights_own[k]) * states[k].astype(F32)
        state_other = state_other + spread(weights_other[k]) * states[k].astype(F32)
    state_got = pair(state_other.astype(BF))
    base, slope, w_here = inner(
        info, doc_lengths, top_own, queries, keys, values, u, norm_in, gate, w_out, heads
    )

    out = tokens
    start = 0
    leaving = []
    for wide in OUT_CHUNKS:
        if start == 0:
            hidden, send, keep = hidden_and_first(
                info, queries, state_own.astype(BF), state_got, base, slope, w_here, wide, heads
            )
        else:
            now = after(leaving[-2], hidden) if len(leaving) > 1 else hidden
            send, keep = next_columns(info, now, w_here, wide, start)
        both = keep.astype(F32) + tensor(send, 1).astype(F32)
        leaving.append(both[:, wide:].astype(BF))
        came = tensor(leaving[-1], 2)
        summed = both[:, :wide] + came.astype(F32)
        columns = slice(start, start + wide)
        out = out.at[:, columns].set((tokens[:, columns].astype(F32) + summed).astype(BF))
        start += wide
    return out


FULL_ACCURACY = lax.Precision.HIGHEST


def plain_shifted(x, axis, by):
    devices = lax.axis_size(axis)
    pairs = [(i, i + by) for i in range(devices) if 0 <= i + by < devices]
    return lax.ppermute(x, axis, pairs)


def segment_of(doc_lengths, positions):
    bounds = jnp.cumsum(doc_lengths)[:-1]
    return jnp.sum((positions[:, None] >= bounds[None, :]).astype(jnp.int32), axis=1)


def combine(earlier, later):
    early_c, early_n, early_m, early_g, early_r = earlier
    late_c, late_n, late_m, late_g, late_r = later
    ceiling = jnp.maximum(early_m + late_g, late_m)
    early_weight = jnp.exp(early_m + late_g - ceiling)
    late_weight = jnp.exp(late_m - ceiling)
    reset_mask = late_r > 0.5
    merged_c = jnp.where(
        reset_mask[:, None, None],
        late_c,
        early_weight[:, None, None] * early_c + late_weight[:, None, None] * late_c,
    )
    merged_n = jnp.where(
        reset_mask[:, None], late_n, early_weight[:, None] * early_n + late_weight[:, None] * late_n
    )
    merged_m = jnp.where(reset_mask, late_m, ceiling)
    return (merged_c, merged_n, merged_m, late_g, jnp.maximum(early_r, late_r))


def block_local(queries, keys, value_rows, input_pre, log_forget, segment, segment_before):
    length = segment.shape[0]
    log_decay = jnp.cumsum(log_forget, axis=0)
    position = jnp.arange(length)
    allowed = (position[:, None] >= position[None, :]) & (segment[:, None] == segment[None, :])
    exponent = log_decay.T[:, :, None] - log_decay.T[:, None, :] + input_pre.T[:, None, :]
    exponent = jnp.where(allowed[None], exponent, -jnp.inf)
    inner_max = jnp.max(exponent, axis=2)
    scores = jnp.einsum("lhk,mhk->hlm", queries, keys, preferred_element_type=jnp.float32)
    weighted = jnp.exp(exponent - inner_max[:, :, None]) * scores
    weighted_bf = weighted.astype(jnp.bfloat16)
    inner_num = jnp.einsum(
        "hlm,mhv->lhv", weighted_bf, value_rows, preferred_element_type=jnp.float32
    )
    inner_den = jnp.sum(weighted, axis=2).T
    in_last = segment == segment[-1]
    tail_expo = log_decay[-1][None, :] - log_decay + input_pre
    tail_expo = jnp.where(in_last[:, None], tail_expo, -jnp.inf)
    tail_max = jnp.max(tail_expo, axis=0)
    key_scaled_rows = (jnp.exp(tail_expo - tail_max[None, :])[:, :, None] * keys).astype(
        jnp.bfloat16
    )
    cell_state_matrix = jnp.einsum(
        "emn,emp->mnp", key_scaled_rows, value_rows, preferred_element_type=jnp.float32
    )
    state_n = jnp.sum(key_scaled_rows.astype(jnp.float32), axis=0)
    reset = (segment[-1] != segment_before).astype(jnp.float32) * jnp.ones_like(tail_max)
    summary = (cell_state_matrix, state_n, tail_max, log_decay[-1], reset)
    return (log_decay, inner_max.T, inner_num, inner_den, summary)


def block_output(
    queries, log_decay, inner_max, inner_num, inner_den, segment, segment_before, incoming
):
    cell_state_matrix, state_n, state_m = incoming
    outer = jnp.where((segment == segment_before)[:, None], log_decay + state_m[None, :], -jnp.inf)
    ceiling = jnp.maximum(inner_max, outer)
    inner_weight = jnp.exp(inner_max - ceiling)
    outer_weight = jnp.exp(outer - ceiling)
    query_single = queries.astype(jnp.float32)
    outer_numerator_sum = jnp.einsum(
        "ciy,iyo->cio", query_single, cell_state_matrix, precision=FULL_ACCURACY
    )
    outer_den = jnp.einsum("lhk,hk->lh", query_single, state_n, precision=FULL_ACCURACY)
    numerator = (
        inner_weight[:, :, None] * inner_num + outer_weight[:, :, None] * outer_numerator_sum
    )
    denominator = inner_weight * inner_den + outer_weight * outer_den
    return numerator / jnp.maximum(jnp.abs(denominator), 1.0)[:, :, None]


def plain_local(
    tokens,
    w_query,
    w_key,
    w_value,
    w_outgate,
    w_gates,
    gate_bias,
    w_out,
    carry_matrix,
    carry_norm,
    carry_max,
    doc_lengths,
):
    length = tokens.shape[0]
    head_count = gate_bias.shape[1]
    query_size = w_query.shape[1] // head_count
    value_size = w_value.shape[1] // head_count
    matrices = (w_query, w_key, w_value, w_outgate)
    zero_init = tuple((jnp.zeros((length, matrix.shape[1]), jnp.float32) for matrix in matrices))
    zero_init = zero_init + (
        jnp.zeros((length, head_count), jnp.float32),
        jnp.zeros((length, head_count), jnp.float32),
    )
    column_block = lax.all_gather(tokens, "tensor", axis=1, tiled=True)
    updated = tuple(
        (jnp.dot(column_block, matrix, preferred_element_type=jnp.float32) for matrix in matrices)
    )
    input_sum = jnp.dot(column_block, w_gates[0], preferred_element_type=jnp.float32)
    forget_sum = jnp.dot(column_block, w_gates[1], preferred_element_type=jnp.float32)
    projected = updated + (input_sum, forget_sum)
    queries = projected[0].astype(jnp.bfloat16).reshape(length, head_count, query_size)
    keys = (
        (projected[1] * query_size ** (-0.5))
        .astype(jnp.bfloat16)
        .reshape(length, head_count, query_size)
    )
    value_rows = projected[2].astype(jnp.bfloat16).reshape(length, head_count, value_size)
    outgate = jax.nn.sigmoid(projected[3])
    input_pre = projected[4] + gate_bias[0][None, :]
    log_forget = jax.nn.log_sigmoid(projected[5] + gate_bias[1][None, :])
    offset = lax.axis_index("seq") * length
    positions = offset + jnp.arange(length, dtype=jnp.int32)
    segment = segment_of(doc_lengths, positions)
    segment_before = segment_of(doc_lengths, jnp.maximum(offset - 1, 0)[None])[0]
    log_decay, inner_max, inner_num, inner_den, summary = block_local(
        queries, keys, value_rows, input_pre, log_forget, segment, segment_before
    )
    start_state = (carry_matrix, carry_norm, carry_max)
    zero_heads = jnp.zeros((head_count,), jnp.float32)
    is_leader = lax.axis_index("seq") == 0

    def relay(iteration, current):
        leaving = combine(current + (zero_heads, zero_heads), summary)[:3]
        arrived = plain_shifted(leaving, "seq", 1)
        return tuple(
            (
                jnp.where(is_leader, initial, received)
                for initial, received in zip(start_state, arrived)
            )
        )

    incoming = lax.fori_loop(0, lax.axis_size("seq") - 1, relay, start_state)
    mixed_heads = block_output(
        queries, log_decay, inner_max, inner_num, inner_den, segment, segment_before, incoming
    )
    hidden = (outgate * mixed_heads.reshape(length, head_count * value_size)).astype(jnp.bfloat16)
    partial_value = jnp.dot(hidden, w_out, preferred_element_type=jnp.float32)
    summed = lax.psum_scatter(
        partial_value.astype(jnp.bfloat16), "tensor", scatter_dimension=1, tiled=True
    ).astype(jnp.float32)
    return (tokens.astype(jnp.float32) + summed).astype(jnp.bfloat16)


def solution(mesh):
    fast = mesh.shape["tensor"] == 4 and mesh.shape["seq"] % 4 == 0
    return jax.shard_map(
        local if fast else plain_local,
        mesh=mesh,
        in_specs=(
            P("seq", "tensor"),
            P(None, "tensor"),
            P(None, "tensor"),
            P(None, "tensor"),
            P(None, "tensor"),
            P(None, None, "tensor"),
            P(None, "tensor"),
            P("tensor", None),
            P("tensor", None, None),
            P("tensor", None),
            P("tensor"),
            P(),
        ),
        out_specs=P("seq", "tensor"),
        check_vma=False,
    )
```

```python
import functools

import jax
import jax.numpy as jnp
from jax import lax
from jax.experimental import pallas as pl
from jax.experimental.pallas import tpu as pltpu
from jax.sharding import PartitionSpec as P

BF = jnp.bfloat16
F32 = jnp.float32
MIB = 1024 * 1024
TOKEN_CHUNKS = ((256, 256), (512,))
OUT_CHUNKS = (256, 256, 256, 256)


def params(mib):
    return pltpu.CompilerParams(vmem_limit_bytes=mib * MIB)


def cost(flops, moved):
    return pl.CostEstimate(flops=int(flops), bytes_accessed=int(moved), transcendentals=0)


def swapped(x, axis, mask):
    size = lax.axis_size(axis)
    return lax.ppermute(x, axis, [(i, i ^ mask) for i in range(size)])


def shifted(x, axis, by):
    size = lax.axis_size(axis)
    return lax.ppermute(x, axis, [(i, (i + by) % size) for i in range(size)])


def after(first, *others):
    out = lax.optimization_barrier((first,) + others)[1:]
    return out[0] if len(out) == 1 else out


SMEM_SPEC = pl.BlockSpec(memory_space=pltpu.SMEM)
VMEM_SPEC = pl.BlockSpec(memory_space=pltpu.VMEM)
HBM_SPEC = pl.BlockSpec(memory_space=pltpu.HBM)


def in_hbm(x):
    return pltpu.with_memory_space_constraint(x, pltpu.HBM)


def split_kernel(starts, tokens, *refs):
    outs, sem = refs[:-1], refs[-1]
    copies = []
    for i, (low, out) in enumerate(zip(starts, outs)):
        source = tokens.at[:, low : low + out.shape[1]]
        copies.append(pltpu.make_async_copy(source, out, sem.at[i]))
        copies[-1].start()
    for copy in copies:
        copy.wait()


def split_tokens(tokens, starts, sizes):
    length = tokens.shape[0]
    return pl.pallas_call(
        functools.partial(split_kernel, starts),
        out_shape=tuple(pltpu.VMEM((length, c), BF) for c in sizes),
        in_specs=[HBM_SPEC],
        out_specs=(VMEM_SPEC,) * len(sizes),
        scratch_shapes=[pltpu.SemaphoreType.DMA((len(sizes),))],
        compiler_params=params(4),
        cost_estimate=cost(1e6, 1e5),
    )(in_hbm(tokens))


def across_tokens(w, x):
    return lax.dot_general(w, x, (((1,), (1,)), ((), ())), preferred_element_type=F32)


def row_start(place, share, owner, first):
    return pl.multiple_of((place ^ owner) * share + first, 128)


def stage_kernel(xs_at, ahead_at, share, with_sum, info, *refs):
    refs = list(refs)
    take = lambda n: [refs.pop(0) for _ in range(n)]
    pieces = len(xs_at)
    xs, ws, (gate_w,) = take(pieces), take(4), take(1)
    sums = take(5) if with_sum else None
    outs = take(5)
    ahead = take(4) if ahead_at else []
    held = take(4)
    sems, ahead_sems = take(2) if ahead_at else (take(1)[0], None)
    place = info[0]

    def copies(at, targets, semaphores):
        result = []
        for i, (w, target) in enumerate(zip(ws, targets)):
            low, group = 0, []
            for p, (owner, first, count) in enumerate(at):
                group.append(
                    pltpu.make_async_copy(
                        w.at[pl.ds(row_start(place, share, owner, first), count)],
                        target.at[pl.ds(low, count)],
                        semaphores.at[i, p],
                    )
                )
                low += count
            result.append(group)
        return result

    now = copies(xs_at, held, sems)
    for group in now:
        for copy in group:
            copy.start()
    later = copies(ahead_at, ahead, ahead_sems) if ahead_at else []
    for group in later:
        for copy in group:
            copy.start()
    gates = sums[4][...] if with_sum else 0.0
    for (owner, first, count), x in zip(xs_at, xs):
        gates = gates + across_tokens(
            gate_w[:, pl.ds(row_start(place, share, owner, first), count)], x[...]
        )
    outs[4][...] = gates
    for i in range(4):
        for copy in now[i]:
            copy.wait()

        def body(j, _, i=i):
            columns = pl.ds(pl.multiple_of(j * 256, 256), 256)
            total = sums[i][:, columns] if with_sum else None
            low = 0
            for (_, _, count), x in zip(xs_at, xs):
                part = jnp.dot(
                    x[...], held[i][low : low + count, columns], preferred_element_type=F32
                )
                total = part if total is None else total + part
                low += count
            outs[i][:, columns] = total
            return 0

        lax.fori_loop(0, outs[i].shape[1] // 256, body, 0)
    for group in later:
        for copy in group:
            copy.wait()


def stage(info, xs, xs_at, weights, gate_w, share, sums=None, ahead_at=None):
    length = xs[0].shape[0]
    count = sum(c for _, _, c in xs_at)
    shapes = [pltpu.VMEM((length, w.shape[1]), F32) for w in weights]
    shapes.append(pltpu.VMEM((gate_w.shape[0], length), F32))
    scratch = [pltpu.VMEM((count, w.shape[1]), BF) for w in weights]
    scratch.append(pltpu.SemaphoreType.DMA((4, len(xs_at))))
    if ahead_at:
        rows = sum(c for _, _, c in ahead_at)
        shapes += [pltpu.VMEM((rows, w.shape[1]), BF) for w in weights]
        scratch.append(pltpu.SemaphoreType.DMA((4, len(ahead_at))))
    operands = [info, *xs, *[in_hbm(w) for w in weights], gate_w]
    specs = [SMEM_SPEC] + [VMEM_SPEC] * len(xs) + [HBM_SPEC] * 4 + [VMEM_SPEC]
    aliases = {}
    if sums is not None:
        aliases = {len(operands) + i: i for i in range(5)}
        operands += sums
        specs += [VMEM_SPEC] * 5
    return pl.pallas_call(
        functools.partial(stage_kernel, xs_at, ahead_at, share, sums is not None),
        out_shape=tuple(shapes),
        in_specs=specs,
        out_specs=(VMEM_SPEC,) * len(shapes),
        scratch_shapes=scratch,
        input_output_aliases=aliases,
        compiler_params=params(24),
        cost_estimate=cost(1e6, 1e5),
    )(*operands)


def last_kernel(xs_count, *refs):
    xs = refs[:xs_count]
    query_w, gate_w, query_sum, gate_sum, query_out, gate_out = refs[xs_count:]
    for w, total, out, finish in (
        (query_w, query_sum, query_out, lambda x: x),
        (gate_w, gate_sum, gate_out, jax.nn.sigmoid),
    ):

        def body(j, _, w=w, total=total, out=out, finish=finish):
            columns = pl.ds(pl.multiple_of(j * 256, 256), 256)
            low, value = 0, total[:, columns]
            for x in xs:
                count = x.shape[1]
                value = value + jnp.dot(
                    x[...], w[low : low + count, columns], preferred_element_type=F32
                )
                low += count
            out[:, columns] = finish(value).astype(out.dtype)
            return 0

        lax.fori_loop(0, out.shape[1] // 256, body, 0)


def last_stage(xs, query_w, gate_w, query_sum, gate_sum):
    return pl.pallas_call(
        functools.partial(last_kernel, len(xs)),
        out_shape=(
            pltpu.VMEM(query_sum.shape, BF),
            pltpu.VMEM(gate_sum.shape, F32),
        ),
        in_specs=[VMEM_SPEC] * (len(xs) + 4),
        out_specs=(VMEM_SPEC,) * 2,
        compiler_params=params(12),
        cost_estimate=cost(1e6, 1e5),
    )(*xs, query_w, gate_w, query_sum, gate_sum)


def segments(docs, positions):
    total = jnp.zeros_like(positions)
    bound = jnp.int32(0)
    for j in range(docs.shape[0] - 1):
        bound = bound + docs[j]
        total = total + (positions >= bound).astype(jnp.int32)
    return total


def gate_rows(both, offset, docs, bias):
    heads, length = both.shape[0] // 2, both.shape[1]
    row = lax.broadcasted_iota(jnp.int32, (heads, length), 0)
    lane = lax.broadcasted_iota(jnp.int32, (heads, length), 1)
    input_bias = jnp.zeros((heads, length), F32)
    forget_bias = jnp.zeros((heads, length), F32)
    for h in range(heads):
        input_bias = jnp.where(row == h, bias[0, h], input_bias)
        forget_bias = jnp.where(row == h, bias[1, h], forget_bias)
    input_pre = both[:heads] + input_bias
    forget = both[heads:] + forget_bias
    decay = jnp.minimum(forget, 0.0) - jnp.log1p(jnp.exp(-jnp.abs(forget)))
    step = 1
    while step < length:
        decay = decay + jnp.where(lane >= step, pltpu.roll(decay, step, 1), 0.0)
        step *= 2
    u = input_pre - decay
    segment = segments(docs, lane + offset)
    last = segments(docs, lane * 0 + (offset + length - 1))
    open_rows = segment == last
    top = jnp.max(jnp.where(open_rows, u, -jnp.inf), axis=1, keepdims=True)
    weight = jnp.where(open_rows, jnp.exp(u - top), 0.0)
    total = decay[:, length - 1 : length]
    narrow = lax.broadcasted_iota(jnp.int32, (heads, 128), 1)
    stats = jnp.where(narrow == 0, total + top, jnp.where(narrow == 1, total, 0.0))
    return u, weight, stats


def summary_kernel(xs_at, share, heads, info, docs, bias, *refs):
    xs = refs[: len(xs_at)]
    key_w, value_w, gate_w, key_sum, value_sum, gate_sum = refs[len(xs_at) : len(xs_at) + 6]
    key_out, value_out, keep_out, send_out, small_out, u_out, state = refs[len(xs_at) + 6 :]
    place, side, offset = info[0], info[1], info[2]
    size, wide = state.shape
    gates = gate_sum[...]
    for (owner, first, count), x in zip(xs_at, xs):
        gates = gates + across_tokens(
            gate_w[:, pl.ds(row_start(place, share, owner, first), count)], x[...]
        )
    u, weight, stats = gate_rows(gates, offset, docs, bias)
    u_out[...] = u
    small_out[:, size:] = stats
    spare = jnp.zeros((128 - weight.shape[0], weight.shape[1]), F32)
    columns = jnp.concatenate([weight, spare], axis=0).T
    half = size // 2
    for h in range(heads):
        key_at, value_at = slice(h * size, (h + 1) * size), slice(h * wide, (h + 1) * wide)
        key, value, low = key_sum[:, key_at], value_sum[:, value_at], 0
        for x in xs:
            count = x.shape[1]
            rows = slice(low, low + count)
            key = key + jnp.dot(x[...], key_w[rows, key_at], preferred_element_type=F32)
            value = value + jnp.dot(x[...], value_w[rows, value_at], preferred_element_type=F32)
            low += count
        key = (key * size ** (-0.5)).astype(BF)
        value = value.astype(BF)
        key_out[:, key_at] = key
        value_out[:, value_at] = value
        scaled = (columns[:, h : h + 1] * key.astype(F32)).astype(BF)
        small_out[h : h + 1, :size] = jnp.sum(scaled.astype(F32), axis=0, keepdims=True)
        state[...] = lax.dot_general(
            scaled, value, (((0,), (0,)), ((), ())), preferred_element_type=F32
        )
        keep_out[h] = state[pl.ds(pl.multiple_of(side * half, half), half)].astype(BF)
        send_out[h] = state[pl.ds(pl.multiple_of((1 - side) * half, half), half)].astype(BF)


def block_summary(
    info, docs, bias, xs, xs_at, key_w, value_w, gate_w, key_sum, value_sum, gates, share, heads
):
    length = xs[0].shape[0]
    size, wide = key_w.shape[1] // heads, value_w.shape[1] // heads
    return pl.pallas_call(
        functools.partial(summary_kernel, xs_at, share, heads),
        out_shape=(
            pltpu.VMEM((length, heads * size), BF),
            pltpu.VMEM((length, heads * wide), BF),
            pltpu.VMEM((heads, size // 2, wide), BF),
            pltpu.VMEM((heads, size // 2, wide), BF),
            pltpu.VMEM((heads, size + 128), F32),
            pltpu.VMEM((heads, length), F32),
        ),
        in_specs=[SMEM_SPEC] * 3 + [VMEM_SPEC] * (len(xs) + 6),
        out_specs=(VMEM_SPEC,) * 6,
        scratch_shapes=[pltpu.VMEM((size, wide), F32)],
        compiler_params=params(16),
        cost_estimate=cost(4e9, 4e6),
    )(info, docs, bias, *xs, key_w, value_w, gate_w, key_sum, value_sum, gates)


def reset_of(docs, index, length):
    first = jnp.maximum(index * length - 1, 0)
    return segments(docs, (index + 1) * length - 1) != segments(docs, first)


def pair_scales(info, docs, length, size, own, other):
    even = info[1] == 0
    first = info[2] // length - info[1]
    m_own, g_own = own[:, size : size + 1], own[:, size + 1 : size + 2]
    m_other, g_other = other[:, size : size + 1], other[:, size + 1 : size + 2]
    m_even, g_even = jnp.where(even, m_own, m_other), jnp.where(even, g_own, g_other)
    m_odd, g_odd = jnp.where(even, m_other, m_own), jnp.where(even, g_other, g_own)
    reset_odd = reset_of(docs, first + 1, length)
    m_pair = jnp.maximum(jnp.where(reset_odd, -jnp.inf, m_even + g_odd), m_odd)
    pair_even = jnp.where(reset_odd, 0.0, jnp.exp(jnp.minimum(m_even + g_odd - m_pair, 0.0)))
    pair_odd = jnp.exp(m_odd - m_pair)
    weights = jnp.where(even, pair_even, pair_odd), jnp.where(even, pair_odd, pair_even)
    return m_even, g_even, g_odd, m_pair, weights


def pair_kernel(length, info, docs, own, other, kept, got, state_out, small_out):
    heads = own.shape[0]
    size = own.shape[1] - 128
    _, g_even, g_odd, m_pair, (w_own, w_other) = pair_scales(
        info, docs, length, size, own[...], other[...]
    )
    small_out[:, :size] = w_own * own[:, :size] + w_other * other[:, :size]
    lane = lax.broadcasted_iota(jnp.int32, (heads, 128), 1)
    small_out[:, size:] = jnp.where(
        lane == 0, m_pair, jnp.where(lane == 1, g_even + g_odd, 0.0)
    )
    for h in range(heads):
        at = slice(h, h + 1)
        state = w_own[at] * kept[h].astype(F32) + w_other[at] * got[h].astype(F32)
        state_out[h] = state.astype(BF)


def pair_summary(info, docs, small, small_other, kept, got, length):
    return pl.pallas_call(
        functools.partial(pair_kernel, length),
        out_shape=(pltpu.VMEM(kept.shape, BF), pltpu.VMEM(small.shape, F32)),
        in_specs=[SMEM_SPEC] * 2 + [VMEM_SPEC] * 4,
        out_specs=(VMEM_SPEC,) * 2,
        compiler_params=params(4),
        cost_estimate=cost(1e6, 1e5),
    )(info, docs, small, small_other, kept, got)


def incoming_kernel(length, reach, info, docs, own, other, kept, got, *refs):
    smalls, states = refs[:reach], refs[reach : 2 * reach]
    carry, carry_norm, carry_max = refs[2 * reach : 2 * reach + 3]
    own_out, other_out, norm_out, top_out = refs[2 * reach + 3 :]
    heads = own.shape[0]
    size = own.shape[1] - 128
    half = size // 2
    side = info[1]
    even = side == 0
    first = info[2] // length - side
    m_even, g_even, _, _, _ = pair_scales(info, docs, length, size, own[...], other[...])
    reset_even = reset_of(docs, first, length)
    expos = []
    passed = jnp.zeros((heads, 1), F32)
    unbroken = jnp.bool_(True)
    for k in range(1, reach + 1):
        there = first >= 2 * k
        index = jnp.maximum(first - 2 * k, 0)
        m_k, g_k = smalls[k - 1][:, size : size + 1], smalls[k - 1][:, size + 1 : size + 2]
        expos.append(jnp.where(there & unbroken, m_k + passed, -jnp.inf))
        passed = passed + jnp.where(there, g_k, 0.0)
        broken = reset_of(docs, index, length) | reset_of(docs, index + 1, length)
        unbroken = unbroken & ~(there & broken)
    in_reach = (first <= 2 * reach) & unbroken
    expos.append(jnp.where(in_reach, carry_max[...] + passed, -jnp.inf))
    top_even = functools.reduce(jnp.maximum, expos)
    expos_odd = [jnp.where(reset_even, -jnp.inf, e + g_even) for e in expos]
    top_odd = functools.reduce(jnp.maximum, expos_odd, m_even)
    w_even = [jnp.exp(e - top_even) for e in expos]
    w_odd = [jnp.exp(e - top_odd) for e in expos_odd]
    direct = jnp.exp(m_even - top_odd)
    w_own = [jnp.where(even, a, b) for a, b in zip(w_even, w_odd)]
    w_other = [jnp.where(even, b, a) for a, b in zip(w_even, w_odd)]
    direct_own = jnp.where(even, 0.0, direct)
    direct_other = jnp.where(even, direct, 0.0)
    top_out[...] = jnp.where(even, top_even, top_odd) + jnp.zeros((heads, 128), F32)
    norm = direct_own * jnp.where(even, own[:, :size], other[:, :size])
    norm = norm + w_own[reach] * carry_norm[...]
    for k in range(reach):
        norm = norm + w_own[k] * smalls[k][:, :size]
    norm_out[...] = norm
    rows = pl.ds(pl.multiple_of(side * half, half), half)
    for h in range(heads):
        at = slice(h, h + 1)
        here = jnp.where(even, kept[h].astype(F32), got[h].astype(F32))
        base = carry[h, rows, :]
        mine = w_own[reach][at] * base + direct_own[at] * here
        theirs = w_other[reach][at] * base + direct_other[at] * here
        for k in range(reach):
            state = states[k][h].astype(F32)
            mine = mine + w_own[k][at] * state
            theirs = theirs + w_other[k][at] * state
        own_out[h] = mine.astype(BF)
        other_out[h] = theirs.astype(BF)


def incoming_state(
    info, docs, small, small_other, kept, got, smalls, states, carry, carry_norm, carry_max, length
):
    heads = small.shape[0]
    return pl.pallas_call(
        functools.partial(incoming_kernel, length, len(smalls)),
        out_shape=(
            pltpu.VMEM(kept.shape, BF),
            pltpu.VMEM(kept.shape, BF),
            pltpu.VMEM(carry_norm.shape, F32),
            pltpu.VMEM((heads, 128), F32),
        ),
        in_specs=[SMEM_SPEC] * 2 + [VMEM_SPEC] * (7 + 2 * len(smalls)),
        out_specs=(VMEM_SPEC,) * 4,
        compiler_params=params(6),
        cost_estimate=cost(1e6, 1e5),
    )(
        info, docs, small, small_other, kept, got, *smalls, *states,
        carry, carry_norm, carry_max[:, None],
    )


def inner_kernel(
    heads, info, docs, top_in, query, key, value, u, norm, gate, w_out,
    base_out, slope_out, w_here, sem,
):
    fetch = pltpu.make_async_copy(w_out, w_here, sem)
    fetch.start()
    length = query.shape[0]
    size, wide = query.shape[1] // heads, value.shape[1] // heads
    offset = info[2]
    chunk = 128
    one = jnp.zeros((chunk, 1), jnp.int32)
    before = segments(docs, one + jnp.maximum(offset - 1, 0))
    for head in range(heads):
        keys_at = slice(head * size, (head + 1) * size)
        values_at = slice(head * wide, (head + 1) * wide)
        u_row = u[head : head + 1, :]
        norm_row = norm[head : head + 1, :]
        top = top_in[head : head + 1, 0:1]
        for low in range(0, length, chunk):
            high = low + chunk
            position_t = lax.broadcasted_iota(jnp.int32, (chunk, 1), 0) + low
            position_s = lax.broadcasted_iota(jnp.int32, (1, high), 1)
            segment_t = segments(docs, position_t + offset)
            segment_s = segments(docs, position_s + offset)
            allowed = (position_s <= position_t) & (segment_s == segment_t)
            expo = jnp.where(allowed, u_row[:, :high], -jnp.inf)
            peak = jnp.max(expo, axis=1, keepdims=True)
            q = query[low:high, keys_at]
            scores = lax.dot_general(
                q, key[:high, keys_at], (((1,), (1,)), ((), ())), preferred_element_type=F32
            )
            weighted = jnp.exp(expo - peak) * scores
            num = jnp.dot(
                weighted.astype(BF), value[:high, values_at], preferred_element_type=F32
            )
            den = jnp.sum(weighted, axis=1, keepdims=True)
            carried = segment_t == before
            ceiling = jnp.where(carried, jnp.maximum(peak, top), peak)
            inner_weight = jnp.exp(peak - ceiling)
            outer_weight = jnp.where(carried, jnp.exp(jnp.minimum(top - ceiling, 0.0)), 0.0)
            outer_den = jnp.sum(q.astype(F32) * norm_row, axis=1, keepdims=True)
            full = inner_weight * den + outer_weight * outer_den
            inverse = 1.0 / jnp.maximum(jnp.abs(full), 1.0)
            g = gate[low:high, values_at]
            base_out[low:high, values_at] = g * (num * (inner_weight * inverse))
            slope_out[low:high, values_at] = g * (outer_weight * inverse)
    fetch.wait()


def inner(info, docs, top, query, key, value, u, norm, gate, w_out, heads):
    length, depth = value.shape
    return pl.pallas_call(
        functools.partial(inner_kernel, heads),
        out_shape=(
            pltpu.VMEM((length, depth), F32),
            pltpu.VMEM((length, depth), F32),
            pltpu.VMEM(w_out.shape, BF),
        ),
        in_specs=[SMEM_SPEC] * 2 + [VMEM_SPEC] * 7 + [HBM_SPEC],
        out_specs=(VMEM_SPEC,) * 3,
        scratch_shapes=[pltpu.SemaphoreType.DMA],
        compiler_params=params(12),
        cost_estimate=cost(1e6, 1e5),
    )(info, docs, top, query, key, value, u, norm, gate, in_hbm(w_out))


def some_columns(info, hidden, w, send, keep, start):
    place = info[0]
    wide = send.shape[1] // 2
    share = w.shape[1] // 4
    for step, owner in enumerate((1, 3, 0, 2)):
        columns = pl.ds(pl.multiple_of((place ^ owner) * share + start, 128), wide)
        part = jnp.dot(hidden[...], w[:, columns], preferred_element_type=F32).astype(BF)
        out = (send, keep)[step // 2]
        low = (step % 2) * wide
        out[:, low : low + wide] = part


def hidden_kernel(heads, info, query, own, other, base, slope, w, hidden, send, keep, state):
    half = own.shape[1]
    side = info[1]
    size, wide = 2 * half, own.shape[2]
    for h in range(heads):
        state[pl.ds(pl.multiple_of(side * half, half), half)] = own[h]
        state[pl.ds(pl.multiple_of((1 - side) * half, half), half)] = other[h]
        outer = jnp.dot(
            query[:, h * size : (h + 1) * size], state[...], preferred_element_type=F32
        )
        columns = slice(h * wide, (h + 1) * wide)
        hidden[:, columns] = (base[:, columns] + slope[:, columns] * outer).astype(BF)
    some_columns(info, hidden, w, send, keep, 0)


def hidden_and_first(info, query, own, other, base, slope, w_here, wide, heads):
    length, depth = base.shape
    return pl.pallas_call(
        functools.partial(hidden_kernel, heads),
        out_shape=(
            pltpu.VMEM((length, depth), BF),
            pltpu.VMEM((length, 2 * wide), BF),
            pltpu.VMEM((length, 2 * wide), BF),
        ),
        in_specs=[SMEM_SPEC] + [VMEM_SPEC] * 6,
        out_specs=(VMEM_SPEC,) * 3,
        scratch_shapes=[pltpu.VMEM((2 * own.shape[1], own.shape[2]), BF)],
        compiler_params=params(12),
        cost_estimate=cost(3e9, 8e6),
    )(info, query, own, other, base, slope, w_here)


def columns_kernel(start, info, hidden, w, send, keep):
    some_columns(info, hidden, w, send, keep, start)


def next_columns(info, hidden, w_here, wide, start):
    length = hidden.shape[0]
    return pl.pallas_call(
        functools.partial(columns_kernel, start),
        out_shape=(pltpu.VMEM((length, 2 * wide), BF),) * 2,
        in_specs=[SMEM_SPEC, VMEM_SPEC, VMEM_SPEC],
        out_specs=(VMEM_SPEC,) * 2,
        compiler_params=params(12),
        cost_estimate=cost(1e6, 1e5),
    )(info, hidden, w_here)


def local(
    tokens,
    w_query,
    w_key,
    w_value,
    w_outgate,
    w_gates,
    gate_bias,
    w_out,
    carry_matrix,
    carry_norm,
    carry_max,
    doc_lengths,
):
    length, share = tokens.shape
    heads = gate_bias.shape[1]
    size = w_query.shape[1] // heads
    place = lax.axis_index("tensor")
    block = lax.axis_index("seq")
    blocks = lax.axis_size("seq")
    offset = (block * length).astype(jnp.int32)
    tensor = lambda x, mask: swapped(x, "tensor", mask)
    pair = lambda x: swapped(x, "seq", 1)
    down = lambda x: shifted(x, "seq", 2)

    beside = tensor(tokens, 1)
    sizes = [c for chunks in TOKEN_CHUNKS for c in chunks]
    starts = [sum(sizes[:i]) for i in range(len(sizes))]
    *pieces, source = split_tokens(tokens, starts + [0], sizes + [share])
    pieces = [(s, c, tensor(x, 2)) for s, c, x in zip(starts, sizes, pieces)]
    groups = []
    for chunks in TOKEN_CHUNKS:
        groups.append(pieces[: len(chunks)])
        pieces = pieces[len(chunks) :]
    gate_w = w_gates.transpose(0, 2, 1).reshape(2 * heads, 4 * share)

    side = (block % 2).astype(jnp.int32)
    info = jnp.stack([place, side, offset]).astype(jnp.int32)
    weights = (w_key, w_value, w_query, w_outgate)
    at = [[(o, s, c) for s, c, _ in group for o in (2, 3)] for group in groups]
    near_at = [(0, 0, share), (1, 0, share)]
    sums = stage(info, [source, beside], near_at, weights, gate_w, share)
    for i, group in enumerate(groups):
        xs = lax.optimization_barrier((*[x for _, _, x in group], *sums))
        xs, sums = xs[: len(group)], xs[len(group) :]
        xs = [y for x in xs for y in (x, tensor(x, 1))]
        if i < len(groups) - 1:
            *sums, w_key_last, w_value_last, w_query_last, w_gate_last = stage(
                info, xs, at[i], weights, gate_w, share, sums, at[-1]
            )
    keys, values, kept, sent, small, u = block_summary(
        info, doc_lengths, gate_bias, xs, at[-1], w_key_last, w_value_last, gate_w,
        sums[0], sums[1], sums[4], share, heads,
    )

    small_other = pair(small)
    got = pair(sent)
    last_xs = after(keys, *xs)
    queries, gate = last_stage(last_xs, w_query_last, w_gate_last, sums[2], sums[3])
    small_other, got, queries = lax.optimization_barrier((small_other, got, queries))
    state_pair, travel = pair_summary(
        info, doc_lengths, small, small_other, kept, got, length
    )
    smalls, states = [], []
    for _ in range(blocks // 4):
        travel, state_pair = lax.optimization_barrier((down(travel), down(state_pair)))
        smalls.append(travel)
        states.append(state_pair)
    state_own, state_other, norm_in, top_own = incoming_state(
        info, doc_lengths, small, small_other, kept, got, smalls, states,
        carry_matrix, carry_norm, carry_max, length,
    )
    state_got = pair(state_other)
    base, slope, w_here = inner(
        info, doc_lengths, top_own, queries, keys, values, u, norm_in, gate, w_out, heads
    )

    start = 0
    leaving, arriving = [], []
    for wide in OUT_CHUNKS:
        if start == 0:
            hidden, send, keep = hidden_and_first(
                info, queries, state_own, state_got, base, slope, w_here, wide, heads
            )
        else:
            now = after(leaving[-2], hidden) if len(leaving) > 1 else hidden
            send, keep = next_columns(info, now, w_here, wide, start)
        both = keep.astype(F32) + tensor(send, 1).astype(F32)
        leaving.append(both[:, wide:].astype(BF))
        arriving.append((start, wide, both[:, :wide], tensor(leaving[-1], 2)))
        start += wide
    out = source
    for start, wide, both, came in arriving[:-1]:
        columns = source[:, start : start + wide].astype(F32) + (both + came.astype(F32))
        out = lax.dynamic_update_slice(out, columns.astype(BF), (0, start))
    start, wide, both, came = arriving[-1]
    columns = source[:, start : start + wide].astype(F32) + (both + came.astype(F32))
    return lax.dynamic_update_slice(out, columns.astype(BF), (0, start))


FULL_ACCURACY = lax.Precision.HIGHEST


def plain_shifted(x, axis, by):
    devices = lax.axis_size(axis)
    pairs = [(i, i + by) for i in range(devices) if 0 <= i + by < devices]
    return lax.ppermute(x, axis, pairs)


def segment_of(doc_lengths, positions):
    bounds = jnp.cumsum(doc_lengths)[:-1]
    return jnp.sum((positions[:, None] >= bounds[None, :]).astype(jnp.int32), axis=1)


def combine(earlier, later):
    early_c, early_n, early_m, early_g, early_r = earlier
    late_c, late_n, late_m, late_g, late_r = later
    ceiling = jnp.maximum(early_m + late_g, late_m)
    early_weight = jnp.exp(early_m + late_g - ceiling)
    late_weight = jnp.exp(late_m - ceiling)
    reset_mask = late_r > 0.5
    merged_c = jnp.where(
        reset_mask[:, None, None],
        late_c,
        early_weight[:, None, None] * early_c + late_weight[:, None, None] * late_c,
    )
    merged_n = jnp.where(
        reset_mask[:, None], late_n, early_weight[:, None] * early_n + late_weight[:, None] * late_n
    )
    merged_m = jnp.where(reset_mask, late_m, ceiling)
    return (merged_c, merged_n, merged_m, late_g, jnp.maximum(early_r, late_r))


def block_local(queries, keys, value_rows, input_pre, log_forget, segment, segment_before):
    length = segment.shape[0]
    log_decay = jnp.cumsum(log_forget, axis=0)
    position = jnp.arange(length)
    allowed = (position[:, None] >= position[None, :]) & (segment[:, None] == segment[None, :])
    exponent = log_decay.T[:, :, None] - log_decay.T[:, None, :] + input_pre.T[:, None, :]
    exponent = jnp.where(allowed[None], exponent, -jnp.inf)
    inner_max = jnp.max(exponent, axis=2)
    scores = jnp.einsum("lhk,mhk->hlm", queries, keys, preferred_element_type=jnp.float32)
    weighted = jnp.exp(exponent - inner_max[:, :, None]) * scores
    weighted_bf = weighted.astype(jnp.bfloat16)
    inner_num = jnp.einsum(
        "hlm,mhv->lhv", weighted_bf, value_rows, preferred_element_type=jnp.float32
    )
    inner_den = jnp.sum(weighted, axis=2).T
    in_last = segment == segment[-1]
    tail_expo = log_decay[-1][None, :] - log_decay + input_pre
    tail_expo = jnp.where(in_last[:, None], tail_expo, -jnp.inf)
    tail_max = jnp.max(tail_expo, axis=0)
    key_scaled_rows = (jnp.exp(tail_expo - tail_max[None, :])[:, :, None] * keys).astype(
        jnp.bfloat16
    )
    cell_state_matrix = jnp.einsum(
        "emn,emp->mnp", key_scaled_rows, value_rows, preferred_element_type=jnp.float32
    )
    state_n = jnp.sum(key_scaled_rows.astype(jnp.float32), axis=0)
    reset = (segment[-1] != segment_before).astype(jnp.float32) * jnp.ones_like(tail_max)
    summary = (cell_state_matrix, state_n, tail_max, log_decay[-1], reset)
    return (log_decay, inner_max.T, inner_num, inner_den, summary)


def block_output(
    queries, log_decay, inner_max, inner_num, inner_den, segment, segment_before, incoming
):
    cell_state_matrix, state_n, state_m = incoming
    outer = jnp.where((segment == segment_before)[:, None], log_decay + state_m[None, :], -jnp.inf)
    ceiling = jnp.maximum(inner_max, outer)
    inner_weight = jnp.exp(inner_max - ceiling)
    outer_weight = jnp.exp(outer - ceiling)
    query_single = queries.astype(jnp.float32)
    outer_numerator_sum = jnp.einsum(
        "ciy,iyo->cio", query_single, cell_state_matrix, precision=FULL_ACCURACY
    )
    outer_den = jnp.einsum("lhk,hk->lh", query_single, state_n, precision=FULL_ACCURACY)
    numerator = (
        inner_weight[:, :, None] * inner_num + outer_weight[:, :, None] * outer_numerator_sum
    )
    denominator = inner_weight * inner_den + outer_weight * outer_den
    return numerator / jnp.maximum(jnp.abs(denominator), 1.0)[:, :, None]


def plain_local(
    tokens,
    w_query,
    w_key,
    w_value,
    w_outgate,
    w_gates,
    gate_bias,
    w_out,
    carry_matrix,
    carry_norm,
    carry_max,
    doc_lengths,
):
    length = tokens.shape[0]
    head_count = gate_bias.shape[1]
    query_size = w_query.shape[1] // head_count
    value_size = w_value.shape[1] // head_count
    matrices = (w_query, w_key, w_value, w_outgate)
    zero_init = tuple((jnp.zeros((length, matrix.shape[1]), jnp.float32) for matrix in matrices))
    zero_init = zero_init + (
        jnp.zeros((length, head_count), jnp.float32),
        jnp.zeros((length, head_count), jnp.float32),
    )
    column_block = lax.all_gather(tokens, "tensor", axis=1, tiled=True)
    updated = tuple(
        (jnp.dot(column_block, matrix, preferred_element_type=jnp.float32) for matrix in matrices)
    )
    input_sum = jnp.dot(column_block, w_gates[0], preferred_element_type=jnp.float32)
    forget_sum = jnp.dot(column_block, w_gates[1], preferred_element_type=jnp.float32)
    projected = updated + (input_sum, forget_sum)
    queries = projected[0].astype(jnp.bfloat16).reshape(length, head_count, query_size)
    keys = (
        (projected[1] * query_size ** (-0.5))
        .astype(jnp.bfloat16)
        .reshape(length, head_count, query_size)
    )
    value_rows = projected[2].astype(jnp.bfloat16).reshape(length, head_count, value_size)
    outgate = jax.nn.sigmoid(projected[3])
    input_pre = projected[4] + gate_bias[0][None, :]
    log_forget = jax.nn.log_sigmoid(projected[5] + gate_bias[1][None, :])
    offset = lax.axis_index("seq") * length
    positions = offset + jnp.arange(length, dtype=jnp.int32)
    segment = segment_of(doc_lengths, positions)
    segment_before = segment_of(doc_lengths, jnp.maximum(offset - 1, 0)[None])[0]
    log_decay, inner_max, inner_num, inner_den, summary = block_local(
        queries, keys, value_rows, input_pre, log_forget, segment, segment_before
    )
    start_state = (carry_matrix, carry_norm, carry_max)
    zero_heads = jnp.zeros((head_count,), jnp.float32)
    is_leader = lax.axis_index("seq") == 0

    def relay(iteration, current):
        leaving = combine(current + (zero_heads, zero_heads), summary)[:3]
        arrived = plain_shifted(leaving, "seq", 1)
        return tuple(
            (
                jnp.where(is_leader, initial, received)
                for initial, received in zip(start_state, arrived)
            )
        )

    incoming = lax.fori_loop(0, lax.axis_size("seq") - 1, relay, start_state)
    mixed_heads = block_output(
        queries, log_decay, inner_max, inner_num, inner_den, segment, segment_before, incoming
    )
    hidden = (outgate * mixed_heads.reshape(length, head_count * value_size)).astype(jnp.bfloat16)
    partial_value = jnp.dot(hidden, w_out, preferred_element_type=jnp.float32)
    summed = lax.psum_scatter(
        partial_value.astype(jnp.bfloat16), "tensor", scatter_dimension=1, tiled=True
    ).astype(jnp.float32)
    return (tokens.astype(jnp.float32) + summed).astype(jnp.bfloat16)


def solution(mesh):
    fast = mesh.shape["tensor"] == 4 and mesh.shape["seq"] % 4 == 0
    return jax.shard_map(
        local if fast else plain_local,
        mesh=mesh,
        in_specs=(
            P("seq", "tensor"),
            P(None, "tensor"),
            P(None, "tensor"),
            P(None, "tensor"),
            P(None, "tensor"),
            P(None, None, "tensor"),
            P(None, "tensor"),
            P("tensor", None),
            P("tensor", None, None),
            P("tensor", None),
            P("tensor"),
            P(),
        ),
        out_specs=P("seq", "tensor"),
        check_vma=False,
    )
```

```python
import functools

import jax
import jax.numpy as jnp
from jax import lax
from jax.experimental import pallas as pl
from jax.experimental.pallas import tpu as pltpu
from jax.sharding import PartitionSpec as P

BF = jnp.bfloat16
F32 = jnp.float32
MIB = 1024 * 1024
TOKEN_CHUNKS = ((256, 256), (512,))
OUT_CHUNKS = (256, 256, 256, 256)


def params(mib):
    return pltpu.CompilerParams(vmem_limit_bytes=mib * MIB)


def cost(flops, moved):
    return pl.CostEstimate(flops=int(flops), bytes_accessed=int(moved), transcendentals=0)


def swapped(x, axis, mask):
    size = lax.axis_size(axis)
    return lax.ppermute(x, axis, [(i, i ^ mask) for i in range(size)])


def shifted(x, axis, by):
    size = lax.axis_size(axis)
    return lax.ppermute(x, axis, [(i, (i + by) % size) for i in range(size)])


def after(first, *others):
    out = lax.optimization_barrier((first,) + others)[1:]
    return out[0] if len(out) == 1 else out


SMEM_SPEC = pl.BlockSpec(memory_space=pltpu.SMEM)
VMEM_SPEC = pl.BlockSpec(memory_space=pltpu.VMEM)
HBM_SPEC = pl.BlockSpec(memory_space=pltpu.HBM)


def in_hbm(x):
    return pltpu.with_memory_space_constraint(x, pltpu.HBM)


def in_vmem(*xs):
    return [pltpu.with_memory_space_constraint(x, pltpu.VMEM) for x in xs]


def holding(kernel, held):
    return (lambda *refs: kernel(*refs[len(held) :])) if held else kernel


def split_kernel(starts, tokens, *refs):
    outs, sem = refs[:-1], refs[-1]
    copies = []
    for i, (low, out) in enumerate(zip(starts, outs)):
        source = tokens.at[:, low : low + out.shape[1]]
        copies.append(pltpu.make_async_copy(source, out, sem.at[i]))
        copies[-1].start()
    for copy in copies:
        copy.wait()


def split_tokens(tokens, starts, sizes):
    length = tokens.shape[0]
    return pl.pallas_call(
        functools.partial(split_kernel, starts),
        out_shape=tuple(pltpu.VMEM((length, c), BF) for c in sizes),
        in_specs=[HBM_SPEC],
        out_specs=(VMEM_SPEC,) * len(sizes),
        scratch_shapes=[pltpu.SemaphoreType.DMA((len(sizes),))],
        compiler_params=params(4),
        cost_estimate=cost(1e6, 1e5),
    )(in_hbm(tokens))


def across_tokens(w, x):
    return lax.dot_general(w, x, (((1,), (1,)), ((), ())), preferred_element_type=F32)


def row_start(place, share, owner, first):
    return pl.multiple_of((place ^ owner) * share + first, 128)


def copies_of(weights, targets, semaphores, at, place, share):
    result = []
    for i, (w, target) in enumerate(zip(weights, targets)):
        low, group = 0, []
        for p, (owner, first, count) in enumerate(at):
            group.append(
                pltpu.make_async_copy(
                    w.at[pl.ds(row_start(place, share, owner, first), count)],
                    target.at[pl.ds(low, count)],
                    semaphores.at[i, p],
                )
            )
            low += count
        result.append(group)
    return result


def stage_kernel(xs_at, ahead_at, share, names, with_sum, finishes, gated, info, *refs):
    refs = list(refs)
    take = lambda n: [refs.pop(0) for _ in range(n)]
    count_w = names
    xs, ws = take(len(xs_at)), take(count_w)
    gate_w = take(1)[0] if gated else None
    sums = take(count_w + gated) if with_sum else None
    outs = take(count_w + gated)
    ahead = take(count_w) if ahead_at else []
    held = take(count_w)
    sems = take(1)[0]
    place = info[0]
    now = copies_of(ws, held, sems, xs_at, place, share)
    later = copies_of(ws, ahead, take(1)[0], ahead_at, place, share) if ahead_at else []
    for group in now + later:
        for copy in group:
            copy.start()
    if gated:
        gates = sums[count_w][...] if with_sum else 0.0
        for (owner, first, count), x in zip(xs_at, xs):
            gates = gates + across_tokens(
                gate_w[:, pl.ds(row_start(place, share, owner, first), count)], x[...]
            )
        outs[count_w][...] = gates
    for i in range(count_w):
        for copy in now[i]:
            copy.wait()

        def body(j, _, i=i):
            columns = pl.ds(pl.multiple_of(j * 256, 256), 256)
            total = sums[i][:, columns] if with_sum else None
            low = 0
            for (_, _, count), x in zip(xs_at, xs):
                part = jnp.dot(
                    x[...], held[i][low : low + count, columns], preferred_element_type=F32
                )
                total = part if total is None else total + part
                low += count
            outs[i][:, columns] = finishes[i](total).astype(outs[i].dtype)
            return 0

        lax.fori_loop(0, outs[i].shape[1] // 256, body, 0)
    for group in later:
        for copy in group:
            copy.wait()


def unchanged(x):
    return x


def stage(info, xs, xs_at, weights, share, gate_w=None, sums=None, ahead_at=None, finishes=None, held=()):
    length = xs[0].shape[0]
    count = sum(c for _, _, c in xs_at)
    gated = int(gate_w is not None)
    kinds = [F32] * len(weights) if finishes is None else [k for _, k in finishes]
    calls = [unchanged] * len(weights) if finishes is None else [f for f, _ in finishes]
    shapes = [pltpu.VMEM((length, w.shape[1]), k) for w, k in zip(weights, kinds)]
    if gated:
        shapes.append(pltpu.VMEM((gate_w.shape[0], length), F32))
    scratch = [pltpu.VMEM((count, w.shape[1]), BF) for w in weights]
    scratch.append(pltpu.SemaphoreType.DMA((len(weights), len(xs_at))))
    if ahead_at:
        rows = sum(c for _, _, c in ahead_at)
        shapes += [pltpu.VMEM((rows, w.shape[1]), BF) for w in weights]
        scratch.append(pltpu.SemaphoreType.DMA((len(weights), len(ahead_at))))
    operands = [*in_vmem(*held), info, *in_vmem(*xs), *[in_hbm(w) for w in weights]]
    specs = [VMEM_SPEC] * len(held) + [SMEM_SPEC] + [VMEM_SPEC] * len(xs) + [HBM_SPEC] * len(weights)
    if gated:
        operands.append(gate_w)
        specs.append(VMEM_SPEC)
    aliases = {}
    if sums is not None:
        if finishes is None:
            aliases = {len(operands) + i: i for i in range(len(sums))}
        operands += in_vmem(*sums)
        specs += [VMEM_SPEC] * len(sums)
    return pl.pallas_call(
        holding(
            functools.partial(
                stage_kernel, xs_at, ahead_at, share, len(weights), sums is not None, calls, gated
            ),
            held,
        ),
        out_shape=tuple(shapes),
        in_specs=specs,
        out_specs=(VMEM_SPEC,) * len(shapes),
        scratch_shapes=scratch,
        input_output_aliases=aliases,
        compiler_params=params(24),
        cost_estimate=cost(1e6, 1e5),
    )(*operands)


def segments(docs, positions):
    total = jnp.zeros_like(positions)
    bound = jnp.int32(0)
    for j in range(docs.shape[0] - 1):
        bound = bound + docs[j]
        total = total + (positions >= bound).astype(jnp.int32)
    return total


def gate_rows(both, offset, docs, bias):
    heads, length = both.shape[0] // 2, both.shape[1]
    row = lax.broadcasted_iota(jnp.int32, (heads, length), 0)
    lane = lax.broadcasted_iota(jnp.int32, (heads, length), 1)
    input_bias = jnp.zeros((heads, length), F32)
    forget_bias = jnp.zeros((heads, length), F32)
    for h in range(heads):
        input_bias = jnp.where(row == h, bias[0, h], input_bias)
        forget_bias = jnp.where(row == h, bias[1, h], forget_bias)
    input_pre = both[:heads] + input_bias
    forget = both[heads:] + forget_bias
    decay = jnp.minimum(forget, 0.0) - jnp.log1p(jnp.exp(-jnp.abs(forget)))
    step = 1
    while step < length:
        decay = decay + jnp.where(lane >= step, pltpu.roll(decay, step, 1), 0.0)
        step *= 2
    u = input_pre - decay
    segment = segments(docs, lane + offset)
    last = segments(docs, lane * 0 + (offset + length - 1))
    open_rows = segment == last
    top = jnp.max(jnp.where(open_rows, u, -jnp.inf), axis=1, keepdims=True)
    weight = jnp.where(open_rows, jnp.exp(u - top), 0.0)
    total = decay[:, length - 1 : length]
    narrow = lax.broadcasted_iota(jnp.int32, (heads, 128), 1)
    stats = jnp.where(narrow == 0, total + top, jnp.where(narrow == 1, total, 0.0))
    return u, weight, stats


def summary_kernel(xs_at, share, heads, info, docs, bias, *refs):
    xs = refs[: len(xs_at)]
    key_w, value_w, gate_w, key_sum, value_sum, gate_sum = refs[len(xs_at) : len(xs_at) + 6]
    key_out, value_out, keep_out, send_out, small_out, u_out, state = refs[len(xs_at) + 6 :]
    place, side, offset = info[0], info[1], info[2]
    size, wide = state.shape
    gates = gate_sum[...]
    for (owner, first, count), x in zip(xs_at, xs):
        gates = gates + across_tokens(
            gate_w[:, pl.ds(row_start(place, share, owner, first), count)], x[...]
        )
    u, weight, stats = gate_rows(gates, offset, docs, bias)
    u_out[...] = u
    small_out[:, size:] = stats
    spare = jnp.zeros((128 - weight.shape[0], weight.shape[1]), F32)
    columns = jnp.concatenate([weight, spare], axis=0).T
    half = size // 2
    for h in range(heads):
        key_at, value_at = slice(h * size, (h + 1) * size), slice(h * wide, (h + 1) * wide)
        key, value, low = key_sum[:, key_at], value_sum[:, value_at], 0
        for x in xs:
            count = x.shape[1]
            rows = slice(low, low + count)
            key = key + jnp.dot(x[...], key_w[rows, key_at], preferred_element_type=F32)
            value = value + jnp.dot(x[...], value_w[rows, value_at], preferred_element_type=F32)
            low += count
        key = (key * size ** (-0.5)).astype(BF)
        value = value.astype(BF)
        key_out[:, key_at] = key
        value_out[:, value_at] = value
        scaled = (columns[:, h : h + 1] * key.astype(F32)).astype(BF)
        small_out[h : h + 1, :size] = jnp.sum(scaled.astype(F32), axis=0, keepdims=True)
        state[...] = lax.dot_general(
            scaled, value, (((0,), (0,)), ((), ())), preferred_element_type=F32
        )
        keep_out[h] = state[pl.ds(pl.multiple_of(side * half, half), half)].astype(BF)
        send_out[h] = state[pl.ds(pl.multiple_of((1 - side) * half, half), half)].astype(BF)


def block_summary(
    info, docs, bias, xs, xs_at, key_w, value_w, gate_w, key_sum, value_sum, gates, share, heads
):
    length = xs[0].shape[0]
    size, wide = key_w.shape[1] // heads, value_w.shape[1] // heads
    return pl.pallas_call(
        functools.partial(summary_kernel, xs_at, share, heads),
        out_shape=(
            pltpu.VMEM((length, heads * size), BF),
            pltpu.VMEM((length, heads * wide), BF),
            pltpu.VMEM((heads, size // 2, wide), BF),
            pltpu.VMEM((heads, size // 2, wide), BF),
            pltpu.VMEM((heads, size + 128), F32),
            pltpu.VMEM((heads, length), F32),
        ),
        in_specs=[SMEM_SPEC] * 3 + [VMEM_SPEC] * (len(xs) + 6),
        out_specs=(VMEM_SPEC,) * 6,
        scratch_shapes=[pltpu.VMEM((size, wide), F32)],
        compiler_params=params(16),
        cost_estimate=cost(4e9, 4e6),
    )(info, docs, bias, *in_vmem(*xs, key_w, value_w), gate_w, *in_vmem(key_sum, value_sum, gates))


def reset_of(docs, index, length):
    first = jnp.maximum(index * length - 1, 0)
    return segments(docs, (index + 1) * length - 1) != segments(docs, first)


def pair_scales(info, docs, length, size, own, other):
    even = info[1] == 0
    first = info[2] // length - info[1]
    m_own, g_own = own[:, size : size + 1], own[:, size + 1 : size + 2]
    m_other, g_other = other[:, size : size + 1], other[:, size + 1 : size + 2]
    m_even, g_even = jnp.where(even, m_own, m_other), jnp.where(even, g_own, g_other)
    m_odd, g_odd = jnp.where(even, m_other, m_own), jnp.where(even, g_other, g_own)
    reset_odd = reset_of(docs, first + 1, length)
    m_pair = jnp.maximum(jnp.where(reset_odd, -jnp.inf, m_even + g_odd), m_odd)
    pair_even = jnp.where(reset_odd, 0.0, jnp.exp(jnp.minimum(m_even + g_odd - m_pair, 0.0)))
    pair_odd = jnp.exp(m_odd - m_pair)
    weights = jnp.where(even, pair_even, pair_odd), jnp.where(even, pair_odd, pair_even)
    return m_even, g_even, g_odd, m_pair, weights


def pair_kernel(length, info, docs, own, other, kept, got, state_out, small_out):
    heads = own.shape[0]
    size = own.shape[1] - 128
    _, g_even, g_odd, m_pair, (w_own, w_other) = pair_scales(
        info, docs, length, size, own[...], other[...]
    )
    small_out[:, :size] = w_own * own[:, :size] + w_other * other[:, :size]
    lane = lax.broadcasted_iota(jnp.int32, (heads, 128), 1)
    small_out[:, size:] = jnp.where(
        lane == 0, m_pair, jnp.where(lane == 1, g_even + g_odd, 0.0)
    )
    for h in range(heads):
        at = slice(h, h + 1)
        state = w_own[at] * kept[h].astype(F32) + w_other[at] * got[h].astype(F32)
        state_out[h] = state.astype(BF)


def pair_summary(info, docs, small, small_other, kept, got, length, held):
    return pl.pallas_call(
        holding(functools.partial(pair_kernel, length), held),
        out_shape=(pltpu.VMEM(kept.shape, BF), pltpu.VMEM(small.shape, F32)),
        in_specs=[VMEM_SPEC] * len(held) + [SMEM_SPEC] * 2 + [VMEM_SPEC] * 4,
        out_specs=(VMEM_SPEC,) * 2,
        compiler_params=params(4),
        cost_estimate=cost(1e6, 1e5),
    )(*in_vmem(*held), info, docs, *in_vmem(small, small_other, kept, got))


def incoming_kernel(length, reach, info, docs, own, other, kept, got, *refs):
    smalls, states = refs[:reach], refs[reach : 2 * reach]
    carry, carry_norm, carry_max = refs[2 * reach : 2 * reach + 3]
    own_out, other_out, norm_out, top_out = refs[2 * reach + 3 :]
    heads = own.shape[0]
    size = own.shape[1] - 128
    side = info[1]
    even = side == 0
    first = info[2] // length - side
    m_even, g_even, _, _, _ = pair_scales(info, docs, length, size, own[...], other[...])
    reset_even = reset_of(docs, first, length)
    expos = []
    passed = jnp.zeros((heads, 1), F32)
    unbroken = jnp.bool_(True)
    for k in range(1, reach + 1):
        there = first >= 2 * k
        index = jnp.maximum(first - 2 * k, 0)
        m_k, g_k = smalls[k - 1][:, size : size + 1], smalls[k - 1][:, size + 1 : size + 2]
        expos.append(jnp.where(there & unbroken, m_k + passed, -jnp.inf))
        passed = passed + jnp.where(there, g_k, 0.0)
        broken = reset_of(docs, index, length) | reset_of(docs, index + 1, length)
        unbroken = unbroken & ~(there & broken)
    in_reach = (first <= 2 * reach) & unbroken
    expos.append(jnp.where(in_reach, carry_max[...] + passed, -jnp.inf))
    top_even = functools.reduce(jnp.maximum, expos)
    expos_odd = [jnp.where(reset_even, -jnp.inf, e + g_even) for e in expos]
    top_odd = functools.reduce(jnp.maximum, expos_odd, m_even)
    w_even = [jnp.exp(e - top_even) for e in expos]
    w_odd = [jnp.exp(e - top_odd) for e in expos_odd]
    direct = jnp.exp(m_even - top_odd)
    w_own = [jnp.where(even, a, b) for a, b in zip(w_even, w_odd)]
    w_other = [jnp.where(even, b, a) for a, b in zip(w_even, w_odd)]
    direct_own = jnp.where(even, 0.0, direct)
    direct_other = jnp.where(even, direct, 0.0)
    top_out[...] = jnp.where(even, top_even, top_odd) + jnp.zeros((heads, 128), F32)
    norm = direct_own * jnp.where(even, own[:, :size], other[:, :size])
    norm = norm + w_own[reach] * carry_norm[...]
    for k in range(reach):
        norm = norm + w_own[k] * smalls[k][:, :size]
    norm_out[...] = norm
    for h in range(heads):
        at = slice(h, h + 1)
        here = jnp.where(even, kept[h].astype(F32), got[h].astype(F32))
        base = carry[h]
        mine = w_own[reach][at] * base + direct_own[at] * here
        theirs = w_other[reach][at] * base + direct_other[at] * here
        for k in range(reach):
            state = states[k][h].astype(F32)
            mine = mine + w_own[k][at] * state
            theirs = theirs + w_other[k][at] * state
        own_out[h] = mine.astype(BF)
        other_out[h] = theirs.astype(BF)


def carry_kernel(info, carry, out, sem):
    half = out.shape[1]
    rows = pl.ds(pl.multiple_of(info[1] * half, half), half)
    copy = pltpu.make_async_copy(carry.at[:, rows], out, sem)
    copy.start()
    copy.wait()


def carry_half(info, carry, held):
    heads, size, wide = carry.shape
    return pl.pallas_call(
        holding(carry_kernel, held),
        out_shape=pltpu.VMEM((heads, size // 2, wide), F32),
        in_specs=[VMEM_SPEC] * len(held) + [SMEM_SPEC, HBM_SPEC],
        out_specs=VMEM_SPEC,
        scratch_shapes=[pltpu.SemaphoreType.DMA],
        compiler_params=params(4),
        cost_estimate=cost(1e6, 1e5),
    )(*in_vmem(*held), info, in_hbm(carry))


def incoming_state(
    info, docs, small, small_other, kept, got, smalls, states, carry, carry_norm, carry_max, length,
    held,
):
    heads = small.shape[0]
    return pl.pallas_call(
        holding(functools.partial(incoming_kernel, length, len(smalls)), held),
        out_shape=(
            pltpu.VMEM(kept.shape, BF),
            pltpu.VMEM(kept.shape, BF),
            pltpu.VMEM(carry_norm.shape, F32),
            pltpu.VMEM((heads, 128), F32),
        ),
        in_specs=[VMEM_SPEC] * len(held)
        + [SMEM_SPEC] * 2
        + [VMEM_SPEC] * (7 + 2 * len(smalls)),
        out_specs=(VMEM_SPEC,) * 4,
        compiler_params=params(6),
        cost_estimate=cost(1e6, 1e5),
    )(
        *in_vmem(*held), info, docs,
        *in_vmem(small, small_other, kept, got, *smalls, *states, carry),
        carry_norm, carry_max[:, None],
    )


def inner_kernel(
    heads, info, docs, top_in, query, key, value, u, norm, gate, w_out,
    base_out, slope_out, w_here, sem,
):
    fetch = pltpu.make_async_copy(w_out, w_here, sem)
    fetch.start()
    length = query.shape[0]
    size, wide = query.shape[1] // heads, value.shape[1] // heads
    offset = info[2]
    chunk = 128
    one = jnp.zeros((chunk, 1), jnp.int32)
    before = segments(docs, one + jnp.maximum(offset - 1, 0))
    for head in range(heads):
        keys_at = slice(head * size, (head + 1) * size)
        values_at = slice(head * wide, (head + 1) * wide)
        u_row = u[head : head + 1, :]
        norm_row = norm[head : head + 1, :]
        top = top_in[head : head + 1, 0:1]
        for low in range(0, length, chunk):
            high = low + chunk
            position_t = lax.broadcasted_iota(jnp.int32, (chunk, 1), 0) + low
            position_s = lax.broadcasted_iota(jnp.int32, (1, high), 1)
            segment_t = segments(docs, position_t + offset)
            segment_s = segments(docs, position_s + offset)
            allowed = (position_s <= position_t) & (segment_s == segment_t)
            expo = jnp.where(allowed, u_row[:, :high], -jnp.inf)
            peak = jnp.max(expo, axis=1, keepdims=True)
            q = query[low:high, keys_at]
            scores = lax.dot_general(
                q, key[:high, keys_at], (((1,), (1,)), ((), ())), preferred_element_type=F32
            )
            weighted = jnp.exp(expo - peak) * scores
            num = jnp.dot(
                weighted.astype(BF), value[:high, values_at], preferred_element_type=F32
            )
            den = jnp.sum(weighted, axis=1, keepdims=True)
            carried = segment_t == before
            ceiling = jnp.where(carried, jnp.maximum(peak, top), peak)
            inner_weight = jnp.exp(peak - ceiling)
            outer_weight = jnp.where(carried, jnp.exp(jnp.minimum(top - ceiling, 0.0)), 0.0)
            outer_den = jnp.sum(q.astype(F32) * norm_row, axis=1, keepdims=True)
            full = inner_weight * den + outer_weight * outer_den
            inverse = 1.0 / jnp.maximum(jnp.abs(full), 1.0)
            g = gate[low:high, values_at]
            base_out[low:high, values_at] = g * (num * (inner_weight * inverse))
            slope_out[low:high, values_at] = g * (outer_weight * inverse)
    fetch.wait()


def inner(info, docs, top, query, key, value, u, norm, gate, w_out, heads):
    length, depth = value.shape
    return pl.pallas_call(
        functools.partial(inner_kernel, heads),
        out_shape=(
            pltpu.VMEM((length, depth), F32),
            pltpu.VMEM((length, depth), F32),
            pltpu.VMEM(w_out.shape, BF),
        ),
        in_specs=[SMEM_SPEC] * 2 + [VMEM_SPEC] * 7 + [HBM_SPEC],
        out_specs=(VMEM_SPEC,) * 3,
        scratch_shapes=[pltpu.SemaphoreType.DMA],
        compiler_params=params(12),
        cost_estimate=cost(1e6, 1e5),
    )(info, docs, *in_vmem(top, query, key, value, u, norm, gate), in_hbm(w_out))


def some_columns(info, hidden, w, send, keep, start):
    place = info[0]
    wide = send.shape[1] // 2
    share = w.shape[1] // 4
    for step, owner in enumerate((1, 3, 0, 2)):
        columns = pl.ds(pl.multiple_of((place ^ owner) * share + start, 128), wide)
        part = jnp.dot(hidden[...], w[:, columns], preferred_element_type=F32).astype(BF)
        out = (send, keep)[step // 2]
        low = (step % 2) * wide
        out[:, low : low + wide] = part


def hidden_kernel(heads, info, query, own, other, base, slope, w, hidden, send, keep, state):
    half = own.shape[1]
    side = info[1]
    size, wide = 2 * half, own.shape[2]
    for h in range(heads):
        state[pl.ds(pl.multiple_of(side * half, half), half)] = own[h]
        state[pl.ds(pl.multiple_of((1 - side) * half, half), half)] = other[h]
        outer = jnp.dot(
            query[:, h * size : (h + 1) * size], state[...], preferred_element_type=F32
        )
        columns = slice(h * wide, (h + 1) * wide)
        hidden[:, columns] = (base[:, columns] + slope[:, columns] * outer).astype(BF)
    some_columns(info, hidden, w, send, keep, 0)


def hidden_and_first(info, query, own, other, base, slope, w_here, wide, heads):
    length, depth = base.shape
    return pl.pallas_call(
        functools.partial(hidden_kernel, heads),
        out_shape=(
            pltpu.VMEM((length, depth), BF),
            pltpu.VMEM((length, 2 * wide), BF),
            pltpu.VMEM((length, 2 * wide), BF),
        ),
        in_specs=[SMEM_SPEC] + [VMEM_SPEC] * 6,
        out_specs=(VMEM_SPEC,) * 3,
        scratch_shapes=[pltpu.VMEM((2 * own.shape[1], own.shape[2]), BF)],
        compiler_params=params(12),
        cost_estimate=cost(3e9, 8e6),
    )(info, *in_vmem(query, own, other, base, slope, w_here))


def columns_kernel(start, info, hidden, w, send, keep):
    some_columns(info, hidden, w, send, keep, start)


def next_columns(info, hidden, w_here, wide, start):
    length = hidden.shape[0]
    return pl.pallas_call(
        functools.partial(columns_kernel, start),
        out_shape=(pltpu.VMEM((length, 2 * wide), BF),) * 2,
        in_specs=[SMEM_SPEC, VMEM_SPEC, VMEM_SPEC],
        out_specs=(VMEM_SPEC,) * 2,
        compiler_params=params(12),
        cost_estimate=cost(1e6, 1e5),
    )(info, *in_vmem(hidden, w_here))


def local(
    tokens,
    w_query,
    w_key,
    w_value,
    w_outgate,
    w_gates,
    gate_bias,
    w_out,
    carry_matrix,
    carry_norm,
    carry_max,
    doc_lengths,
):
    length, share = tokens.shape
    heads = gate_bias.shape[1]
    size = w_query.shape[1] // heads
    place = lax.axis_index("tensor")
    block = lax.axis_index("seq")
    blocks = lax.axis_size("seq")
    offset = (block * length).astype(jnp.int32)
    tensor = lambda x, mask: swapped(x, "tensor", mask)
    pair = lambda x: swapped(x, "seq", 1)
    down = lambda x: shifted(x, "seq", 2)

    beside = tensor(tokens, 1)
    sizes = [c for chunks in TOKEN_CHUNKS for c in chunks]
    starts = [sum(sizes[:i]) for i in range(len(sizes))]
    *pieces, source = split_tokens(tokens, starts + [0], sizes + [share])
    pieces = [(s, c, tensor(x, 2)) for s, c, x in zip(starts, sizes, pieces)]
    groups = []
    for chunks in TOKEN_CHUNKS:
        groups.append(pieces[: len(chunks)])
        pieces = pieces[len(chunks) :]
    gate_w = w_gates.transpose(0, 2, 1).reshape(2 * heads, 4 * share)

    side = (block % 2).astype(jnp.int32)
    info = jnp.stack([place, side, offset]).astype(jnp.int32)
    at = [[(o, s, c) for s, c, _ in group for o in (2, 3)] for group in groups]
    near_at = [(0, 0, share), (1, 0, share)]
    key_value, query_gate = (w_key, w_value), (w_query, w_outgate)
    sums = stage(info, [source, beside], near_at, key_value, share, gate_w)
    later = stage(info, [after(sums[0], source), beside], near_at, query_gate, share)
    all_xs, all_at = [], []
    for i, group in enumerate(groups):
        xs = lax.optimization_barrier((*[x for _, _, x in group], *sums, *later))
        xs, sums, later = xs[: len(group)], xs[len(group) : -2], xs[-2:]
        xs = [y for x in xs for y in (x, tensor(x, 1))]
        all_xs += xs
        all_at += at[i]
        if i < len(groups) - 1:
            last = i == len(groups) - 2
            out = stage(
                info, xs, at[i], key_value, share, gate_w, sums, at[-1] if last else None
            )
            sums = out[:3]
            if last:
                w_key_last, w_value_last = out[3:]
    keys, values, kept, sent, small, u = block_summary(
        info, doc_lengths, gate_bias, xs, at[-1], w_key_last, w_value_last, gate_w,
        sums[0], sums[1], sums[2], share, heads,
    )

    small_other = pair(small)
    got = pair(sent)
    queries, gate = stage(
        info, after(keys, *all_xs), all_at, query_gate, share, None, later,
        finishes=((unchanged, BF), (jax.nn.sigmoid, F32)), held=(keys, values, kept),
    )
    small_other, got, queries = lax.optimization_barrier((small_other, got, queries))
    state_pair, travel = pair_summary(
        info, doc_lengths, small, small_other, kept, got, length, (keys, values, queries, gate)
    )
    smalls, states = [], []
    for _ in range(blocks // 4):
        travel, state_pair = lax.optimization_barrier((down(travel), down(state_pair)))
        smalls.append(travel)
        states.append(state_pair)
        if len(states) == 1:
            held = (keys, values, queries, gate, kept, got)
            carry = carry_half(after(travel, info), carry_matrix, held)
    state_own, state_other, norm_in, top_own = incoming_state(
        info, doc_lengths, small, small_other, kept, got, smalls, states,
        carry, carry_norm, carry_max, length, (keys, values, queries, gate),
    )
    state_got = pair(state_other)
    base, slope, w_here = inner(
        info, doc_lengths, top_own, queries, keys, values, u, norm_in, gate, w_out, heads
    )

    start = 0
    leaving, arriving = [], []
    for wide in OUT_CHUNKS:
        if start == 0:
            hidden, send, keep = hidden_and_first(
                info, queries, state_own, state_got, base, slope, w_here, wide, heads
            )
        else:
            now = after(leaving[-2], hidden) if len(leaving) > 1 else hidden
            send, keep = next_columns(info, now, w_here, wide, start)
        both = keep.astype(F32) + tensor(send, 1).astype(F32)
        leaving.append(both[:, wide:].astype(BF))
        arriving.append((start, wide, both[:, :wide], tensor(leaving[-1], 2)))
        start += wide
    out = source
    for start, wide, both, came in arriving[:-1]:
        columns = source[:, start : start + wide].astype(F32) + (both + came.astype(F32))
        out = lax.dynamic_update_slice(out, columns.astype(BF), (0, start))
    start, wide, both, came = arriving[-1]
    columns = source[:, start : start + wide].astype(F32) + (both + came.astype(F32))
    return lax.dynamic_update_slice(out, columns.astype(BF), (0, start))


FULL_ACCURACY = lax.Precision.HIGHEST


def plain_shifted(x, axis, by):
    devices = lax.axis_size(axis)
    pairs = [(i, i + by) for i in range(devices) if 0 <= i + by < devices]
    return lax.ppermute(x, axis, pairs)


def segment_of(doc_lengths, positions):
    bounds = jnp.cumsum(doc_lengths)[:-1]
    return jnp.sum((positions[:, None] >= bounds[None, :]).astype(jnp.int32), axis=1)


def combine(earlier, later):
    early_c, early_n, early_m, early_g, early_r = earlier
    late_c, late_n, late_m, late_g, late_r = later
    ceiling = jnp.maximum(early_m + late_g, late_m)
    early_weight = jnp.exp(early_m + late_g - ceiling)
    late_weight = jnp.exp(late_m - ceiling)
    reset_mask = late_r > 0.5
    merged_c = jnp.where(
        reset_mask[:, None, None],
        late_c,
        early_weight[:, None, None] * early_c + late_weight[:, None, None] * late_c,
    )
    merged_n = jnp.where(
        reset_mask[:, None], late_n, early_weight[:, None] * early_n + late_weight[:, None] * late_n
    )
    merged_m = jnp.where(reset_mask, late_m, ceiling)
    return (merged_c, merged_n, merged_m, late_g, jnp.maximum(early_r, late_r))


def block_local(queries, keys, value_rows, input_pre, log_forget, segment, segment_before):
    length = segment.shape[0]
    log_decay = jnp.cumsum(log_forget, axis=0)
    position = jnp.arange(length)
    allowed = (position[:, None] >= position[None, :]) & (segment[:, None] == segment[None, :])
    exponent = log_decay.T[:, :, None] - log_decay.T[:, None, :] + input_pre.T[:, None, :]
    exponent = jnp.where(allowed[None], exponent, -jnp.inf)
    inner_max = jnp.max(exponent, axis=2)
    scores = jnp.einsum("lhk,mhk->hlm", queries, keys, preferred_element_type=jnp.float32)
    weighted = jnp.exp(exponent - inner_max[:, :, None]) * scores
    weighted_bf = weighted.astype(jnp.bfloat16)
    inner_num = jnp.einsum(
        "hlm,mhv->lhv", weighted_bf, value_rows, preferred_element_type=jnp.float32
    )
    inner_den = jnp.sum(weighted, axis=2).T
    in_last = segment == segment[-1]
    tail_expo = log_decay[-1][None, :] - log_decay + input_pre
    tail_expo = jnp.where(in_last[:, None], tail_expo, -jnp.inf)
    tail_max = jnp.max(tail_expo, axis=0)
    key_scaled_rows = (jnp.exp(tail_expo - tail_max[None, :])[:, :, None] * keys).astype(
        jnp.bfloat16
    )
    cell_state_matrix = jnp.einsum(
        "emn,emp->mnp", key_scaled_rows, value_rows, preferred_element_type=jnp.float32
    )
    state_n = jnp.sum(key_scaled_rows.astype(jnp.float32), axis=0)
    reset = (segment[-1] != segment_before).astype(jnp.float32) * jnp.ones_like(tail_max)
    summary = (cell_state_matrix, state_n, tail_max, log_decay[-1], reset)
    return (log_decay, inner_max.T, inner_num, inner_den, summary)


def block_output(
    queries, log_decay, inner_max, inner_num, inner_den, segment, segment_before, incoming
):
    cell_state_matrix, state_n, state_m = incoming
    outer = jnp.where((segment == segment_before)[:, None], log_decay + state_m[None, :], -jnp.inf)
    ceiling = jnp.maximum(inner_max, outer)
    inner_weight = jnp.exp(inner_max - ceiling)
    outer_weight = jnp.exp(outer - ceiling)
    query_single = queries.astype(jnp.float32)
    outer_numerator_sum = jnp.einsum(
        "ciy,iyo->cio", query_single, cell_state_matrix, precision=FULL_ACCURACY
    )
    outer_den = jnp.einsum("lhk,hk->lh", query_single, state_n, precision=FULL_ACCURACY)
    numerator = (
        inner_weight[:, :, None] * inner_num + outer_weight[:, :, None] * outer_numerator_sum
    )
    denominator = inner_weight * inner_den + outer_weight * outer_den
    return numerator / jnp.maximum(jnp.abs(denominator), 1.0)[:, :, None]


def plain_local(
    tokens,
    w_query,
    w_key,
    w_value,
    w_outgate,
    w_gates,
    gate_bias,
    w_out,
    carry_matrix,
    carry_norm,
    carry_max,
    doc_lengths,
):
    length = tokens.shape[0]
    head_count = gate_bias.shape[1]
    query_size = w_query.shape[1] // head_count
    value_size = w_value.shape[1] // head_count
    matrices = (w_query, w_key, w_value, w_outgate)
    zero_init = tuple((jnp.zeros((length, matrix.shape[1]), jnp.float32) for matrix in matrices))
    zero_init = zero_init + (
        jnp.zeros((length, head_count), jnp.float32),
        jnp.zeros((length, head_count), jnp.float32),
    )
    column_block = lax.all_gather(tokens, "tensor", axis=1, tiled=True)
    updated = tuple(
        (jnp.dot(column_block, matrix, preferred_element_type=jnp.float32) for matrix in matrices)
    )
    input_sum = jnp.dot(column_block, w_gates[0], preferred_element_type=jnp.float32)
    forget_sum = jnp.dot(column_block, w_gates[1], preferred_element_type=jnp.float32)
    projected = updated + (input_sum, forget_sum)
    queries = projected[0].astype(jnp.bfloat16).reshape(length, head_count, query_size)
    keys = (
        (projected[1] * query_size ** (-0.5))
        .astype(jnp.bfloat16)
        .reshape(length, head_count, query_size)
    )
    value_rows = projected[2].astype(jnp.bfloat16).reshape(length, head_count, value_size)
    outgate = jax.nn.sigmoid(projected[3])
    input_pre = projected[4] + gate_bias[0][None, :]
    log_forget = jax.nn.log_sigmoid(projected[5] + gate_bias[1][None, :])
    offset = lax.axis_index("seq") * length
    positions = offset + jnp.arange(length, dtype=jnp.int32)
    segment = segment_of(doc_lengths, positions)
    segment_before = segment_of(doc_lengths, jnp.maximum(offset - 1, 0)[None])[0]
    log_decay, inner_max, inner_num, inner_den, summary = block_local(
        queries, keys, value_rows, input_pre, log_forget, segment, segment_before
    )
    start_state = (carry_matrix, carry_norm, carry_max)
    zero_heads = jnp.zeros((head_count,), jnp.float32)
    is_leader = lax.axis_index("seq") == 0

    def relay(iteration, current):
        leaving = combine(current + (zero_heads, zero_heads), summary)[:3]
        arrived = plain_shifted(leaving, "seq", 1)
        return tuple(
            (
                jnp.where(is_leader, initial, received)
                for initial, received in zip(start_state, arrived)
            )
        )

    incoming = lax.fori_loop(0, lax.axis_size("seq") - 1, relay, start_state)
    mixed_heads = block_output(
        queries, log_decay, inner_max, inner_num, inner_den, segment, segment_before, incoming
    )
    hidden = (outgate * mixed_heads.reshape(length, head_count * value_size)).astype(jnp.bfloat16)
    partial_value = jnp.dot(hidden, w_out, preferred_element_type=jnp.float32)
    summed = lax.psum_scatter(
        partial_value.astype(jnp.bfloat16), "tensor", scatter_dimension=1, tiled=True
    ).astype(jnp.float32)
    return (tokens.astype(jnp.float32) + summed).astype(jnp.bfloat16)


def solution(mesh):
    fast = mesh.shape["tensor"] == 4 and mesh.shape["seq"] % 4 == 0
    return jax.shard_map(
        local if fast else plain_local,
        mesh=mesh,
        in_specs=(
            P("seq", "tensor"),
            P(None, "tensor"),
            P(None, "tensor"),
            P(None, "tensor"),
            P(None, "tensor"),
            P(None, None, "tensor"),
            P(None, "tensor"),
            P("tensor", None),
            P("tensor", None, None),
            P("tensor", None),
            P("tensor"),
            P(),
        ),
        out_specs=P("seq", "tensor"),
        check_vma=False,
    )
```

```python
import functools

import jax
import jax.numpy as jnp
from jax import lax
from jax.experimental import pallas as pl
from jax.experimental.pallas import tpu as pltpu
from jax.sharding import PartitionSpec as P

BF = jnp.bfloat16
F32 = jnp.float32
MIB = 1024 * 1024
TOKEN_CHUNKS = ((256, 256), (512,))
OUT_CHUNKS = (256, 256, 256, 256)


def params(mib):
    return pltpu.CompilerParams(vmem_limit_bytes=mib * MIB)


def cost(flops, moved):
    return pl.CostEstimate(flops=int(flops), bytes_accessed=int(moved), transcendentals=0)


def swapped(x, axis, mask):
    size = lax.axis_size(axis)
    return lax.ppermute(x, axis, [(i, i ^ mask) for i in range(size)])


def shifted(x, axis, by):
    size = lax.axis_size(axis)
    return lax.ppermute(x, axis, [(i, (i + by) % size) for i in range(size)])


def after(first, *others):
    out = lax.optimization_barrier((first,) + others)[1:]
    return out[0] if len(out) == 1 else out


SMEM_SPEC = pl.BlockSpec(memory_space=pltpu.SMEM)
VMEM_SPEC = pl.BlockSpec(memory_space=pltpu.VMEM)
HBM_SPEC = pl.BlockSpec(memory_space=pltpu.HBM)


def in_hbm(x):
    return pltpu.with_memory_space_constraint(x, pltpu.HBM)


def in_vmem(*xs):
    return [pltpu.with_memory_space_constraint(x, pltpu.VMEM) for x in xs]


def holding(kernel, held):
    return (lambda *refs: kernel(*refs[len(held) :])) if held else kernel


def split_kernel(starts, tokens, *refs):
    outs, sem = refs[:-1], refs[-1]
    copies = []
    for i, (low, out) in enumerate(zip(starts, outs)):
        source = tokens.at[:, low : low + out.shape[1]]
        copies.append(pltpu.make_async_copy(source, out, sem.at[i]))
        copies[-1].start()
    for copy in copies:
        copy.wait()


def split_tokens(tokens, starts, sizes):
    length = tokens.shape[0]
    return pl.pallas_call(
        functools.partial(split_kernel, starts),
        out_shape=tuple(pltpu.VMEM((length, c), BF) for c in sizes),
        in_specs=[HBM_SPEC],
        out_specs=(VMEM_SPEC,) * len(sizes),
        scratch_shapes=[pltpu.SemaphoreType.DMA((len(sizes),))],
        compiler_params=params(4),
        cost_estimate=cost(1e6, 1e5),
    )(in_hbm(tokens))


def across_tokens(w, x):
    return lax.dot_general(w, x, (((1,), (1,)), ((), ())), preferred_element_type=F32)


def row_start(place, share, owner, first):
    return pl.multiple_of((place ^ owner) * share + first, 128)


def copies_of(weights, targets, semaphores, at, place, share):
    result = []
    for i, (w, target) in enumerate(zip(weights, targets)):
        low, group = 0, []
        for p, (owner, first, count) in enumerate(at):
            group.append(
                pltpu.make_async_copy(
                    w.at[pl.ds(row_start(place, share, owner, first), count)],
                    target.at[pl.ds(low, count)],
                    semaphores.at[i, p],
                )
            )
            low += count
        result.append(group)
    return result


def stage_kernel(xs_at, ahead_at, share, names, with_sum, finishes, gated, info, *refs):
    refs = list(refs)
    take = lambda n: [refs.pop(0) for _ in range(n)]
    count_w = names
    xs, ws = take(len(xs_at)), take(count_w)
    gate_w = take(1)[0] if gated else None
    sums = take(count_w + gated) if with_sum else None
    outs = take(count_w + gated)
    ahead = take(count_w) if ahead_at else []
    held = take(count_w)
    sems = take(1)[0]
    place = info[0]
    now = copies_of(ws, held, sems, xs_at, place, share)
    later = copies_of(ws, ahead, take(1)[0], ahead_at, place, share) if ahead_at else []
    for group in now + later:
        for copy in group:
            copy.start()
    if gated:
        gates = sums[count_w][...] if with_sum else 0.0
        for (owner, first, count), x in zip(xs_at, xs):
            gates = gates + across_tokens(
                gate_w[:, pl.ds(row_start(place, share, owner, first), count)], x[...]
            )
        outs[count_w][...] = gates
    for i in range(count_w):
        for copy in now[i]:
            copy.wait()

        def body(j, _, i=i):
            columns = pl.ds(pl.multiple_of(j * 256, 256), 256)
            total = sums[i][:, columns] if with_sum else None
            low = 0
            for (_, _, count), x in zip(xs_at, xs):
                part = jnp.dot(
                    x[...], held[i][low : low + count, columns], preferred_element_type=F32
                )
                total = part if total is None else total + part
                low += count
            outs[i][:, columns] = finishes[i](total).astype(outs[i].dtype)
            return 0

        lax.fori_loop(0, outs[i].shape[1] // 256, body, 0)
    for group in later:
        for copy in group:
            copy.wait()


def unchanged(x):
    return x


def stage(info, xs, xs_at, weights, share, gate_w=None, sums=None, ahead_at=None, finishes=None, held=()):
    length = xs[0].shape[0]
    count = sum(c for _, _, c in xs_at)
    gated = int(gate_w is not None)
    kinds = [F32] * len(weights) if finishes is None else [k for _, k in finishes]
    calls = [unchanged] * len(weights) if finishes is None else [f for f, _ in finishes]
    shapes = [pltpu.VMEM((length, w.shape[1]), k) for w, k in zip(weights, kinds)]
    if gated:
        shapes.append(pltpu.VMEM((gate_w.shape[0], length), F32))
    scratch = [pltpu.VMEM((count, w.shape[1]), BF) for w in weights]
    scratch.append(pltpu.SemaphoreType.DMA((len(weights), len(xs_at))))
    if ahead_at:
        rows = sum(c for _, _, c in ahead_at)
        shapes += [pltpu.VMEM((rows, w.shape[1]), BF) for w in weights]
        scratch.append(pltpu.SemaphoreType.DMA((len(weights), len(ahead_at))))
    operands = [*in_vmem(*held), info, *in_vmem(*xs), *[in_hbm(w) for w in weights]]
    specs = [VMEM_SPEC] * len(held) + [SMEM_SPEC] + [VMEM_SPEC] * len(xs) + [HBM_SPEC] * len(weights)
    if gated:
        operands.append(gate_w)
        specs.append(VMEM_SPEC)
    aliases = {}
    if sums is not None:
        if finishes is None:
            aliases = {len(operands) + i: i for i in range(len(sums))}
        operands += in_vmem(*sums)
        specs += [VMEM_SPEC] * len(sums)
    return pl.pallas_call(
        holding(
            functools.partial(
                stage_kernel, xs_at, ahead_at, share, len(weights), sums is not None, calls, gated
            ),
            held,
        ),
        out_shape=tuple(shapes),
        in_specs=specs,
        out_specs=(VMEM_SPEC,) * len(shapes),
        scratch_shapes=scratch,
        input_output_aliases=aliases,
        compiler_params=params(24),
        cost_estimate=cost(1e6, 1e5),
    )(*operands)


def segments(docs, positions):
    total = jnp.zeros_like(positions)
    bound = jnp.int32(0)
    for j in range(docs.shape[0] - 1):
        bound = bound + docs[j]
        total = total + (positions >= bound).astype(jnp.int32)
    return total


def gate_rows(both, offset, docs, bias):
    heads, length = both.shape[0] // 2, both.shape[1]
    row = lax.broadcasted_iota(jnp.int32, (heads, length), 0)
    lane = lax.broadcasted_iota(jnp.int32, (heads, length), 1)
    input_bias = jnp.zeros((heads, length), F32)
    forget_bias = jnp.zeros((heads, length), F32)
    for h in range(heads):
        input_bias = jnp.where(row == h, bias[0, h], input_bias)
        forget_bias = jnp.where(row == h, bias[1, h], forget_bias)
    input_pre = both[:heads] + input_bias
    forget = both[heads:] + forget_bias
    decay = jnp.minimum(forget, 0.0) - jnp.log1p(jnp.exp(-jnp.abs(forget)))
    step = 1
    while step < length:
        decay = decay + jnp.where(lane >= step, pltpu.roll(decay, step, 1), 0.0)
        step *= 2
    u = input_pre - decay
    segment = segments(docs, lane + offset)
    last = segments(docs, lane * 0 + (offset + length - 1))
    open_rows = segment == last
    top = jnp.max(jnp.where(open_rows, u, -jnp.inf), axis=1, keepdims=True)
    weight = jnp.where(open_rows, jnp.exp(u - top), 0.0)
    total = decay[:, length - 1 : length]
    narrow = lax.broadcasted_iota(jnp.int32, (heads, 128), 1)
    stats = jnp.where(narrow == 0, total + top, jnp.where(narrow == 1, total, 0.0))
    return u, weight, stats


def summary_kernel(xs_at, share, heads, info, docs, bias, *refs):
    xs = refs[: len(xs_at)]
    key_w, value_w, gate_w, key_sum, value_sum, gate_sum = refs[len(xs_at) : len(xs_at) + 6]
    key_out, value_out, keep_out, send_out, small_out, u_out, state = refs[len(xs_at) + 6 :]
    place, side, offset = info[0], info[1], info[2]
    size, wide = state.shape
    gates = gate_sum[...]
    for (owner, first, count), x in zip(xs_at, xs):
        gates = gates + across_tokens(
            gate_w[:, pl.ds(row_start(place, share, owner, first), count)], x[...]
        )
    u, weight, stats = gate_rows(gates, offset, docs, bias)
    u_out[...] = u
    small_out[:, size:] = stats
    spare = jnp.zeros((128 - weight.shape[0], weight.shape[1]), F32)
    columns = jnp.concatenate([weight, spare], axis=0).T
    half = size // 2
    for h in range(heads):
        key_at, value_at = slice(h * size, (h + 1) * size), slice(h * wide, (h + 1) * wide)
        key, value, low = key_sum[:, key_at], value_sum[:, value_at], 0
        for x in xs:
            count = x.shape[1]
            rows = slice(low, low + count)
            key = key + jnp.dot(x[...], key_w[rows, key_at], preferred_element_type=F32)
            value = value + jnp.dot(x[...], value_w[rows, value_at], preferred_element_type=F32)
            low += count
        key = (key * size ** (-0.5)).astype(BF)
        value = value.astype(BF)
        key_out[:, key_at] = key
        value_out[:, value_at] = value
        scaled = (columns[:, h : h + 1] * key.astype(F32)).astype(BF)
        small_out[h : h + 1, :size] = jnp.sum(scaled.astype(F32), axis=0, keepdims=True)
        state[...] = lax.dot_general(
            scaled, value, (((0,), (0,)), ((), ())), preferred_element_type=F32
        )
        keep_out[h] = state[pl.ds(pl.multiple_of(side * half, half), half)].astype(BF)
        send_out[h] = state[pl.ds(pl.multiple_of((1 - side) * half, half), half)].astype(BF)


def block_summary(
    info, docs, bias, xs, xs_at, key_w, value_w, gate_w, key_sum, value_sum, gates, share, heads
):
    length = xs[0].shape[0]
    size, wide = key_w.shape[1] // heads, value_w.shape[1] // heads
    return pl.pallas_call(
        functools.partial(summary_kernel, xs_at, share, heads),
        out_shape=(
            pltpu.VMEM((length, heads * size), BF),
            pltpu.VMEM((length, heads * wide), BF),
            pltpu.VMEM((heads, size // 2, wide), BF),
            pltpu.VMEM((heads, size // 2, wide), BF),
            pltpu.VMEM((heads, size + 128), F32),
            pltpu.VMEM((heads, length), F32),
        ),
        in_specs=[SMEM_SPEC] * 3 + [VMEM_SPEC] * (len(xs) + 6),
        out_specs=(VMEM_SPEC,) * 6,
        scratch_shapes=[pltpu.VMEM((size, wide), F32)],
        compiler_params=params(16),
        cost_estimate=cost(4e9, 4e6),
    )(info, docs, bias, *in_vmem(*xs, key_w, value_w), gate_w, *in_vmem(key_sum, value_sum, gates))


def reset_of(docs, index, length):
    first = jnp.maximum(index * length - 1, 0)
    return segments(docs, (index + 1) * length - 1) != segments(docs, first)


def pair_scales(info, docs, length, size, own, other):
    even = info[1] == 0
    first = info[2] // length - info[1]
    m_own, g_own = own[:, size : size + 1], own[:, size + 1 : size + 2]
    m_other, g_other = other[:, size : size + 1], other[:, size + 1 : size + 2]
    m_even, g_even = jnp.where(even, m_own, m_other), jnp.where(even, g_own, g_other)
    m_odd, g_odd = jnp.where(even, m_other, m_own), jnp.where(even, g_other, g_own)
    reset_odd = reset_of(docs, first + 1, length)
    m_pair = jnp.maximum(jnp.where(reset_odd, -jnp.inf, m_even + g_odd), m_odd)
    pair_even = jnp.where(reset_odd, 0.0, jnp.exp(jnp.minimum(m_even + g_odd - m_pair, 0.0)))
    pair_odd = jnp.exp(m_odd - m_pair)
    weights = jnp.where(even, pair_even, pair_odd), jnp.where(even, pair_odd, pair_even)
    return m_even, g_even, g_odd, m_pair, weights


def pair_kernel(length, info, docs, own, other, kept, got, state_out, small_out):
    heads = own.shape[0]
    size = own.shape[1] - 128
    _, g_even, g_odd, m_pair, (w_own, w_other) = pair_scales(
        info, docs, length, size, own[...], other[...]
    )
    small_out[:, :size] = w_own * own[:, :size] + w_other * other[:, :size]
    lane = lax.broadcasted_iota(jnp.int32, (heads, 128), 1)
    small_out[:, size:] = jnp.where(
        lane == 0, m_pair, jnp.where(lane == 1, g_even + g_odd, 0.0)
    )
    for h in range(heads):
        at = slice(h, h + 1)
        state = w_own[at] * kept[h].astype(F32) + w_other[at] * got[h].astype(F32)
        state_out[h] = state.astype(BF)


def pair_summary(info, docs, small, small_other, kept, got, length, held):
    return pl.pallas_call(
        holding(functools.partial(pair_kernel, length), held),
        out_shape=(pltpu.VMEM(kept.shape, BF), pltpu.VMEM(small.shape, F32)),
        in_specs=[VMEM_SPEC] * len(held) + [SMEM_SPEC] * 2 + [VMEM_SPEC] * 4,
        out_specs=(VMEM_SPEC,) * 2,
        compiler_params=params(4),
        cost_estimate=cost(1e6, 1e5),
    )(*in_vmem(*held), info, docs, *in_vmem(small, small_other, kept, got))


def incoming_kernel(length, reach, info, docs, own, other, kept, got, *refs):
    smalls, states = refs[:reach], refs[reach : 2 * reach]
    carry, carry_norm, carry_max = refs[2 * reach : 2 * reach + 3]
    own_out, other_out, norm_out, top_out = refs[2 * reach + 3 :]
    heads = own.shape[0]
    size = own.shape[1] - 128
    side = info[1]
    even = side == 0
    first = info[2] // length - side
    m_even, g_even, _, _, _ = pair_scales(info, docs, length, size, own[...], other[...])
    reset_even = reset_of(docs, first, length)
    expos = []
    passed = jnp.zeros((heads, 1), F32)
    unbroken = jnp.bool_(True)
    for k in range(1, reach + 1):
        there = first >= 2 * k
        index = jnp.maximum(first - 2 * k, 0)
        m_k, g_k = smalls[k - 1][:, size : size + 1], smalls[k - 1][:, size + 1 : size + 2]
        expos.append(jnp.where(there & unbroken, m_k + passed, -jnp.inf))
        passed = passed + jnp.where(there, g_k, 0.0)
        broken = reset_of(docs, index, length) | reset_of(docs, index + 1, length)
        unbroken = unbroken & ~(there & broken)
    in_reach = (first <= 2 * reach) & unbroken
    expos.append(jnp.where(in_reach, carry_max[...] + passed, -jnp.inf))
    top_even = functools.reduce(jnp.maximum, expos)
    expos_odd = [jnp.where(reset_even, -jnp.inf, e + g_even) for e in expos]
    top_odd = functools.reduce(jnp.maximum, expos_odd, m_even)
    w_even = [jnp.exp(e - top_even) for e in expos]
    w_odd = [jnp.exp(e - top_odd) for e in expos_odd]
    direct = jnp.exp(m_even - top_odd)
    w_own = [jnp.where(even, a, b) for a, b in zip(w_even, w_odd)]
    w_other = [jnp.where(even, b, a) for a, b in zip(w_even, w_odd)]
    direct_own = jnp.where(even, 0.0, direct)
    direct_other = jnp.where(even, direct, 0.0)
    top_out[...] = jnp.where(even, top_even, top_odd) + jnp.zeros((heads, 128), F32)
    norm = direct_own * jnp.where(even, own[:, :size], other[:, :size])
    norm = norm + w_own[reach] * carry_norm[...]
    for k in range(reach):
        norm = norm + w_own[k] * smalls[k][:, :size]
    norm_out[...] = norm
    for h in range(heads):
        at = slice(h, h + 1)
        here = jnp.where(even, kept[h].astype(F32), got[h].astype(F32))
        base = carry[h]
        mine = w_own[reach][at] * base + direct_own[at] * here
        theirs = w_other[reach][at] * base + direct_other[at] * here
        for k in range(reach):
            state = states[k][h].astype(F32)
            mine = mine + w_own[k][at] * state
            theirs = theirs + w_other[k][at] * state
        own_out[h] = mine.astype(BF)
        other_out[h] = theirs.astype(BF)


def carry_kernel(info, carry, out, sem):
    half = out.shape[1]
    rows = pl.ds(pl.multiple_of(info[1] * half, half), half)
    copy = pltpu.make_async_copy(carry.at[:, rows], out, sem)
    copy.start()
    copy.wait()


def carry_half(info, carry, held):
    heads, size, wide = carry.shape
    return pl.pallas_call(
        holding(carry_kernel, held),
        out_shape=pltpu.VMEM((heads, size // 2, wide), F32),
        in_specs=[VMEM_SPEC] * len(held) + [SMEM_SPEC, HBM_SPEC],
        out_specs=VMEM_SPEC,
        scratch_shapes=[pltpu.SemaphoreType.DMA],
        compiler_params=params(4),
        cost_estimate=cost(1e6, 1e5),
    )(*in_vmem(*held), info, in_hbm(carry))


def incoming_state(
    info, docs, small, small_other, kept, got, smalls, states, carry, carry_norm, carry_max, length,
    held,
):
    heads = small.shape[0]
    return pl.pallas_call(
        holding(functools.partial(incoming_kernel, length, len(smalls)), held),
        out_shape=(
            pltpu.VMEM(kept.shape, BF),
            pltpu.VMEM(kept.shape, BF),
            pltpu.VMEM(carry_norm.shape, F32),
            pltpu.VMEM((heads, 128), F32),
        ),
        in_specs=[VMEM_SPEC] * len(held)
        + [SMEM_SPEC] * 2
        + [VMEM_SPEC] * (7 + 2 * len(smalls)),
        out_specs=(VMEM_SPEC,) * 4,
        compiler_params=params(6),
        cost_estimate=cost(1e6, 1e5),
    )(
        *in_vmem(*held), info, docs,
        *in_vmem(small, small_other, kept, got, *smalls, *states, carry),
        carry_norm, carry_max[:, None],
    )


def inner_kernel(
    heads, info, docs, top_in, query, key, value, u, norm, gate, w_out,
    base_out, slope_out, w_here, sem,
):
    fetch = pltpu.make_async_copy(w_out, w_here, sem)
    fetch.start()
    length = query.shape[0]
    size, wide = query.shape[1] // heads, value.shape[1] // heads
    offset = info[2]
    chunk = 128
    one = jnp.zeros((chunk, 1), jnp.int32)
    before = segments(docs, one + jnp.maximum(offset - 1, 0))
    for head in range(heads):
        keys_at = slice(head * size, (head + 1) * size)
        values_at = slice(head * wide, (head + 1) * wide)
        u_row = u[head : head + 1, :]
        norm_row = norm[head : head + 1, :]
        top = top_in[head : head + 1, 0:1]
        for low in range(0, length, chunk):
            high = low + chunk
            position_t = lax.broadcasted_iota(jnp.int32, (chunk, 1), 0) + low
            position_s = lax.broadcasted_iota(jnp.int32, (1, high), 1)
            segment_t = segments(docs, position_t + offset)
            segment_s = segments(docs, position_s + offset)
            allowed = (position_s <= position_t) & (segment_s == segment_t)
            expo = jnp.where(allowed, u_row[:, :high], -jnp.inf)
            peak = jnp.max(expo, axis=1, keepdims=True)
            q = query[low:high, keys_at]
            scores = lax.dot_general(
                q, key[:high, keys_at], (((1,), (1,)), ((), ())), preferred_element_type=F32
            )
            weighted = jnp.exp(expo - peak) * scores
            num = jnp.dot(
                weighted.astype(BF), value[:high, values_at], preferred_element_type=F32
            )
            den = jnp.sum(weighted, axis=1, keepdims=True)
            carried = segment_t == before
            ceiling = jnp.where(carried, jnp.maximum(peak, top), peak)
            inner_weight = jnp.exp(peak - ceiling)
            outer_weight = jnp.where(carried, jnp.exp(jnp.minimum(top - ceiling, 0.0)), 0.0)
            outer_den = jnp.sum(q.astype(F32) * norm_row, axis=1, keepdims=True)
            full = inner_weight * den + outer_weight * outer_den
            inverse = 1.0 / jnp.maximum(jnp.abs(full), 1.0)
            g = gate[low:high, values_at]
            base_out[low:high, values_at] = g * (num * (inner_weight * inverse))
            slope_out[low:high, values_at] = g * (outer_weight * inverse)
    fetch.wait()


def inner(info, docs, top, query, key, value, u, norm, gate, w_out, heads):
    length, depth = value.shape
    return pl.pallas_call(
        functools.partial(inner_kernel, heads),
        out_shape=(
            pltpu.VMEM((length, depth), F32),
            pltpu.VMEM((length, depth), F32),
            pltpu.VMEM(w_out.shape, BF),
        ),
        in_specs=[SMEM_SPEC] * 2 + [VMEM_SPEC] * 7 + [HBM_SPEC],
        out_specs=(VMEM_SPEC,) * 3,
        scratch_shapes=[pltpu.SemaphoreType.DMA],
        compiler_params=params(12),
        cost_estimate=cost(1e6, 1e5),
    )(info, docs, *in_vmem(top, query, key, value, u, norm, gate), in_hbm(w_out))


def some_columns(info, hidden, w, send, keep, start):
    place = info[0]
    wide = send.shape[1] // 2
    share = w.shape[1] // 4
    for step, owner in enumerate((1, 3, 0, 2)):
        columns = pl.ds(pl.multiple_of((place ^ owner) * share + start, 128), wide)
        part = jnp.dot(hidden[...], w[:, columns], preferred_element_type=F32).astype(BF)
        out = (send, keep)[step // 2]
        low = (step % 2) * wide
        out[:, low : low + wide] = part


def hidden_kernel(heads, info, query, own, other, base, slope, w, hidden, send, keep, state):
    half = own.shape[1]
    side = info[1]
    size, wide = 2 * half, own.shape[2]
    for h in range(heads):
        state[pl.ds(pl.multiple_of(side * half, half), half)] = own[h]
        state[pl.ds(pl.multiple_of((1 - side) * half, half), half)] = other[h]
        outer = jnp.dot(
            query[:, h * size : (h + 1) * size], state[...], preferred_element_type=F32
        )
        columns = slice(h * wide, (h + 1) * wide)
        hidden[:, columns] = (base[:, columns] + slope[:, columns] * outer).astype(BF)
    some_columns(info, hidden, w, send, keep, 0)


def hidden_and_first(info, query, own, other, base, slope, w_here, wide, heads):
    length, depth = base.shape
    return pl.pallas_call(
        functools.partial(hidden_kernel, heads),
        out_shape=(
            pltpu.VMEM((length, depth), BF),
            pltpu.VMEM((length, 2 * wide), BF),
            pltpu.VMEM((length, 2 * wide), BF),
        ),
        in_specs=[SMEM_SPEC] + [VMEM_SPEC] * 6,
        out_specs=(VMEM_SPEC,) * 3,
        scratch_shapes=[pltpu.VMEM((2 * own.shape[1], own.shape[2]), BF)],
        compiler_params=params(12),
        cost_estimate=cost(3e9, 8e6),
    )(info, *in_vmem(query, own, other, base, slope, w_here))


def columns_kernel(start, info, hidden, w, send, keep):
    some_columns(info, hidden, w, send, keep, start)


def next_columns(info, hidden, w_here, wide, start):
    length = hidden.shape[0]
    return pl.pallas_call(
        functools.partial(columns_kernel, start),
        out_shape=(pltpu.VMEM((length, 2 * wide), BF),) * 2,
        in_specs=[SMEM_SPEC, VMEM_SPEC, VMEM_SPEC],
        out_specs=(VMEM_SPEC,) * 2,
        compiler_params=params(12),
        cost_estimate=cost(1e6, 1e5),
    )(info, *in_vmem(hidden, w_here))


def local(
    tokens,
    w_query,
    w_key,
    w_value,
    w_outgate,
    w_gates,
    gate_bias,
    w_out,
    carry_matrix,
    carry_norm,
    carry_max,
    doc_lengths,
):
    length, share = tokens.shape
    heads = gate_bias.shape[1]
    size = w_query.shape[1] // heads
    place = lax.axis_index("tensor")
    block = lax.axis_index("seq")
    blocks = lax.axis_size("seq")
    offset = (block * length).astype(jnp.int32)
    tensor = lambda x, mask: swapped(x, "tensor", mask)
    pair = lambda x: swapped(x, "seq", 1)
    down = lambda x: shifted(x, "seq", 2)

    beside = tensor(tokens, 1)
    sizes = [c for chunks in TOKEN_CHUNKS for c in chunks]
    starts = [sum(sizes[:i]) for i in range(len(sizes))]
    pieces = split_tokens(tokens, starts, sizes)
    source = tokens
    pieces = [(s, c, tensor(x, 2)) for s, c, x in zip(starts, sizes, pieces)]
    groups = []
    for chunks in TOKEN_CHUNKS:
        groups.append(pieces[: len(chunks)])
        pieces = pieces[len(chunks) :]
    gate_w = w_gates.transpose(0, 2, 1).reshape(2 * heads, 4 * share)

    side = (block % 2).astype(jnp.int32)
    info = jnp.stack([place, side, offset]).astype(jnp.int32)
    at = [[(o, s, c) for s, c, _ in group for o in (2, 3)] for group in groups]
    near_at = [(0, 0, share), (1, 0, share)]
    key_value, query_gate = (w_key, w_value), (w_query, w_outgate)
    sums = stage(info, [source, beside], near_at, key_value, share, gate_w)
    far = []
    for i, group in enumerate(groups):
        xs = lax.optimization_barrier((*[x for _, _, x in group], *sums))
        xs, sums = xs[: len(group)], xs[len(group) :]
        xs = [y for x in xs for y in (x, tensor(x, 1))]
        far.append(xs)
        if i < len(groups) - 1:
            last = i == len(groups) - 2
            out = stage(
                info, xs, at[i], key_value, share, gate_w, sums, at[-1] if last else None
            )
            sums = out[:3]
            if last:
                w_key_last, w_value_last = out[3:]
    keys, values, kept, sent, small, u = block_summary(
        info, doc_lengths, gate_bias, xs, at[-1], w_key_last, w_value_last, gate_w,
        sums[0], sums[1], sums[2], share, heads,
    )

    small_other = pair(small)
    got = pair(sent)
    held = (keys, values, kept)
    later_xs = after(keys, *[x for xs in far[1:] for x in xs])
    later = stage(info, later_xs, sum(at[1:], []), query_gate, share, held=held)
    small_other, got, *later = lax.optimization_barrier((small_other, got, *later))
    state_pair, travel = pair_summary(
        info, doc_lengths, small, small_other, kept, got, length, (keys, values)
    )
    smalls, states = [], []
    held = (keys, values, kept, got)
    for step in range(blocks // 4):
        before = state_pair
        travel, state_pair = down(travel), down(state_pair)
        if step == 0:
            near_xs = after(before, source, beside)
            later = stage(info, near_xs, near_at, query_gate, share, None, later, held=held)
        elif step == 1:
            last_xs = after(before, *far[0])
            queries, gate = stage(
                info, last_xs, at[0], query_gate, share, None, later,
                finishes=((unchanged, BF), (jax.nn.sigmoid, F32)), held=held,
            )
            carry = carry_half(after(queries, info), carry_matrix, held)
        travel, state_pair, *later = lax.optimization_barrier((travel, state_pair, *later))
        smalls.append(travel)
        states.append(state_pair)
    state_own, state_other, norm_in, top_own = incoming_state(
        info, doc_lengths, small, small_other, kept, got, smalls, states,
        carry, carry_norm, carry_max, length, (keys, values, queries, gate),
    )
    state_got = pair(state_other)
    base, slope, w_here = inner(
        info, doc_lengths, top_own, queries, keys, values, u, norm_in, gate, w_out, heads
    )

    start = 0
    leaving, arriving = [], []
    for wide in OUT_CHUNKS:
        if start == 0:
            hidden, send, keep = hidden_and_first(
                info, queries, state_own, state_got, base, slope, w_here, wide, heads
            )
        else:
            now = after(leaving[-2], hidden) if len(leaving) > 1 else hidden
            send, keep = next_columns(info, now, w_here, wide, start)
        both = keep.astype(F32) + tensor(send, 1).astype(F32)
        leaving.append(both[:, wide:].astype(BF))
        arriving.append((start, wide, both[:, :wide], tensor(leaving[-1], 2)))
        start += wide
    out = source
    for start, wide, both, came in arriving[:-1]:
        columns = source[:, start : start + wide].astype(F32) + (both + came.astype(F32))
        out = lax.dynamic_update_slice(out, columns.astype(BF), (0, start))
    start, wide, both, came = arriving[-1]
    columns = source[:, start : start + wide].astype(F32) + (both + came.astype(F32))
    return lax.dynamic_update_slice(out, columns.astype(BF), (0, start))


FULL_ACCURACY = lax.Precision.HIGHEST


def plain_shifted(x, axis, by):
    devices = lax.axis_size(axis)
    pairs = [(i, i + by) for i in range(devices) if 0 <= i + by < devices]
    return lax.ppermute(x, axis, pairs)


def segment_of(doc_lengths, positions):
    bounds = jnp.cumsum(doc_lengths)[:-1]
    return jnp.sum((positions[:, None] >= bounds[None, :]).astype(jnp.int32), axis=1)


def combine(earlier, later):
    early_c, early_n, early_m, early_g, early_r = earlier
    late_c, late_n, late_m, late_g, late_r = later
    ceiling = jnp.maximum(early_m + late_g, late_m)
    early_weight = jnp.exp(early_m + late_g - ceiling)
    late_weight = jnp.exp(late_m - ceiling)
    reset_mask = late_r > 0.5
    merged_c = jnp.where(
        reset_mask[:, None, None],
        late_c,
        early_weight[:, None, None] * early_c + late_weight[:, None, None] * late_c,
    )
    merged_n = jnp.where(
        reset_mask[:, None], late_n, early_weight[:, None] * early_n + late_weight[:, None] * late_n
    )
    merged_m = jnp.where(reset_mask, late_m, ceiling)
    return (merged_c, merged_n, merged_m, late_g, jnp.maximum(early_r, late_r))


def block_local(queries, keys, value_rows, input_pre, log_forget, segment, segment_before):
    length = segment.shape[0]
    log_decay = jnp.cumsum(log_forget, axis=0)
    position = jnp.arange(length)
    allowed = (position[:, None] >= position[None, :]) & (segment[:, None] == segment[None, :])
    exponent = log_decay.T[:, :, None] - log_decay.T[:, None, :] + input_pre.T[:, None, :]
    exponent = jnp.where(allowed[None], exponent, -jnp.inf)
    inner_max = jnp.max(exponent, axis=2)
    scores = jnp.einsum("lhk,mhk->hlm", queries, keys, preferred_element_type=jnp.float32)
    weighted = jnp.exp(exponent - inner_max[:, :, None]) * scores
    weighted_bf = weighted.astype(jnp.bfloat16)
    inner_num = jnp.einsum(
        "hlm,mhv->lhv", weighted_bf, value_rows, preferred_element_type=jnp.float32
    )
    inner_den = jnp.sum(weighted, axis=2).T
    in_last = segment == segment[-1]
    tail_expo = log_decay[-1][None, :] - log_decay + input_pre
    tail_expo = jnp.where(in_last[:, None], tail_expo, -jnp.inf)
    tail_max = jnp.max(tail_expo, axis=0)
    key_scaled_rows = (jnp.exp(tail_expo - tail_max[None, :])[:, :, None] * keys).astype(
        jnp.bfloat16
    )
    cell_state_matrix = jnp.einsum(
        "emn,emp->mnp", key_scaled_rows, value_rows, preferred_element_type=jnp.float32
    )
    state_n = jnp.sum(key_scaled_rows.astype(jnp.float32), axis=0)
    reset = (segment[-1] != segment_before).astype(jnp.float32) * jnp.ones_like(tail_max)
    summary = (cell_state_matrix, state_n, tail_max, log_decay[-1], reset)
    return (log_decay, inner_max.T, inner_num, inner_den, summary)


def block_output(
    queries, log_decay, inner_max, inner_num, inner_den, segment, segment_before, incoming
):
    cell_state_matrix, state_n, state_m = incoming
    outer = jnp.where((segment == segment_before)[:, None], log_decay + state_m[None, :], -jnp.inf)
    ceiling = jnp.maximum(inner_max, outer)
    inner_weight = jnp.exp(inner_max - ceiling)
    outer_weight = jnp.exp(outer - ceiling)
    query_single = queries.astype(jnp.float32)
    outer_numerator_sum = jnp.einsum(
        "ciy,iyo->cio", query_single, cell_state_matrix, precision=FULL_ACCURACY
    )
    outer_den = jnp.einsum("lhk,hk->lh", query_single, state_n, precision=FULL_ACCURACY)
    numerator = (
        inner_weight[:, :, None] * inner_num + outer_weight[:, :, None] * outer_numerator_sum
    )
    denominator = inner_weight * inner_den + outer_weight * outer_den
    return numerator / jnp.maximum(jnp.abs(denominator), 1.0)[:, :, None]


def plain_local(
    tokens,
    w_query,
    w_key,
    w_value,
    w_outgate,
    w_gates,
    gate_bias,
    w_out,
    carry_matrix,
    carry_norm,
    carry_max,
    doc_lengths,
):
    length = tokens.shape[0]
    head_count = gate_bias.shape[1]
    query_size = w_query.shape[1] // head_count
    value_size = w_value.shape[1] // head_count
    matrices = (w_query, w_key, w_value, w_outgate)
    zero_init = tuple((jnp.zeros((length, matrix.shape[1]), jnp.float32) for matrix in matrices))
    zero_init = zero_init + (
        jnp.zeros((length, head_count), jnp.float32),
        jnp.zeros((length, head_count), jnp.float32),
    )
    column_block = lax.all_gather(tokens, "tensor", axis=1, tiled=True)
    updated = tuple(
        (jnp.dot(column_block, matrix, preferred_element_type=jnp.float32) for matrix in matrices)
    )
    input_sum = jnp.dot(column_block, w_gates[0], preferred_element_type=jnp.float32)
    forget_sum = jnp.dot(column_block, w_gates[1], preferred_element_type=jnp.float32)
    projected = updated + (input_sum, forget_sum)
    queries = projected[0].astype(jnp.bfloat16).reshape(length, head_count, query_size)
    keys = (
        (projected[1] * query_size ** (-0.5))
        .astype(jnp.bfloat16)
        .reshape(length, head_count, query_size)
    )
    value_rows = projected[2].astype(jnp.bfloat16).reshape(length, head_count, value_size)
    outgate = jax.nn.sigmoid(projected[3])
    input_pre = projected[4] + gate_bias[0][None, :]
    log_forget = jax.nn.log_sigmoid(projected[5] + gate_bias[1][None, :])
    offset = lax.axis_index("seq") * length
    positions = offset + jnp.arange(length, dtype=jnp.int32)
    segment = segment_of(doc_lengths, positions)
    segment_before = segment_of(doc_lengths, jnp.maximum(offset - 1, 0)[None])[0]
    log_decay, inner_max, inner_num, inner_den, summary = block_local(
        queries, keys, value_rows, input_pre, log_forget, segment, segment_before
    )
    start_state = (carry_matrix, carry_norm, carry_max)
    zero_heads = jnp.zeros((head_count,), jnp.float32)
    is_leader = lax.axis_index("seq") == 0

    def relay(iteration, current):
        leaving = combine(current + (zero_heads, zero_heads), summary)[:3]
        arrived = plain_shifted(leaving, "seq", 1)
        return tuple(
            (
                jnp.where(is_leader, initial, received)
                for initial, received in zip(start_state, arrived)
            )
        )

    incoming = lax.fori_loop(0, lax.axis_size("seq") - 1, relay, start_state)
    mixed_heads = block_output(
        queries, log_decay, inner_max, inner_num, inner_den, segment, segment_before, incoming
    )
    hidden = (outgate * mixed_heads.reshape(length, head_count * value_size)).astype(jnp.bfloat16)
    partial_value = jnp.dot(hidden, w_out, preferred_element_type=jnp.float32)
    summed = lax.psum_scatter(
        partial_value.astype(jnp.bfloat16), "tensor", scatter_dimension=1, tiled=True
    ).astype(jnp.float32)
    return (tokens.astype(jnp.float32) + summed).astype(jnp.bfloat16)


def solution(mesh):
    fast = mesh.shape["tensor"] == 4 and mesh.shape["seq"] == 8
    return jax.shard_map(
        local if fast else plain_local,
        mesh=mesh,
        in_specs=(
            P("seq", "tensor"),
            P(None, "tensor"),
            P(None, "tensor"),
            P(None, "tensor"),
            P(None, "tensor"),
            P(None, None, "tensor"),
            P(None, "tensor"),
            P("tensor", None),
            P("tensor", None, None),
            P("tensor", None),
            P("tensor"),
            P(),
        ),
        out_specs=P("seq", "tensor"),
        check_vma=False,
    )
```

```python
import functools

import jax
import jax.numpy as jnp
from jax import lax
from jax.experimental import pallas as pl
from jax.experimental.pallas import tpu as pltpu
from jax.sharding import PartitionSpec as P

BF = jnp.bfloat16
F32 = jnp.float32
MIB = 1024 * 1024
TOKEN_CHUNKS = ((256, 256), (512,))
OUT_CHUNKS = (256, 256, 256, 256)


def params(mib):
    return pltpu.CompilerParams(vmem_limit_bytes=mib * MIB)


def cost(flops, moved):
    return pl.CostEstimate(flops=int(flops), bytes_accessed=int(moved), transcendentals=0)


def swapped(x, axis, mask):
    size = lax.axis_size(axis)
    return lax.ppermute(x, axis, [(i, i ^ mask) for i in range(size)])


def shifted(x, axis, by):
    size = lax.axis_size(axis)
    return lax.ppermute(x, axis, [(i, (i + by) % size) for i in range(size)])


def after(first, *others):
    out = lax.optimization_barrier((first,) + others)[1:]
    return out[0] if len(out) == 1 else out


SMEM_SPEC = pl.BlockSpec(memory_space=pltpu.SMEM)
VMEM_SPEC = pl.BlockSpec(memory_space=pltpu.VMEM)
HBM_SPEC = pl.BlockSpec(memory_space=pltpu.HBM)


def in_hbm(x):
    return pltpu.with_memory_space_constraint(x, pltpu.HBM)


def in_vmem(*xs):
    return [pltpu.with_memory_space_constraint(x, pltpu.VMEM) for x in xs]


def holding(kernel, held):
    return (lambda *refs: kernel(*refs[len(held) :])) if held else kernel


def split_kernel(starts, tokens, *refs):
    outs, sem = refs[:-1], refs[-1]
    copies = []
    for i, (low, out) in enumerate(zip(starts, outs)):
        source = tokens.at[:, low : low + out.shape[1]]
        copies.append(pltpu.make_async_copy(source, out, sem.at[i]))
        copies[-1].start()
    for copy in copies:
        copy.wait()


def split_tokens(tokens, starts, sizes):
    length = tokens.shape[0]
    return pl.pallas_call(
        functools.partial(split_kernel, starts),
        out_shape=tuple(pltpu.VMEM((length, c), BF) for c in sizes),
        in_specs=[HBM_SPEC],
        out_specs=(VMEM_SPEC,) * len(sizes),
        scratch_shapes=[pltpu.SemaphoreType.DMA((len(sizes),))],
        compiler_params=params(4),
        cost_estimate=cost(1e6, 1e5),
    )(in_hbm(tokens))


def across_tokens(w, x):
    return lax.dot_general(w, x, (((1,), (1,)), ((), ())), preferred_element_type=F32)


def row_start(place, share, owner, first):
    return pl.multiple_of((place ^ owner) * share + first, 128)


def copies_of(weights, targets, semaphores, at, place, share):
    result = []
    for i, (w, target) in enumerate(zip(weights, targets)):
        low, group = 0, []
        for p, (owner, first, count) in enumerate(at):
            group.append(
                pltpu.make_async_copy(
                    w.at[pl.ds(row_start(place, share, owner, first), count)],
                    target.at[pl.ds(low, count)],
                    semaphores.at[i, p],
                )
            )
            low += count
        result.append(group)
    return result


def stage_kernel(xs_at, ahead_at, share, names, with_sum, finishes, gated, info, *refs):
    refs = list(refs)
    take = lambda n: [refs.pop(0) for _ in range(n)]
    count_w = names
    xs, ws = take(len(xs_at)), take(count_w)
    gate_w = take(1)[0] if gated else None
    sums = take(count_w + gated) if with_sum else None
    outs = take(count_w + gated)
    ahead = take(2) if ahead_at else []
    held = take(count_w)
    sems = take(1)[0]
    place = info[0]
    now = copies_of(ws, held, sems, xs_at, place, share)
    later = copies_of(ws, ahead, take(1)[0], ahead_at, place, share) if ahead_at else []
    for group in now + later:
        for copy in group:
            copy.start()
    if gated:
        gates = sums[count_w][...] if with_sum else 0.0
        for (owner, first, count), x in zip(xs_at, xs):
            gates = gates + across_tokens(
                gate_w[:, pl.ds(row_start(place, share, owner, first), count)], x[...]
            )
        outs[count_w][...] = gates
    for i in range(count_w):
        for copy in now[i]:
            copy.wait()

        def body(j, _, i=i):
            columns = pl.ds(pl.multiple_of(j * 256, 256), 256)
            total = sums[i][:, columns] if with_sum else None
            low = 0
            for (_, _, count), x in zip(xs_at, xs):
                part = jnp.dot(
                    x[...], held[i][low : low + count, columns], preferred_element_type=F32
                )
                total = part if total is None else total + part
                low += count
            outs[i][:, columns] = finishes[i](total).astype(outs[i].dtype)
            return 0

        lax.fori_loop(0, outs[i].shape[1] // 256, body, 0)
    for group in later:
        for copy in group:
            copy.wait()


def unchanged(x):
    return x


def stage(info, xs, xs_at, weights, share, gate_w=None, sums=None, ahead_at=None, finishes=None, held=()):
    length = xs[0].shape[0]
    count = sum(c for _, _, c in xs_at)
    gated = int(gate_w is not None)
    kinds = [F32] * len(weights) if finishes is None else [k for _, k in finishes]
    calls = [unchanged] * len(weights) if finishes is None else [f for f, _ in finishes]
    shapes = [pltpu.VMEM((length, w.shape[1]), k) for w, k in zip(weights, kinds)]
    if gated:
        shapes.append(pltpu.VMEM((gate_w.shape[0], length), F32))
    scratch = [pltpu.VMEM((count, w.shape[1]), BF) for w in weights]
    scratch.append(pltpu.SemaphoreType.DMA((len(weights), len(xs_at))))
    if ahead_at:
        rows = sum(c for _, _, c in ahead_at)
        shapes += [pltpu.VMEM((rows, w.shape[1]), BF) for w in weights[:2]]
        scratch.append(pltpu.SemaphoreType.DMA((2, len(ahead_at))))
    operands = [*in_vmem(*held), info, *in_vmem(*xs), *[in_hbm(w) for w in weights]]
    specs = [VMEM_SPEC] * len(held) + [SMEM_SPEC] + [VMEM_SPEC] * len(xs) + [HBM_SPEC] * len(weights)
    if gated:
        operands.append(gate_w)
        specs.append(VMEM_SPEC)
    aliases = {}
    if sums is not None:
        if finishes is None:
            aliases = {len(operands) + i: i for i in range(len(sums))}
        operands += in_vmem(*sums)
        specs += [VMEM_SPEC] * len(sums)
    return pl.pallas_call(
        holding(
            functools.partial(
                stage_kernel, xs_at, ahead_at, share, len(weights), sums is not None, calls, gated
            ),
            held,
        ),
        out_shape=tuple(shapes),
        in_specs=specs,
        out_specs=(VMEM_SPEC,) * len(shapes),
        scratch_shapes=scratch,
        input_output_aliases=aliases,
        compiler_params=params(24),
        cost_estimate=cost(1e6, 1e5),
    )(*operands)


def segments(docs, positions):
    total = jnp.zeros_like(positions)
    bound = jnp.int32(0)
    for j in range(docs.shape[0] - 1):
        bound = bound + docs[j]
        total = total + (positions >= bound).astype(jnp.int32)
    return total


def gate_rows(both, offset, docs, bias):
    heads, length = both.shape[0] // 2, both.shape[1]
    row = lax.broadcasted_iota(jnp.int32, (heads, length), 0)
    lane = lax.broadcasted_iota(jnp.int32, (heads, length), 1)
    input_bias = jnp.zeros((heads, length), F32)
    forget_bias = jnp.zeros((heads, length), F32)
    for h in range(heads):
        input_bias = jnp.where(row == h, bias[0, h], input_bias)
        forget_bias = jnp.where(row == h, bias[1, h], forget_bias)
    input_pre = both[:heads] + input_bias
    forget = both[heads:] + forget_bias
    decay = jnp.minimum(forget, 0.0) - jnp.log1p(jnp.exp(-jnp.abs(forget)))
    step = 1
    while step < length:
        decay = decay + jnp.where(lane >= step, pltpu.roll(decay, step, 1), 0.0)
        step *= 2
    u = input_pre - decay
    segment = segments(docs, lane + offset)
    last = segments(docs, lane * 0 + (offset + length - 1))
    open_rows = segment == last
    top = jnp.max(jnp.where(open_rows, u, -jnp.inf), axis=1, keepdims=True)
    weight = jnp.where(open_rows, jnp.exp(u - top), 0.0)
    total = decay[:, length - 1 : length]
    narrow = lax.broadcasted_iota(jnp.int32, (heads, 128), 1)
    stats = jnp.where(narrow == 0, total + top, jnp.where(narrow == 1, total, 0.0))
    return u, weight, stats


def summary_kernel(xs_at, share, heads, info, docs, bias, *refs):
    xs = refs[: len(xs_at)]
    key_w, value_w, gate_w, key_sum, value_sum, gate_sum = refs[len(xs_at) : len(xs_at) + 6]
    key_out, value_out, keep_out, send_out, small_out, u_out, state = refs[len(xs_at) + 6 :]
    place, side, offset = info[0], info[1], info[2]
    size, wide = state.shape
    gates = gate_sum[...]
    for (owner, first, count), x in zip(xs_at, xs):
        gates = gates + across_tokens(
            gate_w[:, pl.ds(row_start(place, share, owner, first), count)], x[...]
        )
    u, weight, stats = gate_rows(gates, offset, docs, bias)
    u_out[...] = u
    small_out[:, size:] = stats
    spare = jnp.zeros((128 - weight.shape[0], weight.shape[1]), F32)
    columns = jnp.concatenate([weight, spare], axis=0).T
    half = size // 2
    for h in range(heads):
        key_at, value_at = slice(h * size, (h + 1) * size), slice(h * wide, (h + 1) * wide)
        key, value, low = key_sum[:, key_at], value_sum[:, value_at], 0
        for x in xs:
            count = x.shape[1]
            rows = slice(low, low + count)
            key = key + jnp.dot(x[...], key_w[rows, key_at], preferred_element_type=F32)
            value = value + jnp.dot(x[...], value_w[rows, value_at], preferred_element_type=F32)
            low += count
        key = (key * size ** (-0.5)).astype(BF)
        value = value.astype(BF)
        key_out[:, key_at] = key
        value_out[:, value_at] = value
        scaled = (columns[:, h : h + 1] * key.astype(F32)).astype(BF)
        small_out[h : h + 1, :size] = jnp.sum(scaled.astype(F32), axis=0, keepdims=True)
        state[...] = lax.dot_general(
            scaled, value, (((0,), (0,)), ((), ())), preferred_element_type=F32
        )
        keep_out[h] = state[pl.ds(pl.multiple_of(side * half, half), half)].astype(BF)
        send_out[h] = state[pl.ds(pl.multiple_of((1 - side) * half, half), half)].astype(BF)


def block_summary(
    info, docs, bias, xs, xs_at, key_w, value_w, gate_w, key_sum, value_sum, gates, share, heads
):
    length = xs[0].shape[0]
    size, wide = key_w.shape[1] // heads, value_w.shape[1] // heads
    return pl.pallas_call(
        functools.partial(summary_kernel, xs_at, share, heads),
        out_shape=(
            pltpu.VMEM((length, heads * size), BF),
            pltpu.VMEM((length, heads * wide), BF),
            pltpu.VMEM((heads, size // 2, wide), BF),
            pltpu.VMEM((heads, size // 2, wide), BF),
            pltpu.VMEM((heads, size + 128), F32),
            pltpu.VMEM((heads, length), F32),
        ),
        in_specs=[SMEM_SPEC] * 3 + [VMEM_SPEC] * (len(xs) + 6),
        out_specs=(VMEM_SPEC,) * 6,
        scratch_shapes=[pltpu.VMEM((size, wide), F32)],
        compiler_params=params(16),
        cost_estimate=cost(4e9, 4e6),
    )(info, docs, bias, *in_vmem(*xs, key_w, value_w), gate_w, *in_vmem(key_sum, value_sum, gates))


def reset_of(docs, index, length):
    first = jnp.maximum(index * length - 1, 0)
    return segments(docs, (index + 1) * length - 1) != segments(docs, first)


def pair_scales(info, docs, length, size, own, other):
    even = info[1] == 0
    first = info[2] // length - info[1]
    m_own, g_own = own[:, size : size + 1], own[:, size + 1 : size + 2]
    m_other, g_other = other[:, size : size + 1], other[:, size + 1 : size + 2]
    m_even, g_even = jnp.where(even, m_own, m_other), jnp.where(even, g_own, g_other)
    m_odd, g_odd = jnp.where(even, m_other, m_own), jnp.where(even, g_other, g_own)
    reset_odd = reset_of(docs, first + 1, length)
    m_pair = jnp.maximum(jnp.where(reset_odd, -jnp.inf, m_even + g_odd), m_odd)
    pair_even = jnp.where(reset_odd, 0.0, jnp.exp(jnp.minimum(m_even + g_odd - m_pair, 0.0)))
    pair_odd = jnp.exp(m_odd - m_pair)
    weights = jnp.where(even, pair_even, pair_odd), jnp.where(even, pair_odd, pair_even)
    return m_even, g_even, g_odd, m_pair, weights


def pair_kernel(length, info, docs, own, other, kept, got, state_out, small_out):
    heads = own.shape[0]
    size = own.shape[1] - 128
    _, g_even, g_odd, m_pair, (w_own, w_other) = pair_scales(
        info, docs, length, size, own[...], other[...]
    )
    small_out[:, :size] = w_own * own[:, :size] + w_other * other[:, :size]
    lane = lax.broadcasted_iota(jnp.int32, (heads, 128), 1)
    small_out[:, size:] = jnp.where(
        lane == 0, m_pair, jnp.where(lane == 1, g_even + g_odd, 0.0)
    )
    for h in range(heads):
        at = slice(h, h + 1)
        state = w_own[at] * kept[h].astype(F32) + w_other[at] * got[h].astype(F32)
        state_out[h] = state.astype(BF)


def pair_summary(info, docs, small, small_other, kept, got, length, held):
    return pl.pallas_call(
        holding(functools.partial(pair_kernel, length), held),
        out_shape=(pltpu.VMEM(kept.shape, BF), pltpu.VMEM(small.shape, F32)),
        in_specs=[VMEM_SPEC] * len(held) + [SMEM_SPEC] * 2 + [VMEM_SPEC] * 4,
        out_specs=(VMEM_SPEC,) * 2,
        compiler_params=params(4),
        cost_estimate=cost(1e6, 1e5),
    )(*in_vmem(*held), info, docs, *in_vmem(small, small_other, kept, got))


def incoming_kernel(length, reach, info, docs, own, other, kept, got, *refs):
    smalls, states = refs[:reach], refs[reach : 2 * reach]
    carry, carry_norm, carry_max = refs[2 * reach : 2 * reach + 3]
    own_out, other_out, norm_out, top_out = refs[2 * reach + 3 :]
    heads = own.shape[0]
    size = own.shape[1] - 128
    side = info[1]
    even = side == 0
    first = info[2] // length - side
    m_even, g_even, _, _, _ = pair_scales(info, docs, length, size, own[...], other[...])
    reset_even = reset_of(docs, first, length)
    expos = []
    passed = jnp.zeros((heads, 1), F32)
    unbroken = jnp.bool_(True)
    for k in range(1, reach + 1):
        there = first >= 2 * k
        index = jnp.maximum(first - 2 * k, 0)
        m_k, g_k = smalls[k - 1][:, size : size + 1], smalls[k - 1][:, size + 1 : size + 2]
        expos.append(jnp.where(there & unbroken, m_k + passed, -jnp.inf))
        passed = passed + jnp.where(there, g_k, 0.0)
        broken = reset_of(docs, index, length) | reset_of(docs, index + 1, length)
        unbroken = unbroken & ~(there & broken)
    in_reach = (first <= 2 * reach) & unbroken
    expos.append(jnp.where(in_reach, carry_max[...] + passed, -jnp.inf))
    top_even = functools.reduce(jnp.maximum, expos)
    expos_odd = [jnp.where(reset_even, -jnp.inf, e + g_even) for e in expos]
    top_odd = functools.reduce(jnp.maximum, expos_odd, m_even)
    w_even = [jnp.exp(e - top_even) for e in expos]
    w_odd = [jnp.exp(e - top_odd) for e in expos_odd]
    direct = jnp.exp(m_even - top_odd)
    w_own = [jnp.where(even, a, b) for a, b in zip(w_even, w_odd)]
    w_other = [jnp.where(even, b, a) for a, b in zip(w_even, w_odd)]
    direct_own = jnp.where(even, 0.0, direct)
    direct_other = jnp.where(even, direct, 0.0)
    top_out[...] = jnp.where(even, top_even, top_odd) + jnp.zeros((heads, 128), F32)
    norm = direct_own * jnp.where(even, own[:, :size], other[:, :size])
    norm = norm + w_own[reach] * carry_norm[...]
    for k in range(reach):
        norm = norm + w_own[k] * smalls[k][:, :size]
    norm_out[...] = norm
    for h in range(heads):
        at = slice(h, h + 1)
        here = jnp.where(even, kept[h].astype(F32), got[h].astype(F32))
        base = carry[h]
        mine = w_own[reach][at] * base + direct_own[at] * here
        theirs = w_other[reach][at] * base + direct_other[at] * here
        for k in range(reach):
            state = states[k][h].astype(F32)
            mine = mine + w_own[k][at] * state
            theirs = theirs + w_other[k][at] * state
        own_out[h] = mine.astype(BF)
        other_out[h] = theirs.astype(BF)


def carry_kernel(info, carry, out, sem):
    half = out.shape[1]
    rows = pl.ds(pl.multiple_of(info[1] * half, half), half)
    copy = pltpu.make_async_copy(carry.at[:, rows], out, sem)
    copy.start()
    copy.wait()


def carry_half(info, carry, held):
    heads, size, wide = carry.shape
    return pl.pallas_call(
        holding(carry_kernel, held),
        out_shape=pltpu.VMEM((heads, size // 2, wide), F32),
        in_specs=[VMEM_SPEC] * len(held) + [SMEM_SPEC, HBM_SPEC],
        out_specs=VMEM_SPEC,
        scratch_shapes=[pltpu.SemaphoreType.DMA],
        compiler_params=params(4),
        cost_estimate=cost(1e6, 1e5),
    )(*in_vmem(*held), info, in_hbm(carry))


def incoming_state(
    info, docs, small, small_other, kept, got, smalls, states, carry, carry_norm, carry_max, length,
    held,
):
    heads = small.shape[0]
    return pl.pallas_call(
        holding(functools.partial(incoming_kernel, length, len(smalls)), held),
        out_shape=(
            pltpu.VMEM(kept.shape, BF),
            pltpu.VMEM(kept.shape, BF),
            pltpu.VMEM(carry_norm.shape, F32),
            pltpu.VMEM((heads, 128), F32),
        ),
        in_specs=[VMEM_SPEC] * len(held)
        + [SMEM_SPEC] * 2
        + [VMEM_SPEC] * (7 + 2 * len(smalls)),
        out_specs=(VMEM_SPEC,) * 4,
        compiler_params=params(6),
        cost_estimate=cost(1e6, 1e5),
    )(
        *in_vmem(*held), info, docs,
        *in_vmem(small, small_other, kept, got, *smalls, *states, carry),
        carry_norm, carry_max[:, None],
    )


def inner_kernel(
    heads, info, docs, top_in, query, key, value, u, norm, gate, w_out,
    base_out, slope_out, w_here, sem,
):
    fetch = pltpu.make_async_copy(w_out, w_here, sem)
    fetch.start()
    length = query.shape[0]
    size, wide = query.shape[1] // heads, value.shape[1] // heads
    offset = info[2]
    chunk = 128
    one = jnp.zeros((chunk, 1), jnp.int32)
    before = segments(docs, one + jnp.maximum(offset - 1, 0))
    for head in range(heads):
        keys_at = slice(head * size, (head + 1) * size)
        values_at = slice(head * wide, (head + 1) * wide)
        u_row = u[head : head + 1, :]
        norm_row = norm[head : head + 1, :]
        top = top_in[head : head + 1, 0:1]
        for low in range(0, length, chunk):
            high = low + chunk
            position_t = lax.broadcasted_iota(jnp.int32, (chunk, 1), 0) + low
            position_s = lax.broadcasted_iota(jnp.int32, (1, high), 1)
            segment_t = segments(docs, position_t + offset)
            segment_s = segments(docs, position_s + offset)
            allowed = (position_s <= position_t) & (segment_s == segment_t)
            expo = jnp.where(allowed, u_row[:, :high], -jnp.inf)
            peak = jnp.max(expo, axis=1, keepdims=True)
            q = query[low:high, keys_at]
            scores = lax.dot_general(
                q, key[:high, keys_at], (((1,), (1,)), ((), ())), preferred_element_type=F32
            )
            weighted = jnp.exp(expo - peak) * scores
            num = jnp.dot(
                weighted.astype(BF), value[:high, values_at], preferred_element_type=F32
            )
            den = jnp.sum(weighted, axis=1, keepdims=True)
            carried = segment_t == before
            ceiling = jnp.where(carried, jnp.maximum(peak, top), peak)
            inner_weight = jnp.exp(peak - ceiling)
            outer_weight = jnp.where(carried, jnp.exp(jnp.minimum(top - ceiling, 0.0)), 0.0)
            outer_den = jnp.sum(q.astype(F32) * norm_row, axis=1, keepdims=True)
            full = inner_weight * den + outer_weight * outer_den
            inverse = 1.0 / jnp.maximum(jnp.abs(full), 1.0)
            g = gate[low:high, values_at]
            base_out[low:high, values_at] = g * (num * (inner_weight * inverse))
            slope_out[low:high, values_at] = g * (outer_weight * inverse)
    fetch.wait()


def inner(info, docs, top, query, key, value, u, norm, gate, w_out, heads):
    length, depth = value.shape
    return pl.pallas_call(
        functools.partial(inner_kernel, heads),
        out_shape=(
            pltpu.VMEM((length, depth), F32),
            pltpu.VMEM((length, depth), F32),
            pltpu.VMEM(w_out.shape, BF),
        ),
        in_specs=[SMEM_SPEC] * 2 + [VMEM_SPEC] * 7 + [HBM_SPEC],
        out_specs=(VMEM_SPEC,) * 3,
        scratch_shapes=[pltpu.SemaphoreType.DMA],
        compiler_params=params(12),
        cost_estimate=cost(1e6, 1e5),
    )(info, docs, *in_vmem(top, query, key, value, u, norm, gate), in_hbm(w_out))


def some_columns(info, hidden, w, send, keep, start):
    place = info[0]
    wide = send.shape[1] // 2
    share = w.shape[1] // 4
    for step, owner in enumerate((1, 3, 0, 2)):
        columns = pl.ds(pl.multiple_of((place ^ owner) * share + start, 128), wide)
        part = jnp.dot(hidden[...], w[:, columns], preferred_element_type=F32).astype(BF)
        out = (send, keep)[step // 2]
        low = (step % 2) * wide
        out[:, low : low + wide] = part


def hidden_kernel(heads, info, query, own, other, base, slope, w, hidden, send, keep, state):
    half = own.shape[1]
    side = info[1]
    size, wide = 2 * half, own.shape[2]
    for h in range(heads):
        state[pl.ds(pl.multiple_of(side * half, half), half)] = own[h]
        state[pl.ds(pl.multiple_of((1 - side) * half, half), half)] = other[h]
        outer = jnp.dot(
            query[:, h * size : (h + 1) * size], state[...], preferred_element_type=F32
        )
        columns = slice(h * wide, (h + 1) * wide)
        hidden[:, columns] = (base[:, columns] + slope[:, columns] * outer).astype(BF)
    some_columns(info, hidden, w, send, keep, 0)


def hidden_and_first(info, query, own, other, base, slope, w_here, wide, heads):
    length, depth = base.shape
    return pl.pallas_call(
        functools.partial(hidden_kernel, heads),
        out_shape=(
            pltpu.VMEM((length, depth), BF),
            pltpu.VMEM((length, 2 * wide), BF),
            pltpu.VMEM((length, 2 * wide), BF),
        ),
        in_specs=[SMEM_SPEC] + [VMEM_SPEC] * 6,
        out_specs=(VMEM_SPEC,) * 3,
        scratch_shapes=[pltpu.VMEM((2 * own.shape[1], own.shape[2]), BF)],
        compiler_params=params(12),
        cost_estimate=cost(3e9, 8e6),
    )(info, *in_vmem(query, own, other, base, slope, w_here))


def columns_kernel(start, info, hidden, w, send, keep):
    some_columns(info, hidden, w, send, keep, start)


def next_columns(info, hidden, w_here, wide, start):
    length = hidden.shape[0]
    return pl.pallas_call(
        functools.partial(columns_kernel, start),
        out_shape=(pltpu.VMEM((length, 2 * wide), BF),) * 2,
        in_specs=[SMEM_SPEC, VMEM_SPEC, VMEM_SPEC],
        out_specs=(VMEM_SPEC,) * 2,
        compiler_params=params(12),
        cost_estimate=cost(1e6, 1e5),
    )(info, *in_vmem(hidden, w_here))


def local(
    tokens,
    w_query,
    w_key,
    w_value,
    w_outgate,
    w_gates,
    gate_bias,
    w_out,
    carry_matrix,
    carry_norm,
    carry_max,
    doc_lengths,
):
    length, share = tokens.shape
    heads = gate_bias.shape[1]
    size = w_query.shape[1] // heads
    place = lax.axis_index("tensor")
    block = lax.axis_index("seq")
    blocks = lax.axis_size("seq")
    offset = (block * length).astype(jnp.int32)
    tensor = lambda x, mask: swapped(x, "tensor", mask)
    pair = lambda x: swapped(x, "seq", 1)
    down = lambda x: shifted(x, "seq", 2)

    beside = tensor(tokens, 1)
    sizes = [c for chunks in TOKEN_CHUNKS for c in chunks]
    starts = [sum(sizes[:i]) for i in range(len(sizes))]
    pieces = split_tokens(tokens, starts, sizes)
    source = tokens
    pieces = [(s, c, tensor(x, 2)) for s, c, x in zip(starts, sizes, pieces)]
    groups = []
    for chunks in TOKEN_CHUNKS:
        groups.append(pieces[: len(chunks)])
        pieces = pieces[len(chunks) :]
    gate_w = w_gates.transpose(0, 2, 1).reshape(2 * heads, 4 * share)

    side = (block % 2).astype(jnp.int32)
    info = jnp.stack([place, side, offset]).astype(jnp.int32)
    at = [[(o, s, c) for s, c, _ in group for o in (2, 3)] for group in groups]
    near_at = [(0, 0, share), (1, 0, share)]
    first_three = (w_key, w_value, w_query)
    sums = stage(info, [source, beside], near_at, first_three, share, gate_w)
    far = []
    for i, group in enumerate(groups):
        xs = lax.optimization_barrier((*[x for _, _, x in group], *sums))
        xs, sums = xs[: len(group)], xs[len(group) :]
        xs = [y for x in xs for y in (x, tensor(x, 1))]
        far.append(xs)
        if i < len(groups) - 1:
            last = i == len(groups) - 2
            out = stage(
                info, xs, at[i], first_three, share, gate_w, sums, at[-1] if last else None
            )
            sums = out[:4]
            if last:
                w_key_last, w_value_last = out[4:]
    keys, values, kept, sent, small, u = block_summary(
        info, doc_lengths, gate_bias, xs, at[-1], w_key_last, w_value_last, gate_w,
        sums[0], sums[1], sums[3], share, heads,
    )

    small_other = pair(small)
    got = pair(sent)
    held = (keys, values, kept)
    far_xs = after(keys, *[x for xs in far for x in xs])
    (queries,) = stage(
        info, far_xs[-len(far[-1]) :], at[-1], (w_query,), share, None, [sums[2]],
        finishes=((unchanged, BF),), held=held,
    )
    gate = stage(info, far_xs, sum(at, []), (w_outgate,), share, held=held)
    small_other, got, queries, *gate = lax.optimization_barrier(
        (small_other, got, queries, *gate)
    )
    state_pair, travel = pair_summary(
        info, doc_lengths, small, small_other, kept, got, length, (keys, values, queries)
    )
    smalls, states = [], []
    held = (keys, values, kept, got, queries)
    for step in range(blocks // 4):
        before = state_pair
        travel, state_pair = down(travel), down(state_pair)
        if step == 0:
            near_xs = after(before, source, beside)
            gate = stage(
                info, near_xs, near_at, (w_outgate,), share, None, gate,
                finishes=((jax.nn.sigmoid, F32),), held=held,
            )
            travel, state_pair, *gate = lax.optimization_barrier((travel, state_pair, *gate))
        elif step == 1:
            carry = carry_half(after(before, info), carry_matrix, (*held, *gate))
            travel, state_pair, carry = lax.optimization_barrier((travel, state_pair, carry))
        smalls.append(travel)
        states.append(state_pair)
    (gate,) = gate
    state_own, state_other, norm_in, top_own = incoming_state(
        info, doc_lengths, small, small_other, kept, got, smalls, states,
        carry, carry_norm, carry_max, length, (keys, values, queries, gate),
    )
    state_got = pair(state_other)
    base, slope, w_here = inner(
        info, doc_lengths, top_own, queries, keys, values, u, norm_in, gate, w_out, heads
    )

    start = 0
    leaving, arriving = [], []
    for wide in OUT_CHUNKS:
        if start == 0:
            hidden, send, keep = hidden_and_first(
                info, queries, state_own, state_got, base, slope, w_here, wide, heads
            )
        else:
            now = after(leaving[-2], hidden) if len(leaving) > 1 else hidden
            send, keep = next_columns(info, now, w_here, wide, start)
        both = keep.astype(F32) + tensor(send, 1).astype(F32)
        leaving.append(both[:, wide:].astype(BF))
        arriving.append((start, wide, both[:, :wide], tensor(leaving[-1], 2)))
        start += wide
    out = source
    for start, wide, both, came in arriving[:-1]:
        columns = source[:, start : start + wide].astype(F32) + (both + came.astype(F32))
        out = lax.dynamic_update_slice(out, columns.astype(BF), (0, start))
    start, wide, both, came = arriving[-1]
    columns = source[:, start : start + wide].astype(F32) + (both + came.astype(F32))
    return lax.dynamic_update_slice(out, columns.astype(BF), (0, start))


FULL_ACCURACY = lax.Precision.HIGHEST


def plain_shifted(x, axis, by):
    devices = lax.axis_size(axis)
    pairs = [(i, i + by) for i in range(devices) if 0 <= i + by < devices]
    return lax.ppermute(x, axis, pairs)


def segment_of(doc_lengths, positions):
    bounds = jnp.cumsum(doc_lengths)[:-1]
    return jnp.sum((positions[:, None] >= bounds[None, :]).astype(jnp.int32), axis=1)


def combine(earlier, later):
    early_c, early_n, early_m, early_g, early_r = earlier
    late_c, late_n, late_m, late_g, late_r = later
    ceiling = jnp.maximum(early_m + late_g, late_m)
    early_weight = jnp.exp(early_m + late_g - ceiling)
    late_weight = jnp.exp(late_m - ceiling)
    reset_mask = late_r > 0.5
    merged_c = jnp.where(
        reset_mask[:, None, None],
        late_c,
        early_weight[:, None, None] * early_c + late_weight[:, None, None] * late_c,
    )
    merged_n = jnp.where(
        reset_mask[:, None], late_n, early_weight[:, None] * early_n + late_weight[:, None] * late_n
    )
    merged_m = jnp.where(reset_mask, late_m, ceiling)
    return (merged_c, merged_n, merged_m, late_g, jnp.maximum(early_r, late_r))


def block_local(queries, keys, value_rows, input_pre, log_forget, segment, segment_before):
    length = segment.shape[0]
    log_decay = jnp.cumsum(log_forget, axis=0)
    position = jnp.arange(length)
    allowed = (position[:, None] >= position[None, :]) & (segment[:, None] == segment[None, :])
    exponent = log_decay.T[:, :, None] - log_decay.T[:, None, :] + input_pre.T[:, None, :]
    exponent = jnp.where(allowed[None], exponent, -jnp.inf)
    inner_max = jnp.max(exponent, axis=2)
    scores = jnp.einsum("lhk,mhk->hlm", queries, keys, preferred_element_type=jnp.float32)
    weighted = jnp.exp(exponent - inner_max[:, :, None]) * scores
    weighted_bf = weighted.astype(jnp.bfloat16)
    inner_num = jnp.einsum(
        "hlm,mhv->lhv", weighted_bf, value_rows, preferred_element_type=jnp.float32
    )
    inner_den = jnp.sum(weighted, axis=2).T
    in_last = segment == segment[-1]
    tail_expo = log_decay[-1][None, :] - log_decay + input_pre
    tail_expo = jnp.where(in_last[:, None], tail_expo, -jnp.inf)
    tail_max = jnp.max(tail_expo, axis=0)
    key_scaled_rows = (jnp.exp(tail_expo - tail_max[None, :])[:, :, None] * keys).astype(
        jnp.bfloat16
    )
    cell_state_matrix = jnp.einsum(
        "emn,emp->mnp", key_scaled_rows, value_rows, preferred_element_type=jnp.float32
    )
    state_n = jnp.sum(key_scaled_rows.astype(jnp.float32), axis=0)
    reset = (segment[-1] != segment_before).astype(jnp.float32) * jnp.ones_like(tail_max)
    summary = (cell_state_matrix, state_n, tail_max, log_decay[-1], reset)
    return (log_decay, inner_max.T, inner_num, inner_den, summary)


def block_output(
    queries, log_decay, inner_max, inner_num, inner_den, segment, segment_before, incoming
):
    cell_state_matrix, state_n, state_m = incoming
    outer = jnp.where((segment == segment_before)[:, None], log_decay + state_m[None, :], -jnp.inf)
    ceiling = jnp.maximum(inner_max, outer)
    inner_weight = jnp.exp(inner_max - ceiling)
    outer_weight = jnp.exp(outer - ceiling)
    query_single = queries.astype(jnp.float32)
    outer_numerator_sum = jnp.einsum(
        "ciy,iyo->cio", query_single, cell_state_matrix, precision=FULL_ACCURACY
    )
    outer_den = jnp.einsum("lhk,hk->lh", query_single, state_n, precision=FULL_ACCURACY)
    numerator = (
        inner_weight[:, :, None] * inner_num + outer_weight[:, :, None] * outer_numerator_sum
    )
    denominator = inner_weight * inner_den + outer_weight * outer_den
    return numerator / jnp.maximum(jnp.abs(denominator), 1.0)[:, :, None]


def plain_local(
    tokens,
    w_query,
    w_key,
    w_value,
    w_outgate,
    w_gates,
    gate_bias,
    w_out,
    carry_matrix,
    carry_norm,
    carry_max,
    doc_lengths,
):
    length = tokens.shape[0]
    head_count = gate_bias.shape[1]
    query_size = w_query.shape[1] // head_count
    value_size = w_value.shape[1] // head_count
    matrices = (w_query, w_key, w_value, w_outgate)
    zero_init = tuple((jnp.zeros((length, matrix.shape[1]), jnp.float32) for matrix in matrices))
    zero_init = zero_init + (
        jnp.zeros((length, head_count), jnp.float32),
        jnp.zeros((length, head_count), jnp.float32),
    )
    column_block = lax.all_gather(tokens, "tensor", axis=1, tiled=True)
    updated = tuple(
        (jnp.dot(column_block, matrix, preferred_element_type=jnp.float32) for matrix in matrices)
    )
    input_sum = jnp.dot(column_block, w_gates[0], preferred_element_type=jnp.float32)
    forget_sum = jnp.dot(column_block, w_gates[1], preferred_element_type=jnp.float32)
    projected = updated + (input_sum, forget_sum)
    queries = projected[0].astype(jnp.bfloat16).reshape(length, head_count, query_size)
    keys = (
        (projected[1] * query_size ** (-0.5))
        .astype(jnp.bfloat16)
        .reshape(length, head_count, query_size)
    )
    value_rows = projected[2].astype(jnp.bfloat16).reshape(length, head_count, value_size)
    outgate = jax.nn.sigmoid(projected[3])
    input_pre = projected[4] + gate_bias[0][None, :]
    log_forget = jax.nn.log_sigmoid(projected[5] + gate_bias[1][None, :])
    offset = lax.axis_index("seq") * length
    positions = offset + jnp.arange(length, dtype=jnp.int32)
    segment = segment_of(doc_lengths, positions)
    segment_before = segment_of(doc_lengths, jnp.maximum(offset - 1, 0)[None])[0]
    log_decay, inner_max, inner_num, inner_den, summary = block_local(
        queries, keys, value_rows, input_pre, log_forget, segment, segment_before
    )
    start_state = (carry_matrix, carry_norm, carry_max)
    zero_heads = jnp.zeros((head_count,), jnp.float32)
    is_leader = lax.axis_index("seq") == 0

    def relay(iteration, current):
        leaving = combine(current + (zero_heads, zero_heads), summary)[:3]
        arrived = plain_shifted(leaving, "seq", 1)
        return tuple(
            (
                jnp.where(is_leader, initial, received)
                for initial, received in zip(start_state, arrived)
            )
        )

    incoming = lax.fori_loop(0, lax.axis_size("seq") - 1, relay, start_state)
    mixed_heads = block_output(
        queries, log_decay, inner_max, inner_num, inner_den, segment, segment_before, incoming
    )
    hidden = (outgate * mixed_heads.reshape(length, head_count * value_size)).astype(jnp.bfloat16)
    partial_value = jnp.dot(hidden, w_out, preferred_element_type=jnp.float32)
    summed = lax.psum_scatter(
        partial_value.astype(jnp.bfloat16), "tensor", scatter_dimension=1, tiled=True
    ).astype(jnp.float32)
    return (tokens.astype(jnp.float32) + summed).astype(jnp.bfloat16)


def solution(mesh):
    fast = mesh.shape["tensor"] == 4 and mesh.shape["seq"] == 8
    return jax.shard_map(
        local if fast else plain_local,
        mesh=mesh,
        in_specs=(
            P("seq", "tensor"),
            P(None, "tensor"),
            P(None, "tensor"),
            P(None, "tensor"),
            P(None, "tensor"),
            P(None, None, "tensor"),
            P(None, "tensor"),
            P("tensor", None),
            P("tensor", None, None),
            P("tensor", None),
            P("tensor"),
            P(),
        ),
        out_specs=P("seq", "tensor"),
        check_vma=False,
    )
```

```python
import functools

import jax
import jax.numpy as jnp
from jax import lax
from jax.experimental import pallas as pl
from jax.experimental.pallas import tpu as pltpu
from jax.sharding import PartitionSpec as P

BF = jnp.bfloat16
F32 = jnp.float32
MIB = 1024 * 1024
TOKEN_CHUNKS = ((256, 256), (512,))
OUT_CHUNKS = (256, 256, 256, 256)


def params(mib):
    return pltpu.CompilerParams(vmem_limit_bytes=mib * MIB)


def cost(flops, moved):
    return pl.CostEstimate(flops=int(flops), bytes_accessed=int(moved), transcendentals=0)


def swapped(x, axis, mask):
    size = lax.axis_size(axis)
    return lax.ppermute(x, axis, [(i, i ^ mask) for i in range(size)])


def shifted(x, axis, by):
    size = lax.axis_size(axis)
    return lax.ppermute(x, axis, [(i, (i + by) % size) for i in range(size)])


def after(first, *others):
    out = lax.optimization_barrier((first,) + others)[1:]
    return out[0] if len(out) == 1 else out


SMEM_SPEC = pl.BlockSpec(memory_space=pltpu.SMEM)
VMEM_SPEC = pl.BlockSpec(memory_space=pltpu.VMEM)
HBM_SPEC = pl.BlockSpec(memory_space=pltpu.HBM)


def in_hbm(x):
    return pltpu.with_memory_space_constraint(x, pltpu.HBM)


def in_vmem(*xs):
    return [pltpu.with_memory_space_constraint(x, pltpu.VMEM) for x in xs]


def holding(kernel, held):
    return (lambda *refs: kernel(*refs[len(held) :])) if held else kernel


def split_kernel(starts, tokens, *refs):
    outs, sem = refs[:-1], refs[-1]
    copies = []
    for i, (low, out) in enumerate(zip(starts, outs)):
        source = tokens.at[:, low : low + out.shape[1]]
        copies.append(pltpu.make_async_copy(source, out, sem.at[i]))
        copies[-1].start()
    for copy in copies:
        copy.wait()


def split_tokens(tokens, starts, sizes):
    length = tokens.shape[0]
    return pl.pallas_call(
        functools.partial(split_kernel, starts),
        out_shape=tuple(pltpu.VMEM((length, c), BF) for c in sizes),
        in_specs=[HBM_SPEC],
        out_specs=(VMEM_SPEC,) * len(sizes),
        scratch_shapes=[pltpu.SemaphoreType.DMA((len(sizes),))],
        compiler_params=params(4),
        cost_estimate=cost(1e6, 1e5),
    )(in_hbm(tokens))


def across_tokens(w, x):
    return lax.dot_general(w, x, (((1,), (1,)), ((), ())), preferred_element_type=F32)


def row_start(place, share, owner, first):
    return pl.multiple_of((place ^ owner) * share + first, 128)


def copies_of(weights, targets, semaphores, at, place, share):
    result = []
    for i, (w, target) in enumerate(zip(weights, targets)):
        low, group = 0, []
        for p, (owner, first, count) in enumerate(at[i]):
            group.append(
                pltpu.make_async_copy(
                    w.at[pl.ds(row_start(place, share, owner, first), count)],
                    target.at[pl.ds(low, count)],
                    semaphores.at[i, p],
                )
            )
            low += count
        result.append(group)
    return result


def stage_kernel(xs_at, skips, ahead_at, share, summed, finishes, gated, info, *refs):
    refs = list(refs)
    take = lambda n: [refs.pop(0) for _ in range(n)]
    count_w, with_sum = len(skips), bool(summed)
    xs, ws = take(len(xs_at)), take(count_w)
    gate_w = take(1)[0] if gated else None
    sums = [take(1)[0] if i in summed else None for i in range(count_w + gated)]
    outs = take(count_w + gated)
    ahead = take(2) if ahead_at else []
    held = take(count_w)
    sems = take(1)[0]
    place = info[0]
    at = [xs_at[skip:] for skip in skips]
    now = copies_of(ws, held, sems, at, place, share)
    later = copies_of(ws, ahead, take(1)[0], [ahead_at] * 2, place, share) if ahead_at else []
    for group in now + later:
        for copy in group:
            copy.start()
    if gated:
        gates = sums[count_w][...] if with_sum else 0.0
        for (owner, first, count), x in zip(xs_at, xs):
            gates = gates + across_tokens(
                gate_w[:, pl.ds(row_start(place, share, owner, first), count)], x[...]
            )
        outs[count_w][...] = gates
    for i in range(count_w):
        for copy in now[i]:
            copy.wait()

        def body(j, _, i=i):
            columns = pl.ds(pl.multiple_of(j * 256, 256), 256)
            total = None if sums[i] is None else sums[i][:, columns]
            low = 0
            for (_, _, count), x in zip(at[i], xs[skips[i] :]):
                part = jnp.dot(
                    x[...], held[i][low : low + count, columns], preferred_element_type=F32
                )
                total = part if total is None else total + part
                low += count
            outs[i][:, columns] = finishes[i](total).astype(outs[i].dtype)
            return 0

        lax.fori_loop(0, outs[i].shape[1] // 256, body, 0)
    for group in later:
        for copy in group:
            copy.wait()


def unchanged(x):
    return x


def stage(info, xs, xs_at, weights, share, gate_w=None, sums=None, ahead_at=None, finishes=None, held=(), skips=None):
    length = xs[0].shape[0]
    count = sum(c for _, _, c in xs_at)
    gated = int(gate_w is not None)
    kinds = [F32] * len(weights) if finishes is None else [k for _, k in finishes]
    calls = [unchanged] * len(weights) if finishes is None else [f for f, _ in finishes]
    shapes = [pltpu.VMEM((length, w.shape[1]), k) for w, k in zip(weights, kinds)]
    if gated:
        shapes.append(pltpu.VMEM((gate_w.shape[0], length), F32))
    scratch = [pltpu.VMEM((count, w.shape[1]), BF) for w in weights]
    scratch.append(pltpu.SemaphoreType.DMA((len(weights), len(xs_at))))
    if ahead_at:
        rows = sum(c for _, _, c in ahead_at)
        shapes += [pltpu.VMEM((rows, w.shape[1]), BF) for w in weights[:2]]
        scratch.append(pltpu.SemaphoreType.DMA((2, len(ahead_at))))
    operands = [*in_vmem(*held), info, *in_vmem(*xs), *[in_hbm(w) for w in weights]]
    specs = [VMEM_SPEC] * len(held) + [SMEM_SPEC] + [VMEM_SPEC] * len(xs) + [HBM_SPEC] * len(weights)
    if gated:
        operands.append(gate_w)
        specs.append(VMEM_SPEC)
    aliases, summed = {}, ()
    if sums is not None:
        summed = tuple(i for i, x in enumerate(sums) if x is not None)
        if finishes is None:
            aliases = {len(operands) + i: i for i in range(len(sums))}
        operands += in_vmem(*[x for x in sums if x is not None])
        specs += [VMEM_SPEC] * len(summed)
    return pl.pallas_call(
        holding(
            functools.partial(
                stage_kernel, xs_at, skips or [0] * len(weights), ahead_at, share, summed, calls,
                gated,
            ),
            held,
        ),
        out_shape=tuple(shapes),
        in_specs=specs,
        out_specs=(VMEM_SPEC,) * len(shapes),
        scratch_shapes=scratch,
        input_output_aliases=aliases,
        compiler_params=params(24),
        cost_estimate=cost(1e6, 1e5),
    )(*operands)


def segments(docs, positions):
    total = jnp.zeros_like(positions)
    bound = jnp.int32(0)
    for j in range(docs.shape[0] - 1):
        bound = bound + docs[j]
        total = total + (positions >= bound).astype(jnp.int32)
    return total


def gate_rows(both, offset, docs, bias):
    heads, length = both.shape[0] // 2, both.shape[1]
    row = lax.broadcasted_iota(jnp.int32, (heads, length), 0)
    lane = lax.broadcasted_iota(jnp.int32, (heads, length), 1)
    input_bias = jnp.zeros((heads, length), F32)
    forget_bias = jnp.zeros((heads, length), F32)
    for h in range(heads):
        input_bias = jnp.where(row == h, bias[0, h], input_bias)
        forget_bias = jnp.where(row == h, bias[1, h], forget_bias)
    input_pre = both[:heads] + input_bias
    forget = both[heads:] + forget_bias
    decay = jnp.minimum(forget, 0.0) - jnp.log1p(jnp.exp(-jnp.abs(forget)))
    step = 1
    while step < length:
        decay = decay + jnp.where(lane >= step, pltpu.roll(decay, step, 1), 0.0)
        step *= 2
    u = input_pre - decay
    segment = segments(docs, lane + offset)
    last = segments(docs, lane * 0 + (offset + length - 1))
    open_rows = segment == last
    top = jnp.max(jnp.where(open_rows, u, -jnp.inf), axis=1, keepdims=True)
    weight = jnp.where(open_rows, jnp.exp(u - top), 0.0)
    total = decay[:, length - 1 : length]
    narrow = lax.broadcasted_iota(jnp.int32, (heads, 128), 1)
    stats = jnp.where(narrow == 0, total + top, jnp.where(narrow == 1, total, 0.0))
    return u, weight, stats


def summary_kernel(xs_at, share, heads, info, docs, bias, *refs):
    xs = refs[: len(xs_at)]
    key_w, value_w, gate_w, key_sum, value_sum, gate_sum = refs[len(xs_at) : len(xs_at) + 6]
    key_out, value_out, keep_out, send_out, small_out, u_out, state = refs[len(xs_at) + 6 :]
    place, side, offset = info[0], info[1], info[2]
    size, wide = state.shape
    gates = gate_sum[...]
    for (owner, first, count), x in zip(xs_at, xs):
        gates = gates + across_tokens(
            gate_w[:, pl.ds(row_start(place, share, owner, first), count)], x[...]
        )
    u, weight, stats = gate_rows(gates, offset, docs, bias)
    u_out[...] = u
    small_out[:, size:] = stats
    spare = jnp.zeros((128 - weight.shape[0], weight.shape[1]), F32)
    columns = jnp.concatenate([weight, spare], axis=0).T
    half = size // 2
    for h in range(heads):
        key_at, value_at = slice(h * size, (h + 1) * size), slice(h * wide, (h + 1) * wide)
        key, value, low = key_sum[:, key_at], value_sum[:, value_at], 0
        for x in xs:
            count = x.shape[1]
            rows = slice(low, low + count)
            key = key + jnp.dot(x[...], key_w[rows, key_at], preferred_element_type=F32)
            value = value + jnp.dot(x[...], value_w[rows, value_at], preferred_element_type=F32)
            low += count
        key = (key * size ** (-0.5)).astype(BF)
        value = value.astype(BF)
        key_out[:, key_at] = key
        value_out[:, value_at] = value
        scaled = (columns[:, h : h + 1] * key.astype(F32)).astype(BF)
        small_out[h : h + 1, :size] = jnp.sum(scaled.astype(F32), axis=0, keepdims=True)
        state[...] = lax.dot_general(
            scaled, value, (((0,), (0,)), ((), ())), preferred_element_type=F32
        )
        keep_out[h] = state[pl.ds(pl.multiple_of(side * half, half), half)].astype(BF)
        send_out[h] = state[pl.ds(pl.multiple_of((1 - side) * half, half), half)].astype(BF)


def block_summary(
    info, docs, bias, xs, xs_at, key_w, value_w, gate_w, key_sum, value_sum, gates, share, heads
):
    length = xs[0].shape[0]
    size, wide = key_w.shape[1] // heads, value_w.shape[1] // heads
    return pl.pallas_call(
        functools.partial(summary_kernel, xs_at, share, heads),
        out_shape=(
            pltpu.VMEM((length, heads * size), BF),
            pltpu.VMEM((length, heads * wide), BF),
            pltpu.VMEM((heads, size // 2, wide), BF),
            pltpu.VMEM((heads, size // 2, wide), BF),
            pltpu.VMEM((heads, size + 128), F32),
            pltpu.VMEM((heads, length), F32),
        ),
        in_specs=[SMEM_SPEC] * 3 + [VMEM_SPEC] * (len(xs) + 6),
        out_specs=(VMEM_SPEC,) * 6,
        scratch_shapes=[pltpu.VMEM((size, wide), F32)],
        compiler_params=params(16),
        cost_estimate=cost(4e9, 4e6),
    )(info, docs, bias, *in_vmem(*xs, key_w, value_w), gate_w, *in_vmem(key_sum, value_sum, gates))


def reset_of(docs, index, length):
    first = jnp.maximum(index * length - 1, 0)
    return segments(docs, (index + 1) * length - 1) != segments(docs, first)


def pair_scales(info, docs, length, size, own, other):
    even = info[1] == 0
    first = info[2] // length - info[1]
    m_own, g_own = own[:, size : size + 1], own[:, size + 1 : size + 2]
    m_other, g_other = other[:, size : size + 1], other[:, size + 1 : size + 2]
    m_even, g_even = jnp.where(even, m_own, m_other), jnp.where(even, g_own, g_other)
    m_odd, g_odd = jnp.where(even, m_other, m_own), jnp.where(even, g_other, g_own)
    reset_odd = reset_of(docs, first + 1, length)
    m_pair = jnp.maximum(jnp.where(reset_odd, -jnp.inf, m_even + g_odd), m_odd)
    pair_even = jnp.where(reset_odd, 0.0, jnp.exp(jnp.minimum(m_even + g_odd - m_pair, 0.0)))
    pair_odd = jnp.exp(m_odd - m_pair)
    weights = jnp.where(even, pair_even, pair_odd), jnp.where(even, pair_odd, pair_even)
    return m_even, g_even, g_odd, m_pair, weights


def pair_kernel(length, info, docs, own, other, kept, got, state_out, small_out):
    heads = own.shape[0]
    size = own.shape[1] - 128
    _, g_even, g_odd, m_pair, (w_own, w_other) = pair_scales(
        info, docs, length, size, own[...], other[...]
    )
    small_out[:, :size] = w_own * own[:, :size] + w_other * other[:, :size]
    lane = lax.broadcasted_iota(jnp.int32, (heads, 128), 1)
    small_out[:, size:] = jnp.where(
        lane == 0, m_pair, jnp.where(lane == 1, g_even + g_odd, 0.0)
    )
    for h in range(heads):
        at = slice(h, h + 1)
        state = w_own[at] * kept[h].astype(F32) + w_other[at] * got[h].astype(F32)
        state_out[h] = state.astype(BF)


def pair_summary(info, docs, small, small_other, kept, got, length, held):
    return pl.pallas_call(
        holding(functools.partial(pair_kernel, length), held),
        out_shape=(pltpu.VMEM(kept.shape, BF), pltpu.VMEM(small.shape, F32)),
        in_specs=[VMEM_SPEC] * len(held) + [SMEM_SPEC] * 2 + [VMEM_SPEC] * 4,
        out_specs=(VMEM_SPEC,) * 2,
        compiler_params=params(4),
        cost_estimate=cost(1e6, 1e5),
    )(*in_vmem(*held), info, docs, *in_vmem(small, small_other, kept, got))


def incoming_kernel(length, reach, info, docs, own, other, kept, got, *refs):
    smalls, states = refs[:reach], refs[reach : 2 * reach]
    carry, carry_norm, carry_max = refs[2 * reach : 2 * reach + 3]
    own_out, other_out, norm_out, top_out = refs[2 * reach + 3 :]
    heads = own.shape[0]
    size = own.shape[1] - 128
    side = info[1]
    even = side == 0
    first = info[2] // length - side
    m_even, g_even, _, _, _ = pair_scales(info, docs, length, size, own[...], other[...])
    reset_even = reset_of(docs, first, length)
    expos = []
    passed = jnp.zeros((heads, 1), F32)
    unbroken = jnp.bool_(True)
    for k in range(1, reach + 1):
        there = first >= 2 * k
        index = jnp.maximum(first - 2 * k, 0)
        m_k, g_k = smalls[k - 1][:, size : size + 1], smalls[k - 1][:, size + 1 : size + 2]
        expos.append(jnp.where(there & unbroken, m_k + passed, -jnp.inf))
        passed = passed + jnp.where(there, g_k, 0.0)
        broken = reset_of(docs, index, length) | reset_of(docs, index + 1, length)
        unbroken = unbroken & ~(there & broken)
    in_reach = (first <= 2 * reach) & unbroken
    expos.append(jnp.where(in_reach, carry_max[...] + passed, -jnp.inf))
    top_even = functools.reduce(jnp.maximum, expos)
    expos_odd = [jnp.where(reset_even, -jnp.inf, e + g_even) for e in expos]
    top_odd = functools.reduce(jnp.maximum, expos_odd, m_even)
    w_even = [jnp.exp(e - top_even) for e in expos]
    w_odd = [jnp.exp(e - top_odd) for e in expos_odd]
    direct = jnp.exp(m_even - top_odd)
    w_own = [jnp.where(even, a, b) for a, b in zip(w_even, w_odd)]
    w_other = [jnp.where(even, b, a) for a, b in zip(w_even, w_odd)]
    direct_own = jnp.where(even, 0.0, direct)
    direct_other = jnp.where(even, direct, 0.0)
    top_out[...] = jnp.where(even, top_even, top_odd) + jnp.zeros((heads, 128), F32)
    norm = direct_own * jnp.where(even, own[:, :size], other[:, :size])
    norm = norm + w_own[reach] * carry_norm[...]
    for k in range(reach):
        norm = norm + w_own[k] * smalls[k][:, :size]
    norm_out[...] = norm
    for h in range(heads):
        at = slice(h, h + 1)
        here = jnp.where(even, kept[h].astype(F32), got[h].astype(F32))
        base = carry[h]
        mine = w_own[reach][at] * base + direct_own[at] * here
        theirs = w_other[reach][at] * base + direct_other[at] * here
        for k in range(reach):
            state = states[k][h].astype(F32)
            mine = mine + w_own[k][at] * state
            theirs = theirs + w_other[k][at] * state
        own_out[h] = mine.astype(BF)
        other_out[h] = theirs.astype(BF)


def carry_kernel(info, carry, out, sem):
    half = out.shape[1]
    rows = pl.ds(pl.multiple_of(info[1] * half, half), half)
    copy = pltpu.make_async_copy(carry.at[:, rows], out, sem)
    copy.start()
    copy.wait()


def carry_half(info, carry, held):
    heads, size, wide = carry.shape
    return pl.pallas_call(
        holding(carry_kernel, held),
        out_shape=pltpu.VMEM((heads, size // 2, wide), F32),
        in_specs=[VMEM_SPEC] * len(held) + [SMEM_SPEC, HBM_SPEC],
        out_specs=VMEM_SPEC,
        scratch_shapes=[pltpu.SemaphoreType.DMA],
        compiler_params=params(4),
        cost_estimate=cost(1e6, 1e5),
    )(*in_vmem(*held), info, in_hbm(carry))


def incoming_state(
    info, docs, small, small_other, kept, got, smalls, states, carry, carry_norm, carry_max, length,
    held,
):
    heads = small.shape[0]
    return pl.pallas_call(
        holding(functools.partial(incoming_kernel, length, len(smalls)), held),
        out_shape=(
            pltpu.VMEM(kept.shape, BF),
            pltpu.VMEM(kept.shape, BF),
            pltpu.VMEM(carry_norm.shape, F32),
            pltpu.VMEM((heads, 128), F32),
        ),
        in_specs=[VMEM_SPEC] * len(held)
        + [SMEM_SPEC] * 2
        + [VMEM_SPEC] * (7 + 2 * len(smalls)),
        out_specs=(VMEM_SPEC,) * 4,
        compiler_params=params(6),
        cost_estimate=cost(1e6, 1e5),
    )(
        *in_vmem(*held), info, docs,
        *in_vmem(small, small_other, kept, got, *smalls, *states, carry),
        carry_norm, carry_max[:, None],
    )


def inner_kernel(
    heads, info, docs, top_in, query, key, value, u, norm, gate, w_out,
    base_out, slope_out, w_here, sem,
):
    fetch = pltpu.make_async_copy(w_out, w_here, sem)
    fetch.start()
    length = query.shape[0]
    size, wide = query.shape[1] // heads, value.shape[1] // heads
    offset = info[2]
    chunk = 128
    one = jnp.zeros((chunk, 1), jnp.int32)
    before = segments(docs, one + jnp.maximum(offset - 1, 0))
    for head in range(heads):
        keys_at = slice(head * size, (head + 1) * size)
        values_at = slice(head * wide, (head + 1) * wide)
        u_row = u[head : head + 1, :]
        norm_row = norm[head : head + 1, :]
        top = top_in[head : head + 1, 0:1]
        for low in range(0, length, chunk):
            high = low + chunk
            position_t = lax.broadcasted_iota(jnp.int32, (chunk, 1), 0) + low
            position_s = lax.broadcasted_iota(jnp.int32, (1, high), 1)
            segment_t = segments(docs, position_t + offset)
            segment_s = segments(docs, position_s + offset)
            allowed = (position_s <= position_t) & (segment_s == segment_t)
            expo = jnp.where(allowed, u_row[:, :high], -jnp.inf)
            peak = jnp.max(expo, axis=1, keepdims=True)
            q = query[low:high, keys_at]
            scores = lax.dot_general(
                q, key[:high, keys_at], (((1,), (1,)), ((), ())), preferred_element_type=F32
            )
            weighted = jnp.exp(expo - peak) * scores
            num = jnp.dot(
                weighted.astype(BF), value[:high, values_at], preferred_element_type=F32
            )
            den = jnp.sum(weighted, axis=1, keepdims=True)
            carried = segment_t == before
            ceiling = jnp.where(carried, jnp.maximum(peak, top), peak)
            inner_weight = jnp.exp(peak - ceiling)
            outer_weight = jnp.where(carried, jnp.exp(jnp.minimum(top - ceiling, 0.0)), 0.0)
            outer_den = jnp.sum(q.astype(F32) * norm_row, axis=1, keepdims=True)
            full = inner_weight * den + outer_weight * outer_den
            inverse = 1.0 / jnp.maximum(jnp.abs(full), 1.0)
            g = gate[low:high, values_at]
            base_out[low:high, values_at] = g * (num * (inner_weight * inverse))
            slope_out[low:high, values_at] = g * (outer_weight * inverse)
    fetch.wait()


def inner(info, docs, top, query, key, value, u, norm, gate, w_out, heads):
    length, depth = value.shape
    return pl.pallas_call(
        functools.partial(inner_kernel, heads),
        out_shape=(
            pltpu.VMEM((length, depth), F32),
            pltpu.VMEM((length, depth), F32),
            pltpu.VMEM(w_out.shape, BF),
        ),
        in_specs=[SMEM_SPEC] * 2 + [VMEM_SPEC] * 7 + [HBM_SPEC],
        out_specs=(VMEM_SPEC,) * 3,
        scratch_shapes=[pltpu.SemaphoreType.DMA],
        compiler_params=params(12),
        cost_estimate=cost(1e6, 1e5),
    )(info, docs, *in_vmem(top, query, key, value, u, norm, gate), in_hbm(w_out))


def some_columns(info, hidden, w, out, owners, start):
    share = w.shape[1] // 4
    wide = out.shape[1] // 2
    for step, owner in enumerate(owners):
        columns = pl.ds(pl.multiple_of((info[0] ^ owner) * share + start, 128), wide)
        part = jnp.dot(hidden[...], w[:, columns], preferred_element_type=F32)
        out[:, step * wide : (step + 1) * wide] = part.astype(BF)


def hidden_kernel(heads, info, query, own, other, base, slope, w, hidden, send, state):
    half = own.shape[1]
    side = info[1]
    size, wide = 2 * half, own.shape[2]
    for h in range(heads):
        state[pl.ds(pl.multiple_of(side * half, half), half)] = own[h]
        state[pl.ds(pl.multiple_of((1 - side) * half, half), half)] = other[h]
        outer = jnp.dot(
            query[:, h * size : (h + 1) * size], state[...], preferred_element_type=F32
        )
        columns = slice(h * wide, (h + 1) * wide)
        hidden[:, columns] = (base[:, columns] + slope[:, columns] * outer).astype(BF)
    some_columns(info, hidden, w, send, (1, 3), 0)


def hidden_and_first(info, query, own, other, base, slope, w_here, wide, heads):
    length, depth = base.shape
    return pl.pallas_call(
        functools.partial(hidden_kernel, heads),
        out_shape=(pltpu.VMEM((length, depth), BF), pltpu.VMEM((length, 2 * wide), BF)),
        in_specs=[SMEM_SPEC] + [VMEM_SPEC] * 6,
        out_specs=(VMEM_SPEC,) * 2,
        scratch_shapes=[pltpu.VMEM((2 * own.shape[1], own.shape[2]), BF)],
        compiler_params=params(12),
        cost_estimate=cost(3e9, 8e6),
    )(info, *in_vmem(query, own, other, base, slope, w_here))


def columns_kernel(start, following, info, hidden, w, keep, *send):
    if send:
        some_columns(info, hidden, w, send[0], (1, 3), following)
    some_columns(info, hidden, w, keep, (0, 2), start)


def next_columns(info, hidden, w_here, start, wide, following):
    length = hidden.shape[0]
    shapes = [pltpu.VMEM((length, 2 * wide), BF)]
    if following:
        shapes.append(pltpu.VMEM((length, 2 * following), BF))
    return pl.pallas_call(
        functools.partial(columns_kernel, start, start + wide),
        out_shape=tuple(shapes),
        in_specs=[SMEM_SPEC, VMEM_SPEC, VMEM_SPEC],
        out_specs=(VMEM_SPEC,) * len(shapes),
        compiler_params=params(12),
        cost_estimate=cost(1e6, 1e5),
    )(info, *in_vmem(hidden, w_here))


def local(
    tokens,
    w_query,
    w_key,
    w_value,
    w_outgate,
    w_gates,
    gate_bias,
    w_out,
    carry_matrix,
    carry_norm,
    carry_max,
    doc_lengths,
):
    length, share = tokens.shape
    heads = gate_bias.shape[1]
    size = w_query.shape[1] // heads
    place = lax.axis_index("tensor")
    block = lax.axis_index("seq")
    blocks = lax.axis_size("seq")
    offset = (block * length).astype(jnp.int32)
    tensor = lambda x, mask: swapped(x, "tensor", mask)
    pair = lambda x: swapped(x, "seq", 1)
    down = lambda x: shifted(x, "seq", 2)

    beside = tensor(tokens, 1)
    sizes = [c for chunks in TOKEN_CHUNKS for c in chunks]
    starts = [sum(sizes[:i]) for i in range(len(sizes))]
    first = split_tokens(tokens, starts[:1], sizes[:1])
    others = split_tokens(after(beside, tokens), starts[1:], sizes[1:])
    pieces = [*first, *others]
    source = tokens
    pieces = [(s, c, tensor(x, 2)) for s, c, x in zip(starts, sizes, pieces)]
    groups = []
    for chunks in TOKEN_CHUNKS:
        groups.append(pieces[: len(chunks)])
        pieces = pieces[len(chunks) :]
    gate_w = w_gates.transpose(0, 2, 1).reshape(2 * heads, 4 * share)

    side = (block % 2).astype(jnp.int32)
    info = jnp.stack([place, side, offset]).astype(jnp.int32)
    at = [[(o, s, c) for s, c, _ in group for o in (2, 3)] for group in groups]
    near_at = [(0, 0, share), (1, 0, share)]
    first_three = (w_key, w_value, w_query)
    sums = stage(info, [source, beside], near_at, first_three, share, gate_w)
    far = []
    for i, group in enumerate(groups):
        xs = lax.optimization_barrier((*[x for _, _, x in group], *sums))
        xs, sums = xs[: len(group)], xs[len(group) :]
        xs = [y for x in xs for y in (x, tensor(x, 1))]
        far.append(xs)
        if i < len(groups) - 1:
            last = i == len(groups) - 2
            out = stage(
                info, xs, at[i], first_three, share, gate_w, sums, at[-1] if last else None
            )
            sums = out[:4]
            if last:
                w_key_last, w_value_last = out[4:]
    keys, values, kept, sent, small, u = block_summary(
        info, doc_lengths, gate_bias, xs, at[-1], w_key_last, w_value_last, gate_w,
        sums[0], sums[1], sums[3], share, heads,
    )

    small_other = pair(small)
    got = pair(sent)
    held = (keys, values, kept)
    far_xs = after(keys, *[x for xs in far for x in xs])
    queries, *gate = stage(
        info, far_xs, sum(at, []), (w_query, w_outgate), share, None, [sums[2], None],
        finishes=((unchanged, BF), (unchanged, F32)), held=held,
        skips=[len(far_xs) - len(far[-1]), 0],
    )
    small_other, got, queries, *gate = lax.optimization_barrier(
        (small_other, got, queries, *gate)
    )
    state_pair, travel = pair_summary(
        info, doc_lengths, small, small_other, kept, got, length, (keys, values, queries)
    )
    smalls, states = [], []
    held = (keys, values, kept, got, queries)
    for step in range(blocks // 4):
        before = state_pair
        travel, state_pair = down(travel), down(state_pair)
        if step == 0:
            near_xs = after(before, source, beside)
            gate = stage(
                info, near_xs, near_at, (w_outgate,), share, None, gate,
                finishes=((jax.nn.sigmoid, F32),), held=held,
            )
            travel, state_pair, *gate = lax.optimization_barrier((travel, state_pair, *gate))
        elif step == 1:
            carry = carry_half(after(before, info), carry_matrix, (*held, *gate))
            travel, state_pair, carry = lax.optimization_barrier((travel, state_pair, carry))
        smalls.append(travel)
        states.append(state_pair)
    (gate,) = gate
    state_own, state_other, norm_in, top_own = incoming_state(
        info, doc_lengths, small, small_other, kept, got, smalls, states,
        carry, carry_norm, carry_max, length, (keys, values, queries, gate),
    )
    state_got = pair(state_other)
    base, slope, w_here = inner(
        info, doc_lengths, top_own, queries, keys, values, u, norm_in, gate, w_out, heads
    )

    hidden, send = hidden_and_first(
        info, queries, state_own, state_got, base, slope, w_here, OUT_CHUNKS[0], heads
    )
    start = 0
    leaving, arriving = [], []
    for wide, following in zip(OUT_CHUNKS, OUT_CHUNKS[1:] + (0,)):
        came = tensor(send, 1)
        now = after(leaving[max(len(leaving) - 1, 0)], hidden) if leaving else hidden
        keep, *send = next_columns(info, now, w_here, start, wide, following)
        send = send[0] if send else None
        both = keep.astype(F32) + came.astype(F32)
        leaving.append(both[:, wide:].astype(BF))
        arriving.append((start, wide, both[:, :wide], tensor(leaving[-1], 2)))
        start += wide
    out = source
    for start, wide, both, came in arriving[:-1]:
        columns = source[:, start : start + wide].astype(F32) + (both + came.astype(F32))
        out = lax.dynamic_update_slice(out, columns.astype(BF), (0, start))
    start, wide, both, came = arriving[-1]
    columns = source[:, start : start + wide].astype(F32) + (both + came.astype(F32))
    return lax.dynamic_update_slice(out, columns.astype(BF), (0, start))


FULL_ACCURACY = lax.Precision.HIGHEST


def plain_shifted(x, axis, by):
    devices = lax.axis_size(axis)
    pairs = [(i, i + by) for i in range(devices) if 0 <= i + by < devices]
    return lax.ppermute(x, axis, pairs)


def segment_of(doc_lengths, positions):
    bounds = jnp.cumsum(doc_lengths)[:-1]
    return jnp.sum((positions[:, None] >= bounds[None, :]).astype(jnp.int32), axis=1)


def combine(earlier, later):
    early_c, early_n, early_m, early_g, early_r = earlier
    late_c, late_n, late_m, late_g, late_r = later
    ceiling = jnp.maximum(early_m + late_g, late_m)
    early_weight = jnp.exp(early_m + late_g - ceiling)
    late_weight = jnp.exp(late_m - ceiling)
    reset_mask = late_r > 0.5
    merged_c = jnp.where(
        reset_mask[:, None, None],
        late_c,
        early_weight[:, None, None] * early_c + late_weight[:, None, None] * late_c,
    )
    merged_n = jnp.where(
        reset_mask[:, None], late_n, early_weight[:, None] * early_n + late_weight[:, None] * late_n
    )
    merged_m = jnp.where(reset_mask, late_m, ceiling)
    return (merged_c, merged_n, merged_m, late_g, jnp.maximum(early_r, late_r))


def block_local(queries, keys, value_rows, input_pre, log_forget, segment, segment_before):
    length = segment.shape[0]
    log_decay = jnp.cumsum(log_forget, axis=0)
    position = jnp.arange(length)
    allowed = (position[:, None] >= position[None, :]) & (segment[:, None] == segment[None, :])
    exponent = log_decay.T[:, :, None] - log_decay.T[:, None, :] + input_pre.T[:, None, :]
    exponent = jnp.where(allowed[None], exponent, -jnp.inf)
    inner_max = jnp.max(exponent, axis=2)
    scores = jnp.einsum("lhk,mhk->hlm", queries, keys, preferred_element_type=jnp.float32)
    weighted = jnp.exp(exponent - inner_max[:, :, None]) * scores
    weighted_bf = weighted.astype(jnp.bfloat16)
    inner_num = jnp.einsum(
        "hlm,mhv->lhv", weighted_bf, value_rows, preferred_element_type=jnp.float32
    )
    inner_den = jnp.sum(weighted, axis=2).T
    in_last = segment == segment[-1]
    tail_expo = log_decay[-1][None, :] - log_decay + input_pre
    tail_expo = jnp.where(in_last[:, None], tail_expo, -jnp.inf)
    tail_max = jnp.max(tail_expo, axis=0)
    key_scaled_rows = (jnp.exp(tail_expo - tail_max[None, :])[:, :, None] * keys).astype(
        jnp.bfloat16
    )
    cell_state_matrix = jnp.einsum(
        "emn,emp->mnp", key_scaled_rows, value_rows, preferred_element_type=jnp.float32
    )
    state_n = jnp.sum(key_scaled_rows.astype(jnp.float32), axis=0)
    reset = (segment[-1] != segment_before).astype(jnp.float32) * jnp.ones_like(tail_max)
    summary = (cell_state_matrix, state_n, tail_max, log_decay[-1], reset)
    return (log_decay, inner_max.T, inner_num, inner_den, summary)


def block_output(
    queries, log_decay, inner_max, inner_num, inner_den, segment, segment_before, incoming
):
    cell_state_matrix, state_n, state_m = incoming
    outer = jnp.where((segment == segment_before)[:, None], log_decay + state_m[None, :], -jnp.inf)
    ceiling = jnp.maximum(inner_max, outer)
    inner_weight = jnp.exp(inner_max - ceiling)
    outer_weight = jnp.exp(outer - ceiling)
    query_single = queries.astype(jnp.float32)
    outer_numerator_sum = jnp.einsum(
        "ciy,iyo->cio", query_single, cell_state_matrix, precision=FULL_ACCURACY
    )
    outer_den = jnp.einsum("lhk,hk->lh", query_single, state_n, precision=FULL_ACCURACY)
    numerator = (
        inner_weight[:, :, None] * inner_num + outer_weight[:, :, None] * outer_numerator_sum
    )
    denominator = inner_weight * inner_den + outer_weight * outer_den
    return numerator / jnp.maximum(jnp.abs(denominator), 1.0)[:, :, None]


def plain_local(
    tokens,
    w_query,
    w_key,
    w_value,
    w_outgate,
    w_gates,
    gate_bias,
    w_out,
    carry_matrix,
    carry_norm,
    carry_max,
    doc_lengths,
):
    length = tokens.shape[0]
    head_count = gate_bias.shape[1]
    query_size = w_query.shape[1] // head_count
    value_size = w_value.shape[1] // head_count
    matrices = (w_query, w_key, w_value, w_outgate)
    zero_init = tuple((jnp.zeros((length, matrix.shape[1]), jnp.float32) for matrix in matrices))
    zero_init = zero_init + (
        jnp.zeros((length, head_count), jnp.float32),
        jnp.zeros((length, head_count), jnp.float32),
    )
    column_block = lax.all_gather(tokens, "tensor", axis=1, tiled=True)
    updated = tuple(
        (jnp.dot(column_block, matrix, preferred_element_type=jnp.float32) for matrix in matrices)
    )
    input_sum = jnp.dot(column_block, w_gates[0], preferred_element_type=jnp.float32)
    forget_sum = jnp.dot(column_block, w_gates[1], preferred_element_type=jnp.float32)
    projected = updated + (input_sum, forget_sum)
    queries = projected[0].astype(jnp.bfloat16).reshape(length, head_count, query_size)
    keys = (
        (projected[1] * query_size ** (-0.5))
        .astype(jnp.bfloat16)
        .reshape(length, head_count, query_size)
    )
    value_rows = projected[2].astype(jnp.bfloat16).reshape(length, head_count, value_size)
    outgate = jax.nn.sigmoid(projected[3])
    input_pre = projected[4] + gate_bias[0][None, :]
    log_forget = jax.nn.log_sigmoid(projected[5] + gate_bias[1][None, :])
    offset = lax.axis_index("seq") * length
    positions = offset + jnp.arange(length, dtype=jnp.int32)
    segment = segment_of(doc_lengths, positions)
    segment_before = segment_of(doc_lengths, jnp.maximum(offset - 1, 0)[None])[0]
    log_decay, inner_max, inner_num, inner_den, summary = block_local(
        queries, keys, value_rows, input_pre, log_forget, segment, segment_before
    )
    start_state = (carry_matrix, carry_norm, carry_max)
    zero_heads = jnp.zeros((head_count,), jnp.float32)
    is_leader = lax.axis_index("seq") == 0

    def relay(iteration, current):
        leaving = combine(current + (zero_heads, zero_heads), summary)[:3]
        arrived = plain_shifted(leaving, "seq", 1)
        return tuple(
            (
                jnp.where(is_leader, initial, received)
                for initial, received in zip(start_state, arrived)
            )
        )

    incoming = lax.fori_loop(0, lax.axis_size("seq") - 1, relay, start_state)
    mixed_heads = block_output(
        queries, log_decay, inner_max, inner_num, inner_den, segment, segment_before, incoming
    )
    hidden = (outgate * mixed_heads.reshape(length, head_count * value_size)).astype(jnp.bfloat16)
    partial_value = jnp.dot(hidden, w_out, preferred_element_type=jnp.float32)
    summed = lax.psum_scatter(
        partial_value.astype(jnp.bfloat16), "tensor", scatter_dimension=1, tiled=True
    ).astype(jnp.float32)
    return (tokens.astype(jnp.float32) + summed).astype(jnp.bfloat16)


def solution(mesh):
    fast = mesh.shape["tensor"] == 4 and mesh.shape["seq"] == 8
    return jax.shard_map(
        local if fast else plain_local,
        mesh=mesh,
        in_specs=(
            P("seq", "tensor"),
            P(None, "tensor"),
            P(None, "tensor"),
            P(None, "tensor"),
            P(None, "tensor"),
            P(None, None, "tensor"),
            P(None, "tensor"),
            P("tensor", None),
            P("tensor", None, None),
            P("tensor", None),
            P("tensor"),
            P(),
        ),
        out_specs=P("seq", "tensor"),
        check_vma=False,
    )
```

```python
import functools

import jax
import jax.numpy as jnp
from jax import lax
from jax.experimental import pallas as pl
from jax.experimental.pallas import tpu as pltpu
from jax.sharding import PartitionSpec as P

BF = jnp.bfloat16
F32 = jnp.float32
MIB = 1024 * 1024
TOKEN_CHUNKS = ((256, 256), (512,))
OUT_CHUNKS = (256, 256, 256, 256)


def params(mib):
    return pltpu.CompilerParams(vmem_limit_bytes=mib * MIB)


def cost(flops, moved):
    return pl.CostEstimate(flops=int(flops), bytes_accessed=int(moved), transcendentals=0)


def swapped(x, axis, mask):
    size = lax.axis_size(axis)
    return lax.ppermute(x, axis, [(i, i ^ mask) for i in range(size)])


def shifted(x, axis, by):
    size = lax.axis_size(axis)
    return lax.ppermute(x, axis, [(i, (i + by) % size) for i in range(size)])


def after(first, *others):
    out = lax.optimization_barrier((first,) + others)[1:]
    return out[0] if len(out) == 1 else out


SMEM_SPEC = pl.BlockSpec(memory_space=pltpu.SMEM)
VMEM_SPEC = pl.BlockSpec(memory_space=pltpu.VMEM)
HBM_SPEC = pl.BlockSpec(memory_space=pltpu.HBM)


def in_hbm(x):
    return pltpu.with_memory_space_constraint(x, pltpu.HBM)


def in_vmem(*xs):
    return [pltpu.with_memory_space_constraint(x, pltpu.VMEM) for x in xs]


def holding(kernel, held):
    return (lambda *refs: kernel(*refs[len(held) :])) if held else kernel


def split_kernel(starts, tokens, *refs):
    outs, sem = refs[:-1], refs[-1]
    copies = []
    for i, (low, out) in enumerate(zip(starts, outs)):
        source = tokens.at[:, low : low + out.shape[1]]
        copies.append(pltpu.make_async_copy(source, out, sem.at[i]))
        copies[-1].start()
    for copy in copies:
        copy.wait()


def split_tokens(tokens, starts, sizes):
    length = tokens.shape[0]
    return pl.pallas_call(
        functools.partial(split_kernel, starts),
        out_shape=tuple(pltpu.VMEM((length, c), BF) for c in sizes),
        in_specs=[HBM_SPEC],
        out_specs=(VMEM_SPEC,) * len(sizes),
        scratch_shapes=[pltpu.SemaphoreType.DMA((len(sizes),))],
        compiler_params=params(4),
        cost_estimate=cost(1e6, 1e5),
    )(in_hbm(tokens))


def across_tokens(w, x):
    return lax.dot_general(w, x, (((1,), (1,)), ((), ())), preferred_element_type=F32)


def row_start(place, share, owner, first):
    return pl.multiple_of((place ^ owner) * share + first, 128)


def copies_of(weights, targets, semaphores, at, place, share):
    result = []
    for i, (w, target) in enumerate(zip(weights, targets)):
        low, group = 0, []
        for p, (owner, first, count) in enumerate(at[i]):
            group.append(
                pltpu.make_async_copy(
                    w.at[pl.ds(row_start(place, share, owner, first), count)],
                    target.at[pl.ds(low, count)],
                    semaphores.at[i, p],
                )
            )
            low += count
        result.append(group)
    return result


def stage_kernel(xs_at, skips, ahead_at, share, summed, finishes, gated, info, *refs):
    refs = list(refs)
    take = lambda n: [refs.pop(0) for _ in range(n)]
    count_w = len(skips)
    xs, ws = take(len(xs_at)), take(count_w)
    gate_w = take(1)[0] if gated else None
    sums = [take(1)[0] if i in summed else None for i in range(count_w + gated)]
    outs = take(count_w + gated)
    ahead = take(2) if ahead_at else []
    held = take(count_w)
    sems = take(1)[0]
    place = info[0]
    at = [xs_at[skip:] for skip in skips]
    now = copies_of(ws, held, sems, at, place, share)
    later = copies_of(ws, ahead, take(1)[0], [ahead_at] * 2, place, share) if ahead_at else []
    for group in now + later:
        for copy in group:
            copy.start()
    if gated:
        gates = 0.0 if sums[count_w] is None else sums[count_w][...]
        for (owner, first, count), x in zip(xs_at, xs):
            gates = gates + across_tokens(
                gate_w[:, pl.ds(row_start(place, share, owner, first), count)], x[...]
            )
        outs[count_w][...] = gates
    for i in range(count_w):
        for copy in now[i]:
            copy.wait()

        def body(j, _, i=i):
            columns = pl.ds(pl.multiple_of(j * 256, 256), 256)
            total = None if sums[i] is None else sums[i][:, columns]
            low = 0
            for (_, _, count), x in zip(at[i], xs[skips[i] :]):
                part = jnp.dot(
                    x[...], held[i][low : low + count, columns], preferred_element_type=F32
                )
                total = part if total is None else total + part
                low += count
            outs[i][:, columns] = finishes[i](total).astype(outs[i].dtype)
            return 0

        lax.fori_loop(0, outs[i].shape[1] // 256, body, 0)
    for group in later:
        for copy in group:
            copy.wait()


def unchanged(x):
    return x


def twin_kernel(at, share, info, x, key_w, value_w, gate_w, *refs):
    owner, first, count = at
    for w, total, out in zip((key_w, value_w), refs[:2], refs[3:5]):
        for low in range(0, out.shape[1], 512):
            columns = slice(low, low + 512)
            part = jnp.dot(x[...], w[:count, columns], preferred_element_type=F32)
            out[:, columns] = total[:, columns] + part
    rows = gate_w[:, pl.ds(row_start(info[0], share, owner, first), count)]
    refs[5][...] = refs[2][...] + across_tokens(rows, x[...])


def twin_stage(info, x, at, key_w, value_w, gate_w, sums, share):
    return pl.pallas_call(
        functools.partial(twin_kernel, at, share),
        out_shape=tuple(pltpu.VMEM(y.shape, F32) for y in sums),
        in_specs=[SMEM_SPEC] + [VMEM_SPEC] * 7,
        out_specs=(VMEM_SPEC,) * 3,
        input_output_aliases={5 + i: i for i in range(3)},
        compiler_params=params(8),
        cost_estimate=cost(1e6, 1e5),
    )(info, *in_vmem(x, key_w, value_w), gate_w, *in_vmem(*sums))


def stage(info, xs, xs_at, weights, share, gate_w=None, sums=None, ahead_at=None, finishes=None, held=(), skips=None):
    length = xs[0].shape[0]
    count = sum(c for _, _, c in xs_at)
    gated = int(gate_w is not None)
    kinds = [F32] * len(weights) if finishes is None else [k for _, k in finishes]
    calls = [unchanged] * len(weights) if finishes is None else [f for f, _ in finishes]
    shapes = [pltpu.VMEM((length, w.shape[1]), k) for w, k in zip(weights, kinds)]
    if gated:
        shapes.append(pltpu.VMEM((gate_w.shape[0], length), F32))
    scratch = [pltpu.VMEM((count, w.shape[1]), BF) for w in weights]
    scratch.append(pltpu.SemaphoreType.DMA((len(weights), len(xs_at))))
    if ahead_at:
        rows = sum(c for _, _, c in ahead_at)
        shapes += [pltpu.VMEM((rows, w.shape[1]), BF) for w in weights[:2]]
        scratch.append(pltpu.SemaphoreType.DMA((2, len(ahead_at))))
    operands = [*in_vmem(*held), info, *in_vmem(*xs), *[in_hbm(w) for w in weights]]
    specs = [VMEM_SPEC] * len(held) + [SMEM_SPEC] + [VMEM_SPEC] * len(xs) + [HBM_SPEC] * len(weights)
    if gated:
        operands.append(gate_w)
        specs.append(VMEM_SPEC)
    aliases, summed = {}, ()
    if sums is not None:
        summed = tuple(i for i, x in enumerate(sums) if x is not None)
        if finishes is None:
            aliases = {len(operands) + n: i for n, i in enumerate(summed)}
        operands += in_vmem(*[x for x in sums if x is not None])
        specs += [VMEM_SPEC] * len(summed)
    return pl.pallas_call(
        holding(
            functools.partial(
                stage_kernel, xs_at, skips or [0] * len(weights), ahead_at, share, summed, calls,
                gated,
            ),
            held,
        ),
        out_shape=tuple(shapes),
        in_specs=specs,
        out_specs=(VMEM_SPEC,) * len(shapes),
        scratch_shapes=scratch,
        input_output_aliases=aliases,
        compiler_params=params(24),
        cost_estimate=cost(1e6, 1e5),
    )(*operands)


def segments(docs, positions):
    total = jnp.zeros_like(positions)
    bound = jnp.int32(0)
    for j in range(docs.shape[0] - 1):
        bound = bound + docs[j]
        total = total + (positions >= bound).astype(jnp.int32)
    return total


def gate_rows(both, offset, docs, bias):
    heads, length = both.shape[0] // 2, both.shape[1]
    row = lax.broadcasted_iota(jnp.int32, (heads, length), 0)
    lane = lax.broadcasted_iota(jnp.int32, (heads, length), 1)
    input_bias = jnp.zeros((heads, length), F32)
    forget_bias = jnp.zeros((heads, length), F32)
    for h in range(heads):
        input_bias = jnp.where(row == h, bias[0, h], input_bias)
        forget_bias = jnp.where(row == h, bias[1, h], forget_bias)
    input_pre = both[:heads] + input_bias
    forget = both[heads:] + forget_bias
    decay = jnp.minimum(forget, 0.0) - jnp.log1p(jnp.exp(-jnp.abs(forget)))
    step = 1
    while step < length:
        decay = decay + jnp.where(lane >= step, pltpu.roll(decay, step, 1), 0.0)
        step *= 2
    u = input_pre - decay
    segment = segments(docs, lane + offset)
    last = segments(docs, lane * 0 + (offset + length - 1))
    open_rows = segment == last
    top = jnp.max(jnp.where(open_rows, u, -jnp.inf), axis=1, keepdims=True)
    weight = jnp.where(open_rows, jnp.exp(u - top), 0.0)
    total = decay[:, length - 1 : length]
    narrow = lax.broadcasted_iota(jnp.int32, (heads, 128), 1)
    stats = jnp.where(narrow == 0, total + top, jnp.where(narrow == 1, total, 0.0))
    return u, weight, stats


def summary_kernel(xs_at, skip, share, heads, info, docs, bias, *refs):
    xs = refs[: len(xs_at)]
    key_w, value_w, gate_w, key_sum, value_sum, gate_sum = refs[len(xs_at) : len(xs_at) + 6]
    key_out, value_out, keep_out, send_out, small_out, u_out, state = refs[len(xs_at) + 6 :]
    place, side, offset = info[0], info[1], info[2]
    size, wide = state.shape
    gates = gate_sum[...]
    for (owner, first, count), x in zip(xs_at, xs):
        gates = gates + across_tokens(
            gate_w[:, pl.ds(row_start(place, share, owner, first), count)], x[...]
        )
    u, weight, stats = gate_rows(gates, offset, docs, bias)
    u_out[...] = u
    small_out[:, size:] = stats
    spare = jnp.zeros((128 - weight.shape[0], weight.shape[1]), F32)
    columns = jnp.concatenate([weight, spare], axis=0).T
    half = size // 2
    for h in range(heads):
        key_at, value_at = slice(h * size, (h + 1) * size), slice(h * wide, (h + 1) * wide)
        key, value, low = key_sum[:, key_at], value_sum[:, value_at], skip
        for x in xs:
            count = x.shape[1]
            rows = slice(low, low + count)
            key = key + jnp.dot(x[...], key_w[rows, key_at], preferred_element_type=F32)
            value = value + jnp.dot(x[...], value_w[rows, value_at], preferred_element_type=F32)
            low += count
        key = (key * size ** (-0.5)).astype(BF)
        value = value.astype(BF)
        key_out[:, key_at] = key
        value_out[:, value_at] = value
        scaled = (columns[:, h : h + 1] * key.astype(F32)).astype(BF)
        small_out[h : h + 1, :size] = jnp.sum(scaled.astype(F32), axis=0, keepdims=True)
        state[...] = lax.dot_general(
            scaled, value, (((0,), (0,)), ((), ())), preferred_element_type=F32
        )
        keep_out[h] = state[pl.ds(pl.multiple_of(side * half, half), half)].astype(BF)
        send_out[h] = state[pl.ds(pl.multiple_of((1 - side) * half, half), half)].astype(BF)


def block_summary(
    info, docs, bias, xs, xs_at, skip, key_w, value_w, gate_w, key_sum, value_sum, gates, share,
    heads,
):
    length = xs[0].shape[0]
    size, wide = key_w.shape[1] // heads, value_w.shape[1] // heads
    return pl.pallas_call(
        functools.partial(summary_kernel, xs_at, skip, share, heads),
        out_shape=(
            pltpu.VMEM((length, heads * size), BF),
            pltpu.VMEM((length, heads * wide), BF),
            pltpu.VMEM((heads, size // 2, wide), BF),
            pltpu.VMEM((heads, size // 2, wide), BF),
            pltpu.VMEM((heads, size + 128), F32),
            pltpu.VMEM((heads, length), F32),
        ),
        in_specs=[SMEM_SPEC] * 3 + [VMEM_SPEC] * (len(xs) + 6),
        out_specs=(VMEM_SPEC,) * 6,
        scratch_shapes=[pltpu.VMEM((size, wide), F32)],
        compiler_params=params(16),
        cost_estimate=cost(4e9, 4e6),
    )(info, docs, bias, *in_vmem(*xs, key_w, value_w), gate_w, *in_vmem(key_sum, value_sum, gates))


def reset_of(docs, index, length):
    first = jnp.maximum(index * length - 1, 0)
    return segments(docs, (index + 1) * length - 1) != segments(docs, first)


def pair_scales(info, docs, length, size, own, other):
    even = info[1] == 0
    first = info[2] // length - info[1]
    m_own, g_own = own[:, size : size + 1], own[:, size + 1 : size + 2]
    m_other, g_other = other[:, size : size + 1], other[:, size + 1 : size + 2]
    m_even, g_even = jnp.where(even, m_own, m_other), jnp.where(even, g_own, g_other)
    m_odd, g_odd = jnp.where(even, m_other, m_own), jnp.where(even, g_other, g_own)
    reset_odd = reset_of(docs, first + 1, length)
    m_pair = jnp.maximum(jnp.where(reset_odd, -jnp.inf, m_even + g_odd), m_odd)
    pair_even = jnp.where(reset_odd, 0.0, jnp.exp(jnp.minimum(m_even + g_odd - m_pair, 0.0)))
    pair_odd = jnp.exp(m_odd - m_pair)
    weights = jnp.where(even, pair_even, pair_odd), jnp.where(even, pair_odd, pair_even)
    return m_even, g_even, g_odd, m_pair, weights


def pair_kernel(length, info, docs, own, other, kept, got, state_out, small_out):
    heads = own.shape[0]
    size = own.shape[1] - 128
    _, g_even, g_odd, m_pair, (w_own, w_other) = pair_scales(
        info, docs, length, size, own[...], other[...]
    )
    small_out[:, :size] = w_own * own[:, :size] + w_other * other[:, :size]
    lane = lax.broadcasted_iota(jnp.int32, (heads, 128), 1)
    small_out[:, size:] = jnp.where(
        lane == 0, m_pair, jnp.where(lane == 1, g_even + g_odd, 0.0)
    )
    for h in range(heads):
        at = slice(h, h + 1)
        state = w_own[at] * kept[h].astype(F32) + w_other[at] * got[h].astype(F32)
        state_out[h] = state.astype(BF)


def pair_summary(info, docs, small, small_other, kept, got, length, held):
    return pl.pallas_call(
        holding(functools.partial(pair_kernel, length), held),
        out_shape=(pltpu.VMEM(kept.shape, BF), pltpu.VMEM(small.shape, F32)),
        in_specs=[VMEM_SPEC] * len(held) + [SMEM_SPEC] * 2 + [VMEM_SPEC] * 4,
        out_specs=(VMEM_SPEC,) * 2,
        compiler_params=params(4),
        cost_estimate=cost(1e6, 1e5),
    )(*in_vmem(*held), info, docs, *in_vmem(small, small_other, kept, got))


def incoming_kernel(length, reach, info, docs, own, other, kept, got, *refs):
    smalls, states = refs[:reach], refs[reach : 2 * reach]
    carry, carry_norm, carry_max = refs[2 * reach : 2 * reach + 3]
    own_out, other_out, norm_out, top_out = refs[2 * reach + 3 :]
    heads = own.shape[0]
    size = own.shape[1] - 128
    side = info[1]
    even = side == 0
    first = info[2] // length - side
    m_even, g_even, _, _, _ = pair_scales(info, docs, length, size, own[...], other[...])
    reset_even = reset_of(docs, first, length)
    expos = []
    passed = jnp.zeros((heads, 1), F32)
    unbroken = jnp.bool_(True)
    for k in range(1, reach + 1):
        there = first >= 2 * k
        index = jnp.maximum(first - 2 * k, 0)
        m_k, g_k = smalls[k - 1][:, size : size + 1], smalls[k - 1][:, size + 1 : size + 2]
        expos.append(jnp.where(there & unbroken, m_k + passed, -jnp.inf))
        passed = passed + jnp.where(there, g_k, 0.0)
        broken = reset_of(docs, index, length) | reset_of(docs, index + 1, length)
        unbroken = unbroken & ~(there & broken)
    in_reach = (first <= 2 * reach) & unbroken
    expos.append(jnp.where(in_reach, carry_max[...] + passed, -jnp.inf))
    top_even = functools.reduce(jnp.maximum, expos)
    expos_odd = [jnp.where(reset_even, -jnp.inf, e + g_even) for e in expos]
    top_odd = functools.reduce(jnp.maximum, expos_odd, m_even)
    w_even = [jnp.exp(e - top_even) for e in expos]
    w_odd = [jnp.exp(e - top_odd) for e in expos_odd]
    direct = jnp.exp(m_even - top_odd)
    w_own = [jnp.where(even, a, b) for a, b in zip(w_even, w_odd)]
    w_other = [jnp.where(even, b, a) for a, b in zip(w_even, w_odd)]
    direct_own = jnp.where(even, 0.0, direct)
    direct_other = jnp.where(even, direct, 0.0)
    top_out[...] = jnp.where(even, top_even, top_odd) + jnp.zeros((heads, 128), F32)
    norm = direct_own * jnp.where(even, own[:, :size], other[:, :size])
    norm = norm + w_own[reach] * carry_norm[...]
    for k in range(reach):
        norm = norm + w_own[k] * smalls[k][:, :size]
    norm_out[...] = norm
    for h in range(heads):
        at = slice(h, h + 1)
        here = jnp.where(even, kept[h].astype(F32), got[h].astype(F32))
        base = carry[h]
        mine = w_own[reach][at] * base + direct_own[at] * here
        theirs = w_other[reach][at] * base + direct_other[at] * here
        for k in range(reach):
            state = states[k][h].astype(F32)
            mine = mine + w_own[k][at] * state
            theirs = theirs + w_other[k][at] * state
        own_out[h] = mine.astype(BF)
        other_out[h] = theirs.astype(BF)


def carry_kernel(info, carry, out, sem):
    half = out.shape[1]
    rows = pl.ds(pl.multiple_of(info[1] * half, half), half)
    copy = pltpu.make_async_copy(carry.at[:, rows], out, sem)
    copy.start()
    copy.wait()


def carry_half(info, carry, held):
    heads, size, wide = carry.shape
    return pl.pallas_call(
        holding(carry_kernel, held),
        out_shape=pltpu.VMEM((heads, size // 2, wide), F32),
        in_specs=[VMEM_SPEC] * len(held) + [SMEM_SPEC, HBM_SPEC],
        out_specs=VMEM_SPEC,
        scratch_shapes=[pltpu.SemaphoreType.DMA],
        compiler_params=params(4),
        cost_estimate=cost(1e6, 1e5),
    )(*in_vmem(*held), info, in_hbm(carry))


def incoming_state(
    info, docs, small, small_other, kept, got, smalls, states, carry, carry_norm, carry_max, length,
    held,
):
    heads = small.shape[0]
    return pl.pallas_call(
        holding(functools.partial(incoming_kernel, length, len(smalls)), held),
        out_shape=(
            pltpu.VMEM(kept.shape, BF),
            pltpu.VMEM(kept.shape, BF),
            pltpu.VMEM(carry_norm.shape, F32),
            pltpu.VMEM((heads, 128), F32),
        ),
        in_specs=[VMEM_SPEC] * len(held)
        + [SMEM_SPEC] * 2
        + [VMEM_SPEC] * (7 + 2 * len(smalls)),
        out_specs=(VMEM_SPEC,) * 4,
        compiler_params=params(6),
        cost_estimate=cost(1e6, 1e5),
    )(
        *in_vmem(*held), info, docs,
        *in_vmem(small, small_other, kept, got, *smalls, *states, carry),
        carry_norm, carry_max[:, None],
    )


def inner_kernel(
    heads, info, docs, top_in, query, key, value, u, norm, gate, w_out,
    base_out, slope_out, w_here, sem,
):
    fetch = pltpu.make_async_copy(w_out, w_here, sem)
    fetch.start()
    length = query.shape[0]
    size, wide = query.shape[1] // heads, value.shape[1] // heads
    offset = info[2]
    chunk = 128
    one = jnp.zeros((chunk, 1), jnp.int32)
    before = segments(docs, one + jnp.maximum(offset - 1, 0))
    for head in range(heads):
        keys_at = slice(head * size, (head + 1) * size)
        values_at = slice(head * wide, (head + 1) * wide)
        u_row = u[head : head + 1, :]
        norm_row = norm[head : head + 1, :]
        top = top_in[head : head + 1, 0:1]
        for low in range(0, length, chunk):
            high = low + chunk
            position_t = lax.broadcasted_iota(jnp.int32, (chunk, 1), 0) + low
            position_s = lax.broadcasted_iota(jnp.int32, (1, high), 1)
            segment_t = segments(docs, position_t + offset)
            segment_s = segments(docs, position_s + offset)
            allowed = (position_s <= position_t) & (segment_s == segment_t)
            expo = jnp.where(allowed, u_row[:, :high], -jnp.inf)
            peak = jnp.max(expo, axis=1, keepdims=True)
            q = query[low:high, keys_at]
            scores = lax.dot_general(
                q, key[:high, keys_at], (((1,), (1,)), ((), ())), preferred_element_type=F32
            )
            weighted = jnp.exp(expo - peak) * scores
            num = jnp.dot(
                weighted.astype(BF), value[:high, values_at], preferred_element_type=F32
            )
            den = jnp.sum(weighted, axis=1, keepdims=True)
            carried = segment_t == before
            ceiling = jnp.where(carried, jnp.maximum(peak, top), peak)
            inner_weight = jnp.exp(peak - ceiling)
            outer_weight = jnp.where(carried, jnp.exp(jnp.minimum(top - ceiling, 0.0)), 0.0)
            outer_den = jnp.sum(q.astype(F32) * norm_row, axis=1, keepdims=True)
            full = inner_weight * den + outer_weight * outer_den
            inverse = 1.0 / jnp.maximum(jnp.abs(full), 1.0)
            g = gate[low:high, values_at]
            base_out[low:high, values_at] = g * (num * (inner_weight * inverse))
            slope_out[low:high, values_at] = g * (outer_weight * inverse)
    fetch.wait()


def inner(info, docs, top, query, key, value, u, norm, gate, w_out, heads):
    length, depth = value.shape
    return pl.pallas_call(
        functools.partial(inner_kernel, heads),
        out_shape=(
            pltpu.VMEM((length, depth), F32),
            pltpu.VMEM((length, depth), F32),
            pltpu.VMEM(w_out.shape, BF),
        ),
        in_specs=[SMEM_SPEC] * 2 + [VMEM_SPEC] * 7 + [HBM_SPEC],
        out_specs=(VMEM_SPEC,) * 3,
        scratch_shapes=[pltpu.SemaphoreType.DMA],
        compiler_params=params(12),
        cost_estimate=cost(1e6, 1e5),
    )(info, docs, *in_vmem(top, query, key, value, u, norm, gate), in_hbm(w_out))


def some_columns(info, hidden, w, out, owners, start):
    share = w.shape[1] // 4
    wide = out.shape[1] // 2
    for step, owner in enumerate(owners):
        columns = pl.ds(pl.multiple_of((info[0] ^ owner) * share + start, 128), wide)
        part = jnp.dot(hidden[...], w[:, columns], preferred_element_type=F32)
        out[:, step * wide : (step + 1) * wide] = part.astype(BF)


def hidden_kernel(heads, info, query, own, other, base, slope, w, hidden, send, state):
    half = own.shape[1]
    side = info[1]
    size, wide = 2 * half, own.shape[2]
    for h in range(heads):
        state[pl.ds(pl.multiple_of(side * half, half), half)] = own[h]
        state[pl.ds(pl.multiple_of((1 - side) * half, half), half)] = other[h]
        outer = jnp.dot(
            query[:, h * size : (h + 1) * size], state[...], preferred_element_type=F32
        )
        columns = slice(h * wide, (h + 1) * wide)
        hidden[:, columns] = (base[:, columns] + slope[:, columns] * outer).astype(BF)
    some_columns(info, hidden, w, send, (1, 3), 0)


def hidden_and_first(info, query, own, other, base, slope, w_here, wide, heads):
    length, depth = base.shape
    return pl.pallas_call(
        functools.partial(hidden_kernel, heads),
        out_shape=(pltpu.VMEM((length, depth), BF), pltpu.VMEM((length, 2 * wide), BF)),
        in_specs=[SMEM_SPEC] + [VMEM_SPEC] * 6,
        out_specs=(VMEM_SPEC,) * 2,
        scratch_shapes=[pltpu.VMEM((2 * own.shape[1], own.shape[2]), BF)],
        compiler_params=params(12),
        cost_estimate=cost(3e9, 8e6),
    )(info, *in_vmem(query, own, other, base, slope, w_here))


def columns_kernel(start, following, info, hidden, w, keep, *send):
    if send:
        some_columns(info, hidden, w, send[0], (1, 3), following)
    some_columns(info, hidden, w, keep, (0, 2), start)


def next_columns(info, hidden, w_here, start, wide, following):
    length = hidden.shape[0]
    shapes = [pltpu.VMEM((length, 2 * wide), BF)]
    if following:
        shapes.append(pltpu.VMEM((length, 2 * following), BF))
    return pl.pallas_call(
        functools.partial(columns_kernel, start, start + wide),
        out_shape=tuple(shapes),
        in_specs=[SMEM_SPEC, VMEM_SPEC, VMEM_SPEC],
        out_specs=(VMEM_SPEC,) * len(shapes),
        compiler_params=params(12),
        cost_estimate=cost(1e6, 1e5),
    )(info, *in_vmem(hidden, w_here))


def local(
    tokens,
    w_query,
    w_key,
    w_value,
    w_outgate,
    w_gates,
    gate_bias,
    w_out,
    carry_matrix,
    carry_norm,
    carry_max,
    doc_lengths,
):
    length, share = tokens.shape
    heads = gate_bias.shape[1]
    size = w_query.shape[1] // heads
    place = lax.axis_index("tensor")
    block = lax.axis_index("seq")
    blocks = lax.axis_size("seq")
    offset = (block * length).astype(jnp.int32)
    tensor = lambda x, mask: swapped(x, "tensor", mask)
    pair = lambda x: swapped(x, "seq", 1)
    down = lambda x: shifted(x, "seq", 2)

    beside = tensor(tokens, 1)
    sizes = [c for chunks in TOKEN_CHUNKS for c in chunks]
    starts = [sum(sizes[:i]) for i in range(len(sizes))]
    first = split_tokens(tokens, starts[:1], sizes[:1])
    others = split_tokens(after(beside, tokens), starts[1:], sizes[1:])
    pieces = [*first, *others]
    source = tokens
    pieces = [(s, c, tensor(x, 2)) for s, c, x in zip(starts, sizes, pieces)]
    groups = []
    for chunks in TOKEN_CHUNKS:
        groups.append(pieces[: len(chunks)])
        pieces = pieces[len(chunks) :]
    gate_w = w_gates.transpose(0, 2, 1).reshape(2 * heads, 4 * share)

    side = (block % 2).astype(jnp.int32)
    info = jnp.stack([place, side, offset]).astype(jnp.int32)
    at = [[(o, s, c) for s, c, _ in group for o in (2, 3)] for group in groups]
    near_at = [(0, 0, share), (1, 0, share)]
    first_three = (w_key, w_value, w_query)
    sums = stage(info, [source, beside], near_at, first_three, share, gate_w)
    far = []
    for i, group in enumerate(groups):
        xs = lax.optimization_barrier((*[x for _, _, x in group], *sums))
        xs, sums = xs[: len(group)], xs[len(group) :]
        if i == 0:
            sums = [*sums[:3], None, sums[3]]
        xs = [y for x in xs for y in (x, tensor(x, 1))]
        far.append(xs)
        if i < len(groups) - 1:
            last = i == len(groups) - 2
            out = stage(
                info, xs, at[i], (*first_three, w_outgate), share, gate_w, sums,
                at[-1] if last else None,
            )
            sums = out[:5]
            if last:
                w_key_last, w_value_last = out[5:]
    kv_sums = twin_stage(
        info, xs[0], at[-1][0], w_key_last, w_value_last, gate_w, (*sums[:2], sums[4]), share
    )
    keys, values, kept, sent, small, u = block_summary(
        info, doc_lengths, gate_bias, xs[1:], at[-1][1:], at[-1][0][2], w_key_last, w_value_last,
        gate_w, *kv_sums, share, heads,
    )

    small_other = pair(small)
    got = pair(sent)
    held = (keys, values, kept)
    now_xs = after(keys, beside, *far[-1])
    queries, *gate = stage(
        info, now_xs, near_at[1:] + at[-1], (w_query, w_outgate), share, None, [sums[2], sums[3]],
        finishes=((unchanged, BF), (unchanged, F32)), held=held, skips=[1, 0],
    )
    small_other, got, queries, *gate = lax.optimization_barrier(
        (small_other, got, queries, *gate)
    )
    state_pair, travel = pair_summary(
        info, doc_lengths, small, small_other, kept, got, length, (keys, values, queries)
    )
    smalls, states = [], []
    held = (keys, values, kept, got, queries)
    for step in range(blocks // 4):
        before = state_pair
        travel, state_pair = down(travel), down(state_pair)
        if step == 0:
            near_xs = [after(before, source)]
            gate = stage(
                info, near_xs, near_at[:1], (w_outgate,), share, None, gate,
                finishes=((jax.nn.sigmoid, F32),), held=held,
            )
            travel, state_pair, *gate = lax.optimization_barrier((travel, state_pair, *gate))
        elif step == 1:
            carry = carry_half(after(before, info), carry_matrix, (*held, *gate))
            travel, state_pair, carry = lax.optimization_barrier((travel, state_pair, carry))
        smalls.append(travel)
        states.append(state_pair)
    (gate,) = gate
    state_own, state_other, norm_in, top_own = incoming_state(
        info, doc_lengths, small, small_other, kept, got, smalls, states,
        carry, carry_norm, carry_max, length, (keys, values, queries, gate),
    )
    state_got = pair(state_other)
    base, slope, w_here = inner(
        info, doc_lengths, top_own, queries, keys, values, u, norm_in, gate, w_out, heads
    )

    hidden, send = hidden_and_first(
        info, queries, state_own, state_got, base, slope, w_here, OUT_CHUNKS[0], heads
    )
    start = 0
    leaving, arriving = [], []
    for wide, following in zip(OUT_CHUNKS, OUT_CHUNKS[1:] + (0,)):
        came = tensor(send, 1)
        now = after(leaving[max(len(leaving) - 1, 0)], hidden) if leaving else hidden
        keep, *send = next_columns(info, now, w_here, start, wide, following)
        send = send[0] if send else None
        both = keep.astype(F32) + came.astype(F32)
        leaving.append(both[:, wide:].astype(BF))
        arriving.append((start, wide, both[:, :wide], tensor(leaving[-1], 2)))
        start += wide
    out = source
    for start, wide, both, came in arriving[:-1]:
        columns = source[:, start : start + wide].astype(F32) + (both + came.astype(F32))
        out = lax.dynamic_update_slice(out, columns.astype(BF), (0, start))
    start, wide, both, came = arriving[-1]
    columns = source[:, start : start + wide].astype(F32) + (both + came.astype(F32))
    return lax.dynamic_update_slice(out, columns.astype(BF), (0, start))


FULL_ACCURACY = lax.Precision.HIGHEST


def plain_shifted(x, axis, by):
    devices = lax.axis_size(axis)
    pairs = [(i, i + by) for i in range(devices) if 0 <= i + by < devices]
    return lax.ppermute(x, axis, pairs)


def segment_of(doc_lengths, positions):
    bounds = jnp.cumsum(doc_lengths)[:-1]
    return jnp.sum((positions[:, None] >= bounds[None, :]).astype(jnp.int32), axis=1)


def combine(earlier, later):
    early_c, early_n, early_m, early_g, early_r = earlier
    late_c, late_n, late_m, late_g, late_r = later
    ceiling = jnp.maximum(early_m + late_g, late_m)
    early_weight = jnp.exp(early_m + late_g - ceiling)
    late_weight = jnp.exp(late_m - ceiling)
    reset_mask = late_r > 0.5
    merged_c = jnp.where(
        reset_mask[:, None, None],
        late_c,
        early_weight[:, None, None] * early_c + late_weight[:, None, None] * late_c,
    )
    merged_n = jnp.where(
        reset_mask[:, None], late_n, early_weight[:, None] * early_n + late_weight[:, None] * late_n
    )
    merged_m = jnp.where(reset_mask, late_m, ceiling)
    return (merged_c, merged_n, merged_m, late_g, jnp.maximum(early_r, late_r))


def block_local(queries, keys, value_rows, input_pre, log_forget, segment, segment_before):
    length = segment.shape[0]
    log_decay = jnp.cumsum(log_forget, axis=0)
    position = jnp.arange(length)
    allowed = (position[:, None] >= position[None, :]) & (segment[:, None] == segment[None, :])
    exponent = log_decay.T[:, :, None] - log_decay.T[:, None, :] + input_pre.T[:, None, :]
    exponent = jnp.where(allowed[None], exponent, -jnp.inf)
    inner_max = jnp.max(exponent, axis=2)
    scores = jnp.einsum("lhk,mhk->hlm", queries, keys, preferred_element_type=jnp.float32)
    weighted = jnp.exp(exponent - inner_max[:, :, None]) * scores
    weighted_bf = weighted.astype(jnp.bfloat16)
    inner_num = jnp.einsum(
        "hlm,mhv->lhv", weighted_bf, value_rows, preferred_element_type=jnp.float32
    )
    inner_den = jnp.sum(weighted, axis=2).T
    in_last = segment == segment[-1]
    tail_expo = log_decay[-1][None, :] - log_decay + input_pre
    tail_expo = jnp.where(in_last[:, None], tail_expo, -jnp.inf)
    tail_max = jnp.max(tail_expo, axis=0)
    key_scaled_rows = (jnp.exp(tail_expo - tail_max[None, :])[:, :, None] * keys).astype(
        jnp.bfloat16
    )
    cell_state_matrix = jnp.einsum(
        "emn,emp->mnp", key_scaled_rows, value_rows, preferred_element_type=jnp.float32
    )
    state_n = jnp.sum(key_scaled_rows.astype(jnp.float32), axis=0)
    reset = (segment[-1] != segment_before).astype(jnp.float32) * jnp.ones_like(tail_max)
    summary = (cell_state_matrix, state_n, tail_max, log_decay[-1], reset)
    return (log_decay, inner_max.T, inner_num, inner_den, summary)


def block_output(
    queries, log_decay, inner_max, inner_num, inner_den, segment, segment_before, incoming
):
    cell_state_matrix, state_n, state_m = incoming
    outer = jnp.where((segment == segment_before)[:, None], log_decay + state_m[None, :], -jnp.inf)
    ceiling = jnp.maximum(inner_max, outer)
    inner_weight = jnp.exp(inner_max - ceiling)
    outer_weight = jnp.exp(outer - ceiling)
    query_single = queries.astype(jnp.float32)
    outer_numerator_sum = jnp.einsum(
        "ciy,iyo->cio", query_single, cell_state_matrix, precision=FULL_ACCURACY
    )
    outer_den = jnp.einsum("lhk,hk->lh", query_single, state_n, precision=FULL_ACCURACY)
    numerator = (
        inner_weight[:, :, None] * inner_num + outer_weight[:, :, None] * outer_numerator_sum
    )
    denominator = inner_weight * inner_den + outer_weight * outer_den
    return numerator / jnp.maximum(jnp.abs(denominator), 1.0)[:, :, None]


def plain_local(
    tokens,
    w_query,
    w_key,
    w_value,
    w_outgate,
    w_gates,
    gate_bias,
    w_out,
    carry_matrix,
    carry_norm,
    carry_max,
    doc_lengths,
):
    length = tokens.shape[0]
    head_count = gate_bias.shape[1]
    query_size = w_query.shape[1] // head_count
    value_size = w_value.shape[1] // head_count
    matrices = (w_query, w_key, w_value, w_outgate)
    zero_init = tuple((jnp.zeros((length, matrix.shape[1]), jnp.float32) for matrix in matrices))
    zero_init = zero_init + (
        jnp.zeros((length, head_count), jnp.float32),
        jnp.zeros((length, head_count), jnp.float32),
    )
    column_block = lax.all_gather(tokens, "tensor", axis=1, tiled=True)
    updated = tuple(
        (jnp.dot(column_block, matrix, preferred_element_type=jnp.float32) for matrix in matrices)
    )
    input_sum = jnp.dot(column_block, w_gates[0], preferred_element_type=jnp.float32)
    forget_sum = jnp.dot(column_block, w_gates[1], preferred_element_type=jnp.float32)
    projected = updated + (input_sum, forget_sum)
    queries = projected[0].astype(jnp.bfloat16).reshape(length, head_count, query_size)
    keys = (
        (projected[1] * query_size ** (-0.5))
        .astype(jnp.bfloat16)
        .reshape(length, head_count, query_size)
    )
    value_rows = projected[2].astype(jnp.bfloat16).reshape(length, head_count, value_size)
    outgate = jax.nn.sigmoid(projected[3])
    input_pre = projected[4] + gate_bias[0][None, :]
    log_forget = jax.nn.log_sigmoid(projected[5] + gate_bias[1][None, :])
    offset = lax.axis_index("seq") * length
    positions = offset + jnp.arange(length, dtype=jnp.int32)
    segment = segment_of(doc_lengths, positions)
    segment_before = segment_of(doc_lengths, jnp.maximum(offset - 1, 0)[None])[0]
    log_decay, inner_max, inner_num, inner_den, summary = block_local(
        queries, keys, value_rows, input_pre, log_forget, segment, segment_before
    )
    start_state = (carry_matrix, carry_norm, carry_max)
    zero_heads = jnp.zeros((head_count,), jnp.float32)
    is_leader = lax.axis_index("seq") == 0

    def relay(iteration, current):
        leaving = combine(current + (zero_heads, zero_heads), summary)[:3]
        arrived = plain_shifted(leaving, "seq", 1)
        return tuple(
            (
                jnp.where(is_leader, initial, received)
                for initial, received in zip(start_state, arrived)
            )
        )

    incoming = lax.fori_loop(0, lax.axis_size("seq") - 1, relay, start_state)
    mixed_heads = block_output(
        queries, log_decay, inner_max, inner_num, inner_den, segment, segment_before, incoming
    )
    hidden = (outgate * mixed_heads.reshape(length, head_count * value_size)).astype(jnp.bfloat16)
    partial_value = jnp.dot(hidden, w_out, preferred_element_type=jnp.float32)
    summed = lax.psum_scatter(
        partial_value.astype(jnp.bfloat16), "tensor", scatter_dimension=1, tiled=True
    ).astype(jnp.float32)
    return (tokens.astype(jnp.float32) + summed).astype(jnp.bfloat16)


def solution(mesh):
    fast = mesh.shape["tensor"] == 4 and mesh.shape["seq"] == 8
    return jax.shard_map(
        local if fast else plain_local,
        mesh=mesh,
        in_specs=(
            P("seq", "tensor"),
            P(None, "tensor"),
            P(None, "tensor"),
            P(None, "tensor"),
            P(None, "tensor"),
            P(None, None, "tensor"),
            P(None, "tensor"),
            P("tensor", None),
            P("tensor", None, None),
            P("tensor", None),
            P("tensor"),
            P(),
        ),
        out_specs=P("seq", "tensor"),
        check_vma=False,
    )
```

```python
import functools

import jax
import jax.numpy as jnp
from jax import lax
from jax.experimental import pallas as pl
from jax.experimental.pallas import tpu as pltpu
from jax.sharding import PartitionSpec as P

BF = jnp.bfloat16
F32 = jnp.float32
MIB = 1024 * 1024
TOKEN_CHUNKS = ((256, 256), (512,))
OUT_CHUNKS = (256, 256, 256, 256)


def params(mib):
    return pltpu.CompilerParams(vmem_limit_bytes=mib * MIB)


def cost(flops, moved):
    return pl.CostEstimate(flops=int(flops), bytes_accessed=int(moved), transcendentals=0)


def swapped(x, axis, mask):
    size = lax.axis_size(axis)
    return lax.ppermute(x, axis, [(i, i ^ mask) for i in range(size)])


def shifted(x, axis, by):
    size = lax.axis_size(axis)
    return lax.ppermute(x, axis, [(i, (i + by) % size) for i in range(size)])


def after(first, *others):
    out = lax.optimization_barrier((first,) + others)[1:]
    return out[0] if len(out) == 1 else out


SMEM_SPEC = pl.BlockSpec(memory_space=pltpu.SMEM)
VMEM_SPEC = pl.BlockSpec(memory_space=pltpu.VMEM)
HBM_SPEC = pl.BlockSpec(memory_space=pltpu.HBM)


def in_hbm(x):
    return pltpu.with_memory_space_constraint(x, pltpu.HBM)


def in_vmem(*xs):
    return [pltpu.with_memory_space_constraint(x, pltpu.VMEM) for x in xs]


def holding(kernel, held):
    return (lambda *refs: kernel(*refs[len(held) :])) if held else kernel


def split_kernel(starts, tokens, *refs):
    outs, sem = refs[:-1], refs[-1]
    copies = []
    for i, (low, out) in enumerate(zip(starts, outs)):
        source = tokens.at[:, low : low + out.shape[1]]
        copies.append(pltpu.make_async_copy(source, out, sem.at[i]))
        copies[-1].start()
    for copy in copies:
        copy.wait()


def split_tokens(tokens, starts, sizes):
    length = tokens.shape[0]
    return pl.pallas_call(
        functools.partial(split_kernel, starts),
        out_shape=tuple(pltpu.VMEM((length, c), BF) for c in sizes),
        in_specs=[HBM_SPEC],
        out_specs=(VMEM_SPEC,) * len(sizes),
        scratch_shapes=[pltpu.SemaphoreType.DMA((len(sizes),))],
        compiler_params=params(4),
        cost_estimate=cost(1e6, 1e5),
    )(in_hbm(tokens))


def across_tokens(w, x):
    return lax.dot_general(w, x, (((1,), (1,)), ((), ())), preferred_element_type=F32)


def row_start(place, share, owner, first):
    return pl.multiple_of((place ^ owner) * share + first, 128)


def copies_of(weights, targets, semaphores, at, place, share):
    result = []
    for i, (w, target) in enumerate(zip(weights, targets)):
        low, group = 0, []
        for p, (owner, first, count) in enumerate(at[i]):
            group.append(
                pltpu.make_async_copy(
                    w.at[pl.ds(row_start(place, share, owner, first), count)],
                    target.at[pl.ds(low, count)],
                    semaphores.at[i, p],
                )
            )
            low += count
        result.append(group)
    return result


def stage_kernel(xs_at, skips, ahead_at, share, summed, finishes, gated, info, *refs):
    refs = list(refs)
    take = lambda n: [refs.pop(0) for _ in range(n)]
    count_w = len(skips)
    xs, ws = take(len(xs_at)), take(count_w)
    gate_w = take(1)[0] if gated else None
    sums = [take(1)[0] if i in summed else None for i in range(count_w + gated)]
    outs = take(count_w + gated)
    ahead = take(2) if ahead_at else []
    held = take(count_w)
    sems = take(1)[0]
    place = info[0]
    at = [xs_at[skip:] for skip in skips]
    now = copies_of(ws, held, sems, at, place, share)
    later = copies_of(ws, ahead, take(1)[0], [ahead_at] * 2, place, share) if ahead_at else []
    for group in now + later:
        for copy in group:
            copy.start()
    if gated:
        gates = 0.0 if sums[count_w] is None else sums[count_w][...]
        for (owner, first, count), x in zip(xs_at, xs):
            gates = gates + across_tokens(
                gate_w[:, pl.ds(row_start(place, share, owner, first), count)], x[...]
            )
        outs[count_w][...] = gates
    for i in range(count_w):
        for copy in now[i]:
            copy.wait()

        def body(j, _, i=i):
            columns = pl.ds(pl.multiple_of(j * 256, 256), 256)
            total = None if sums[i] is None else sums[i][:, columns]
            low = 0
            for (_, _, count), x in zip(at[i], xs[skips[i] :]):
                part = jnp.dot(
                    x[...], held[i][low : low + count, columns], preferred_element_type=F32
                )
                total = part if total is None else total + part
                low += count
            outs[i][:, columns] = finishes[i](total).astype(outs[i].dtype)
            return 0

        lax.fori_loop(0, outs[i].shape[1] // 256, body, 0)
    for group in later:
        for copy in group:
            copy.wait()


def unchanged(x):
    return x


def twin_kernel(at, share, info, x, key_w, value_w, gate_w, *refs):
    owner, first, count = at
    for w, total, out in zip((key_w, value_w), refs[:2], refs[3:5]):
        for low in range(0, out.shape[1], 512):
            columns = slice(low, low + 512)
            part = jnp.dot(x[...], w[:count, columns], preferred_element_type=F32)
            out[:, columns] = total[:, columns] + part
    rows = gate_w[:, pl.ds(row_start(info[0], share, owner, first), count)]
    refs[5][...] = refs[2][...] + across_tokens(rows, x[...])


def twin_stage(info, x, at, key_w, value_w, gate_w, sums, share):
    return pl.pallas_call(
        functools.partial(twin_kernel, at, share),
        out_shape=tuple(pltpu.VMEM(y.shape, F32) for y in sums),
        in_specs=[SMEM_SPEC] + [VMEM_SPEC] * 7,
        out_specs=(VMEM_SPEC,) * 3,
        input_output_aliases={5 + i: i for i in range(3)},
        compiler_params=params(8),
        cost_estimate=cost(1e6, 1e5),
    )(info, *in_vmem(x, key_w, value_w), gate_w, *in_vmem(*sums))


def stage(info, xs, xs_at, weights, share, gate_w=None, sums=None, ahead_at=None, finishes=None, held=(), skips=None):
    length = xs[0].shape[0]
    count = sum(c for _, _, c in xs_at)
    gated = int(gate_w is not None)
    kinds = [F32] * len(weights) if finishes is None else [k for _, k in finishes]
    calls = [unchanged] * len(weights) if finishes is None else [f for f, _ in finishes]
    shapes = [pltpu.VMEM((length, w.shape[1]), k) for w, k in zip(weights, kinds)]
    if gated:
        shapes.append(pltpu.VMEM((gate_w.shape[0], length), F32))
    scratch = [pltpu.VMEM((count, w.shape[1]), BF) for w in weights]
    scratch.append(pltpu.SemaphoreType.DMA((len(weights), len(xs_at))))
    if ahead_at:
        rows = sum(c for _, _, c in ahead_at)
        shapes += [pltpu.VMEM((rows, w.shape[1]), BF) for w in weights[:2]]
        scratch.append(pltpu.SemaphoreType.DMA((2, len(ahead_at))))
    operands = [*in_vmem(*held), info, *in_vmem(*xs), *[in_hbm(w) for w in weights]]
    specs = [VMEM_SPEC] * len(held) + [SMEM_SPEC] + [VMEM_SPEC] * len(xs) + [HBM_SPEC] * len(weights)
    if gated:
        operands.append(gate_w)
        specs.append(VMEM_SPEC)
    aliases, summed = {}, ()
    if sums is not None:
        summed = tuple(i for i, x in enumerate(sums) if x is not None)
        if finishes is None:
            aliases = {len(operands) + n: i for n, i in enumerate(summed)}
        operands += in_vmem(*[x for x in sums if x is not None])
        specs += [VMEM_SPEC] * len(summed)
    return pl.pallas_call(
        holding(
            functools.partial(
                stage_kernel, xs_at, skips or [0] * len(weights), ahead_at, share, summed, calls,
                gated,
            ),
            held,
        ),
        out_shape=tuple(shapes),
        in_specs=specs,
        out_specs=(VMEM_SPEC,) * len(shapes),
        scratch_shapes=scratch,
        input_output_aliases=aliases,
        compiler_params=params(24),
        cost_estimate=cost(1e6, 1e5),
    )(*operands)


def segments(docs, positions):
    total = jnp.zeros_like(positions)
    bound = jnp.int32(0)
    for j in range(docs.shape[0] - 1):
        bound = bound + docs[j]
        total = total + (positions >= bound).astype(jnp.int32)
    return total


def gate_rows(both, offset, docs, bias):
    heads, length = both.shape[0] // 2, both.shape[1]
    row = lax.broadcasted_iota(jnp.int32, (heads, length), 0)
    lane = lax.broadcasted_iota(jnp.int32, (heads, length), 1)
    input_bias = jnp.zeros((heads, length), F32)
    forget_bias = jnp.zeros((heads, length), F32)
    for h in range(heads):
        input_bias = jnp.where(row == h, bias[0, h], input_bias)
        forget_bias = jnp.where(row == h, bias[1, h], forget_bias)
    input_pre = both[:heads] + input_bias
    forget = both[heads:] + forget_bias
    decay = jnp.minimum(forget, 0.0) - jnp.log1p(jnp.exp(-jnp.abs(forget)))
    step = 1
    while step < length:
        decay = decay + jnp.where(lane >= step, pltpu.roll(decay, step, 1), 0.0)
        step *= 2
    u = input_pre - decay
    segment = segments(docs, lane + offset)
    last = segments(docs, lane * 0 + (offset + length - 1))
    open_rows = segment == last
    top = jnp.max(jnp.where(open_rows, u, -jnp.inf), axis=1, keepdims=True)
    weight = jnp.where(open_rows, jnp.exp(u - top), 0.0)
    total = decay[:, length - 1 : length]
    narrow = lax.broadcasted_iota(jnp.int32, (heads, 128), 1)
    stats = jnp.where(narrow == 0, total + top, jnp.where(narrow == 1, total, 0.0))
    return u, weight, stats


def summary_kernel(xs_at, skip, share, heads, info, docs, bias, *refs):
    xs = refs[: len(xs_at)]
    key_w, value_w, gate_w, key_sum, value_sum, gate_sum = refs[len(xs_at) : len(xs_at) + 6]
    key_out, value_out, keep_out, send_out, small_out, u_out, state = refs[len(xs_at) + 6 :]
    place, side, offset = info[0], info[1], info[2]
    size, wide = state.shape
    gates = gate_sum[...]
    for (owner, first, count), x in zip(xs_at, xs):
        gates = gates + across_tokens(
            gate_w[:, pl.ds(row_start(place, share, owner, first), count)], x[...]
        )
    u, weight, stats = gate_rows(gates, offset, docs, bias)
    u_out[...] = u
    small_out[:, size:] = stats
    spare = jnp.zeros((128 - weight.shape[0], weight.shape[1]), F32)
    columns = jnp.concatenate([weight, spare], axis=0).T
    half = size // 2
    for h in range(heads):
        key_at, value_at = slice(h * size, (h + 1) * size), slice(h * wide, (h + 1) * wide)
        key, value, low = key_sum[:, key_at], value_sum[:, value_at], skip
        for x in xs:
            count = x.shape[1]
            rows = slice(low, low + count)
            key = key + jnp.dot(x[...], key_w[rows, key_at], preferred_element_type=F32)
            value = value + jnp.dot(x[...], value_w[rows, value_at], preferred_element_type=F32)
            low += count
        key = (key * size ** (-0.5)).astype(BF)
        value = value.astype(BF)
        key_out[:, key_at] = key
        value_out[:, value_at] = value
        scaled = (columns[:, h : h + 1] * key.astype(F32)).astype(BF)
        small_out[h : h + 1, :size] = jnp.sum(scaled.astype(F32), axis=0, keepdims=True)
        state[...] = lax.dot_general(
            scaled, value, (((0,), (0,)), ((), ())), preferred_element_type=F32
        )
        keep_out[h] = state[pl.ds(pl.multiple_of(side * half, half), half)].astype(BF)
        send_out[h] = state[pl.ds(pl.multiple_of((1 - side) * half, half), half)].astype(BF)


def block_summary(
    info, docs, bias, xs, xs_at, skip, key_w, value_w, gate_w, key_sum, value_sum, gates, share,
    heads,
):
    length = xs[0].shape[0]
    size, wide = key_w.shape[1] // heads, value_w.shape[1] // heads
    return pl.pallas_call(
        functools.partial(summary_kernel, xs_at, skip, share, heads),
        out_shape=(
            pltpu.VMEM((length, heads * size), BF),
            pltpu.VMEM((length, heads * wide), BF),
            pltpu.VMEM((heads, size // 2, wide), BF),
            pltpu.VMEM((heads, size // 2, wide), BF),
            pltpu.VMEM((heads, size + 128), F32),
            pltpu.VMEM((heads, length), F32),
        ),
        in_specs=[SMEM_SPEC] * 3 + [VMEM_SPEC] * (len(xs) + 6),
        out_specs=(VMEM_SPEC,) * 6,
        scratch_shapes=[pltpu.VMEM((size, wide), F32)],
        compiler_params=params(16),
        cost_estimate=cost(4e9, 4e6),
    )(info, docs, bias, *in_vmem(*xs, key_w, value_w), gate_w, *in_vmem(key_sum, value_sum, gates))


def reset_of(docs, index, length):
    first = jnp.maximum(index * length - 1, 0)
    return segments(docs, (index + 1) * length - 1) != segments(docs, first)


def pair_scales(info, docs, length, size, own, other):
    even = info[1] == 0
    first = info[2] // length - info[1]
    m_own, g_own = own[:, size : size + 1], own[:, size + 1 : size + 2]
    m_other, g_other = other[:, size : size + 1], other[:, size + 1 : size + 2]
    m_even, g_even = jnp.where(even, m_own, m_other), jnp.where(even, g_own, g_other)
    m_odd, g_odd = jnp.where(even, m_other, m_own), jnp.where(even, g_other, g_own)
    reset_odd = reset_of(docs, first + 1, length)
    m_pair = jnp.maximum(jnp.where(reset_odd, -jnp.inf, m_even + g_odd), m_odd)
    pair_even = jnp.where(reset_odd, 0.0, jnp.exp(jnp.minimum(m_even + g_odd - m_pair, 0.0)))
    pair_odd = jnp.exp(m_odd - m_pair)
    weights = jnp.where(even, pair_even, pair_odd), jnp.where(even, pair_odd, pair_even)
    return m_even, g_even, g_odd, m_pair, weights


def pair_kernel(length, info, docs, own, other, kept, got, small_out, *state_out):
    heads = own.shape[0]
    size = own.shape[1] - 128
    _, g_even, g_odd, m_pair, (w_own, w_other) = pair_scales(
        info, docs, length, size, own[...], other[...]
    )
    small_out[:, :size] = w_own * own[:, :size] + w_other * other[:, :size]
    lane = lax.broadcasted_iota(jnp.int32, (heads, 128), 1)
    small_out[:, size:] = jnp.where(
        lane == 0, m_pair, jnp.where(lane == 1, g_even + g_odd, 0.0)
    )
    for h in range(heads):
        at = slice(h, h + 1)
        state = w_own[at] * kept[h].astype(F32) + w_other[at] * got[h].astype(F32)
        state_out[h][0] = state.astype(BF)


def pair_summary(info, docs, small, small_other, kept, got, length, held):
    return pl.pallas_call(
        holding(functools.partial(pair_kernel, length), held),
        out_shape=(pltpu.VMEM(small.shape, F32),)
        + (pltpu.VMEM((1,) + kept.shape[1:], BF),) * kept.shape[0],
        in_specs=[VMEM_SPEC] * len(held) + [SMEM_SPEC] * 2 + [VMEM_SPEC] * 4,
        out_specs=(VMEM_SPEC,) * (1 + kept.shape[0]),
        compiler_params=params(4),
        cost_estimate=cost(1e6, 1e5),
    )(*in_vmem(*held), info, docs, *in_vmem(small, small_other, kept, got))


def incoming_kernel(length, reach, info, docs, own, other, kept, got, *refs):
    heads = own.shape[0]
    smalls, refs = refs[:reach], refs[reach:]
    states = [refs[k * heads : (k + 1) * heads] for k in range(reach)]
    carry, carry_norm, carry_max, own_out, other_out, norm_out, top_out = refs[reach * heads :]
    size = own.shape[1] - 128
    side = info[1]
    even = side == 0
    first = info[2] // length - side
    m_even, g_even, _, _, _ = pair_scales(info, docs, length, size, own[...], other[...])
    reset_even = reset_of(docs, first, length)
    expos = []
    passed = jnp.zeros((heads, 1), F32)
    unbroken = jnp.bool_(True)
    for k in range(1, reach + 1):
        there = first >= 2 * k
        index = jnp.maximum(first - 2 * k, 0)
        m_k, g_k = smalls[k - 1][:, size : size + 1], smalls[k - 1][:, size + 1 : size + 2]
        expos.append(jnp.where(there & unbroken, m_k + passed, -jnp.inf))
        passed = passed + jnp.where(there, g_k, 0.0)
        broken = reset_of(docs, index, length) | reset_of(docs, index + 1, length)
        unbroken = unbroken & ~(there & broken)
    in_reach = (first <= 2 * reach) & unbroken
    expos.append(jnp.where(in_reach, carry_max[...] + passed, -jnp.inf))
    top_even = functools.reduce(jnp.maximum, expos)
    expos_odd = [jnp.where(reset_even, -jnp.inf, e + g_even) for e in expos]
    top_odd = functools.reduce(jnp.maximum, expos_odd, m_even)
    w_even = [jnp.exp(e - top_even) for e in expos]
    w_odd = [jnp.exp(e - top_odd) for e in expos_odd]
    direct = jnp.exp(m_even - top_odd)
    w_own = [jnp.where(even, a, b) for a, b in zip(w_even, w_odd)]
    w_other = [jnp.where(even, b, a) for a, b in zip(w_even, w_odd)]
    direct_own = jnp.where(even, 0.0, direct)
    direct_other = jnp.where(even, direct, 0.0)
    top_out[...] = jnp.where(even, top_even, top_odd) + jnp.zeros((heads, 128), F32)
    norm = direct_own * jnp.where(even, own[:, :size], other[:, :size])
    norm = norm + w_own[reach] * carry_norm[...]
    for k in range(reach):
        norm = norm + w_own[k] * smalls[k][:, :size]
    norm_out[...] = norm
    for h in range(heads):
        at = slice(h, h + 1)
        here = jnp.where(even, kept[h].astype(F32), got[h].astype(F32))
        base = carry[h]
        mine = w_own[reach][at] * base + direct_own[at] * here
        theirs = w_other[reach][at] * base + direct_other[at] * here
        for k in range(reach):
            state = states[k][h][0].astype(F32)
            mine = mine + w_own[k][at] * state
            theirs = theirs + w_other[k][at] * state
        own_out[h] = mine.astype(BF)
        other_out[h] = theirs.astype(BF)


def carry_kernel(info, carry, out, sem):
    half = out.shape[1]
    rows = pl.ds(pl.multiple_of(info[1] * half, half), half)
    copy = pltpu.make_async_copy(carry.at[:, rows], out, sem)
    copy.start()
    copy.wait()


def carry_half(info, carry, held):
    heads, size, wide = carry.shape
    return pl.pallas_call(
        holding(carry_kernel, held),
        out_shape=pltpu.VMEM((heads, size // 2, wide), F32),
        in_specs=[VMEM_SPEC] * len(held) + [SMEM_SPEC, HBM_SPEC],
        out_specs=VMEM_SPEC,
        scratch_shapes=[pltpu.SemaphoreType.DMA],
        compiler_params=params(4),
        cost_estimate=cost(1e6, 1e5),
    )(*in_vmem(*held), info, in_hbm(carry))


def incoming_state(
    info, docs, small, small_other, kept, got, smalls, states, carry, carry_norm, carry_max, length,
    held,
):
    heads = small.shape[0]
    return pl.pallas_call(
        holding(functools.partial(incoming_kernel, length, len(smalls)), held),
        out_shape=(
            pltpu.VMEM(kept.shape, BF),
            pltpu.VMEM(kept.shape, BF),
            pltpu.VMEM(carry_norm.shape, F32),
            pltpu.VMEM((heads, 128), F32),
        ),
        in_specs=[VMEM_SPEC] * len(held)
        + [SMEM_SPEC] * 2
        + [VMEM_SPEC] * (7 + (1 + heads) * len(smalls)),
        out_specs=(VMEM_SPEC,) * 4,
        compiler_params=params(6),
        cost_estimate=cost(1e6, 1e5),
    )(
        *in_vmem(*held), info, docs,
        *in_vmem(small, small_other, kept, got, *smalls, *sum(states, []), carry),
        carry_norm, carry_max[:, None],
    )


def inner_kernel(
    heads, info, docs, top_in, query, key, value, u, norm, gate, w_out,
    base_out, slope_out, w_here, sem,
):
    fetch = pltpu.make_async_copy(w_out, w_here, sem)
    fetch.start()
    length = query.shape[0]
    size, wide = query.shape[1] // heads, value.shape[1] // heads
    offset = info[2]
    chunk = 128
    one = jnp.zeros((chunk, 1), jnp.int32)
    before = segments(docs, one + jnp.maximum(offset - 1, 0))
    for head in range(heads):
        keys_at = slice(head * size, (head + 1) * size)
        values_at = slice(head * wide, (head + 1) * wide)
        u_row = u[head : head + 1, :]
        norm_row = norm[head : head + 1, :]
        top = top_in[head : head + 1, 0:1]
        for low in range(0, length, chunk):
            high = low + chunk
            position_t = lax.broadcasted_iota(jnp.int32, (chunk, 1), 0) + low
            position_s = lax.broadcasted_iota(jnp.int32, (1, high), 1)
            segment_t = segments(docs, position_t + offset)
            segment_s = segments(docs, position_s + offset)
            allowed = (position_s <= position_t) & (segment_s == segment_t)
            expo = jnp.where(allowed, u_row[:, :high], -jnp.inf)
            peak = jnp.max(expo, axis=1, keepdims=True)
            q = query[low:high, keys_at]
            scores = lax.dot_general(
                q, key[:high, keys_at], (((1,), (1,)), ((), ())), preferred_element_type=F32
            )
            weighted = jnp.exp(expo - peak) * scores
            num = jnp.dot(
                weighted.astype(BF), value[:high, values_at], preferred_element_type=F32
            )
            den = jnp.sum(weighted, axis=1, keepdims=True)
            carried = segment_t == before
            ceiling = jnp.where(carried, jnp.maximum(peak, top), peak)
            inner_weight = jnp.exp(peak - ceiling)
            outer_weight = jnp.where(carried, jnp.exp(jnp.minimum(top - ceiling, 0.0)), 0.0)
            outer_den = jnp.sum(q.astype(F32) * norm_row, axis=1, keepdims=True)
            full = inner_weight * den + outer_weight * outer_den
            inverse = 1.0 / jnp.maximum(jnp.abs(full), 1.0)
            g = gate[low:high, values_at]
            base_out[low:high, values_at] = g * (num * (inner_weight * inverse))
            slope_out[low:high, values_at] = g * (outer_weight * inverse)
    fetch.wait()


def inner(info, docs, top, query, key, value, u, norm, gate, w_out, heads):
    length, depth = value.shape
    return pl.pallas_call(
        functools.partial(inner_kernel, heads),
        out_shape=(
            pltpu.VMEM((length, depth), F32),
            pltpu.VMEM((length, depth), F32),
            pltpu.VMEM(w_out.shape, BF),
        ),
        in_specs=[SMEM_SPEC] * 2 + [VMEM_SPEC] * 7 + [HBM_SPEC],
        out_specs=(VMEM_SPEC,) * 3,
        scratch_shapes=[pltpu.SemaphoreType.DMA],
        compiler_params=params(12),
        cost_estimate=cost(1e6, 1e5),
    )(info, docs, *in_vmem(top, query, key, value, u, norm, gate), in_hbm(w_out))


def some_columns(info, hidden, w, out, owners, start):
    share = w.shape[1] // 4
    wide = out.shape[1] // 2
    for step, owner in enumerate(owners):
        columns = pl.ds(pl.multiple_of((info[0] ^ owner) * share + start, 128), wide)
        part = jnp.dot(hidden[...], w[:, columns], preferred_element_type=F32)
        out[:, step * wide : (step + 1) * wide] = part.astype(BF)


def hidden_kernel(heads, info, query, own, other, base, slope, w, hidden, send, state):
    half = own.shape[1]
    side = info[1]
    size, wide = 2 * half, own.shape[2]
    for h in range(heads):
        state[pl.ds(pl.multiple_of(side * half, half), half)] = own[h]
        state[pl.ds(pl.multiple_of((1 - side) * half, half), half)] = other[h]
        outer = jnp.dot(
            query[:, h * size : (h + 1) * size], state[...], preferred_element_type=F32
        )
        columns = slice(h * wide, (h + 1) * wide)
        hidden[:, columns] = (base[:, columns] + slope[:, columns] * outer).astype(BF)
    some_columns(info, hidden, w, send, (1, 3), 0)


def hidden_and_first(info, query, own, other, base, slope, w_here, wide, heads):
    length, depth = base.shape
    return pl.pallas_call(
        functools.partial(hidden_kernel, heads),
        out_shape=(pltpu.VMEM((length, depth), BF), pltpu.VMEM((length, 2 * wide), BF)),
        in_specs=[SMEM_SPEC] + [VMEM_SPEC] * 6,
        out_specs=(VMEM_SPEC,) * 2,
        scratch_shapes=[pltpu.VMEM((2 * own.shape[1], own.shape[2]), BF)],
        compiler_params=params(12),
        cost_estimate=cost(3e9, 8e6),
    )(info, *in_vmem(query, own, other, base, slope, w_here))


def columns_kernel(start, following, info, hidden, w, keep, *send):
    if send:
        some_columns(info, hidden, w, send[0], (1, 3), following)
    some_columns(info, hidden, w, keep, (0, 2), start)


def next_columns(info, hidden, w_here, start, wide, following):
    length = hidden.shape[0]
    shapes = [pltpu.VMEM((length, 2 * wide), BF)]
    if following:
        shapes.append(pltpu.VMEM((length, 2 * following), BF))
    return pl.pallas_call(
        functools.partial(columns_kernel, start, start + wide),
        out_shape=tuple(shapes),
        in_specs=[SMEM_SPEC, VMEM_SPEC, VMEM_SPEC],
        out_specs=(VMEM_SPEC,) * len(shapes),
        compiler_params=params(12),
        cost_estimate=cost(1e6, 1e5),
    )(info, *in_vmem(hidden, w_here))


def local(
    tokens,
    w_query,
    w_key,
    w_value,
    w_outgate,
    w_gates,
    gate_bias,
    w_out,
    carry_matrix,
    carry_norm,
    carry_max,
    doc_lengths,
):
    length, share = tokens.shape
    heads = gate_bias.shape[1]
    size = w_query.shape[1] // heads
    place = lax.axis_index("tensor")
    block = lax.axis_index("seq")
    blocks = lax.axis_size("seq")
    offset = (block * length).astype(jnp.int32)
    tensor = lambda x, mask: swapped(x, "tensor", mask)
    pair = lambda x: swapped(x, "seq", 1)
    down = lambda x: shifted(x, "seq", 2)

    beside = tensor(tokens, 1)
    sizes = [c for chunks in TOKEN_CHUNKS for c in chunks]
    starts = [sum(sizes[:i]) for i in range(len(sizes))]
    first = split_tokens(tokens, starts[:1], sizes[:1])
    others = split_tokens(after(beside, tokens), starts[1:], sizes[1:])
    pieces = [*first, *others]
    source = tokens
    pieces = [(s, c, tensor(x, 2)) for s, c, x in zip(starts, sizes, pieces)]
    groups = []
    for chunks in TOKEN_CHUNKS:
        groups.append(pieces[: len(chunks)])
        pieces = pieces[len(chunks) :]
    gate_w = w_gates.transpose(0, 2, 1).reshape(2 * heads, 4 * share)

    side = (block % 2).astype(jnp.int32)
    info = jnp.stack([place, side, offset]).astype(jnp.int32)
    at = [[(o, s, c) for s, c, _ in group for o in (2, 3)] for group in groups]
    near_at = [(0, 0, share), (1, 0, share)]
    first_three = (w_key, w_value, w_query)
    sums = stage(info, [source, beside], near_at, first_three, share, gate_w)
    far = []
    for i, group in enumerate(groups):
        xs = lax.optimization_barrier((*[x for _, _, x in group], *sums))
        xs, sums = xs[: len(group)], xs[len(group) :]
        if i == 0:
            sums = [*sums[:3], None, sums[3]]
        xs = [y for x in xs for y in (x, tensor(x, 1))]
        far.append(xs)
        if i < len(groups) - 1:
            last = i == len(groups) - 2
            out = stage(
                info, xs, at[i], (*first_three, w_outgate), share, gate_w, sums,
                at[-1] if last else None,
            )
            sums = out[:5]
            if last:
                w_key_last, w_value_last = out[5:]
    kv_sums = twin_stage(
        info, xs[0], at[-1][0], w_key_last, w_value_last, gate_w, (*sums[:2], sums[4]), share
    )
    keys, values, kept, sent, small, u = block_summary(
        info, doc_lengths, gate_bias, xs[1:], at[-1][1:], at[-1][0][2], w_key_last, w_value_last,
        gate_w, *kv_sums, share, heads,
    )

    small_other = pair(small)
    got = pair(sent)
    held = (keys, values, kept, u)
    now_xs = after(keys, beside, *far[-1])
    queries, *gate = stage(
        info, now_xs, near_at[1:] + at[-1], (w_query, w_outgate), share, None, [sums[2], sums[3]],
        finishes=((unchanged, BF), (unchanged, F32)), held=held, skips=[1, 0],
    )
    small_other, got, queries, *gate = lax.optimization_barrier(
        (small_other, got, queries, *gate)
    )
    travel, *state_pair = pair_summary(
        info, doc_lengths, small, small_other, kept, got, length, (keys, values, queries, u)
    )
    smalls, states = [], []
    held = (keys, values, kept, got, queries, u)
    for step in range(blocks // 4):
        before = state_pair[0]
        first = down(state_pair[0])
        travel = down(travel)
        state_pair = [first] + [down(x) for x in state_pair[1:]]
        if step == 0:
            near_xs = [after(before, source)]
            gate = stage(
                info, near_xs, near_at[:1], (w_outgate,), share, None, gate,
                finishes=((jax.nn.sigmoid, F32),), held=held,
            )
            travel, first, *gate = lax.optimization_barrier((travel, state_pair[0], *gate))
            state_pair[0] = first
        elif step == 1:
            carry = carry_half(after(before, info), carry_matrix, (*held, *gate))
            travel, carry, *state_pair = lax.optimization_barrier((travel, carry, *state_pair))
        smalls.append(travel)
        states.append(state_pair)
    (gate,) = gate
    state_own, state_other, norm_in, top_own = incoming_state(
        info, doc_lengths, small, small_other, kept, got, smalls, states,
        carry, carry_norm, carry_max, length, (keys, values, queries, gate, u),
    )
    state_got = pair(state_other)
    base, slope, w_here = inner(
        info, doc_lengths, top_own, queries, keys, values, u, norm_in, gate, w_out, heads
    )

    hidden, send = hidden_and_first(
        info, queries, state_own, state_got, base, slope, w_here, OUT_CHUNKS[0], heads
    )
    start = 0
    leaving, arriving = [], []
    for wide, following in zip(OUT_CHUNKS, OUT_CHUNKS[1:] + (0,)):
        came = tensor(send, 1)
        now = after(leaving[max(len(leaving) - 1, 0)], hidden) if leaving else hidden
        keep, *send = next_columns(info, now, w_here, start, wide, following)
        send = send[0] if send else None
        both = keep.astype(F32) + came.astype(F32)
        leaving.append(both[:, wide:].astype(BF))
        arriving.append((start, wide, both[:, :wide], tensor(leaving[-1], 2)))
        start += wide
    out = source
    for start, wide, both, came in arriving[:-1]:
        columns = source[:, start : start + wide].astype(F32) + (both + came.astype(F32))
        out = lax.dynamic_update_slice(out, columns.astype(BF), (0, start))
    start, wide, both, came = arriving[-1]
    columns = source[:, start : start + wide].astype(F32) + (both + came.astype(F32))
    return lax.dynamic_update_slice(out, columns.astype(BF), (0, start))


FULL_ACCURACY = lax.Precision.HIGHEST


def plain_shifted(x, axis, by):
    devices = lax.axis_size(axis)
    pairs = [(i, i + by) for i in range(devices) if 0 <= i + by < devices]
    return lax.ppermute(x, axis, pairs)


def segment_of(doc_lengths, positions):
    bounds = jnp.cumsum(doc_lengths)[:-1]
    return jnp.sum((positions[:, None] >= bounds[None, :]).astype(jnp.int32), axis=1)


def combine(earlier, later):
    early_c, early_n, early_m, early_g, early_r = earlier
    late_c, late_n, late_m, late_g, late_r = later
    ceiling = jnp.maximum(early_m + late_g, late_m)
    early_weight = jnp.exp(early_m + late_g - ceiling)
    late_weight = jnp.exp(late_m - ceiling)
    reset_mask = late_r > 0.5
    merged_c = jnp.where(
        reset_mask[:, None, None],
        late_c,
        early_weight[:, None, None] * early_c + late_weight[:, None, None] * late_c,
    )
    merged_n = jnp.where(
        reset_mask[:, None], late_n, early_weight[:, None] * early_n + late_weight[:, None] * late_n
    )
    merged_m = jnp.where(reset_mask, late_m, ceiling)
    return (merged_c, merged_n, merged_m, late_g, jnp.maximum(early_r, late_r))


def block_local(queries, keys, value_rows, input_pre, log_forget, segment, segment_before):
    length = segment.shape[0]
    log_decay = jnp.cumsum(log_forget, axis=0)
    position = jnp.arange(length)
    allowed = (position[:, None] >= position[None, :]) & (segment[:, None] == segment[None, :])
    exponent = log_decay.T[:, :, None] - log_decay.T[:, None, :] + input_pre.T[:, None, :]
    exponent = jnp.where(allowed[None], exponent, -jnp.inf)
    inner_max = jnp.max(exponent, axis=2)
    scores = jnp.einsum("lhk,mhk->hlm", queries, keys, preferred_element_type=jnp.float32)
    weighted = jnp.exp(exponent - inner_max[:, :, None]) * scores
    weighted_bf = weighted.astype(jnp.bfloat16)
    inner_num = jnp.einsum(
        "hlm,mhv->lhv", weighted_bf, value_rows, preferred_element_type=jnp.float32
    )
    inner_den = jnp.sum(weighted, axis=2).T
    in_last = segment == segment[-1]
    tail_expo = log_decay[-1][None, :] - log_decay + input_pre
    tail_expo = jnp.where(in_last[:, None], tail_expo, -jnp.inf)
    tail_max = jnp.max(tail_expo, axis=0)
    key_scaled_rows = (jnp.exp(tail_expo - tail_max[None, :])[:, :, None] * keys).astype(
        jnp.bfloat16
    )
    cell_state_matrix = jnp.einsum(
        "emn,emp->mnp", key_scaled_rows, value_rows, preferred_element_type=jnp.float32
    )
    state_n = jnp.sum(key_scaled_rows.astype(jnp.float32), axis=0)
    reset = (segment[-1] != segment_before).astype(jnp.float32) * jnp.ones_like(tail_max)
    summary = (cell_state_matrix, state_n, tail_max, log_decay[-1], reset)
    return (log_decay, inner_max.T, inner_num, inner_den, summary)


def block_output(
    queries, log_decay, inner_max, inner_num, inner_den, segment, segment_before, incoming
):
    cell_state_matrix, state_n, state_m = incoming
    outer = jnp.where((segment == segment_before)[:, None], log_decay + state_m[None, :], -jnp.inf)
    ceiling = jnp.maximum(inner_max, outer)
    inner_weight = jnp.exp(inner_max - ceiling)
    outer_weight = jnp.exp(outer - ceiling)
    query_single = queries.astype(jnp.float32)
    outer_numerator_sum = jnp.einsum(
        "ciy,iyo->cio", query_single, cell_state_matrix, precision=FULL_ACCURACY
    )
    outer_den = jnp.einsum("lhk,hk->lh", query_single, state_n, precision=FULL_ACCURACY)
    numerator = (
        inner_weight[:, :, None] * inner_num + outer_weight[:, :, None] * outer_numerator_sum
    )
    denominator = inner_weight * inner_den + outer_weight * outer_den
    return numerator / jnp.maximum(jnp.abs(denominator), 1.0)[:, :, None]


def plain_local(
    tokens,
    w_query,
    w_key,
    w_value,
    w_outgate,
    w_gates,
    gate_bias,
    w_out,
    carry_matrix,
    carry_norm,
    carry_max,
    doc_lengths,
):
    length = tokens.shape[0]
    head_count = gate_bias.shape[1]
    query_size = w_query.shape[1] // head_count
    value_size = w_value.shape[1] // head_count
    matrices = (w_query, w_key, w_value, w_outgate)
    zero_init = tuple((jnp.zeros((length, matrix.shape[1]), jnp.float32) for matrix in matrices))
    zero_init = zero_init + (
        jnp.zeros((length, head_count), jnp.float32),
        jnp.zeros((length, head_count), jnp.float32),
    )
    column_block = lax.all_gather(tokens, "tensor", axis=1, tiled=True)
    updated = tuple(
        (jnp.dot(column_block, matrix, preferred_element_type=jnp.float32) for matrix in matrices)
    )
    input_sum = jnp.dot(column_block, w_gates[0], preferred_element_type=jnp.float32)
    forget_sum = jnp.dot(column_block, w_gates[1], preferred_element_type=jnp.float32)
    projected = updated + (input_sum, forget_sum)
    queries = projected[0].astype(jnp.bfloat16).reshape(length, head_count, query_size)
    keys = (
        (projected[1] * query_size ** (-0.5))
        .astype(jnp.bfloat16)
        .reshape(length, head_count, query_size)
    )
    value_rows = projected[2].astype(jnp.bfloat16).reshape(length, head_count, value_size)
    outgate = jax.nn.sigmoid(projected[3])
    input_pre = projected[4] + gate_bias[0][None, :]
    log_forget = jax.nn.log_sigmoid(projected[5] + gate_bias[1][None, :])
    offset = lax.axis_index("seq") * length
    positions = offset + jnp.arange(length, dtype=jnp.int32)
    segment = segment_of(doc_lengths, positions)
    segment_before = segment_of(doc_lengths, jnp.maximum(offset - 1, 0)[None])[0]
    log_decay, inner_max, inner_num, inner_den, summary = block_local(
        queries, keys, value_rows, input_pre, log_forget, segment, segment_before
    )
    start_state = (carry_matrix, carry_norm, carry_max)
    zero_heads = jnp.zeros((head_count,), jnp.float32)
    is_leader = lax.axis_index("seq") == 0

    def relay(iteration, current):
        leaving = combine(current + (zero_heads, zero_heads), summary)[:3]
        arrived = plain_shifted(leaving, "seq", 1)
        return tuple(
            (
                jnp.where(is_leader, initial, received)
                for initial, received in zip(start_state, arrived)
            )
        )

    incoming = lax.fori_loop(0, lax.axis_size("seq") - 1, relay, start_state)
    mixed_heads = block_output(
        queries, log_decay, inner_max, inner_num, inner_den, segment, segment_before, incoming
    )
    hidden = (outgate * mixed_heads.reshape(length, head_count * value_size)).astype(jnp.bfloat16)
    partial_value = jnp.dot(hidden, w_out, preferred_element_type=jnp.float32)
    summed = lax.psum_scatter(
        partial_value.astype(jnp.bfloat16), "tensor", scatter_dimension=1, tiled=True
    ).astype(jnp.float32)
    return (tokens.astype(jnp.float32) + summed).astype(jnp.bfloat16)


def solution(mesh):
    fast = mesh.shape["tensor"] == 4 and mesh.shape["seq"] == 8
    return jax.shard_map(
        local if fast else plain_local,
        mesh=mesh,
        in_specs=(
            P("seq", "tensor"),
            P(None, "tensor"),
            P(None, "tensor"),
            P(None, "tensor"),
            P(None, "tensor"),
            P(None, None, "tensor"),
            P(None, "tensor"),
            P("tensor", None),
            P("tensor", None, None),
            P("tensor", None),
            P("tensor"),
            P(),
        ),
        out_specs=P("seq", "tensor"),
        check_vma=False,
    )
```

```python
import functools

import jax
import jax.numpy as jnp
from jax import lax
from jax.experimental import pallas as pl
from jax.experimental.pallas import tpu as pltpu
from jax.sharding import PartitionSpec as P

BF = jnp.bfloat16
F32 = jnp.float32
MIB = 1024 * 1024
TOKEN_CHUNKS = ((256, 256), (512,))
OUT_CHUNKS = (256, 256, 256, 256)


def params(mib):
    return pltpu.CompilerParams(vmem_limit_bytes=mib * MIB)


def cost(flops, moved):
    return pl.CostEstimate(flops=int(flops), bytes_accessed=int(moved), transcendentals=0)


def swapped(x, axis, mask):
    size = lax.axis_size(axis)
    return lax.ppermute(x, axis, [(i, i ^ mask) for i in range(size)])


def shifted(x, axis, by):
    size = lax.axis_size(axis)
    return lax.ppermute(x, axis, [(i, (i + by) % size) for i in range(size)])


def after(first, *others):
    out = lax.optimization_barrier((first,) + others)[1:]
    return out[0] if len(out) == 1 else out


SMEM_SPEC = pl.BlockSpec(memory_space=pltpu.SMEM)
VMEM_SPEC = pl.BlockSpec(memory_space=pltpu.VMEM)
HBM_SPEC = pl.BlockSpec(memory_space=pltpu.HBM)


def in_hbm(x):
    return pltpu.with_memory_space_constraint(x, pltpu.HBM)


def in_vmem(*xs):
    return [pltpu.with_memory_space_constraint(x, pltpu.VMEM) for x in xs]


def holding(kernel, held):
    return (lambda *refs: kernel(*refs[len(held) :])) if held else kernel


def same_kernel(x, out):
    out[...] = x[...]


def hold(x, held):
    return pl.pallas_call(
        holding(same_kernel, held),
        out_shape=pltpu.VMEM(x.shape, x.dtype),
        in_specs=[VMEM_SPEC] * (len(held) + 1),
        out_specs=VMEM_SPEC,
        compiler_params=params(4),
        cost_estimate=cost(1e6, 1e5),
    )(*in_vmem(*held, x))


def split_kernel(starts, tokens, *refs):
    outs, sem = refs[:-1], refs[-1]
    copies = []
    for i, (low, out) in enumerate(zip(starts, outs)):
        source = tokens.at[:, low : low + out.shape[1]]
        copies.append(pltpu.make_async_copy(source, out, sem.at[i]))
        copies[-1].start()
    for copy in copies:
        copy.wait()


def split_tokens(tokens, starts, sizes):
    length = tokens.shape[0]
    return pl.pallas_call(
        functools.partial(split_kernel, starts),
        out_shape=tuple(pltpu.VMEM((length, c), BF) for c in sizes),
        in_specs=[HBM_SPEC],
        out_specs=(VMEM_SPEC,) * len(sizes),
        scratch_shapes=[pltpu.SemaphoreType.DMA((len(sizes),))],
        compiler_params=params(4),
        cost_estimate=cost(1e6, 1e5),
    )(in_hbm(tokens))


def across_tokens(w, x):
    return lax.dot_general(w, x, (((1,), (1,)), ((), ())), preferred_element_type=F32)


def row_start(place, share, owner, first):
    return pl.multiple_of((place ^ owner) * share + first, 128)


def copies_of(weights, targets, semaphores, at, place, share):
    result = []
    for i, (w, target) in enumerate(zip(weights, targets)):
        low, group = 0, []
        for p, (owner, first, count) in enumerate(at[i]):
            group.append(
                pltpu.make_async_copy(
                    w.at[pl.ds(row_start(place, share, owner, first), count)],
                    target.at[pl.ds(low, count)],
                    semaphores.at[i, p],
                )
            )
            low += count
        result.append(group)
    return result


def stage_kernel(xs_at, skips, ahead_at, share, summed, finishes, gated, info, *refs):
    refs = list(refs)
    take = lambda n: [refs.pop(0) for _ in range(n)]
    count_w = len(skips)
    xs, ws = take(len(xs_at)), take(count_w)
    gate_w = take(1)[0] if gated else None
    sums = [take(1)[0] if i in summed else None for i in range(count_w + gated)]
    outs = take(count_w + gated)
    ahead = take(2) if ahead_at else []
    held = take(count_w)
    sems = take(1)[0]
    place = info[0]
    at = [xs_at[skip:] for skip in skips]
    now = copies_of(ws, held, sems, at, place, share)
    later = copies_of(ws, ahead, take(1)[0], [ahead_at] * 2, place, share) if ahead_at else []
    for group in now + later:
        for copy in group:
            copy.start()
    if gated:
        gates = 0.0 if sums[count_w] is None else sums[count_w][...]
        for (owner, first, count), x in zip(xs_at, xs):
            gates = gates + across_tokens(
                gate_w[:, pl.ds(row_start(place, share, owner, first), count)], x[...]
            )
        outs[count_w][...] = gates
    for i in range(count_w):
        for copy in now[i]:
            copy.wait()

        def body(j, _, i=i):
            columns = pl.ds(pl.multiple_of(j * 256, 256), 256)
            total = None if sums[i] is None else sums[i][:, columns]
            low = 0
            for (_, _, count), x in zip(at[i], xs[skips[i] :]):
                part = jnp.dot(
                    x[...], held[i][low : low + count, columns], preferred_element_type=F32
                )
                total = part if total is None else total + part
                low += count
            outs[i][:, columns] = finishes[i](total).astype(outs[i].dtype)
            return 0

        lax.fori_loop(0, outs[i].shape[1] // 256, body, 0)
    for group in later:
        for copy in group:
            copy.wait()


def unchanged(x):
    return x


def twin_kernel(at, share, info, x, key_w, value_w, gate_w, *refs):
    owner, first, count = at
    for w, total, out in zip((key_w, value_w), refs[:2], refs[3:5]):
        for low in range(0, out.shape[1], 512):
            columns = slice(low, low + 512)
            part = jnp.dot(x[...], w[:count, columns], preferred_element_type=F32)
            out[:, columns] = total[:, columns] + part
    rows = gate_w[:, pl.ds(row_start(info[0], share, owner, first), count)]
    refs[5][...] = refs[2][...] + across_tokens(rows, x[...])


def twin_stage(info, x, at, key_w, value_w, gate_w, sums, share):
    return pl.pallas_call(
        functools.partial(twin_kernel, at, share),
        out_shape=tuple(pltpu.VMEM(y.shape, F32) for y in sums),
        in_specs=[SMEM_SPEC] + [VMEM_SPEC] * 7,
        out_specs=(VMEM_SPEC,) * 3,
        input_output_aliases={5 + i: i for i in range(3)},
        compiler_params=params(8),
        cost_estimate=cost(1e6, 1e5),
    )(info, *in_vmem(x, key_w, value_w), gate_w, *in_vmem(*sums))


def stage(info, xs, xs_at, weights, share, gate_w=None, sums=None, ahead_at=None, finishes=None, held=(), skips=None):
    length = xs[0].shape[0]
    count = sum(c for _, _, c in xs_at)
    gated = int(gate_w is not None)
    kinds = [F32] * len(weights) if finishes is None else [k for _, k in finishes]
    calls = [unchanged] * len(weights) if finishes is None else [f for f, _ in finishes]
    shapes = [pltpu.VMEM((length, w.shape[1]), k) for w, k in zip(weights, kinds)]
    if gated:
        shapes.append(pltpu.VMEM((gate_w.shape[0], length), F32))
    scratch = [pltpu.VMEM((count, w.shape[1]), BF) for w in weights]
    scratch.append(pltpu.SemaphoreType.DMA((len(weights), len(xs_at))))
    if ahead_at:
        rows = sum(c for _, _, c in ahead_at)
        shapes += [pltpu.VMEM((rows, w.shape[1]), BF) for w in weights[:2]]
        scratch.append(pltpu.SemaphoreType.DMA((2, len(ahead_at))))
    operands = [*in_vmem(*held), info, *in_vmem(*xs), *[in_hbm(w) for w in weights]]
    specs = [VMEM_SPEC] * len(held) + [SMEM_SPEC] + [VMEM_SPEC] * len(xs) + [HBM_SPEC] * len(weights)
    if gated:
        operands.append(gate_w)
        specs.append(VMEM_SPEC)
    aliases, summed = {}, ()
    if sums is not None:
        summed = tuple(i for i, x in enumerate(sums) if x is not None)
        if finishes is None:
            aliases = {len(operands) + n: i for n, i in enumerate(summed)}
        operands += in_vmem(*[x for x in sums if x is not None])
        specs += [VMEM_SPEC] * len(summed)
    return pl.pallas_call(
        holding(
            functools.partial(
                stage_kernel, xs_at, skips or [0] * len(weights), ahead_at, share, summed, calls,
                gated,
            ),
            held,
        ),
        out_shape=tuple(shapes),
        in_specs=specs,
        out_specs=(VMEM_SPEC,) * len(shapes),
        scratch_shapes=scratch,
        input_output_aliases=aliases,
        compiler_params=params(24),
        cost_estimate=cost(1e6, 1e5),
    )(*operands)


def segments(docs, positions):
    total = jnp.zeros_like(positions)
    bound = jnp.int32(0)
    for j in range(docs.shape[0] - 1):
        bound = bound + docs[j]
        total = total + (positions >= bound).astype(jnp.int32)
    return total


def gate_rows(both, offset, docs, bias):
    heads, length = both.shape[0] // 2, both.shape[1]
    row = lax.broadcasted_iota(jnp.int32, (heads, length), 0)
    lane = lax.broadcasted_iota(jnp.int32, (heads, length), 1)
    input_bias = jnp.zeros((heads, length), F32)
    forget_bias = jnp.zeros((heads, length), F32)
    for h in range(heads):
        input_bias = jnp.where(row == h, bias[0, h], input_bias)
        forget_bias = jnp.where(row == h, bias[1, h], forget_bias)
    input_pre = both[:heads] + input_bias
    forget = both[heads:] + forget_bias
    decay = jnp.minimum(forget, 0.0) - jnp.log1p(jnp.exp(-jnp.abs(forget)))
    step = 1
    while step < length:
        decay = decay + jnp.where(lane >= step, pltpu.roll(decay, step, 1), 0.0)
        step *= 2
    u = input_pre - decay
    segment = segments(docs, lane + offset)
    last = segments(docs, lane * 0 + (offset + length - 1))
    open_rows = segment == last
    top = jnp.max(jnp.where(open_rows, u, -jnp.inf), axis=1, keepdims=True)
    weight = jnp.where(open_rows, jnp.exp(u - top), 0.0)
    total = decay[:, length - 1 : length]
    narrow = lax.broadcasted_iota(jnp.int32, (heads, 128), 1)
    stats = jnp.where(narrow == 0, total + top, jnp.where(narrow == 1, total, 0.0))
    return u, weight, stats


def summary_kernel(xs_at, skip, share, heads, info, docs, bias, *refs):
    xs = refs[: len(xs_at)]
    key_w, value_w, gate_w, key_sum, value_sum, gate_sum = refs[len(xs_at) : len(xs_at) + 6]
    key_out, value_out, keep_out, send_out, small_out, u_out, state = refs[len(xs_at) + 6 :]
    place, side, offset = info[0], info[1], info[2]
    size, wide = state.shape
    gates = gate_sum[...]
    for (owner, first, count), x in zip(xs_at, xs):
        gates = gates + across_tokens(
            gate_w[:, pl.ds(row_start(place, share, owner, first), count)], x[...]
        )
    u, weight, stats = gate_rows(gates, offset, docs, bias)
    u_out[...] = u
    small_out[:, size:] = stats
    spare = jnp.zeros((128 - weight.shape[0], weight.shape[1]), F32)
    columns = jnp.concatenate([weight, spare], axis=0).T
    half = size // 2
    for h in range(heads):
        key_at, value_at = slice(h * size, (h + 1) * size), slice(h * wide, (h + 1) * wide)
        key, value, low = key_sum[:, key_at], value_sum[:, value_at], skip
        for x in xs:
            count = x.shape[1]
            rows = slice(low, low + count)
            key = key + jnp.dot(x[...], key_w[rows, key_at], preferred_element_type=F32)
            value = value + jnp.dot(x[...], value_w[rows, value_at], preferred_element_type=F32)
            low += count
        key = (key * size ** (-0.5)).astype(BF)
        value = value.astype(BF)
        key_out[:, key_at] = key
        value_out[:, value_at] = value
        scaled = (columns[:, h : h + 1] * key.astype(F32)).astype(BF)
        small_out[h : h + 1, :size] = jnp.sum(scaled.astype(F32), axis=0, keepdims=True)
        state[...] = lax.dot_general(
            scaled, value, (((0,), (0,)), ((), ())), preferred_element_type=F32
        )
        keep_out[h] = state[pl.ds(pl.multiple_of(side * half, half), half)].astype(BF)
        send_out[h] = state[pl.ds(pl.multiple_of((1 - side) * half, half), half)].astype(BF)


def block_summary(
    info, docs, bias, xs, xs_at, skip, key_w, value_w, gate_w, key_sum, value_sum, gates, share,
    heads,
):
    length = xs[0].shape[0]
    size, wide = key_w.shape[1] // heads, value_w.shape[1] // heads
    return pl.pallas_call(
        functools.partial(summary_kernel, xs_at, skip, share, heads),
        out_shape=(
            pltpu.VMEM((length, heads * size), BF),
            pltpu.VMEM((length, heads * wide), BF),
            pltpu.VMEM((heads, size // 2, wide), BF),
            pltpu.VMEM((heads, size // 2, wide), BF),
            pltpu.VMEM((heads, size + 128), F32),
            pltpu.VMEM((heads, length), F32),
        ),
        in_specs=[SMEM_SPEC] * 3 + [VMEM_SPEC] * (len(xs) + 6),
        out_specs=(VMEM_SPEC,) * 6,
        scratch_shapes=[pltpu.VMEM((size, wide), F32)],
        compiler_params=params(16),
        cost_estimate=cost(4e9, 4e6),
    )(info, docs, bias, *in_vmem(*xs, key_w, value_w), gate_w, *in_vmem(key_sum, value_sum, gates))


def reset_of(docs, index, length):
    first = jnp.maximum(index * length - 1, 0)
    return segments(docs, (index + 1) * length - 1) != segments(docs, first)


def pair_scales(info, docs, length, size, own, other):
    even = info[1] == 0
    first = info[2] // length - info[1]
    m_own, g_own = own[:, size : size + 1], own[:, size + 1 : size + 2]
    m_other, g_other = other[:, size : size + 1], other[:, size + 1 : size + 2]
    m_even, g_even = jnp.where(even, m_own, m_other), jnp.where(even, g_own, g_other)
    m_odd, g_odd = jnp.where(even, m_other, m_own), jnp.where(even, g_other, g_own)
    reset_odd = reset_of(docs, first + 1, length)
    m_pair = jnp.maximum(jnp.where(reset_odd, -jnp.inf, m_even + g_odd), m_odd)
    pair_even = jnp.where(reset_odd, 0.0, jnp.exp(jnp.minimum(m_even + g_odd - m_pair, 0.0)))
    pair_odd = jnp.exp(m_odd - m_pair)
    weights = jnp.where(even, pair_even, pair_odd), jnp.where(even, pair_odd, pair_even)
    return m_even, g_even, g_odd, m_pair, weights


def pair_kernel(length, info, docs, own, other, kept, got, small_out, *state_out):
    heads = own.shape[0]
    size = own.shape[1] - 128
    _, g_even, g_odd, m_pair, (w_own, w_other) = pair_scales(
        info, docs, length, size, own[...], other[...]
    )
    small_out[:, :size] = w_own * own[:, :size] + w_other * other[:, :size]
    lane = lax.broadcasted_iota(jnp.int32, (heads, 128), 1)
    small_out[:, size:] = jnp.where(
        lane == 0, m_pair, jnp.where(lane == 1, g_even + g_odd, 0.0)
    )
    for h in range(heads):
        at = slice(h, h + 1)
        state = w_own[at] * kept[h].astype(F32) + w_other[at] * got[h].astype(F32)
        state_out[h][0] = state.astype(BF)


def pair_summary(info, docs, small, small_other, kept, got, length, held):
    return pl.pallas_call(
        holding(functools.partial(pair_kernel, length), held),
        out_shape=(pltpu.VMEM(small.shape, F32),)
        + (pltpu.VMEM((1,) + kept.shape[1:], BF),) * kept.shape[0],
        in_specs=[VMEM_SPEC] * len(held) + [SMEM_SPEC] * 2 + [VMEM_SPEC] * 4,
        out_specs=(VMEM_SPEC,) * (1 + kept.shape[0]),
        compiler_params=params(4),
        cost_estimate=cost(1e6, 1e5),
    )(*in_vmem(*held), info, docs, *in_vmem(small, small_other, kept, got))


def incoming_kernel(length, reach, info, docs, own, other, kept, got, *refs):
    heads = own.shape[0]
    smalls, refs = refs[:reach], refs[reach:]
    states = [refs[k * heads : (k + 1) * heads] for k in range(reach)]
    carry, carry_norm, carry_max, own_out, other_out, norm_out, top_out, base, sem = refs[
        reach * heads :
    ]
    half = base.shape[1]
    rows = pl.ds(pl.multiple_of(info[1] * half, half), half)
    fetch = pltpu.make_async_copy(carry.at[:, rows], base, sem)
    fetch.start()
    size = own.shape[1] - 128
    side = info[1]
    even = side == 0
    first = info[2] // length - side
    m_even, g_even, _, _, _ = pair_scales(info, docs, length, size, own[...], other[...])
    reset_even = reset_of(docs, first, length)
    expos = []
    passed = jnp.zeros((heads, 1), F32)
    unbroken = jnp.bool_(True)
    for k in range(1, reach + 1):
        there = first >= 2 * k
        index = jnp.maximum(first - 2 * k, 0)
        m_k, g_k = smalls[k - 1][:, size : size + 1], smalls[k - 1][:, size + 1 : size + 2]
        expos.append(jnp.where(there & unbroken, m_k + passed, -jnp.inf))
        passed = passed + jnp.where(there, g_k, 0.0)
        broken = reset_of(docs, index, length) | reset_of(docs, index + 1, length)
        unbroken = unbroken & ~(there & broken)
    in_reach = (first <= 2 * reach) & unbroken
    expos.append(jnp.where(in_reach, carry_max[...] + passed, -jnp.inf))
    top_even = functools.reduce(jnp.maximum, expos)
    expos_odd = [jnp.where(reset_even, -jnp.inf, e + g_even) for e in expos]
    top_odd = functools.reduce(jnp.maximum, expos_odd, m_even)
    w_even = [jnp.exp(e - top_even) for e in expos]
    w_odd = [jnp.exp(e - top_odd) for e in expos_odd]
    direct = jnp.exp(m_even - top_odd)
    w_own = [jnp.where(even, a, b) for a, b in zip(w_even, w_odd)]
    w_other = [jnp.where(even, b, a) for a, b in zip(w_even, w_odd)]
    direct_own = jnp.where(even, 0.0, direct)
    direct_other = jnp.where(even, direct, 0.0)
    top_out[...] = jnp.where(even, top_even, top_odd) + jnp.zeros((heads, 128), F32)
    norm = direct_own * jnp.where(even, own[:, :size], other[:, :size])
    norm = norm + w_own[reach] * carry_norm[...]
    for k in range(reach):
        norm = norm + w_own[k] * smalls[k][:, :size]
    norm_out[...] = norm
    fetch.wait()
    for h in range(heads):
        at = slice(h, h + 1)
        here = jnp.where(even, kept[h].astype(F32), got[h].astype(F32))
        mine = w_own[reach][at] * base[h] + direct_own[at] * here
        theirs = w_other[reach][at] * base[h] + direct_other[at] * here
        for k in range(reach):
            state = states[k][h][0].astype(F32)
            mine = mine + w_own[k][at] * state
            theirs = theirs + w_other[k][at] * state
        own_out[h] = mine.astype(BF)
        other_out[h] = theirs.astype(BF)


def incoming_state(
    info, docs, small, small_other, kept, got, smalls, states, carry, carry_norm, carry_max, length,
    held,
):
    heads = small.shape[0]
    return pl.pallas_call(
        holding(functools.partial(incoming_kernel, length, len(smalls)), held),
        out_shape=(
            pltpu.VMEM(kept.shape, BF),
            pltpu.VMEM(kept.shape, BF),
            pltpu.VMEM(carry_norm.shape, F32),
            pltpu.VMEM((heads, 128), F32),
        ),
        in_specs=[VMEM_SPEC] * len(held)
        + [SMEM_SPEC] * 2
        + [VMEM_SPEC] * (4 + (1 + heads) * len(smalls))
        + [HBM_SPEC, VMEM_SPEC, VMEM_SPEC],
        out_specs=(VMEM_SPEC,) * 4,
        scratch_shapes=[pltpu.VMEM(kept.shape, F32), pltpu.SemaphoreType.DMA],
        compiler_params=params(6),
        cost_estimate=cost(1e6, 1e5),
    )(
        *in_vmem(*held), info, docs,
        *in_vmem(small, small_other, kept, got, *smalls, *sum(states, [])),
        in_hbm(carry), carry_norm, carry_max[:, None],
    )


def inner_kernel(
    heads, info, docs, top_in, query, key, value, u, norm, gate, w_out,
    base_out, slope_out, w_here, sem,
):
    fetch = pltpu.make_async_copy(w_out, w_here, sem)
    fetch.start()
    length = query.shape[0]
    size, wide = query.shape[1] // heads, value.shape[1] // heads
    offset = info[2]
    chunk = 128
    one = jnp.zeros((chunk, 1), jnp.int32)
    before = segments(docs, one + jnp.maximum(offset - 1, 0))
    for head in range(heads):
        keys_at = slice(head * size, (head + 1) * size)
        values_at = slice(head * wide, (head + 1) * wide)
        u_row = u[head : head + 1, :]
        norm_row = norm[head : head + 1, :]
        top = top_in[head : head + 1, 0:1]
        for low in range(0, length, chunk):
            high = low + chunk
            position_t = lax.broadcasted_iota(jnp.int32, (chunk, 1), 0) + low
            position_s = lax.broadcasted_iota(jnp.int32, (1, high), 1)
            segment_t = segments(docs, position_t + offset)
            segment_s = segments(docs, position_s + offset)
            allowed = (position_s <= position_t) & (segment_s == segment_t)
            expo = jnp.where(allowed, u_row[:, :high], -jnp.inf)
            peak = jnp.max(expo, axis=1, keepdims=True)
            q = query[low:high, keys_at]
            scores = lax.dot_general(
                q, key[:high, keys_at], (((1,), (1,)), ((), ())), preferred_element_type=F32
            )
            weighted = jnp.exp(expo - peak) * scores
            num = jnp.dot(
                weighted.astype(BF), value[:high, values_at], preferred_element_type=F32
            )
            den = jnp.sum(weighted, axis=1, keepdims=True)
            carried = segment_t == before
            ceiling = jnp.where(carried, jnp.maximum(peak, top), peak)
            inner_weight = jnp.exp(peak - ceiling)
            outer_weight = jnp.where(carried, jnp.exp(jnp.minimum(top - ceiling, 0.0)), 0.0)
            outer_den = jnp.sum(q.astype(F32) * norm_row, axis=1, keepdims=True)
            full = inner_weight * den + outer_weight * outer_den
            inverse = 1.0 / jnp.maximum(jnp.abs(full), 1.0)
            g = gate[low:high, values_at]
            base_out[low:high, values_at] = g * (num * (inner_weight * inverse))
            slope_out[low:high, values_at] = g * (outer_weight * inverse)
    fetch.wait()


def inner(info, docs, top, query, key, value, u, norm, gate, w_out, heads):
    length, depth = value.shape
    return pl.pallas_call(
        functools.partial(inner_kernel, heads),
        out_shape=(
            pltpu.VMEM((length, depth), F32),
            pltpu.VMEM((length, depth), F32),
            pltpu.VMEM(w_out.shape, BF),
        ),
        in_specs=[SMEM_SPEC] * 2 + [VMEM_SPEC] * 7 + [HBM_SPEC],
        out_specs=(VMEM_SPEC,) * 3,
        scratch_shapes=[pltpu.SemaphoreType.DMA],
        compiler_params=params(12),
        cost_estimate=cost(1e6, 1e5),
    )(info, docs, *in_vmem(top, query, key, value, u, norm, gate), in_hbm(w_out))


def some_columns(info, hidden, w, out, owners, start):
    share = w.shape[1] // 4
    wide = out.shape[1] // 2
    for step, owner in enumerate(owners):
        columns = pl.ds(pl.multiple_of((info[0] ^ owner) * share + start, 128), wide)
        part = jnp.dot(hidden[...], w[:, columns], preferred_element_type=F32)
        out[:, step * wide : (step + 1) * wide] = part.astype(BF)


def hidden_kernel(heads, info, query, own, other, base, slope, w, hidden, send, state):
    half = own.shape[1]
    side = info[1]
    size, wide = 2 * half, own.shape[2]
    for h in range(heads):
        state[pl.ds(pl.multiple_of(side * half, half), half)] = own[h]
        state[pl.ds(pl.multiple_of((1 - side) * half, half), half)] = other[h]
        outer = jnp.dot(
            query[:, h * size : (h + 1) * size], state[...], preferred_element_type=F32
        )
        columns = slice(h * wide, (h + 1) * wide)
        hidden[:, columns] = (base[:, columns] + slope[:, columns] * outer).astype(BF)
    some_columns(info, hidden, w, send, (1, 3), 0)


def hidden_and_first(info, query, own, other, base, slope, w_here, wide, heads):
    length, depth = base.shape
    return pl.pallas_call(
        functools.partial(hidden_kernel, heads),
        out_shape=(pltpu.VMEM((length, depth), BF), pltpu.VMEM((length, 2 * wide), BF)),
        in_specs=[SMEM_SPEC] + [VMEM_SPEC] * 6,
        out_specs=(VMEM_SPEC,) * 2,
        scratch_shapes=[pltpu.VMEM((2 * own.shape[1], own.shape[2]), BF)],
        compiler_params=params(12),
        cost_estimate=cost(3e9, 8e6),
    )(info, *in_vmem(query, own, other, base, slope, w_here))


def columns_kernel(start, following, info, hidden, w, keep, *send):
    if send:
        some_columns(info, hidden, w, send[0], (1, 3), following)
    some_columns(info, hidden, w, keep, (0, 2), start)


def next_columns(info, hidden, w_here, start, wide, following):
    length = hidden.shape[0]
    shapes = [pltpu.VMEM((length, 2 * wide), BF)]
    if following:
        shapes.append(pltpu.VMEM((length, 2 * following), BF))
    return pl.pallas_call(
        functools.partial(columns_kernel, start, start + wide),
        out_shape=tuple(shapes),
        in_specs=[SMEM_SPEC, VMEM_SPEC, VMEM_SPEC],
        out_specs=(VMEM_SPEC,) * len(shapes),
        compiler_params=params(12),
        cost_estimate=cost(1e6, 1e5),
    )(info, *in_vmem(hidden, w_here))


def local(
    tokens,
    w_query,
    w_key,
    w_value,
    w_outgate,
    w_gates,
    gate_bias,
    w_out,
    carry_matrix,
    carry_norm,
    carry_max,
    doc_lengths,
):
    length, share = tokens.shape
    heads = gate_bias.shape[1]
    size = w_query.shape[1] // heads
    place = lax.axis_index("tensor")
    block = lax.axis_index("seq")
    blocks = lax.axis_size("seq")
    offset = (block * length).astype(jnp.int32)
    tensor = lambda x, mask: swapped(x, "tensor", mask)
    pair = lambda x: swapped(x, "seq", 1)
    down = lambda x: shifted(x, "seq", 2)

    beside = tensor(tokens, 1)
    sizes = [c for chunks in TOKEN_CHUNKS for c in chunks]
    starts = [sum(sizes[:i]) for i in range(len(sizes))]
    first = split_tokens(tokens, starts[:1], sizes[:1])
    others = split_tokens(after(beside, tokens), starts[1:], sizes[1:])
    pieces = [*first, *others]
    source = tokens
    pieces = [(s, c, tensor(x, 2)) for s, c, x in zip(starts, sizes, pieces)]
    groups = []
    for chunks in TOKEN_CHUNKS:
        groups.append(pieces[: len(chunks)])
        pieces = pieces[len(chunks) :]
    gate_w = w_gates.transpose(0, 2, 1).reshape(2 * heads, 4 * share)

    side = (block % 2).astype(jnp.int32)
    info = jnp.stack([place, side, offset]).astype(jnp.int32)
    at = [[(o, s, c) for s, c, _ in group for o in (2, 3)] for group in groups]
    near_at = [(0, 0, share), (1, 0, share)]
    first_three = (w_key, w_value, w_query)
    sums = stage(info, [source, beside], near_at, first_three, share, gate_w)
    far = []
    for i, group in enumerate(groups):
        xs = lax.optimization_barrier((*[x for _, _, x in group], *sums))
        xs, sums = xs[: len(group)], xs[len(group) :]
        if i == 0:
            sums = [*sums[:3], None, sums[3]]
        xs = [y for x in xs for y in (x, tensor(x, 1))]
        far.append(xs)
        if i < len(groups) - 1:
            last = i == len(groups) - 2
            out = stage(
                info, xs, at[i], (*first_three, w_outgate), share, gate_w, sums,
                at[-1] if last else None,
            )
            sums = out[:5]
            if last:
                w_key_last, w_value_last = out[5:]
    kv_sums = twin_stage(
        info, xs[0], at[-1][0], w_key_last, w_value_last, gate_w, (*sums[:2], sums[4]), share
    )
    keys, values, kept, sent, small, u = block_summary(
        info, doc_lengths, gate_bias, xs[1:], at[-1][1:], at[-1][0][2], w_key_last, w_value_last,
        gate_w, *kv_sums, share, heads,
    )

    small_other = pair(small)
    got = pair(sent)
    held = (keys, values, kept, u)
    now_xs = after(keys, beside, *far[-1])
    queries, *gate = stage(
        info, now_xs, near_at[1:] + at[-1], (w_query, w_outgate), share, None, [sums[2], sums[3]],
        finishes=((unchanged, BF), (unchanged, F32)), held=held, skips=[1, 0],
    )
    small_other, got, queries, *gate = lax.optimization_barrier(
        (small_other, got, queries, *gate)
    )
    travel, *state_pair = pair_summary(
        info, doc_lengths, small, small_other, kept, got, length, (keys, values, queries, u)
    )
    smalls, states = [], []
    held = (keys, values, kept, got, queries, u)
    for step in range(blocks // 4):
        before = state_pair[0]
        first = down(state_pair[0])
        travel = down(travel)
        state_pair = [first] + [down(x) for x in state_pair[1:]]
        if step == 0:
            small_here = hold(after(before, small), (*held, *gate))
            travel, first, small = lax.optimization_barrier((travel, state_pair[0], small_here))
            state_pair[0] = first
        elif step == 1:
            near_xs = [after(before, source)]
            gate = stage(
                info, near_xs, near_at[:1], (w_outgate,), share, None, gate,
                finishes=((jax.nn.sigmoid, F32),), held=held,
            )
            travel, *rest = lax.optimization_barrier((travel, *gate, *state_pair))
            gate, state_pair = rest[:1], rest[1:]
        smalls.append(travel)
        states.append(state_pair)
    (gate,) = gate
    state_own, state_other, norm_in, top_own = incoming_state(
        info, doc_lengths, small, small_other, kept, got, smalls, states,
        carry_matrix, carry_norm, carry_max, length, (keys, values, queries, gate, u),
    )
    state_got = pair(state_other)
    base, slope, w_here = inner(
        info, doc_lengths, top_own, queries, keys, values, u, norm_in, gate, w_out, heads
    )

    hidden, send = hidden_and_first(
        info, queries, state_own, state_got, base, slope, w_here, OUT_CHUNKS[0], heads
    )
    start = 0
    leaving, arriving = [], []
    for wide, following in zip(OUT_CHUNKS, OUT_CHUNKS[1:] + (0,)):
        came = tensor(send, 1)
        now = after(leaving[max(len(leaving) - 1, 0)], hidden) if leaving else hidden
        keep, *send = next_columns(info, now, w_here, start, wide, following)
        send = send[0] if send else None
        both = keep.astype(F32) + came.astype(F32)
        leaving.append(both[:, wide:].astype(BF))
        arriving.append((start, wide, both[:, :wide], tensor(leaving[-1], 2)))
        start += wide
    out = source
    for start, wide, both, came in arriving[:-1]:
        columns = source[:, start : start + wide].astype(F32) + (both + came.astype(F32))
        out = lax.dynamic_update_slice(out, columns.astype(BF), (0, start))
    start, wide, both, came = arriving[-1]
    columns = source[:, start : start + wide].astype(F32) + (both + came.astype(F32))
    return lax.dynamic_update_slice(out, columns.astype(BF), (0, start))


FULL_ACCURACY = lax.Precision.HIGHEST


def plain_shifted(x, axis, by):
    devices = lax.axis_size(axis)
    pairs = [(i, i + by) for i in range(devices) if 0 <= i + by < devices]
    return lax.ppermute(x, axis, pairs)


def segment_of(doc_lengths, positions):
    bounds = jnp.cumsum(doc_lengths)[:-1]
    return jnp.sum((positions[:, None] >= bounds[None, :]).astype(jnp.int32), axis=1)


def combine(earlier, later):
    early_c, early_n, early_m, early_g, early_r = earlier
    late_c, late_n, late_m, late_g, late_r = later
    ceiling = jnp.maximum(early_m + late_g, late_m)
    early_weight = jnp.exp(early_m + late_g - ceiling)
    late_weight = jnp.exp(late_m - ceiling)
    reset_mask = late_r > 0.5
    merged_c = jnp.where(
        reset_mask[:, None, None],
        late_c,
        early_weight[:, None, None] * early_c + late_weight[:, None, None] * late_c,
    )
    merged_n = jnp.where(
        reset_mask[:, None], late_n, early_weight[:, None] * early_n + late_weight[:, None] * late_n
    )
    merged_m = jnp.where(reset_mask, late_m, ceiling)
    return (merged_c, merged_n, merged_m, late_g, jnp.maximum(early_r, late_r))


def block_local(queries, keys, value_rows, input_pre, log_forget, segment, segment_before):
    length = segment.shape[0]
    log_decay = jnp.cumsum(log_forget, axis=0)
    position = jnp.arange(length)
    allowed = (position[:, None] >= position[None, :]) & (segment[:, None] == segment[None, :])
    exponent = log_decay.T[:, :, None] - log_decay.T[:, None, :] + input_pre.T[:, None, :]
    exponent = jnp.where(allowed[None], exponent, -jnp.inf)
    inner_max = jnp.max(exponent, axis=2)
    scores = jnp.einsum("lhk,mhk->hlm", queries, keys, preferred_element_type=jnp.float32)
    weighted = jnp.exp(exponent - inner_max[:, :, None]) * scores
    weighted_bf = weighted.astype(jnp.bfloat16)
    inner_num = jnp.einsum(
        "hlm,mhv->lhv", weighted_bf, value_rows, preferred_element_type=jnp.float32
    )
    inner_den = jnp.sum(weighted, axis=2).T
    in_last = segment == segment[-1]
    tail_expo = log_decay[-1][None, :] - log_decay + input_pre
    tail_expo = jnp.where(in_last[:, None], tail_expo, -jnp.inf)
    tail_max = jnp.max(tail_expo, axis=0)
    key_scaled_rows = (jnp.exp(tail_expo - tail_max[None, :])[:, :, None] * keys).astype(
        jnp.bfloat16
    )
    cell_state_matrix = jnp.einsum(
        "emn,emp->mnp", key_scaled_rows, value_rows, preferred_element_type=jnp.float32
    )
    state_n = jnp.sum(key_scaled_rows.astype(jnp.float32), axis=0)
    reset = (segment[-1] != segment_before).astype(jnp.float32) * jnp.ones_like(tail_max)
    summary = (cell_state_matrix, state_n, tail_max, log_decay[-1], reset)
    return (log_decay, inner_max.T, inner_num, inner_den, summary)


def block_output(
    queries, log_decay, inner_max, inner_num, inner_den, segment, segment_before, incoming
):
    cell_state_matrix, state_n, state_m = incoming
    outer = jnp.where((segment == segment_before)[:, None], log_decay + state_m[None, :], -jnp.inf)
    ceiling = jnp.maximum(inner_max, outer)
    inner_weight = jnp.exp(inner_max - ceiling)
    outer_weight = jnp.exp(outer - ceiling)
    query_single = queries.astype(jnp.float32)
    outer_numerator_sum = jnp.einsum(
        "ciy,iyo->cio", query_single, cell_state_matrix, precision=FULL_ACCURACY
    )
    outer_den = jnp.einsum("lhk,hk->lh", query_single, state_n, precision=FULL_ACCURACY)
    numerator = (
        inner_weight[:, :, None] * inner_num + outer_weight[:, :, None] * outer_numerator_sum
    )
    denominator = inner_weight * inner_den + outer_weight * outer_den
    return numerator / jnp.maximum(jnp.abs(denominator), 1.0)[:, :, None]


def plain_local(
    tokens,
    w_query,
    w_key,
    w_value,
    w_outgate,
    w_gates,
    gate_bias,
    w_out,
    carry_matrix,
    carry_norm,
    carry_max,
    doc_lengths,
):
    length = tokens.shape[0]
    head_count = gate_bias.shape[1]
    query_size = w_query.shape[1] // head_count
    value_size = w_value.shape[1] // head_count
    matrices = (w_query, w_key, w_value, w_outgate)
    zero_init = tuple((jnp.zeros((length, matrix.shape[1]), jnp.float32) for matrix in matrices))
    zero_init = zero_init + (
        jnp.zeros((length, head_count), jnp.float32),
        jnp.zeros((length, head_count), jnp.float32),
    )
    column_block = lax.all_gather(tokens, "tensor", axis=1, tiled=True)
    updated = tuple(
        (jnp.dot(column_block, matrix, preferred_element_type=jnp.float32) for matrix in matrices)
    )
    input_sum = jnp.dot(column_block, w_gates[0], preferred_element_type=jnp.float32)
    forget_sum = jnp.dot(column_block, w_gates[1], preferred_element_type=jnp.float32)
    projected = updated + (input_sum, forget_sum)
    queries = projected[0].astype(jnp.bfloat16).reshape(length, head_count, query_size)
    keys = (
        (projected[1] * query_size ** (-0.5))
        .astype(jnp.bfloat16)
        .reshape(length, head_count, query_size)
    )
    value_rows = projected[2].astype(jnp.bfloat16).reshape(length, head_count, value_size)
    outgate = jax.nn.sigmoid(projected[3])
    input_pre = projected[4] + gate_bias[0][None, :]
    log_forget = jax.nn.log_sigmoid(projected[5] + gate_bias[1][None, :])
    offset = lax.axis_index("seq") * length
    positions = offset + jnp.arange(length, dtype=jnp.int32)
    segment = segment_of(doc_lengths, positions)
    segment_before = segment_of(doc_lengths, jnp.maximum(offset - 1, 0)[None])[0]
    log_decay, inner_max, inner_num, inner_den, summary = block_local(
        queries, keys, value_rows, input_pre, log_forget, segment, segment_before
    )
    start_state = (carry_matrix, carry_norm, carry_max)
    zero_heads = jnp.zeros((head_count,), jnp.float32)
    is_leader = lax.axis_index("seq") == 0

    def relay(iteration, current):
        leaving = combine(current + (zero_heads, zero_heads), summary)[:3]
        arrived = plain_shifted(leaving, "seq", 1)
        return tuple(
            (
                jnp.where(is_leader, initial, received)
                for initial, received in zip(start_state, arrived)
            )
        )

    incoming = lax.fori_loop(0, lax.axis_size("seq") - 1, relay, start_state)
    mixed_heads = block_output(
        queries, log_decay, inner_max, inner_num, inner_den, segment, segment_before, incoming
    )
    hidden = (outgate * mixed_heads.reshape(length, head_count * value_size)).astype(jnp.bfloat16)
    partial_value = jnp.dot(hidden, w_out, preferred_element_type=jnp.float32)
    summed = lax.psum_scatter(
        partial_value.astype(jnp.bfloat16), "tensor", scatter_dimension=1, tiled=True
    ).astype(jnp.float32)
    return (tokens.astype(jnp.float32) + summed).astype(jnp.bfloat16)


def solution(mesh):
    fast = mesh.shape["tensor"] == 4 and mesh.shape["seq"] == 8
    return jax.shard_map(
        local if fast else plain_local,
        mesh=mesh,
        in_specs=(
            P("seq", "tensor"),
            P(None, "tensor"),
            P(None, "tensor"),
            P(None, "tensor"),
            P(None, "tensor"),
            P(None, None, "tensor"),
            P(None, "tensor"),
            P("tensor", None),
            P("tensor", None, None),
            P("tensor", None),
            P("tensor"),
            P(),
        ),
        out_specs=P("seq", "tensor"),
        check_vma=False,
    )
```
